32 devices in a mesh: dp: 4 (over z), row: 4 (over x, core), col: 2 (over y).
Axes of the slice: x: 2, y: 2, z: 4, core: 2. Of those that a mesh axis runs over, the one named last changes fastest.
Arguments:
- tokens: bfloat16 [8192, 1024], P('dp', 'row'), may hold values from -6 to 6
- segments: int32 [8192], P('dp'), may hold values from 0 to 31, as said below
- norm_gain: bfloat16 [2, 2, 1024], P(None, None, 'row'), may hold values from 0.5 to 1.5
- norm_shift: bfloat16 [2, 2, 1024], P(None, None, 'row'), may hold values from -3 to 3
- triple_weight: bfloat16 [2, 1024, 3, 1024], P(None, 'row', None, 'col')
- triple_bias: bfloat16 [2, 2, 1024], P(None, None, ('col', 'row')), may hold values from -3 to 3
- output_weight: bfloat16 [2, 1024, 1024], P(None, 'col', 'row'), may hold values from -1 to 1
- output_bias: bfloat16 [2, 1024], P(None, 'row'), may hold values from -3 to 3
- up_weight: bfloat16 [2, 1024, 4096], P(None, 'row', 'col')
- up_bias: bfloat16 [2, 4096], P(None, ('col', 'row')), may hold values from -3 to 3
- down_weight: bfloat16 [2, 4096, 1024], P(None, 'col', 'row'), may hold values from -0.09375 to 0.09375
- down_bias: bfloat16 [2, 1024], P(None, 'row'), may hold values from -3 to 3
- cotangent: bfloat16 [8192, 1024], P('dp', 'row'), may hold values from -6 to 6
Outputs:
- result: bfloat16 [8192, 1024], P('dp', 'row')
- input_grad: float32 [8192, 1024], P('dp', 'row')
- gain_grad: float32 [2, 2, 1024], P(None, None, 'row')
- shift_grad: float32 [2, 2, 1024], P(None, None, 'row')
- triple_grad: float32 [2, 1024, 3, 1024], P(None, 'row', None, 'col')
- triple_bias_grad: float32 [2, 2, 1024], P(None, None, ('col', 'row'))
- output_grad: float32 [2, 1024, 1024], P(None, 'col', 'row')
- output_bias_grad: float32 [2, 1024], P(None, 'row')
- up_grad: float32 [2, 1024, 4096], P(None, 'row', 'col')
- up_bias_grad: float32 [2, 4096], P(None, ('col', 'row'))
- down_grad: float32 [2, 4096, 1024], P(None, 'col', 'row')
- down_bias_grad: float32 [2, 1024], P(None, 'row')
The draws below stay inside these ranges and needn't reach their ends.
Inputs may be any that keep to these rules, and one draw needn't show every extreme that they name: `segments`: segment numbers never fall along the tokens; every pack of 1024 tokens holds exactly 4 documents, the first starting at the pack's first token, so no number spans two packs.
All inputs are finite; a program needn't handle non-finite values.
Results may differ from the reference program's by a relative error of at most 0.019.
Values may be sent and summed in bfloat16 or wider, within the bound.
A program may use at most 192 MiB of HBM per device.

```python
import math
import jax
import jax.numpy as jnp
from jax import lax

D = 1024
HEADS = 16
HD = 64
FF = 4096
LAYERS = 2
LEN = 1024
TOKENS = 8192


def draw_segments(key, part):
    pack_count = TOKENS // LEN
    pack_keys = jax.random.split(key, pack_count)

    def one_pack(pack_key):
        chosen = jax.random.permutation(pack_key, LEN - 1)[:3] + 1
        return jnp.zeros((LEN,), jnp.int32).at[chosen].set(1).at[0].set(1)
    starts = jax.vmap(one_pack)(pack_keys).reshape(TOKENS)
    return (jnp.cumsum(starts) - 1).astype(jnp.int32)


def shared_mean(key, full_shape, common_shape, fan_in):
    jitter_key = jax.random.fold_in(key, 17)
    common_key = jax.random.fold_in(key, 29)
    jitter = jax.random.normal(jitter_key, full_shape, jnp.float32)
    common = 0.5 * jax.random.normal(common_key, common_shape, jnp.float32)
    return ((jitter + common) * fan_in ** (-0.5)).astype(jnp.bfloat16)


def draw_triple_weight(key, part):
    return shared_mean(key, (LAYERS, D, 3, D), (LAYERS, 1, 3, D), D)


def draw_up_weight(key, part):
    return shared_mean(key, (LAYERS, D, FF), (LAYERS, 1, FF), D)


def block_scale(rng, dims, shards, low, high):
    loudness, own = 1.0, jax.random.fold_in(rng, 6)
    for dim, parts in shards:
        heights = jnp.exp(jax.random.uniform(jax.random.fold_in(own, dim), (parts,), jnp.float32, low / len(shards), high / len(shards)))
        loudness = loudness * jnp.repeat(heights, dims[dim] // parts).reshape([-1 if axis == dim else 1 for axis in range(len(dims))])
    return loudness


def centred(stream_key, shape, width, bound, cuts=(), held_as=jnp.bfloat16):
    level = block_scale(stream_key, shape, cuts, -0.22, 0.18) if cuts else 1.0
    array = jax.random.normal(stream_key, shape, jnp.float32) * width * level
    return jnp.minimum(jnp.maximum(array, -bound), bound).astype(held_as)


def setup_inputs(seed: int = 0) -> dict:
    keys = jax.random.split(jax.random.key(seed), 14)
    tokens = centred(keys[0], (TOKENS, D), 1.0, 6.0, ((0, 4), (1, 4)))
    segments = draw_segments(jax.random.fold_in(keys[13], 71), 0)
    norm_gain = jnp.clip(1.0 + 0.1 * jax.random.normal(keys[2], (LAYERS, 2, D), jnp.float32), 0.5, 1.5).astype(jnp.bfloat16)
    norm_shift = centred(keys[3], (LAYERS, 2, D), 0.5, 3.0, ((2, 4),))
    triple_weight = draw_triple_weight(jax.random.fold_in(keys[13], 71), 0)
    triple_bias = centred(keys[5], (LAYERS, 2, D), 0.5, 3.0, ((2, 8),))
    output_weight = centred(keys[6], (LAYERS, D, D), (D // 32) ** -0.5, 1.0, ((1, 2), (2, 4)))
    output_bias = centred(keys[7], (LAYERS, D), 0.5, 3.0, ((1, 4),))
    up_weight = draw_up_weight(jax.random.fold_in(keys[13], 71), 0)
    up_bias = centred(keys[9], (LAYERS, FF), 0.5, 3.0, ((1, 8),))
    down_weight = centred(keys[10], (LAYERS, FF, D), FF ** -0.5, 0.09375, ((1, 2), (2, 4)))
    down_bias = centred(keys[11], (LAYERS, D), 0.5, 3.0, ((1, 4),))
    cotangent = centred(keys[12], (TOKENS, D), 1.0, 6.0, ((0, 4), (1, 4)))
    return {"tokens": tokens, "segments": segments, "norm_gain": norm_gain, "norm_shift": norm_shift, "triple_weight": triple_weight, "triple_bias": triple_bias, "output_weight": output_weight, "output_bias": output_bias, "up_weight": up_weight, "up_bias": up_bias, "down_weight": down_weight, "down_bias": down_bias, "cotangent": cotangent}


eps = 1e-05
masked = -1000000000.0
highest = lax.Precision.HIGHEST

@jax.custom_vjp
def low(v):
    return lax.optimization_barrier(v.astype(jnp.bfloat16)).astype(jnp.float32)

@jax.custom_vjp
def low_back(v):
    return v

def low_keep(v):
    return (low(v), None)

def low_pass(kept, grad):
    return (grad,)

def back_keep(v):
    return (v, None)

def back_low(kept, grad):
    return (low(grad),)
low.defvjp(low_keep, low_pass)
low_back.defvjp(back_keep, back_low)

def matmul(left, right):
    return jnp.dot(left, right, precision=highest)

def norm(stream, gain, shift):
    center = lax.optimization_barrier(jnp.mean(stream, axis=-1, keepdims=True))
    second = lax.optimization_barrier(jnp.mean(stream * stream, axis=-1, keepdims=True)) - center * center
    return (stream - center) * lax.rsqrt(second + eps) * gain + shift

def attend_pack(queries, key_rows, value_rows, seg_pack):
    scale = 1.0 / math.sqrt(HD)
    scores = low_back(jnp.einsum('qhd,khd->hqk', queries, key_rows, precision=highest) * scale)
    position = jnp.arange(LEN)
    allowed = (seg_pack[:, None] == seg_pack[None, :]) & (position[None, :] <= position[:, None])
    scores = jnp.where(allowed[None], scores, masked)
    chances = low(jax.nn.softmax(scores, axis=-1))
    return jnp.einsum('hqk,khd->qhd', chances, value_rows, precision=highest)

def layer(stream, seg_group, params):
    gain, shift, triple_w, triple_b, output_w, output_b, up_w, up_b, down_w, down_b = params
    length = stream.shape[0]
    attn_in = low(norm(stream, gain[0], shift[0]))
    triple = jnp.einsum('td,dke->tke', attn_in, triple_w, precision=highest)
    bias_rows = jnp.stack([triple_b[0], jnp.zeros_like(triple_b[0]), triple_b[1]])
    triple = triple + bias_rows
    queries = low(low_back(triple[:, 0]))
    key_rows = low(low_back(triple[:, 1]))
    value_rows = low(low_back(triple[:, 2]))
    count = length // LEN
    mixed = lax.map(jax.checkpoint(lambda pieces: attend_pack(pieces[0], pieces[1], pieces[2], pieces[3])), (queries.reshape(count, LEN, HEADS, HD), key_rows.reshape(count, LEN, HEADS, HD), value_rows.reshape(count, LEN, HEADS, HD), seg_group.reshape(count, LEN)))
    mixed = low(low_back(mixed.reshape(length, D)))
    middle = stream + low_back(matmul(mixed, output_w) + output_b)
    mlp_in = low(norm(middle, gain[1], shift[1]))
    hidden_pre = low_back(matmul(mlp_in, up_w) + up_b)
    active = low(jax.nn.gelu(hidden_pre, approximate=True))
    return middle + low_back(matmul(active, down_w) + down_b)

def reference(tokens, segments, norm_gain, norm_shift, triple_weight, triple_bias, output_weight, output_bias, up_weight, up_bias, down_weight, down_bias, cotangent):
    params = tuple((arr.astype(jnp.float32) for arr in (norm_gain, norm_shift, triple_weight, triple_bias, output_weight, output_bias, up_weight, up_bias, down_weight, down_bias)))
    group = math.gcd(TOKENS, 4096)
    count = TOKENS // group
    streams = tokens.astype(jnp.float32).reshape(count, group, D)
    cotangents = cotangent.astype(jnp.float32).reshape(count, group, D)
    seg_groups = segments.reshape(count, group)

    def forward(weights, stream, seg_group):
        for layer_id in range(LAYERS):
            stream = layer(stream, seg_group, tuple((arr[layer_id] for arr in weights)))
        return stream

    def one_group(totals, pieces):
        stream, seg_group, grad_out = pieces
        final, pull = jax.vjp(lambda weights, start: forward(weights, start, seg_group), params, stream)
        weight_grads, start_grad = pull(grad_out)
        totals = jax.tree.map(lambda left, right: left + right, totals, weight_grads)
        return (totals, (final.astype(jnp.bfloat16), start_grad))
    totals, (finals, start_grads) = lax.scan(one_group, jax.tree.map(jnp.zeros_like, params), (streams, seg_groups, cotangents))
    return (finals.reshape(TOKENS, D), start_grads.reshape(TOKENS, D), totals[0], totals[1], totals[2], totals[3], totals[4], totals[5], totals[6], totals[7], totals[8], totals[9])
```

```python
import math

import jax
import jax.numpy as jnp
from jax import lax
from jax.experimental import pallas as pl
from jax.experimental.pallas import tpu as pltpu
from jax.sharding import PartitionSpec as P

D = 1024
HD = 64
LAYERS = 2
LEN = 1024


eps = 1e-05
masked = -1000000000.0


def norm_forward(stream, gain, shift):
    totals = lax.psum((jnp.sum(stream, axis=1), jnp.sum(stream * stream, axis=1)), "row")
    center = totals[0] / D
    second = totals[1] / D - center * center
    inv_std = lax.rsqrt(second + eps)
    normed = (stream - center[:, None]) * inv_std[:, None]
    return (normed, inv_std, normed * gain + shift)


def norm_backward(grad_out, normed, inv_std, gain):
    scaled = grad_out * gain
    totals = lax.psum((jnp.sum(scaled, axis=1), jnp.sum(scaled * normed, axis=1)), "row")
    grad_in = inv_std[:, None] * (
        scaled - totals[0][:, None] / D - normed * (totals[1][:, None] / D)
    )
    return (grad_in, jnp.sum(grad_out * normed, axis=0), jnp.sum(grad_out, axis=0))


def gather_rows(block):
    return lax.all_gather(block, "row", axis=1, tiled=True)


def col_total(partial_sums):
    return lax.psum(partial_sums, "col")


def rows_back(partial_sums):
    return lax.psum_scatter(
        partial_sums.astype(jnp.bfloat16), "row", scatter_dimension=1, tiled=True
    ).astype(jnp.float32)


def in_parts(partial_sums):
    return lax.psum_scatter(partial_sums, "row", scatter_dimension=2, tiled=True)


def grad_gather(block):
    return lax.all_gather(block, "row", axis=2, tiled=True)


def pack_scores(queries, key_rows, seg_pack, scale):
    position = jnp.arange(queries.shape[0])
    allowed = (seg_pack[:, None] == seg_pack[None, :]) & (position[None, :] <= position[:, None])
    scores = (
        jnp.einsum("qhd,khd->hqk", queries, key_rows, preferred_element_type=jnp.float32) * scale
    )
    return jnp.where(allowed[None], scores, masked)


def split_packs(triple, seg_rows):
    length, three, width = triple.shape
    count = length // LEN
    return (triple.reshape(count, LEN, three, width // HD, HD), seg_rows.reshape(count, LEN))


def attend_forward(triple, seg_rows, scale):
    length, three, width = triple.shape
    packs, seg_packs = split_packs(triple, seg_rows)

    def one_pack(pieces):
        pack_rows, seg_pack = pieces
        scores = pack_scores(pack_rows[:, 0], pack_rows[:, 1], seg_pack, scale)
        row_peak = jnp.max(scores, axis=-1, keepdims=True)
        exponent = jnp.exp(scores - row_peak)
        denominator = jnp.sum(exponent, axis=-1, keepdims=True)
        soft_weights = (exponent / denominator).astype(jnp.bfloat16)
        blended = jnp.einsum(
            "hqk,khd->qhd", soft_weights, pack_rows[:, 2], preferred_element_type=jnp.float32
        )
        return (blended.astype(jnp.bfloat16), (row_peak + jnp.log(denominator))[..., 0])

    blended, log_totals = lax.map(one_pack, (packs, seg_packs))
    return (blended.reshape(length, width), log_totals)


def attend_backward(triple, seg_rows, log_totals, grad_mixed, scale):
    length, three, width = triple.shape
    packs, seg_packs = split_packs(triple, seg_rows)
    grad_packs = grad_mixed.reshape(length // LEN, LEN, width // HD, HD)

    def one_pack(pieces):
        pack_rows, seg_pack, pack_totals, grad_pack = pieces
        queries = pack_rows[:, 0]
        key_rows = pack_rows[:, 1]
        value_rows = pack_rows[:, 2]
        scores = pack_scores(queries, key_rows, seg_pack, scale)
        chances = jnp.exp(scores - pack_totals[:, :, None])
        chance_grad = jnp.einsum(
            "qhd,khd->hqk", grad_pack, value_rows, preferred_element_type=jnp.float32
        )
        inner = jnp.sum(chances * chance_grad, axis=-1, keepdims=True)
        score_grad = (chances * (chance_grad - inner)).astype(jnp.bfloat16)
        query_grad = (
            jnp.einsum("hqk,khd->qhd", score_grad, key_rows, preferred_element_type=jnp.float32)
            * scale
        )
        key_grad = (
            jnp.einsum("hqk,qhd->khd", score_grad, queries, preferred_element_type=jnp.float32)
            * scale
        )
        value_grad = jnp.einsum(
            "hqk,qhd->khd",
            chances.astype(jnp.bfloat16),
            grad_pack,
            preferred_element_type=jnp.float32,
        )
        return jnp.stack([query_grad, key_grad, value_grad], axis=1).astype(jnp.bfloat16)

    triple_rows = lax.map(one_pack, (packs, seg_packs, log_totals, grad_packs))
    return triple_rows.reshape(length, three, width)


def layer_forward(stream, weights, small, seg_rows):
    triple_w, output_w, up_w, down_w = weights
    gains, shifts, triple_b, output_b, up_b, down_b = small
    scale = 1.0 / math.sqrt(HD)
    normed_one, inv_one, attn_in = norm_forward(stream, gains[0], shifts[0])
    attn_in = attn_in.astype(jnp.bfloat16)
    triple = in_parts(
        jnp.einsum("td,dke->tke", attn_in, triple_w, preferred_element_type=jnp.float32)
    )
    bias_rows = jnp.stack([triple_b[0], jnp.zeros_like(triple_b[0]), triple_b[1]])
    triple = (triple + bias_rows).astype(jnp.bfloat16)
    mixed, log_totals = attend_forward(triple, seg_rows, scale)
    mixed_full = gather_rows(mixed)
    middle = stream + (
        col_total(jnp.dot(mixed_full, output_w, preferred_element_type=jnp.float32)) + output_b
    )
    normed_two, inv_two, mlp_in = norm_forward(middle, gains[1], shifts[1])
    mlp_in = mlp_in.astype(jnp.bfloat16)
    hidden_pre = (
        in_parts(jnp.dot(mlp_in, up_w, preferred_element_type=jnp.float32)[:, None, :])[:, 0] + up_b
    )
    active = jax.nn.gelu(hidden_pre, approximate=True).astype(jnp.bfloat16)
    active_full = gather_rows(active)
    after = middle + (
        col_total(jnp.dot(active_full, down_w, preferred_element_type=jnp.float32)) + down_b
    )
    saved = (
        normed_one,
        inv_one,
        attn_in,
        triple,
        log_totals,
        mixed_full,
        normed_two,
        inv_two,
        mlp_in,
        hidden_pre,
        active_full,
        None,
    )
    return (after, saved)


def layer_backward(grad, saved, weights, gains, seg_rows):
    (
        normed_one,
        inv_one,
        attn_rows,
        triple,
        log_totals,
        mixed_full,
        normed_two,
        inv_two,
        mlp_rows,
        hidden_pre,
        active_full,
        columns_in,
    ) = saved
    triple_w, output_w, up_w, down_w = weights
    scale = 1.0 / math.sqrt(HD)
    down_in = grad.astype(jnp.bfloat16)
    down_bias_grad = jnp.sum(down_in, axis=0, dtype=jnp.float32)
    down_grad = jnp.einsum("tf,td->fd", active_full, down_in, preferred_element_type=jnp.float32)
    active_grad = rows_back(
        jnp.einsum("td,fd->tf", down_in, down_w, preferred_element_type=jnp.float32)
    )
    gelu_pull = jax.vjp(lambda value: jax.nn.gelu(value, approximate=True), hidden_pre)[1]
    hidden_grad = gelu_pull(active_grad)[0].astype(jnp.bfloat16)
    up_bias_grad = jnp.sum(hidden_grad, axis=0, dtype=jnp.float32)
    hidden_rows = grad_gather(hidden_grad[:, None, :])[:, 0]
    up_grad = jnp.einsum("td,tf->df", mlp_rows, hidden_rows, preferred_element_type=jnp.float32)
    mlp_grad = col_total(
        jnp.einsum("tf,df->td", hidden_rows, up_w, preferred_element_type=jnp.float32)
    )
    norm_two_grad, gain_two, shift_two = norm_backward(mlp_grad, normed_two, inv_two, gains[1])
    middle_grad = grad + norm_two_grad
    branch_grad = middle_grad.astype(jnp.bfloat16)
    output_bias_grad = jnp.sum(branch_grad, axis=0, dtype=jnp.float32)
    output_grad = jnp.einsum(
        "td,te->de", mixed_full, branch_grad, preferred_element_type=jnp.float32
    )
    mixed_grad = rows_back(
        jnp.einsum("te,de->td", branch_grad, output_w, preferred_element_type=jnp.float32)
    ).astype(jnp.bfloat16)
    triple_rows = attend_backward(triple, seg_rows, log_totals, mixed_grad, scale)
    triple_bias_grad = jnp.sum(triple_rows[:, 0::2], axis=0, dtype=jnp.float32)
    full_rows = grad_gather(triple_rows)
    triple_grad = jnp.einsum(
        "td,tke->dke", attn_rows, full_rows, preferred_element_type=jnp.float32
    )
    attn_grad = col_total(
        jnp.einsum("tke,dke->td", full_rows, triple_w, preferred_element_type=jnp.float32)
    )
    norm_one_grad, gain_one, shift_one = norm_backward(attn_grad, normed_one, inv_one, gains[0])
    start_grad = middle_grad + norm_one_grad
    terms = (
        jnp.stack([gain_one, gain_two]),
        jnp.stack([shift_one, shift_two]),
        triple_grad,
        triple_bias_grad,
        output_grad,
        output_bias_grad,
        up_grad,
        up_bias_grad,
        down_grad,
        down_bias_grad,
    )
    return (start_grad, terms)


def general_plan(
    tokens,
    segments,
    norm_gain,
    norm_shift,
    triple_weight,
    triple_bias,
    output_weight,
    output_bias,
    up_weight,
    up_bias,
    down_weight,
    down_bias,
    cotangent,
):

    def weights_of(layer_id):
        return (
            triple_weight[layer_id],
            output_weight[layer_id],
            up_weight[layer_id],
            down_weight[layer_id],
        )

    def small_of(layer_id):
        return (
            norm_gain[layer_id].astype(jnp.float32),
            norm_shift[layer_id].astype(jnp.float32),
            triple_bias[layer_id].astype(jnp.float32),
            output_bias[layer_id].astype(jnp.float32),
            up_bias[layer_id].astype(jnp.float32),
            down_bias[layer_id].astype(jnp.float32),
        )

    stream = tokens.astype(jnp.float32)
    stored = []
    for layer_id in range(LAYERS):
        stream, saved = layer_forward(stream, weights_of(layer_id), small_of(layer_id), segments)
        stored.append(saved)
    result = stream.astype(jnp.bfloat16)
    grad = cotangent.astype(jnp.float32)
    summed = [None] * LAYERS
    for layer_id in reversed(range(LAYERS)):
        grad, terms = layer_backward(
            grad, stored[layer_id], weights_of(layer_id), small_of(layer_id)[0], segments
        )
        summed[layer_id] = (
            lax.psum(terms[0].astype(jnp.bfloat16), "dp").astype(jnp.float32),
            lax.psum(terms[1].astype(jnp.bfloat16), "dp").astype(jnp.float32),
            lax.psum(terms[2].astype(jnp.bfloat16), "dp").astype(jnp.float32),
            lax.psum(terms[3].astype(jnp.bfloat16), "dp").astype(jnp.float32),
            lax.psum(terms[4].astype(jnp.bfloat16), "dp").astype(jnp.float32),
            lax.psum(terms[5].astype(jnp.bfloat16), "dp").astype(jnp.float32),
            lax.psum(terms[6].astype(jnp.bfloat16), "dp").astype(jnp.float32),
            lax.psum(terms[7].astype(jnp.bfloat16), "dp").astype(jnp.float32),
            lax.psum(terms[8].astype(jnp.bfloat16), "dp").astype(jnp.float32),
            lax.psum(terms[9].astype(jnp.bfloat16), "dp").astype(jnp.float32),
        )
    stacks = [
        jnp.stack([summed[layer_id][member] for layer_id in range(LAYERS)]) for member in range(10)
    ]
    return (
        result,
        grad,
        stacks[0],
        stacks[1],
        stacks[2],
        stacks[3],
        stacks[4],
        stacks[5],
        stacks[6],
        stacks[7],
        stacks[8],
        stacks[9],
    )


f32 = jnp.float32
bf16 = jnp.bfloat16
CHUNKS = 2
SPAN = LEN // CHUNKS
OWN = SPAN // 2
WIDTH = D // 4
QB = 256


def fits_pairs(shape, arrays):
    return (
        shape["row"] == 4
        and shape["col"] == 2
        and shape["dp"] == 4
        and arrays[0].shape == (2 * LEN, WIDTH)
        and arrays[8].shape[2] == 8 * WIDTH
    )


def swap_row(value, bits):
    return lax.ppermute(value, "row", [(i, i ^ bits) for i in range(4)])


def swap_core(value):
    return swap_row(value, 1)


def swap_chip(value):
    return swap_row(value, 2)


def swap_col(value):
    return lax.ppermute(value, "col", [(0, 1), (1, 0)])


def after(value, *others):
    return lax.optimization_barrier((value, *others))[0]


def dp_total(value):
    place = lax.axis_index("dp")
    inner = (place == 1) | (place == 2)
    kind = value.dtype
    from_end = lax.ppermute(value, "dp", [(0, 1), (3, 2)])
    half = (value.astype(f32) + from_end.astype(f32)).astype(kind)
    from_inner = lax.ppermute(half, "dp", [(1, 2), (2, 1)])
    whole = (half.astype(f32) + from_inner.astype(f32)).astype(kind)
    back = lax.ppermute(whole, "dp", [(1, 0), (2, 3)])
    return jnp.where(inner, whole, back)


def half_of(value, index, axis):
    size = value.shape[axis] // 2
    return lax.dynamic_slice_in_dim(value, index * size, size, axis)


def in_place(first, mine, other, axis):
    return jnp.where(
        first,
        jnp.concatenate([mine, other], axis=axis),
        jnp.concatenate([other, mine], axis=axis),
    )


def gather_weight(core, own, cut, join):
    peer = swap_chip(own)
    mine = [half_of(v, core, cut) for v in (own, peer)]
    theirs = jnp.stack([half_of(v, 1 - core, cut) for v in (own, peer)])
    theirs = swap_core(theirs)
    return jnp.concatenate([mine[0], theirs[0], mine[1], theirs[1]], axis=join), peer


def spread_grad(keep, give):
    got = swap_core(give)
    away = swap_chip(jnp.stack([keep[1], got[1]]))
    own = jnp.stack([keep[0], got[0]])
    total = dp_total((own.astype(f32) + away.astype(f32)).astype(bf16)).astype(f32)
    return total[0], total[1]


def dot(a, b):
    return lax.dot_general(a, b, (((1,), (0,)), ((), ())), preferred_element_type=f32)


def dot_nt(a, b):
    return lax.dot_general(a, b, (((1,), (1,)), ((), ())), preferred_element_type=f32)


def dot_tn(a, b):
    return lax.dot_general(a, b, (((0,), (0,)), ((), ())), preferred_element_type=f32)


def kernel_call(body, outs, args, flops, grid=None, in_specs=None, out_specs=None, scratch=(), limit=40):
    moved = sum(math.prod(v.shape) * v.dtype.itemsize for v in (*outs, *args))
    whole = pl.BlockSpec(memory_space=pltpu.VMEM)
    if in_specs is None:
        in_specs = [
            pl.BlockSpec(memory_space=pltpu.SMEM) if v.dtype == jnp.int32 and v.size == 1 else whole
            for v in args
        ]
    extra = {} if grid is None else {"grid": grid}
    return pl.pallas_call(
        body,
        out_shape=outs,
        in_specs=in_specs,
        out_specs=out_specs if out_specs is not None else [whole] * len(outs),
        scratch_shapes=list(scratch),
        compiler_params=pltpu.CompilerParams(vmem_limit_bytes=limit * 1024 * 1024),
        cost_estimate=pl.CostEstimate(flops=flops, bytes_accessed=moved, transcendentals=0),
        **extra,
    )(*args)


def like(shape, kind):
    return jax.ShapeDtypeStruct(shape, kind)


def other_order(value):
    b = [value[:, k * WIDTH : (k + 1) * WIDTH] for k in range(4)]
    return jnp.concatenate([b[1], b[0], b[3], b[2]], axis=1)


def part_rows(index):
    return pl.ds(pl.multiple_of(index * OWN, OWN), OWN)


def join_tokens(core_ref, own_ref, sib_ref, full_ref):
    core = core_ref[0]
    full_ref[part_rows(core), :] = own_ref[...]
    full_ref[part_rows(1 - core), :] = other_order(sib_ref[...])


def part_tokens(core_ref, sums_ref, mine_ref, other_ref):
    core = core_ref[0]
    mine_ref[...] = sums_ref[part_rows(core), :]
    other_ref[...] = other_order(sums_ref[part_rows(1 - core), :]).astype(bf16)


def head_lanes(h):
    lane = lax.broadcasted_iota(jnp.int32, (1, WIDTH), 1)
    return (lane >= h * HD) & (lane < (h + 1) * HD)


def allowed_pairs(seg_col, seg_row, start, keys):
    same = seg_col == seg_row
    query = lax.broadcasted_iota(jnp.int32, (QB, keys), 0) + start
    key = lax.broadcasted_iota(jnp.int32, (QB, keys), 1)
    return same & (key <= query)


HEADS_HERE = WIDTH // HD


def attend_body(chunk, *refs):
    core_ref, own_ref, sib_ref, triple_w_ref, bias_ref, output_w_ref, col_ref, row_ref = refs[:8]
    earlier = refs[8 : 8 + chunk]
    full_ref, triple_ref, mixed_ref, log_ref, mine_ref, other_ref = refs[8 + chunk : 14 + chunk]
    kv_ref, sums_ref = refs[14 + chunk :]
    scale = 1.0 / math.sqrt(HD)
    join_tokens(core_ref, own_ref, sib_ref, full_ref)
    for part in range(3):
        cols = slice(part * WIDTH, (part + 1) * WIDTH)
        triple_ref[:, cols] = (
            dot(full_ref[...], triple_w_ref[:, cols]) + bias_ref[:, cols]
        ).astype(bf16)
    for k in range(chunk):
        kv_ref[k * SPAN : (k + 1) * SPAN, :] = earlier[k][:, WIDTH:]
    kv_ref[chunk * SPAN :, :] = triple_ref[:, WIDTH:]
    for block in range(SPAN // QB):
        rows = slice(block * QB, (block + 1) * QB)
        start = chunk * SPAN + block * QB
        keys = start + QB
        allowed = allowed_pairs(col_ref[start : start + QB, :], row_ref[:, :keys], start, keys)
        queries = triple_ref[rows, :WIDTH] * scale
        key_rows = kv_ref[:keys, :WIDTH]
        value_rows = kv_ref[:keys, WIDTH:]
        blended = jnp.zeros((QB, WIDTH), f32)
        for h in range(HEADS_HERE):
            lanes = head_lanes(h)
            scores = dot_nt(jnp.where(lanes, queries, 0).astype(bf16), key_rows)
            scores = jnp.where(allowed, scores, masked)
            peak = jnp.max(scores, axis=1, keepdims=True)
            exponent = jnp.exp(scores - peak)
            total = jnp.sum(exponent, axis=1, keepdims=True)
            soft = (exponent * (1.0 / total)).astype(bf16)
            blended = jnp.where(lanes, dot(soft, value_rows), blended)
            log_ref[rows, h : h + 1] = peak + jnp.log(total)
        mixed_ref[rows, :] = blended.astype(bf16)
    sums_ref[...] = dot(mixed_ref[...], output_w_ref[...])
    part_tokens(core_ref, sums_ref, mine_ref, other_ref)


def attend_call(chunk, core, own, sib, triple_w, bias, output_w, seg_col, seg_row, earlier):
    return kernel_call(
        lambda *refs: attend_body(chunk, *refs),
        [
            like((SPAN, D), bf16),
            like((SPAN, 3 * WIDTH), bf16),
            like((SPAN, WIDTH), bf16),
            like((SPAN, 128), f32),
            like((OWN, D), f32),
            like((OWN, D), bf16),
        ],
        (core, own, sib, triple_w, bias, output_w, seg_col, seg_row, *earlier),
        2 * SPAN * D * 4 * WIDTH + 8 * 4 * SPAN * (chunk + 1) * SPAN * WIDTH,
        scratch=[pltpu.VMEM(((chunk + 1) * SPAN, 2 * WIDTH), bf16), pltpu.VMEM((SPAN, D), f32)],
    )


GELU = math.sqrt(2.0 / math.pi)


def mlp_body(core_ref, own_ref, sib_ref, up_ref, bias_ref, down_ref, *refs):
    full_ref, pre_ref, active_ref, mine_ref, other_ref, sums_ref = refs
    step = pl.program_id(0)

    @pl.when(step == 0)
    def _():
        join_tokens(core_ref, own_ref, sib_ref, full_ref)

    pre = dot(full_ref[...], up_ref[...]) + bias_ref[...]
    pre_ref[...] = pre
    curve = jnp.tanh(GELU * (pre + 0.044715 * (pre * pre * pre)))
    active = (0.5 * pre * (1.0 + curve)).astype(bf16)
    active_ref[...] = active
    sums = dot(active, down_ref[...])

    @pl.when(step == 0)
    def _():
        sums_ref[...] = sums

    @pl.when(step > 0)
    def _():
        sums_ref[...] += sums

    @pl.when(step == pl.num_programs(0) - 1)
    def _():
        part_tokens(core_ref, sums_ref, mine_ref, other_ref)


def mlp_call(core, own, sib, up_w, bias, down_w):
    units = up_w.shape[1]
    step = 256
    whole = pl.BlockSpec((OWN, D), lambda i: (0, 0))
    return kernel_call(
        mlp_body,
        [
            like((SPAN, D), bf16),
            like((SPAN, units), f32),
            like((SPAN, units), bf16),
            like((OWN, D), f32),
            like((OWN, D), bf16),
        ],
        (core, own, sib, up_w, bias, down_w),
        4 * SPAN * D * units,
        grid=(units // step,),
        in_specs=[
            pl.BlockSpec(memory_space=pltpu.SMEM),
            whole,
            whole,
            pl.BlockSpec((D, step), lambda i: (0, i)),
            pl.BlockSpec((1, step), lambda i: (0, i)),
            pl.BlockSpec((step, D), lambda i: (i, 0)),
        ],
        out_specs=[
            pl.BlockSpec((SPAN, D), lambda i: (0, 0)),
            pl.BlockSpec((SPAN, step), lambda i: (0, i)),
            pl.BlockSpec((SPAN, step), lambda i: (0, i)),
            whole,
            whole,
        ],
        scratch=[pltpu.VMEM((SPAN, D), f32)],
    )


def mlp_back_body(core_ref, own_ref, sib_ref, down_ref, pre_ref, up_ref, *refs):
    full_ref, hidden_ref, bias_ref, mine_ref, other_ref, sums_ref = refs
    step = pl.program_id(0)

    @pl.when(step == 0)
    def _():
        join_tokens(core_ref, own_ref, sib_ref, full_ref)

    active_grad = dot_nt(full_ref[...], down_ref[...])
    pre = pre_ref[...]
    square = pre * pre
    curve = jnp.tanh(GELU * (pre + 0.044715 * (square * pre)))
    slope = 0.5 * (1.0 + curve) + (0.5 * GELU) * pre * (1.0 - curve * curve) * (
        1.0 + (3.0 * 0.044715) * square
    )
    hidden = (active_grad * slope).astype(bf16)
    hidden_ref[...] = hidden
    bias_ref[...] = jnp.sum(hidden.astype(f32), axis=0, keepdims=True)
    sums = dot_nt(hidden, up_ref[...])

    @pl.when(step == 0)
    def _():
        sums_ref[...] = sums

    @pl.when(step > 0)
    def _():
        sums_ref[...] += sums

    @pl.when(step == pl.num_programs(0) - 1)
    def _():
        part_tokens(core_ref, sums_ref, mine_ref, other_ref)


def mlp_back_call(core, own, sib, down_w, pre, up_w):
    units = up_w.shape[1]
    step = 256
    whole = pl.BlockSpec((OWN, D), lambda i: (0, 0))
    return kernel_call(
        mlp_back_body,
        [
            like((SPAN, D), bf16),
            like((SPAN, units), bf16),
            like((1, units), f32),
            like((OWN, D), f32),
            like((OWN, D), bf16),
        ],
        (core, own, sib, down_w, pre, up_w),
        4 * SPAN * D * units,
        grid=(units // step,),
        in_specs=[
            pl.BlockSpec(memory_space=pltpu.SMEM),
            whole,
            whole,
            pl.BlockSpec((step, D), lambda i: (i, 0)),
            pl.BlockSpec((SPAN, step), lambda i: (0, i)),
            pl.BlockSpec((D, step), lambda i: (0, i)),
        ],
        out_specs=[
            pl.BlockSpec((SPAN, D), lambda i: (0, 0)),
            pl.BlockSpec((SPAN, step), lambda i: (0, i)),
            pl.BlockSpec((1, step), lambda i: (0, i)),
            whole,
            whole,
        ],
        scratch=[pltpu.VMEM((SPAN, D), f32)],
    )


def attend_back_body(chunk, later, *refs):
    core_ref, own_ref, sib_ref, output_w_ref, triple_w_ref, log_ref, col_ref, row_ref = refs[:8]
    triples = refs[8 : 9 + chunk]
    refs = refs[9 + chunk :]
    if later:
        carried_ref, refs = refs[0], refs[1:]
    full_ref, rows_ref, bias_ref, mine_ref, other_ref = refs[:5]
    refs = refs[5:]
    if chunk:
        carry_ref, refs = refs[0], refs[1:]
    kv_ref, grad_ref, total_ref, sums_ref = refs
    scale = 1.0 / math.sqrt(HD)
    triple_ref = triples[chunk]
    join_tokens(core_ref, own_ref, sib_ref, full_ref)
    grad_ref[...] = dot_nt(full_ref[...], output_w_ref[...]).astype(bf16)
    for k in range(chunk + 1):
        kv_ref[k * SPAN : (k + 1) * SPAN, :] = triples[k][:, WIDTH:]
    if later:
        total_ref[...] = carried_ref[...]
    else:
        total_ref[...] = jnp.zeros_like(total_ref)
    for block in range(SPAN // QB):
        rows = slice(block * QB, (block + 1) * QB)
        start = chunk * SPAN + block * QB
        keys = start + QB
        allowed = allowed_pairs(col_ref[start : start + QB, :], row_ref[:, :keys], start, keys)
        queries = triple_ref[rows, :WIDTH] * scale
        grads = grad_ref[rows, :]
        key_rows = kv_ref[:keys, :WIDTH]
        value_rows = kv_ref[:keys, WIDTH:]
        query_grad = jnp.zeros((QB, WIDTH), f32)
        for h in range(HEADS_HERE):
            lanes = head_lanes(h)
            query = jnp.where(lanes, queries, 0).astype(bf16)
            grad = jnp.where(lanes, grads, 0).astype(bf16)
            scores = jnp.where(allowed, dot_nt(query, key_rows), masked)
            chances = jnp.exp(scores - log_ref[rows, h : h + 1])
            product = chances * dot_nt(grad, value_rows)
            inner = jnp.sum(product, axis=1, keepdims=True)
            score_grad = (product - chances * inner).astype(bf16)
            query_grad = jnp.where(lanes, dot(score_grad, key_rows), query_grad)
            total_ref[:keys, :WIDTH] += dot_tn(score_grad, query)
            total_ref[:keys, WIDTH:] += dot_tn(chances.astype(bf16), grad)
        rows_ref[rows, :WIDTH] = (query_grad * scale).astype(bf16)
    rows_ref[:, WIDTH:] = total_ref[chunk * SPAN :, :].astype(bf16)
    if chunk:
        carry_ref[...] = total_ref[: chunk * SPAN, :]
    bias_ref[0:1, :] = jnp.sum(rows_ref[:, :WIDTH].astype(f32), axis=0, keepdims=True)
    bias_ref[1:2, :] = jnp.sum(rows_ref[:, 2 * WIDTH :].astype(f32), axis=0, keepdims=True)
    sums_ref[...] = dot_nt(rows_ref[...], triple_w_ref[...])
    part_tokens(core_ref, sums_ref, mine_ref, other_ref)


def attend_back_call(
    chunk, core, own, sib, output_w, triple_w, logs, seg_col, seg_row, triples, carried
):
    outs = [
        like((SPAN, D), bf16),
        like((SPAN, 3 * WIDTH), bf16),
        like((2, WIDTH), f32),
        like((OWN, D), f32),
        like((OWN, D), bf16),
    ]
    if chunk:
        outs.append(like((chunk * SPAN, 2 * WIDTH), f32))
    later = () if carried is None else (carried,)
    return kernel_call(
        lambda *refs: attend_back_body(chunk, bool(later), *refs),
        outs,
        (core, own, sib, output_w, triple_w, logs, seg_col, seg_row, *triples, *later),
        2 * SPAN * D * 4 * WIDTH + 20 * 4 * SPAN * (chunk + 1) * SPAN * WIDTH,
        scratch=[
            pltpu.VMEM(((chunk + 1) * SPAN, 2 * WIDTH), bf16),
            pltpu.VMEM((SPAN, WIDTH), bf16),
            pltpu.VMEM(((chunk + 1) * SPAN, 2 * WIDTH), f32),
            pltpu.VMEM((SPAN, D), f32),
        ],
    )


def weight_grad_body(join, *refs):
    left, right = refs[:CHUNKS], refs[CHUNKS : 2 * CHUNKS]
    keep_ref, give_ref = refs[2 * CHUNKS :]
    total = dot_tn(left[0][...], right[0][...])
    for k in range(1, CHUNKS):
        total += dot_tn(left[k][...], right[k][...])
    total = total.astype(bf16)
    if join == 0:
        keep_ref[0] = total[:WIDTH]
        give_ref[0] = total[WIDTH:]
    else:
        for k in range(2):
            keep_ref[k] = total[:, 2 * k * WIDTH : (2 * k + 1) * WIDTH]
            give_ref[k] = total[:, (2 * k + 1) * WIDTH : (2 * k + 2) * WIDTH]


def weight_grad(left, right, join):
    high, across = left[0].shape[1], right[0].shape[1]
    part = min(512, high)
    steps = high // part
    if join == 0:
        shape = (2, WIDTH, across)
        out = pl.BlockSpec((1, WIDTH, across), lambda i: (i, 0, 0))
    else:
        shape = (2, high, WIDTH)
        out = pl.BlockSpec((2, part, WIDTH), lambda i: (0, i, 0))
    return kernel_call(
        lambda *refs: weight_grad_body(join, *refs),
        [like(shape, bf16)] * 2,
        (*left, *right),
        2 * LEN * high * across,
        grid=(steps,),
        in_specs=[pl.BlockSpec((SPAN, part), lambda i: (0, i))] * CHUNKS
        + [pl.BlockSpec((SPAN, across), lambda i: (0, 0))] * CHUNKS,
        out_specs=[out, out],
    )


def mean_lanes(v):
    return jnp.sum(v, axis=1, keepdims=True) * (1.0 / D)


def norm_parts(v):
    center = mean_lanes(v)
    second = mean_lanes(v * v) - center * center
    inv_std = lax.rsqrt(second + eps)
    return (v - center) * inv_std, inv_std


def norm_body(stream_ref, chip_ref, got_ref, bias_ref, gain_ref, shift_ref, after_ref, out_ref):
    total = chip_ref[...].astype(f32) + got_ref[...].astype(f32)
    after_sum = stream_ref[...] + (total + bias_ref[...])
    after_ref[...] = after_sum
    normed, _ = norm_parts(after_sum)
    out_ref[...] = (normed * gain_ref[...] + shift_ref[...]).astype(bf16)


def norm_call(stream, chip, got, bias, gain, shift):
    return kernel_call(
        norm_body,
        [like((OWN, D), f32), like((OWN, D), bf16)],
        (stream, chip, got, bias[None], gain[None], shift[None]),
        20 * OWN * D,
    )


def norm_back_body(grad_ref, chip_ref, got_ref, stream_ref, gain_ref, out_ref, low_ref, sums_ref):
    grad_out = chip_ref[...].astype(f32) + got_ref[...].astype(f32)
    normed, inv_std = norm_parts(stream_ref[...])
    scaled = grad_out * gain_ref[...]
    total = grad_ref[...] + inv_std * (
        scaled - mean_lanes(scaled) - normed * mean_lanes(scaled * normed)
    )
    low = total.astype(bf16)
    out_ref[...] = total
    low_ref[...] = low
    sums_ref[0:1, :] = jnp.sum(grad_out * normed, axis=0, keepdims=True)
    sums_ref[1:2, :] = jnp.sum(grad_out, axis=0, keepdims=True)
    sums_ref[2:3, :] = jnp.sum(low.astype(f32), axis=0, keepdims=True)


def norm_back_call(grad, chip, got, stream, gain):
    return kernel_call(
        norm_back_body,
        [like((OWN, D), f32), like((OWN, D), bf16), like((3, D), f32)],
        (grad, chip, got, stream, gain[None]),
        30 * OWN * D,
    )


def chip_total(mine, other):
    return (mine + swap_core(other).astype(f32)).astype(bf16)


def pair_plan(
    tokens,
    segments,
    norm_gain,
    norm_shift,
    triple_weight,
    triple_bias,
    output_weight,
    output_bias,
    up_weight,
    up_bias,
    down_weight,
    down_bias,
    cotangent,
):
    row = lax.axis_index("row")
    core = row % 2
    chip = row // 2
    first = core == 0
    core_id = core.astype(jnp.int32).reshape(1)
    chunks = range(CHUNKS)

    def to_tokens(block):
        def of_owner(j):
            start = (row ^ j) // 2 * LEN + (row ^ j) % 2 * OWN
            return jnp.concatenate(
                [lax.dynamic_slice_in_dim(block, start + k * SPAN, OWN, 0) for k in chunks]
            )

        parts = [of_owner(j) for j in range(4)]
        got = [parts[0]] + [swap_row(parts[j], j) for j in range(1, 4)]
        whole = jnp.concatenate(got, axis=1)
        return [whole[k * OWN : (k + 1) * OWN] for k in chunks]

    def to_features(pieces):
        whole = jnp.concatenate(pieces)
        parts = jnp.split(whole, 4, axis=1)
        got = [parts[0]] + [swap_row(parts[j], j) for j in range(1, 4)]
        halves = [jnp.stack(pair).reshape(2, CHUNKS, OWN, WIDTH) for pair in (got[:2], got[2:])]
        packs = []
        for pair in halves:
            pair = jnp.where(first, pair, pair[::-1])
            packs.append(jnp.swapaxes(pair, 0, 1).reshape(LEN, WIDTH))
        return jnp.where(
            chip == 0,
            jnp.concatenate(packs),
            jnp.concatenate(packs[::-1]),
        )

    streams = [v.astype(f32) for v in to_tokens(tokens)]
    seg_pack = lax.dynamic_slice_in_dim(segments, chip * LEN, LEN, 0)
    seg_col, seg_row = seg_pack[:, None], seg_pack[None, :]

    flat = jnp.concatenate(
        [
            v.reshape(-1)
            for v in (norm_gain, norm_shift, output_bias, down_bias, triple_bias, up_bias)
        ]
    ).reshape(-1, 128)
    small = jnp.stack([flat] + [swap_row(flat, j) for j in range(1, 4)]).astype(f32)
    small = small.reshape(4, -1)
    at = 0

    def take(shape):
        nonlocal at
        size = math.prod(shape)
        part = small[:, at : at + size].reshape((4,) + shape)
        at += size
        return part

    def wide(part):
        return jnp.moveaxis(part, 0, -2).reshape(part.shape[1:-1] + (-1,))

    def of_core(part):
        pick = [
            lax.dynamic_index_in_dim(part, row ^ (2 * core + b), 0, keepdims=False)
            for b in range(2)
        ]
        return jnp.concatenate(pick, axis=-1)

    gains = wide(take((LAYERS, 2, WIDTH)))
    shifts = wide(take((LAYERS, 2, WIDTH)))
    output_b = wide(take((LAYERS, WIDTH)))
    down_b = wide(take((LAYERS, WIDTH)))
    triple_b = of_core(take((LAYERS, 2, D // 8)))
    up_b = of_core(take((LAYERS,) + up_bias.shape[1:]))

    weights = []
    last = [streams[0], streams[0]]
    for layer in range(LAYERS):
        triple_w, p0 = gather_weight(
            core, after(jnp.swapaxes(triple_weight[layer], 0, 1), last[0]), 2, 1
        )
        triple_w = jnp.concatenate([triple_w[0], triple_w[1], triple_w[2]], axis=1)
        output_w, p1 = gather_weight(core, after(output_weight[layer], last[1]), 0, 1)
        up_w, p2 = gather_weight(core, after(up_weight[layer], p0), 1, 0)
        down_w, p3 = gather_weight(core, after(down_weight[layer], p1), 0, 1)
        last = [p2, p3]
        weights.append((triple_w, output_w, up_w, down_w))

    stored = []
    low = []
    for k in chunks:
        normed, _ = norm_parts(streams[k])
        low.append((normed * gains[0, 0] + shifts[0, 0]).astype(bf16))
    for layer in range(LAYERS):
        triple_w, output_w, up_w, down_w = weights[layer]
        bias = jnp.concatenate(
            [triple_b[layer, 0], jnp.zeros_like(triple_b[layer, 0]), triple_b[layer, 1]]
        )[None]
        saved = {name: [] for name in ("start", "attn", "triple", "mixed", "logs", "middle")}
        saved.update({name: [] for name in ("mlp", "pre", "active")})
        saved["start"] = streams
        for k in chunks:
            attn, triple, mixed, logs, mine, other = attend_call(
                k,
                core_id,
                low[k],
                swap_core(low[k]),
                triple_w,
                bias,
                output_w,
                seg_col,
                seg_row,
                saved["triple"],
            )
            total = chip_total(mine, other)
            middle, mlp_own = norm_call(
                streams[k], total, swap_col(total), output_b[layer], gains[layer, 1], shifts[layer, 1]
            )
            for name, value in (
                ("attn", attn),
                ("triple", triple),
                ("mixed", mixed),
                ("logs", logs),
                ("middle", middle),
            ):
                saved[name].append(value)
            low[k] = mlp_own
        streams = []
        for k in chunks:
            mlp, pre, active, mine, other = mlp_call(
                core_id, low[k], swap_core(low[k]), up_w, up_b[layer][None], down_w
            )
            total = chip_total(mine, other)
            if layer + 1 < LAYERS:
                stream, low[k] = norm_call(
                    saved["middle"][k],
                    total,
                    swap_col(total),
                    down_b[layer],
                    gains[layer + 1, 0],
                    shifts[layer + 1, 0],
                )
            else:
                both = total.astype(f32) + swap_col(total).astype(f32)
                stream = saved["middle"][k] + (both + down_b[layer])
            for name, value in (("mlp", mlp), ("pre", pre), ("active", active)):
                saved[name].append(value)
            streams.append(stream)
        stored.append(saved)

    result = to_features([v.astype(bf16) for v in streams])
    low = to_tokens(cotangent)
    grad = [v.astype(f32) for v in low]
    low_sums = sum(jnp.sum(v, axis=0) for v in grad)
    grads = [None] * LAYERS
    for layer in reversed(range(LAYERS)):
        triple_w, output_w, up_w, down_w = weights[layer]
        saved = stored[layer]
        down_bias_grad = low_sums
        down_in, hidden, branch, triple_rows = ([None] * CHUNKS for _ in range(4))
        sums_two, sums_one = [], []
        up_bias_grad, triple_bias_grad = [], []
        for k in reversed(chunks):
            down_in[k], hidden[k], bias, mine, other = mlp_back_call(
                core_id, low[k], swap_core(low[k]), down_w, saved["pre"][k], up_w
            )
            up_bias_grad.append(bias[0])
            total = chip_total(mine, other)
            grad[k], low[k], sums = norm_back_call(
                grad[k], total, swap_col(total), saved["middle"][k], gains[layer, 1]
            )
            sums_two.append(sums)
        down_grad = spread_grad(*weight_grad(saved["active"], down_in, 1))
        up_grad = spread_grad(*weight_grad(saved["mlp"], hidden, 0))
        carried = None
        for k in reversed(chunks):
            branch[k], triple_rows[k], bias, mine, other, *carry = attend_back_call(
                k,
                core_id,
                low[k],
                swap_core(low[k]),
                output_w,
                triple_w,
                saved["logs"][k],
                seg_col,
                seg_row,
                saved["triple"][: k + 1],
                carried,
            )
            carried = carry[0] if carry else None
            triple_bias_grad.append(bias)
            total = chip_total(mine, other)
            grad[k], low[k], sums = norm_back_call(
                grad[k], total, swap_col(total), saved["start"][k], gains[layer, 0]
            )
            sums_one.append(sums)
        output_grad = spread_grad(*weight_grad(saved["mixed"], branch, 1))
        triple_grad = spread_grad(*weight_grad(saved["attn"], triple_rows, 0))
        sums_one, sums_two = sum(sums_one), sum(sums_two)
        up_bias_grad, triple_bias_grad = sum(up_bias_grad), sum(triple_bias_grad)
        low_sums = sums_one[2]

        full = jnp.stack(
            [sums_one[0], sums_two[0], sums_one[1], sums_two[1], sums_two[2], down_bias_grad]
        )
        full = jnp.moveaxis(full.reshape(6, 4, WIDTH), 1, 0)
        theirs = swap_core(full)
        full = full + jnp.stack([theirs[1], theirs[0], theirs[3], theirs[2]])
        full = full[0] + swap_chip(full[2])
        pieces = jnp.concatenate(
            [
                jnp.moveaxis(triple_bias_grad.reshape(2, 2, D // 8), 1, 0).reshape(2, -1),
                up_bias_grad.reshape(2, -1),
            ],
            axis=1,
        )
        pieces = pieces + swap_chip(pieces)
        give = lax.dynamic_index_in_dim(pieces, 1 - core, 0, keepdims=False)
        keep = lax.dynamic_index_in_dim(pieces, core, 0, keepdims=False)
        share = jnp.where(chip == core, keep, swap_core(give))
        packed = jnp.concatenate([full.reshape(-1), share]).reshape(-1, 128)
        packed = dp_total(packed).reshape(-1)
        full = packed[: 6 * WIDTH].reshape(6, WIDTH)
        share = packed[6 * WIDTH :]
        thirds = [slice(part * WIDTH, (part + 1) * WIDTH) for part in range(3)]
        grads[layer] = (
            full[0:2],
            full[2:4],
            jnp.stack(
                [in_place(first, triple_grad[0][:, s], triple_grad[1][:, s], 1) for s in thirds],
                axis=1,
            ),
            share[: D // 4].reshape(2, D // 8),
            in_place(first, output_grad[0], output_grad[1], 0),
            full[4],
            in_place(first, up_grad[0], up_grad[1], 1),
            share[D // 4 :],
            in_place(first, down_grad[0], down_grad[1], 0),
            full[5],
        )
    input_grad = to_features(low).astype(f32)
    stacks = [jnp.stack([grads[layer][k] for layer in range(LAYERS)]) for k in range(10)]
    return (result, input_grad, *stacks)


def solution(mesh):
    in_specs = (
        P("dp", "row"),
        P("dp"),
        P(None, None, "row"),
        P(None, None, "row"),
        P(None, "row", None, "col"),
        P(None, None, ("col", "row")),
        P(None, "col", "row"),
        P(None, "row"),
        P(None, "row", "col"),
        P(None, ("col", "row")),
        P(None, "col", "row"),
        P(None, "row"),
        P("dp", "row"),
    )
    out_specs = (
        P("dp", "row"),
        P("dp", "row"),
        P(None, None, "row"),
        P(None, None, "row"),
        P(None, "row", None, "col"),
        P(None, None, ("col", "row")),
        P(None, "col", "row"),
        P(None, "row"),
        P(None, "row", "col"),
        P(None, ("col", "row")),
        P(None, "col", "row"),
        P(None, "row"),
    )
    shape = mesh.shape

    def on_device(*arrays):
        if fits_pairs(shape, arrays):
            return pair_plan(*arrays)
        return general_plan(*arrays)

    return jax.shard_map(
        on_device, mesh=mesh, in_specs=in_specs, out_specs=out_specs, check_vma=False
    )
```

```python
import math

import jax
import jax.numpy as jnp
from jax import lax
from jax.experimental import pallas as pl
from jax.experimental.pallas import tpu as pltpu
from jax.sharding import PartitionSpec as P

D = 1024
HD = 64
LAYERS = 2
LEN = 1024


eps = 1e-05
masked = -1000000000.0


def norm_forward(stream, gain, shift):
    totals = lax.psum((jnp.sum(stream, axis=1), jnp.sum(stream * stream, axis=1)), "row")
    center = totals[0] / D
    second = totals[1] / D - center * center
    inv_std = lax.rsqrt(second + eps)
    normed = (stream - center[:, None]) * inv_std[:, None]
    return (normed, inv_std, normed * gain + shift)


def norm_backward(grad_out, normed, inv_std, gain):
    scaled = grad_out * gain
    totals = lax.psum((jnp.sum(scaled, axis=1), jnp.sum(scaled * normed, axis=1)), "row")
    grad_in = inv_std[:, None] * (
        scaled - totals[0][:, None] / D - normed * (totals[1][:, None] / D)
    )
    return (grad_in, jnp.sum(grad_out * normed, axis=0), jnp.sum(grad_out, axis=0))


def gather_rows(block):
    return lax.all_gather(block, "row", axis=1, tiled=True)


def col_total(partial_sums):
    return lax.psum(partial_sums, "col")


def rows_back(partial_sums):
    return lax.psum_scatter(
        partial_sums.astype(jnp.bfloat16), "row", scatter_dimension=1, tiled=True
    ).astype(jnp.float32)


def in_parts(partial_sums):
    return lax.psum_scatter(partial_sums, "row", scatter_dimension=2, tiled=True)


def grad_gather(block):
    return lax.all_gather(block, "row", axis=2, tiled=True)


def pack_scores(queries, key_rows, seg_pack, scale):
    position = jnp.arange(queries.shape[0])
    allowed = (seg_pack[:, None] == seg_pack[None, :]) & (position[None, :] <= position[:, None])
    scores = (
        jnp.einsum("qhd,khd->hqk", queries, key_rows, preferred_element_type=jnp.float32) * scale
    )
    return jnp.where(allowed[None], scores, masked)


def split_packs(triple, seg_rows):
    length, three, width = triple.shape
    count = length // LEN
    return (triple.reshape(count, LEN, three, width // HD, HD), seg_rows.reshape(count, LEN))


def attend_forward(triple, seg_rows, scale):
    length, three, width = triple.shape
    packs, seg_packs = split_packs(triple, seg_rows)

    def one_pack(pieces):
        pack_rows, seg_pack = pieces
        scores = pack_scores(pack_rows[:, 0], pack_rows[:, 1], seg_pack, scale)
        row_peak = jnp.max(scores, axis=-1, keepdims=True)
        exponent = jnp.exp(scores - row_peak)
        denominator = jnp.sum(exponent, axis=-1, keepdims=True)
        soft_weights = (exponent / denominator).astype(jnp.bfloat16)
        blended = jnp.einsum(
            "hqk,khd->qhd", soft_weights, pack_rows[:, 2], preferred_element_type=jnp.float32
        )
        return (blended.astype(jnp.bfloat16), (row_peak + jnp.log(denominator))[..., 0])

    blended, log_totals = lax.map(one_pack, (packs, seg_packs))
    return (blended.reshape(length, width), log_totals)


def attend_backward(triple, seg_rows, log_totals, grad_mixed, scale):
    length, three, width = triple.shape
    packs, seg_packs = split_packs(triple, seg_rows)
    grad_packs = grad_mixed.reshape(length // LEN, LEN, width // HD, HD)

    def one_pack(pieces):
        pack_rows, seg_pack, pack_totals, grad_pack = pieces
        queries = pack_rows[:, 0]
        key_rows = pack_rows[:, 1]
        value_rows = pack_rows[:, 2]
        scores = pack_scores(queries, key_rows, seg_pack, scale)
        chances = jnp.exp(scores - pack_totals[:, :, None])
        chance_grad = jnp.einsum(
            "qhd,khd->hqk", grad_pack, value_rows, preferred_element_type=jnp.float32
        )
        inner = jnp.sum(chances * chance_grad, axis=-1, keepdims=True)
        score_grad = (chances * (chance_grad - inner)).astype(jnp.bfloat16)
        query_grad = (
            jnp.einsum("hqk,khd->qhd", score_grad, key_rows, preferred_element_type=jnp.float32)
            * scale
        )
        key_grad = (
            jnp.einsum("hqk,qhd->khd", score_grad, queries, preferred_element_type=jnp.float32)
            * scale
        )
        value_grad = jnp.einsum(
            "hqk,qhd->khd",
            chances.astype(jnp.bfloat16),
            grad_pack,
            preferred_element_type=jnp.float32,
        )
        return jnp.stack([query_grad, key_grad, value_grad], axis=1).astype(jnp.bfloat16)

    triple_rows = lax.map(one_pack, (packs, seg_packs, log_totals, grad_packs))
    return triple_rows.reshape(length, three, width)


def layer_forward(stream, weights, small, seg_rows):
    triple_w, output_w, up_w, down_w = weights
    gains, shifts, triple_b, output_b, up_b, down_b = small
    scale = 1.0 / math.sqrt(HD)
    normed_one, inv_one, attn_in = norm_forward(stream, gains[0], shifts[0])
    attn_in = attn_in.astype(jnp.bfloat16)
    triple = in_parts(
        jnp.einsum("td,dke->tke", attn_in, triple_w, preferred_element_type=jnp.float32)
    )
    bias_rows = jnp.stack([triple_b[0], jnp.zeros_like(triple_b[0]), triple_b[1]])
    triple = (triple + bias_rows).astype(jnp.bfloat16)
    mixed, log_totals = attend_forward(triple, seg_rows, scale)
    mixed_full = gather_rows(mixed)
    middle = stream + (
        col_total(jnp.dot(mixed_full, output_w, preferred_element_type=jnp.float32)) + output_b
    )
    normed_two, inv_two, mlp_in = norm_forward(middle, gains[1], shifts[1])
    mlp_in = mlp_in.astype(jnp.bfloat16)
    hidden_pre = (
        in_parts(jnp.dot(mlp_in, up_w, preferred_element_type=jnp.float32)[:, None, :])[:, 0] + up_b
    )
    active = jax.nn.gelu(hidden_pre, approximate=True).astype(jnp.bfloat16)
    active_full = gather_rows(active)
    after = middle + (
        col_total(jnp.dot(active_full, down_w, preferred_element_type=jnp.float32)) + down_b
    )
    saved = (
        normed_one,
        inv_one,
        attn_in,
        triple,
        log_totals,
        mixed_full,
        normed_two,
        inv_two,
        mlp_in,
        hidden_pre,
        active_full,
        None,
    )
    return (after, saved)


def layer_backward(grad, saved, weights, gains, seg_rows):
    (
        normed_one,
        inv_one,
        attn_rows,
        triple,
        log_totals,
        mixed_full,
        normed_two,
        inv_two,
        mlp_rows,
        hidden_pre,
        active_full,
        columns_in,
    ) = saved
    triple_w, output_w, up_w, down_w = weights
    scale = 1.0 / math.sqrt(HD)
    down_in = grad.astype(jnp.bfloat16)
    down_bias_grad = jnp.sum(down_in, axis=0, dtype=jnp.float32)
    down_grad = jnp.einsum("tf,td->fd", active_full, down_in, preferred_element_type=jnp.float32)
    active_grad = rows_back(
        jnp.einsum("td,fd->tf", down_in, down_w, preferred_element_type=jnp.float32)
    )
    gelu_pull = jax.vjp(lambda value: jax.nn.gelu(value, approximate=True), hidden_pre)[1]
    hidden_grad = gelu_pull(active_grad)[0].astype(jnp.bfloat16)
    up_bias_grad = jnp.sum(hidden_grad, axis=0, dtype=jnp.float32)
    hidden_rows = grad_gather(hidden_grad[:, None, :])[:, 0]
    up_grad = jnp.einsum("td,tf->df", mlp_rows, hidden_rows, preferred_element_type=jnp.float32)
    mlp_grad = col_total(
        jnp.einsum("tf,df->td", hidden_rows, up_w, preferred_element_type=jnp.float32)
    )
    norm_two_grad, gain_two, shift_two = norm_backward(mlp_grad, normed_two, inv_two, gains[1])
    middle_grad = grad + norm_two_grad
    branch_grad = middle_grad.astype(jnp.bfloat16)
    output_bias_grad = jnp.sum(branch_grad, axis=0, dtype=jnp.float32)
    output_grad = jnp.einsum(
        "td,te->de", mixed_full, branch_grad, preferred_element_type=jnp.float32
    )
    mixed_grad = rows_back(
        jnp.einsum("te,de->td", branch_grad, output_w, preferred_element_type=jnp.float32)
    ).astype(jnp.bfloat16)
    triple_rows = attend_backward(triple, seg_rows, log_totals, mixed_grad, scale)
    triple_bias_grad = jnp.sum(triple_rows[:, 0::2], axis=0, dtype=jnp.float32)
    full_rows = grad_gather(triple_rows)
    triple_grad = jnp.einsum(
        "td,tke->dke", attn_rows, full_rows, preferred_element_type=jnp.float32
    )
    attn_grad = col_total(
        jnp.einsum("tke,dke->td", full_rows, triple_w, preferred_element_type=jnp.float32)
    )
    norm_one_grad, gain_one, shift_one = norm_backward(attn_grad, normed_one, inv_one, gains[0])
    start_grad = middle_grad + norm_one_grad
    terms = (
        jnp.stack([gain_one, gain_two]),
        jnp.stack([shift_one, shift_two]),
        triple_grad,
        triple_bias_grad,
        output_grad,
        output_bias_grad,
        up_grad,
        up_bias_grad,
        down_grad,
        down_bias_grad,
    )
    return (start_grad, terms)


def general_plan(
    tokens,
    segments,
    norm_gain,
    norm_shift,
    triple_weight,
    triple_bias,
    output_weight,
    output_bias,
    up_weight,
    up_bias,
    down_weight,
    down_bias,
    cotangent,
):

    def weights_of(layer_id):
        return (
            triple_weight[layer_id],
            output_weight[layer_id],
            up_weight[layer_id],
            down_weight[layer_id],
        )

    def small_of(layer_id):
        return (
            norm_gain[layer_id].astype(jnp.float32),
            norm_shift[layer_id].astype(jnp.float32),
            triple_bias[layer_id].astype(jnp.float32),
            output_bias[layer_id].astype(jnp.float32),
            up_bias[layer_id].astype(jnp.float32),
            down_bias[layer_id].astype(jnp.float32),
        )

    stream = tokens.astype(jnp.float32)
    stored = []
    for layer_id in range(LAYERS):
        stream, saved = layer_forward(stream, weights_of(layer_id), small_of(layer_id), segments)
        stored.append(saved)
    result = stream.astype(jnp.bfloat16)
    grad = cotangent.astype(jnp.float32)
    summed = [None] * LAYERS
    for layer_id in reversed(range(LAYERS)):
        grad, terms = layer_backward(
            grad, stored[layer_id], weights_of(layer_id), small_of(layer_id)[0], segments
        )
        summed[layer_id] = (
            lax.psum(terms[0].astype(jnp.bfloat16), "dp").astype(jnp.float32),
            lax.psum(terms[1].astype(jnp.bfloat16), "dp").astype(jnp.float32),
            lax.psum(terms[2].astype(jnp.bfloat16), "dp").astype(jnp.float32),
            lax.psum(terms[3].astype(jnp.bfloat16), "dp").astype(jnp.float32),
            lax.psum(terms[4].astype(jnp.bfloat16), "dp").astype(jnp.float32),
            lax.psum(terms[5].astype(jnp.bfloat16), "dp").astype(jnp.float32),
            lax.psum(terms[6].astype(jnp.bfloat16), "dp").astype(jnp.float32),
            lax.psum(terms[7].astype(jnp.bfloat16), "dp").astype(jnp.float32),
            lax.psum(terms[8].astype(jnp.bfloat16), "dp").astype(jnp.float32),
            lax.psum(terms[9].astype(jnp.bfloat16), "dp").astype(jnp.float32),
        )
    stacks = [
        jnp.stack([summed[layer_id][member] for layer_id in range(LAYERS)]) for member in range(10)
    ]
    return (
        result,
        grad,
        stacks[0],
        stacks[1],
        stacks[2],
        stacks[3],
        stacks[4],
        stacks[5],
        stacks[6],
        stacks[7],
        stacks[8],
        stacks[9],
    )


f32 = jnp.float32
bf16 = jnp.bfloat16
CHUNKS = 2
SPAN = LEN // CHUNKS
OWN = SPAN // 2
WIDTH = D // 4
QB = 256


def fits_pairs(shape, arrays):
    return (
        shape["row"] == 4
        and shape["col"] == 2
        and shape["dp"] == 4
        and arrays[0].shape == (2 * LEN, WIDTH)
        and arrays[8].shape[2] == 8 * WIDTH
    )


def swap_row(value, bits):
    return lax.ppermute(value, "row", [(i, i ^ bits) for i in range(4)])


def swap_core(value):
    return swap_row(value, 1)


def swap_chip(value):
    return swap_row(value, 2)


def swap_col(value):
    return lax.ppermute(value, "col", [(0, 1), (1, 0)])


def after(value, *others):
    return lax.optimization_barrier((value, *others))[0]


def dp_total(value):
    place = lax.axis_index("dp")
    inner = (place == 1) | (place == 2)
    kind = value.dtype
    from_end = lax.ppermute(value, "dp", [(0, 1), (3, 2)])
    half = (value.astype(f32) + from_end.astype(f32)).astype(kind)
    from_inner = lax.ppermute(half, "dp", [(1, 2), (2, 1)])
    whole = (half.astype(f32) + from_inner.astype(f32)).astype(kind)
    back = lax.ppermute(whole, "dp", [(1, 0), (2, 3)])
    return jnp.where(inner, whole, back)


def half_of(value, index, axis):
    size = value.shape[axis] // 2
    return lax.dynamic_slice_in_dim(value, index * size, size, axis)


def in_place(first, mine, other, axis):
    return jnp.where(
        first,
        jnp.concatenate([mine, other], axis=axis),
        jnp.concatenate([other, mine], axis=axis),
    )


def gather_weight(core, own, cut, join):
    peer = swap_chip(own)
    mine = [half_of(v, core, cut) for v in (own, peer)]
    theirs = jnp.stack([half_of(v, 1 - core, cut) for v in (own, peer)])
    theirs = swap_core(theirs)
    return jnp.concatenate([mine[0], theirs[0], mine[1], theirs[1]], axis=join), peer


def spread_grad(keep, give):
    row = lax.axis_index("row")
    keep, give = [jnp.where(row % 2 == 0, a, b) for a, b in ((keep, give), (give, keep))]
    keep, give = [jnp.where(row // 2 == 0, v, v[::-1]) for v in (keep, give)]
    got = swap_core(give)
    away = swap_chip(jnp.stack([keep[1], got[1]]))
    own = jnp.stack([keep[0], got[0]])
    total = dp_total((own.astype(f32) + away.astype(f32)).astype(bf16)).astype(f32)
    return total[0], total[1]


def dot(a, b):
    return lax.dot_general(a, b, (((1,), (0,)), ((), ())), preferred_element_type=f32)


def dot_nt(a, b):
    return lax.dot_general(a, b, (((1,), (1,)), ((), ())), preferred_element_type=f32)


def dot_tn(a, b):
    return lax.dot_general(a, b, (((0,), (0,)), ((), ())), preferred_element_type=f32)


def kernel_call(body, outs, args, flops, grid=None, in_specs=None, out_specs=None, scratch=(), limit=40):
    moved = sum(math.prod(v.shape) * v.dtype.itemsize for v in (*outs, *args))
    whole = pl.BlockSpec(memory_space=pltpu.VMEM)
    if in_specs is None:
        in_specs = [
            pl.BlockSpec(memory_space=pltpu.SMEM) if v.dtype == jnp.int32 and v.size == 1 else whole
            for v in args
        ]
    extra = {} if grid is None else {"grid": grid}
    return pl.pallas_call(
        body,
        out_shape=outs,
        in_specs=in_specs,
        out_specs=out_specs if out_specs is not None else [whole] * len(outs),
        scratch_shapes=list(scratch),
        compiler_params=pltpu.CompilerParams(vmem_limit_bytes=limit * 1024 * 1024),
        cost_estimate=pl.CostEstimate(flops=flops, bytes_accessed=moved, transcendentals=0),
        **extra,
    )(*args)


def like(shape, kind):
    return jax.ShapeDtypeStruct(shape, kind)


def other_order(value):
    return value


def part_rows(index):
    return pl.ds(pl.multiple_of(index * OWN, OWN), OWN)


def join_tokens(core_ref, own_ref, sib_ref, full_ref):
    core = core_ref[0]
    full_ref[part_rows(core), :] = own_ref[...]
    full_ref[part_rows(1 - core), :] = other_order(sib_ref[...])


def part_tokens(core_ref, sums_ref, mine_ref, other_ref):
    core = core_ref[0]
    mine_ref[...] = sums_ref[part_rows(core), :]
    other_ref[...] = other_order(sums_ref[part_rows(1 - core), :]).astype(bf16)


def head_lanes(h):
    lane = lax.broadcasted_iota(jnp.int32, (1, WIDTH), 1)
    return (lane >= h * HD) & (lane < (h + 1) * HD)


def allowed_pairs(seg_col, seg_row, start, keys):
    same = seg_col == seg_row
    query = lax.broadcasted_iota(jnp.int32, (QB, keys), 0) + start
    key = lax.broadcasted_iota(jnp.int32, (QB, keys), 1)
    return same & (key <= query)


HEADS_HERE = WIDTH // HD


def attend_body(chunk, *refs):
    core_ref, own_ref, sib_ref, triple_w_ref, bias_ref, output_w_ref, col_ref, row_ref = refs[:8]
    earlier = refs[8 : 8 + chunk]
    full_ref, triple_ref, mixed_ref, log_ref, mine_ref, other_ref = refs[8 + chunk : 14 + chunk]
    kv_ref, sums_ref = refs[14 + chunk :]
    scale = 1.0 / math.sqrt(HD)
    join_tokens(core_ref, own_ref, sib_ref, full_ref)
    for part in range(3):
        cols = slice(part * WIDTH, (part + 1) * WIDTH)
        triple_ref[:, cols] = (
            dot(full_ref[...], triple_w_ref[:, cols]) + bias_ref[:, cols]
        ).astype(bf16)
    for k in range(chunk):
        kv_ref[k * SPAN : (k + 1) * SPAN, :] = earlier[k][:, WIDTH:]
    kv_ref[chunk * SPAN :, :] = triple_ref[:, WIDTH:]
    for block in range(SPAN // QB):
        rows = slice(block * QB, (block + 1) * QB)
        start = chunk * SPAN + block * QB
        keys = start + QB
        allowed = allowed_pairs(col_ref[start : start + QB, :], row_ref[:, :keys], start, keys)
        queries = triple_ref[rows, :WIDTH] * scale
        key_rows = kv_ref[:keys, :WIDTH]
        value_rows = kv_ref[:keys, WIDTH:]
        blended = jnp.zeros((QB, WIDTH), f32)
        for h in range(HEADS_HERE):
            lanes = head_lanes(h)
            scores = dot_nt(jnp.where(lanes, queries, 0).astype(bf16), key_rows)
            scores = jnp.where(allowed, scores, masked)
            peak = jnp.max(scores, axis=1, keepdims=True)
            exponent = jnp.exp(scores - peak)
            total = jnp.sum(exponent, axis=1, keepdims=True)
            soft = (exponent * (1.0 / total)).astype(bf16)
            blended = jnp.where(lanes, dot(soft, value_rows), blended)
            log_ref[rows, h : h + 1] = peak + jnp.log(total)
        mixed_ref[rows, :] = blended.astype(bf16)
    sums_ref[...] = dot(mixed_ref[...], output_w_ref[...])
    part_tokens(core_ref, sums_ref, mine_ref, other_ref)


def attend_call(chunk, core, own, sib, triple_w, bias, output_w, seg_col, seg_row, earlier):
    return kernel_call(
        lambda *refs: attend_body(chunk, *refs),
        [
            like((SPAN, D), bf16),
            like((SPAN, 3 * WIDTH), bf16),
            like((SPAN, WIDTH), bf16),
            like((SPAN, 128), f32),
            like((OWN, D), f32),
            like((OWN, D), bf16),
        ],
        (core, own, sib, triple_w, bias, output_w, seg_col, seg_row, *earlier),
        2 * SPAN * D * 4 * WIDTH + 8 * 4 * SPAN * (chunk + 1) * SPAN * WIDTH,
        scratch=[pltpu.VMEM(((chunk + 1) * SPAN, 2 * WIDTH), bf16), pltpu.VMEM((SPAN, D), f32)],
    )


GELU = math.sqrt(2.0 / math.pi)


def mlp_body(core_ref, own_ref, sib_ref, up_ref, bias_ref, down_ref, *refs):
    full_ref, pre_ref, active_ref, mine_ref, other_ref, sums_ref = refs
    step = pl.program_id(0)

    @pl.when(step == 0)
    def _():
        join_tokens(core_ref, own_ref, sib_ref, full_ref)

    pre = dot(full_ref[...], up_ref[...]) + bias_ref[...]
    pre_ref[...] = pre
    curve = jnp.tanh(GELU * (pre + 0.044715 * (pre * pre * pre)))
    active = (0.5 * pre * (1.0 + curve)).astype(bf16)
    active_ref[...] = active
    sums = dot(active, down_ref[...])

    @pl.when(step == 0)
    def _():
        sums_ref[...] = sums

    @pl.when(step > 0)
    def _():
        sums_ref[...] += sums

    @pl.when(step == pl.num_programs(0) - 1)
    def _():
        part_tokens(core_ref, sums_ref, mine_ref, other_ref)


def mlp_call(core, own, sib, up_w, bias, down_w):
    units = up_w.shape[1]
    step = 256
    whole = pl.BlockSpec((OWN, D), lambda i: (0, 0))
    return kernel_call(
        mlp_body,
        [
            like((SPAN, D), bf16),
            like((SPAN, units), f32),
            like((SPAN, units), bf16),
            like((OWN, D), f32),
            like((OWN, D), bf16),
        ],
        (core, own, sib, up_w, bias, down_w),
        4 * SPAN * D * units,
        grid=(units // step,),
        in_specs=[
            pl.BlockSpec(memory_space=pltpu.SMEM),
            whole,
            whole,
            pl.BlockSpec((D, step), lambda i: (0, i)),
            pl.BlockSpec((1, step), lambda i: (0, i)),
            pl.BlockSpec((step, D), lambda i: (i, 0)),
        ],
        out_specs=[
            pl.BlockSpec((SPAN, D), lambda i: (0, 0)),
            pl.BlockSpec((SPAN, step), lambda i: (0, i)),
            pl.BlockSpec((SPAN, step), lambda i: (0, i)),
            whole,
            whole,
        ],
        scratch=[pltpu.VMEM((SPAN, D), f32)],
    )


def mlp_back_body(core_ref, own_ref, sib_ref, down_ref, pre_ref, up_ref, *refs):
    full_ref, hidden_ref, bias_ref, mine_ref, other_ref, sums_ref = refs
    step = pl.program_id(0)

    @pl.when(step == 0)
    def _():
        join_tokens(core_ref, own_ref, sib_ref, full_ref)

    active_grad = dot_nt(full_ref[...], down_ref[...])
    hidden = (active_grad * pre_ref[...].astype(f32)).astype(bf16)
    hidden_ref[...] = hidden
    bias_ref[...] = jnp.sum(hidden.astype(f32), axis=0, keepdims=True)
    sums = dot_nt(hidden, up_ref[...])

    @pl.when(step == 0)
    def _():
        sums_ref[...] = sums

    @pl.when(step > 0)
    def _():
        sums_ref[...] += sums

    @pl.when(step == pl.num_programs(0) - 1)
    def _():
        part_tokens(core_ref, sums_ref, mine_ref, other_ref)


def mlp_back_call(core, own, sib, down_w, pre, up_w):
    units = up_w.shape[1]
    step = 256
    whole = pl.BlockSpec((OWN, D), lambda i: (0, 0))
    return kernel_call(
        mlp_back_body,
        [
            like((SPAN, D), bf16),
            like((SPAN, units), bf16),
            like((1, units), f32),
            like((OWN, D), f32),
            like((OWN, D), bf16),
        ],
        (core, own, sib, down_w, pre, up_w),
        4 * SPAN * D * units,
        grid=(units // step,),
        in_specs=[
            pl.BlockSpec(memory_space=pltpu.SMEM),
            whole,
            whole,
            pl.BlockSpec((step, D), lambda i: (i, 0)),
            pl.BlockSpec((SPAN, step), lambda i: (0, i)),
            pl.BlockSpec((D, step), lambda i: (0, i)),
        ],
        out_specs=[
            pl.BlockSpec((SPAN, D), lambda i: (0, 0)),
            pl.BlockSpec((SPAN, step), lambda i: (0, i)),
            pl.BlockSpec((1, step), lambda i: (0, i)),
            whole,
            whole,
        ],
        scratch=[pltpu.VMEM((SPAN, D), f32)],
    )


def attend_back_body(chunk, later, *refs):
    core_ref, own_ref, sib_ref, output_w_ref, triple_w_ref, log_ref, col_ref, row_ref = refs[:8]
    triples = refs[8 : 9 + chunk]
    refs = refs[9 + chunk :]
    if later:
        carried_ref, refs = refs[0], refs[1:]
    full_ref, rows_ref, bias_ref, mine_ref, other_ref = refs[:5]
    refs = refs[5:]
    if chunk:
        carry_ref, refs = refs[0], refs[1:]
    kv_ref, grad_ref, total_ref, sums_ref = refs
    scale = 1.0 / math.sqrt(HD)
    triple_ref = triples[chunk]
    join_tokens(core_ref, own_ref, sib_ref, full_ref)
    grad_ref[...] = dot_nt(full_ref[...], output_w_ref[...]).astype(bf16)
    for k in range(chunk + 1):
        kv_ref[k * SPAN : (k + 1) * SPAN, :] = triples[k][:, WIDTH:]
    if later:
        total_ref[...] = carried_ref[...]
    else:
        total_ref[...] = jnp.zeros_like(total_ref)
    for block in range(SPAN // QB):
        rows = slice(block * QB, (block + 1) * QB)
        start = chunk * SPAN + block * QB
        keys = start + QB
        allowed = allowed_pairs(col_ref[start : start + QB, :], row_ref[:, :keys], start, keys)
        queries = triple_ref[rows, :WIDTH] * scale
        grads = grad_ref[rows, :]
        key_rows = kv_ref[:keys, :WIDTH]
        value_rows = kv_ref[:keys, WIDTH:]
        query_grad = jnp.zeros((QB, WIDTH), f32)
        for h in range(HEADS_HERE):
            lanes = head_lanes(h)
            query = jnp.where(lanes, queries, 0).astype(bf16)
            grad = jnp.where(lanes, grads, 0).astype(bf16)
            scores = jnp.where(allowed, dot_nt(query, key_rows), masked)
            chances = jnp.exp(scores - log_ref[rows, h : h + 1])
            product = chances * dot_nt(grad, value_rows)
            inner = jnp.sum(product, axis=1, keepdims=True)
            score_grad = (product - chances * inner).astype(bf16)
            query_grad = jnp.where(lanes, dot(score_grad, key_rows), query_grad)
            total_ref[:keys, :WIDTH] += dot_tn(score_grad, query)
            total_ref[:keys, WIDTH:] += dot_tn(chances.astype(bf16), grad)
        rows_ref[rows, :WIDTH] = (query_grad * scale).astype(bf16)
    rows_ref[:, WIDTH:] = total_ref[chunk * SPAN :, :].astype(bf16)
    if chunk:
        carry_ref[...] = total_ref[: chunk * SPAN, :]
    bias_ref[0:1, :] = jnp.sum(rows_ref[:, :WIDTH].astype(f32), axis=0, keepdims=True)
    bias_ref[1:2, :] = jnp.sum(rows_ref[:, 2 * WIDTH :].astype(f32), axis=0, keepdims=True)
    sums_ref[...] = dot_nt(rows_ref[...], triple_w_ref[...])
    part_tokens(core_ref, sums_ref, mine_ref, other_ref)


def attend_back_call(
    chunk, core, own, sib, output_w, triple_w, logs, seg_col, seg_row, triples, carried
):
    outs = [
        like((SPAN, D), bf16),
        like((SPAN, 3 * WIDTH), bf16),
        like((2, WIDTH), f32),
        like((OWN, D), f32),
        like((OWN, D), bf16),
    ]
    if chunk:
        outs.append(like((chunk * SPAN, 2 * WIDTH), f32))
    later = () if carried is None else (carried,)
    return kernel_call(
        lambda *refs: attend_back_body(chunk, bool(later), *refs),
        outs,
        (core, own, sib, output_w, triple_w, logs, seg_col, seg_row, *triples, *later),
        2 * SPAN * D * 4 * WIDTH + 20 * 4 * SPAN * (chunk + 1) * SPAN * WIDTH,
        scratch=[
            pltpu.VMEM(((chunk + 1) * SPAN, 2 * WIDTH), bf16),
            pltpu.VMEM((SPAN, WIDTH), bf16),
            pltpu.VMEM(((chunk + 1) * SPAN, 2 * WIDTH), f32),
            pltpu.VMEM((SPAN, D), f32),
        ],
    )


def weight_grad_body(join, *refs):
    left, right = refs[:CHUNKS], refs[CHUNKS : 2 * CHUNKS]
    keep_ref, give_ref = refs[2 * CHUNKS :]
    total = dot_tn(left[0][...], right[0][...])
    for k in range(1, CHUNKS):
        total += dot_tn(left[k][...], right[k][...])
    total = total.astype(bf16)
    if join == 0:
        keep_ref[0] = total[:WIDTH]
        give_ref[0] = total[WIDTH:]
    else:
        for k in range(2):
            keep_ref[k] = total[:, 2 * k * WIDTH : (2 * k + 1) * WIDTH]
            give_ref[k] = total[:, (2 * k + 1) * WIDTH : (2 * k + 2) * WIDTH]


def weight_grad(left, right, join):
    high, across = left[0].shape[1], right[0].shape[1]
    part = min(512, high)
    steps = high // part
    if join == 0:
        shape = (2, WIDTH, across)
        out = pl.BlockSpec((1, WIDTH, across), lambda i: (i, 0, 0))
    else:
        shape = (2, high, WIDTH)
        out = pl.BlockSpec((2, part, WIDTH), lambda i: (0, i, 0))
    return kernel_call(
        lambda *refs: weight_grad_body(join, *refs),
        [like(shape, bf16)] * 2,
        (*left, *right),
        2 * LEN * high * across,
        grid=(steps,),
        in_specs=[pl.BlockSpec((SPAN, part), lambda i: (0, i))] * CHUNKS
        + [pl.BlockSpec((SPAN, across), lambda i: (0, 0))] * CHUNKS,
        out_specs=[out, out],
    )


def mean_lanes(v):
    return jnp.sum(v, axis=1, keepdims=True) * (1.0 / D)


def norm_parts(v):
    center = mean_lanes(v)
    second = mean_lanes(v * v) - center * center
    inv_std = lax.rsqrt(second + eps)
    return (v - center) * inv_std, inv_std


def norm_body(stream_ref, chip_ref, got_ref, bias_ref, gain_ref, shift_ref, after_ref, out_ref):
    total = chip_ref[...].astype(f32) + got_ref[...].astype(f32)
    after_sum = stream_ref[...] + (total + bias_ref[...])
    after_ref[...] = after_sum
    normed, _ = norm_parts(after_sum)
    out_ref[...] = (normed * gain_ref[...] + shift_ref[...]).astype(bf16)


def norm_call(stream, chip, got, bias, gain, shift):
    return kernel_call(
        norm_body,
        [like((OWN, D), f32), like((OWN, D), bf16)],
        (stream, chip, got, bias[None], gain[None], shift[None]),
        20 * OWN * D,
    )


def norm_back_body(grad_ref, chip_ref, got_ref, stream_ref, gain_ref, out_ref, low_ref, sums_ref):
    grad_out = chip_ref[...].astype(f32) + got_ref[...].astype(f32)
    normed, inv_std = norm_parts(stream_ref[...])
    scaled = grad_out * gain_ref[...]
    total = grad_ref[...] + inv_std * (
        scaled - mean_lanes(scaled) - normed * mean_lanes(scaled * normed)
    )
    low = total.astype(bf16)
    out_ref[...] = total
    low_ref[...] = low
    sums_ref[0:1, :] = jnp.sum(grad_out * normed, axis=0, keepdims=True)
    sums_ref[1:2, :] = jnp.sum(grad_out, axis=0, keepdims=True)
    sums_ref[2:3, :] = jnp.sum(low.astype(f32), axis=0, keepdims=True)


def norm_back_call(grad, chip, got, stream, gain):
    return kernel_call(
        norm_back_body,
        [like((OWN, D), f32), like((OWN, D), bf16), like((3, D), f32)],
        (grad, chip, got, stream, gain[None]),
        30 * OWN * D,
    )


def chip_total(mine, other):
    return (mine + swap_core(other).astype(f32)).astype(bf16)


MESH = pl.DeviceIdType.MESH
HEADS_HERE = WIDTH // HD
SMALL = 24


class Place:
    def __init__(self):
        self.row = lax.axis_index("row")
        self.col = lax.axis_index("col")
        self.dp = lax.axis_index("dp")
        self.core = self.row % 2
        self.chip = self.row // 2
        self.half = self.dp % 2
        sibling = self.row + 1 - 2 * self.core
        self.rows = [self.row, sibling, (self.row + 2) % 4, (sibling + 2) % 4]
        self.cores = [self.core, 1 - self.core, self.core, 1 - self.core]

    def to_row(self, j):
        return {"row": self.rows[j]}

    def to_col(self):
        return {"col": 1 - self.col}

    def to_dp(self):
        return {"dp": self.dp + 1 - 2 * self.half}


class Copies:
    def __init__(self, sems):
        self.sems = sems
        self.used = 0
        self.open = []

    def sem(self):
        self.used += 1
        return self.sems.at[self.used - 1]

    def local(self, src, dst):
        copy = pltpu.make_async_copy(src, dst, self.sem())
        copy.start()
        return copy

    def save(self, src, dst):
        self.open.append(self.local(src, dst).wait)

    def trade(self, src, dst, landing, device):
        sent, got = self.sem(), self.sem()
        out = pltpu.make_async_remote_copy(src, dst, sent, got, device_id=device, device_id_type=MESH)
        back = pltpu.make_async_remote_copy(
            landing, landing, sent, got, device_id=device, device_id_type=MESH
        )
        out.start()
        return out.wait_send, back.wait_recv

    def finish(self):
        for wait in self.open:
            wait()


def greet(place, devices):
    barrier = pltpu.get_barrier_semaphore()
    for device in devices:
        pl.semaphore_signal(barrier, inc=1, device_id=device, device_id_type=MESH)
    pl.semaphore_wait(barrier, len(devices))


def span(start, size):
    return pl.ds(pl.multiple_of(start, size), size)


def weight_cuts(kind, layer, wide, local):
    w = WIDTH
    if kind == 0:

        def source(core, half):
            rows = slice(None) if half is None else span(half * (w // 2), w // 2)
            return local.at[layer, :, rows, span(core * w, w)]

        def target(row, half):
            rows = span(row * w, w) if half is None else span(row * w + half * (w // 2), w // 2)
            return wide.at[layer, :, rows, :]

    elif kind == 2:
        units = wide.shape[2]

        def source(core, half):
            rows = slice(None) if half is None else span(half * (w // 2), w // 2)
            return local.at[layer, rows, span(core * units, units)]

        def target(row, half):
            rows = span(row * w, w) if half is None else span(row * w + half * (w // 2), w // 2)
            return wide.at[layer, rows, :]

    else:
        high = wide.shape[1]

        def source(core, half):
            if half is None:
                return local.at[layer, span(core * high, high), :]
            return local.at[layer, span(core * high + half * (high // 2), high // 2), :]

        def target(row, half):
            rows = slice(None) if half is None else span(half * (high // 2), high // 2)
            return wide.at[layer, rows, span(row * w, w)]

    return source, target


def strips(count, body):
    def step(i, carry):
        body(pl.multiple_of(i * 32, 32))
        return carry

    lax.fori_loop(0, count // 32, step, 0)


def causal(seg_col, seg_row, start, keys):
    query = lax.broadcasted_iota(jnp.int32, (QB, keys), 0) + start
    key = lax.broadcasted_iota(jnp.int32, (QB, keys), 1)
    return (seg_col == seg_row) & (key <= query)


def lanes_of(h):
    lane = lax.broadcasted_iota(jnp.int32, (1, WIDTH), 1)
    return (lane >= h * HD) & (lane < (h + 1) * HD)


def attend_chunk(k, triples, seg_col_ref, seg_row_ref, kv_ref, mixed_ref, log_ref):
    scale = 1.0 / math.sqrt(HD)
    kv_ref[k * SPAN : (k + 1) * SPAN, :] = triples[k][:, WIDTH:]
    for block in range(SPAN // QB):
        rows = slice(block * QB, (block + 1) * QB)
        start = k * SPAN + block * QB
        keys = start + QB
        allowed = causal(seg_col_ref[start : start + QB, :], seg_row_ref[:, :keys], start, keys)
        queries = triples[k][rows, :WIDTH] * scale
        key_rows = kv_ref[:keys, :WIDTH]
        value_rows = kv_ref[:keys, WIDTH:]
        blended = jnp.zeros((QB, WIDTH), f32)
        for h in range(HEADS_HERE):
            lanes = lanes_of(h)
            scores = dot_nt(jnp.where(lanes, queries, 0).astype(bf16), key_rows)
            scores = jnp.where(allowed, scores, masked)
            peak = jnp.max(scores, axis=1, keepdims=True)
            exponent = jnp.exp(scores - peak)
            total = jnp.sum(exponent, axis=1, keepdims=True)
            soft = (exponent * (1.0 / total)).astype(bf16)
            blended = jnp.where(lanes, dot(soft, value_rows), blended)
            log_ref[rows, h : h + 1] = peak + jnp.log(total)
        mixed_ref[rows, :] = blended.astype(bf16)


def forward_body(*refs):
    (
        tokens_ref,
        cotangent_ref,
        small_ref,
        seg_col_ref,
        seg_row_ref,
        triple_in,
        output_in,
        up_in,
        down_in,
        result_ref,
        grad_ref,
        wide_out,
        triple_out,
        output_out,
        up_out,
        down_out,
        attn_out,
        rows_out,
        mixed_out,
        log_out,
        mlp_out,
        slope_out,
        active_out,
        stream_out,
        triple_w,
        output_w,
        up_w,
        down_w,
        attn,
        rows,
        mixed,
        logs,
        mlp,
        slope,
        active,
        stream,
        taken,
        wide,
        kv,
        mine,
        give,
        got_core,
        chip_sum,
        got_col,
        final,
        sems,
    ) = refs
    place = Place()
    copies = Copies(sems)
    core, sibling = place.core, 1 - place.core
    greet(place, [place.to_row(1), place.to_row(2), place.to_row(3), place.to_col(), place.to_dp()])

    own_lanes = span(place.row * WIDTH, WIDTH)

    def held(j, k):
        return span(place.rows[j] // 2 * LEN + k * SPAN + place.cores[j] * OWN, OWN)

    def part(c):
        return span(c * OWN, OWN)

    small_waits = []
    copy = copies.local(small_ref, wide.at[:, own_lanes])
    small_waits.append(copy.wait)
    for j in range(1, 4):
        sent, got = copies.trade(
            small_ref,
            wide.at[:, own_lanes],
            wide.at[:, span(place.rows[j] * WIDTH, WIDTH)],
            place.to_row(j),
        )
        copies.open.append(sent)
        small_waits.append(got)
    token_waits = [[] for _ in range(CHUNKS)]

    def scatter_in(block_ref, target, k, waits):
        waits.append(copies.local(block_ref.at[held(0, k), :], target.at[k, :, own_lanes]).wait)
        for j in range(1, 4):
            sent, got = copies.trade(
                block_ref.at[held(j, k), :],
                target.at[k, :, own_lanes],
                target.at[k, :, span(place.rows[j] * WIDTH, WIDTH)],
                place.to_row(j),
            )
            copies.open.append(sent)
            waits.append(got)

    arrivals, ready_waits = {}, {}

    def send_weight(layer, kind):
        local = (triple_in, output_in, up_in, down_in)[kind]
        whole = (triple_w, output_w, up_w, down_w)[kind]
        source, target = weight_cuts(kind, layer, whole, local)
        here = []
        for j in (2, 3):
            sent, got = copies.trade(
                source(place.cores[j], place.half),
                target(place.row, place.half),
                target(place.rows[j], place.half),
                place.to_row(j),
            )
            copies.open.append(sent)
            here.append((got, target(place.rows[j], place.half), target(place.rows[j], 1 - place.half)))
        arrivals[layer, kind] = here
        sent, got = copies.trade(
            source(sibling, None),
            target(place.row, None),
            target(place.rows[1], None),
            place.to_row(1),
        )
        copies.open.append(sent)
        own = copies.local(source(core, None), target(place.row, None))
        ready_waits[layer, kind] = [got, own.wait]

    def relay_weight(layer, kind):
        for got, arrived, missing in arrivals[layer, kind]:
            got()
            sent, back = copies.trade(arrived, arrived, missing, place.to_dp())
            copies.open.append(sent)
            ready_waits[layer, kind].append(back)

    def ready_weight(layer, kind):
        for wait in ready_waits[layer, kind]:
            wait()
        whole = (triple_w, output_w, up_w, down_w)[kind]
        out = (triple_out, output_out, up_out, down_out)[kind]
        copies.save(whole.at[layer], out.at[layer])

    scatter_in(tokens_ref, taken, 0, token_waits[0])
    send_weight(0, 0)
    scatter_in(tokens_ref, taken, 1, token_waits[1])
    for layer, kind in ((0, 1), (0, 2), (0, 3), (1, 0), (1, 1), (1, 2), (1, 3)):
        send_weight(layer, kind)
    grad_waits = []
    for k in range(CHUNKS):
        scatter_in(cotangent_ref, grad_ref, k, grad_waits)

    for wait in small_waits:
        wait()
    copies.save(wide, wide_out)

    def gain(layer, which):
        return wide[2 * layer + which : 2 * layer + which + 1, :]

    def shift(layer, which):
        return wide[4 + 2 * layer + which : 5 + 2 * layer + which, :]

    def output_bias(layer):
        return wide[8 + layer : 9 + layer, :]

    def down_bias(layer):
        return wide[10 + layer : 11 + layer, :]

    def of_core(line, start, size):
        return wide[line : line + 1, span(start, size)]

    def triple_bias(layer, which):
        at = 2 * core * WIDTH + which * (WIDTH // 2)
        size = WIDTH // 2
        return jnp.concatenate(
            [of_core(12 + layer, at, size), of_core(12 + layer, at + WIDTH, size)], axis=1
        )

    def up_bias(layer):
        line, at = 14 + 2 * layer, 2 * core * WIDTH
        return jnp.concatenate(
            [of_core(line + a, at + b * WIDTH, WIDTH) for b in range(2) for a in range(2)], axis=1
        )

    def norm_to(value, layer, which, target, at):
        center = jnp.mean(value, axis=1, keepdims=True)
        second = jnp.mean(value * value, axis=1, keepdims=True) - center * center
        normed = (value - center) * lax.rsqrt(second + eps)
        target[pl.ds(pl.multiple_of(core * OWN + at, 32), 32), :] = (
            normed * gain(layer, which) + shift(layer, which)
        ).astype(bf16)

    def share(target):
        return copies.trade(target.at[part(core)], target.at[part(core)], target.at[part(sibling)], place.to_row(1))

    def give_rows(k, value):
        give[k] = value.astype(bf16)

    sent_core, sent_col = [None] * CHUNKS, [None] * CHUNKS
    col_waits = [None] * CHUNKS
    saves = {}

    def settle(stage, k, got):
        got()
        if sent_col[k] is not None:
            sent_col[k]()

        def add(at):
            lines = pl.ds(at, 32)
            chip_sum[k, lines, :] = (
                mine[k, lines, :] + got_core[stage, k, lines, :].astype(f32)
            ).astype(bf16)

        strips(OWN, add)
        sent_col[k], col_waits[k] = copies.trade(
            chip_sum.at[k], got_col.at[stage, k], got_col.at[stage, k], place.to_col()
        )

    def start_core(stage, k):
        sent, got = copies.trade(
            give.at[k], got_core.at[stage, k], got_core.at[stage, k], place.to_row(1)
        )
        sent_core[k] = sent
        return got

    def take_col(stage, k, layer, bias, after_ref):
        col_waits[k]()

        def add(at):
            lines = pl.ds(at, 32)
            total = chip_sum[k, lines, :].astype(f32) + got_col[stage, k, lines, :].astype(f32)
            value = stream[stage, k, lines, :] + (total + bias)
            stream[1 - stage, k, lines, :] = value
            after_ref(value, at)

        strips(OWN, add)

    shares = [None] * CHUNKS
    for k in range(CHUNKS):
        for wait in token_waits[k]:
            wait()
        if k == 0:
            pass

        def first(at, k=k):
            value = taken[k, pl.ds(at, 32), :].astype(f32)
            stream[0, k, pl.ds(at, 32), :] = value
            norm_to(value, 0, 0, attn.at[0, k], at)

        strips(OWN, first)
        saves[0, 0, k] = copies.local(stream.at[0, k], stream_out.at[0, 0, k])
        shares[k] = share(attn.at[0, k])
        if k == 0:
            relay_weight(0, 0)
    relay_weight(0, 1)
    pump = [(0, 2), (0, 3), (1, 0), (1, 1), (1, 2), (1, 3)]

    def pump_one():
        if pump:
            relay_weight(*pump.pop(0))

    for layer in range(LAYERS):
        for k in range(CHUNKS):
            if layer:
                saves.pop((layer - 1, 0, k)).wait()
                take_col(
                    1, k, layer, down_bias(layer - 1), lambda v, at, k=k: norm_to(v, layer, 0, attn.at[layer, k], at)
                )
                saves[layer, 0, k] = copies.local(stream.at[0, k], stream_out.at[layer, 0, k])
                shares[k] = share(attn.at[layer, k])
            if k == 0:
                ready_weight(layer, 0)
            bias = [triple_bias(layer, 0), None, triple_bias(layer, 1)]

            def project(c, k=k, bias=bias):
                for third in range(3):
                    value = dot(attn[layer, k, part(c), :], triple_w[layer, third])
                    if bias[third] is not None:
                        value = value + bias[third]
                    rows[layer, k, part(c), third * WIDTH : (third + 1) * WIDTH] = value.astype(bf16)

            project(core)
            sent, got = shares[k]
            got()
            project(sibling)
            attend_chunk(
                k,
                [rows.at[layer, i] for i in range(k + 1)],
                seg_col_ref,
                seg_row_ref,
                kv,
                mixed.at[layer, k],
                logs.at[layer, k],
            )
            if k == 0:
                ready_weight(layer, 1)
            if sent_core[k] is not None:
                sent_core[k]()
            give[k] = dot(mixed[layer, k, part(sibling), :], output_w[layer]).astype(bf16)
            got = start_core(0, k)
            mine[k] = dot(mixed[layer, k, part(core), :], output_w[layer])
            sent()
            copies.save(attn.at[layer, k], attn_out.at[layer, k])
            copies.save(rows.at[layer, k], rows_out.at[layer, k])
            copies.save(mixed.at[layer, k], mixed_out.at[layer, k])
            copies.save(logs.at[layer, k], log_out.at[layer, k])
            settle(0, k, got)
            pump_one()
        for k in range(CHUNKS):
            if layer:
                saves.pop((layer - 1, 1, k)).wait()
            take_col(
                0, k, layer, output_bias(layer), lambda v, at, k=k: norm_to(v, layer, 1, mlp.at[layer, k], at)
            )
            saves[layer, 1, k] = copies.local(stream.at[1, k], stream_out.at[layer, 1, k])
            shares[k] = share(mlp.at[layer, k])
            if k == 0:
                ready_weight(layer, 2)
            bias = up_bias(layer)

            def widen(c, k=k, bias=bias):
                for block in range(4):
                    cols = slice(block * WIDTH, (block + 1) * WIDTH)
                    pre = dot(mlp[layer, k, part(c), :], up_w[layer, :, cols]) + bias[:, cols]
                    square = pre * pre
                    curve = jnp.tanh(GELU * (pre + 0.044715 * (square * pre)))
                    upper = 0.5 * (1.0 + curve)
                    active[layer, k, part(c), cols] = (pre * upper).astype(bf16)
                    slope[layer, k, part(c), cols] = (
                        upper
                        + (0.5 * GELU) * pre * (1.0 - curve * curve) * (1.0 + (3.0 * 0.044715) * square)
                    ).astype(bf16)

            widen(core)
            sent, got = shares[k]
            got()
            widen(sibling)
            if k == 0:
                ready_weight(layer, 3)
            sent_core[k]()
            give[k] = dot(active[layer, k, part(sibling), :], down_w[layer]).astype(bf16)
            got = start_core(1, k)
            mine[k] = dot(active[layer, k, part(core), :], down_w[layer])
            sent()
            copies.save(mlp.at[layer, k], mlp_out.at[layer, k])
            copies.save(slope.at[layer, k], slope_out.at[layer, k])
            copies.save(active.at[layer, k], active_out.at[layer, k])
            settle(1, k, got)
            pump_one()
    result_waits = []
    for k in range(CHUNKS):
        saves.pop((LAYERS - 1, 0, k)).wait()

        def finish(v, at, k=k):
            final[k, pl.ds(at, 32), :] = v.astype(bf16)

        take_col(1, k, LAYERS, down_bias(LAYERS - 1), finish)
        result_waits.append(copies.local(final.at[k, :, own_lanes], result_ref.at[held(0, k), :]).wait)
        for j in range(1, 4):
            sent, got = copies.trade(
                final.at[k, :, span(place.rows[j] * WIDTH, WIDTH)],
                result_ref.at[held(0, k), :],
                result_ref.at[held(j, k), :],
                place.to_row(j),
            )
            result_waits += [sent, got]
    for k in range(CHUNKS):
        saves.pop((LAYERS - 1, 1, k)).wait()
        sent_core[k]()
        sent_col[k]()
    for wait in result_waits + grad_waits:
        wait()
    copies.finish()


def forward_call(tokens, cotangent, small, seg_col, seg_row, triple_w, output_w, up_w, down_w):
    units = up_w.shape[2] // 2
    per_layer = [
        ((LAYERS, CHUNKS, SPAN, D), bf16),
        ((LAYERS, CHUNKS, SPAN, 3 * WIDTH), bf16),
        ((LAYERS, CHUNKS, SPAN, WIDTH), bf16),
        ((LAYERS, CHUNKS, SPAN, 128), f32),
        ((LAYERS, CHUNKS, SPAN, D), bf16),
        ((LAYERS, CHUNKS, SPAN, units), bf16),
        ((LAYERS, CHUNKS, SPAN, units), bf16),
    ]
    wide = [
        ((LAYERS, 3, D, WIDTH), bf16),
        ((LAYERS, WIDTH, D), bf16),
        ((LAYERS, D, units), bf16),
        ((LAYERS, units, D), bf16),
    ]
    outs = [
        (tokens.shape, bf16),
        ((CHUNKS, OWN, D), bf16),
        ((SMALL, D), f32),
        *wide,
        *per_layer,
        ((LAYERS, 2, CHUNKS, OWN, D), f32),
    ]
    scratch = [
        *wide,
        *per_layer,
        ((2, CHUNKS, OWN, D), f32),
        ((CHUNKS, OWN, D), bf16),
        ((SMALL, D), f32),
        ((LEN, 2 * WIDTH), bf16),
        ((CHUNKS, OWN, D), f32),
        ((CHUNKS, OWN, D), bf16),
        ((2, CHUNKS, OWN, D), bf16),
        ((CHUNKS, OWN, D), bf16),
        ((2, CHUNKS, OWN, D), bf16),
        ((CHUNKS, OWN, D), bf16),
    ]
    anywhere = pl.BlockSpec(memory_space=pl.ANY)
    inside = pl.BlockSpec(memory_space=pltpu.VMEM)
    return pl.pallas_call(
        forward_body,
        out_shape=[like(*v) for v in outs],
        in_specs=[anywhere] * 2 + [inside] * 3 + [anywhere] * 4,
        out_specs=[anywhere] * len(outs),
        scratch_shapes=[pltpu.VMEM(*v) for v in scratch] + [pltpu.SemaphoreType.DMA((320,))],
        compiler_params=pltpu.CompilerParams(
            collective_id=0, has_side_effects=True, vmem_limit_bytes=60 * 1024 * 1024
        ),
    )(tokens, cotangent, small, seg_col, seg_row, triple_w, output_w, up_w, down_w)


def pack_small(norm_gain, norm_shift, output_bias, down_bias, triple_bias, up_bias):
    lines = [
        norm_gain.reshape(-1, WIDTH),
        norm_shift.reshape(-1, WIDTH),
        output_bias,
        down_bias,
        triple_bias.reshape(-1, WIDTH),
        up_bias.reshape(-1, WIDTH),
    ]
    lines = jnp.concatenate(lines).astype(f32)
    return jnp.pad(lines, ((0, SMALL - lines.shape[0]), (0, 0)))


def pair_plan(
    tokens,
    segments,
    norm_gain,
    norm_shift,
    triple_weight,
    triple_bias,
    output_weight,
    output_bias,
    up_weight,
    up_bias,
    down_weight,
    down_bias,
    cotangent,
):
    row = lax.axis_index("row")
    core = row % 2
    chip = row // 2
    first = core == 0
    core_id = core.astype(jnp.int32).reshape(1)
    chunks = range(CHUNKS)

    def to_features(pieces):
        whole = jnp.concatenate(pieces)
        parts = [lax.dynamic_slice_in_dim(whole, (row ^ j) * WIDTH, WIDTH, 1) for j in range(4)]
        got = [parts[0]] + [swap_row(parts[j], j) for j in range(1, 4)]
        halves = [jnp.stack(pair).reshape(2, CHUNKS, OWN, WIDTH) for pair in (got[:2], got[2:])]
        packs = []
        for pair in halves:
            pair = jnp.where(first, pair, pair[::-1])
            packs.append(jnp.swapaxes(pair, 0, 1).reshape(LEN, WIDTH))
        return jnp.where(
            chip == 0,
            jnp.concatenate(packs),
            jnp.concatenate(packs[::-1]),
        )

    seg_pack = lax.dynamic_slice_in_dim(segments, chip * LEN, LEN, 0)
    seg_col, seg_row = seg_pack[:, None], seg_pack[None, :]
    (
        result,
        grad_in,
        wide,
        triple_wide,
        output_wide,
        up_wide,
        down_wide,
        attn_all,
        rows_all,
        mixed_all,
        log_all,
        mlp_all,
        slope_all,
        active_all,
        stream_all,
    ) = forward_call(
        tokens,
        cotangent,
        pack_small(norm_gain, norm_shift, output_bias, down_bias, triple_bias, up_bias),
        seg_col,
        seg_row,
        jnp.swapaxes(triple_weight, 1, 2),
        output_weight,
        up_weight,
        down_weight,
    )
    low = [grad_in[k] for k in chunks]
    gains = wide[:4].reshape(LAYERS, 2, D)
    weights = []
    stored = []
    for layer in range(LAYERS):
        t = triple_wide[layer]
        weights.append(
            (jnp.concatenate([t[0], t[1], t[2]], axis=1), output_wide[layer], up_wide[layer], down_wide[layer])
        )
        stored.append(
            {
                "start": [stream_all[layer, 0, k] for k in chunks],
                "middle": [stream_all[layer, 1, k] for k in chunks],
                "attn": [attn_all[layer, k] for k in chunks],
                "triple": [rows_all[layer, k] for k in chunks],
                "mixed": [mixed_all[layer, k] for k in chunks],
                "logs": [log_all[layer, k] for k in chunks],
                "mlp": [mlp_all[layer, k] for k in chunks],
                "pre": [slope_all[layer, k] for k in chunks],
                "active": [active_all[layer, k] for k in chunks],
            }
        )
    grad = [v.astype(f32) for v in low]
    low_sums = sum(jnp.sum(v, axis=0) for v in grad)
    grads = [None] * LAYERS
    for layer in reversed(range(LAYERS)):
        triple_w, output_w, up_w, down_w = weights[layer]
        saved = stored[layer]
        down_bias_grad = low_sums
        down_in, hidden, branch, triple_rows = ([None] * CHUNKS for _ in range(4))
        sums_two, sums_one = [], []
        up_bias_grad, triple_bias_grad = [], []
        for k in reversed(chunks):
            down_in[k], hidden[k], bias, mine, other = mlp_back_call(
                core_id, low[k], swap_core(low[k]), down_w, saved["pre"][k], up_w
            )
            up_bias_grad.append(bias[0])
            total = chip_total(mine, other)
            grad[k], low[k], sums = norm_back_call(
                grad[k], total, swap_col(total), saved["middle"][k], gains[layer, 1]
            )
            sums_two.append(sums)
        down_grad = spread_grad(*weight_grad(saved["active"], down_in, 1))
        up_grad = spread_grad(*weight_grad(saved["mlp"], hidden, 0))
        carried = None
        for k in reversed(chunks):
            branch[k], triple_rows[k], bias, mine, other, *carry = attend_back_call(
                k,
                core_id,
                low[k],
                swap_core(low[k]),
                output_w,
                triple_w,
                saved["logs"][k],
                seg_col,
                seg_row,
                saved["triple"][: k + 1],
                carried,
            )
            carried = carry[0] if carry else None
            triple_bias_grad.append(bias)
            total = chip_total(mine, other)
            grad[k], low[k], sums = norm_back_call(
                grad[k], total, swap_col(total), saved["start"][k], gains[layer, 0]
            )
            sums_one.append(sums)
        output_grad = spread_grad(*weight_grad(saved["mixed"], branch, 1))
        triple_grad = spread_grad(*weight_grad(saved["attn"], triple_rows, 0))
        sums_one, sums_two = sum(sums_one), sum(sums_two)
        up_bias_grad, triple_bias_grad = sum(up_bias_grad), sum(triple_bias_grad)
        low_sums = sums_one[2]

        full = jnp.stack(
            [sums_one[0], sums_two[0], sums_one[1], sums_two[1], sums_two[2], down_bias_grad]
        )
        full = jnp.moveaxis(full.reshape(6, 4, WIDTH), 1, 0)
        full = jnp.stack(
            [lax.dynamic_index_in_dim(full, row ^ j, 0, keepdims=False) for j in range(4)]
        )
        theirs = swap_core(full)
        full = full + jnp.stack([theirs[1], theirs[0], theirs[3], theirs[2]])
        full = full[0] + swap_chip(full[2])
        pieces = jnp.concatenate(
            [
                jnp.moveaxis(triple_bias_grad.reshape(2, 2, D // 8), 1, 0).reshape(2, -1),
                up_bias_grad.reshape(2, -1),
            ],
            axis=1,
        )
        pieces = pieces + swap_chip(pieces)
        give = lax.dynamic_index_in_dim(pieces, 1 - core, 0, keepdims=False)
        keep = lax.dynamic_index_in_dim(pieces, core, 0, keepdims=False)
        share = jnp.where(chip == core, keep, swap_core(give))
        packed = jnp.concatenate([full.reshape(-1), share]).reshape(-1, 128)
        packed = dp_total(packed).reshape(-1)
        full = packed[: 6 * WIDTH].reshape(6, WIDTH)
        share = packed[6 * WIDTH :]
        thirds = [slice(part * WIDTH, (part + 1) * WIDTH) for part in range(3)]
        grads[layer] = (
            full[0:2],
            full[2:4],
            jnp.stack(
                [in_place(first, triple_grad[0][:, s], triple_grad[1][:, s], 1) for s in thirds],
                axis=1,
            ),
            share[: D // 4].reshape(2, D // 8),
            in_place(first, output_grad[0], output_grad[1], 0),
            full[4],
            in_place(first, up_grad[0], up_grad[1], 1),
            share[D // 4 :],
            in_place(first, down_grad[0], down_grad[1], 0),
            full[5],
        )
    input_grad = to_features(low).astype(f32)
    stacks = [jnp.stack([grads[layer][k] for layer in range(LAYERS)]) for k in range(10)]
    return (result, input_grad, *stacks)


def solution(mesh):
    in_specs = (
        P("dp", "row"),
        P("dp"),
        P(None, None, "row"),
        P(None, None, "row"),
        P(None, "row", None, "col"),
        P(None, None, ("col", "row")),
        P(None, "col", "row"),
        P(None, "row"),
        P(None, "row", "col"),
        P(None, ("col", "row")),
        P(None, "col", "row"),
        P(None, "row"),
        P("dp", "row"),
    )
    out_specs = (
        P("dp", "row"),
        P("dp", "row"),
        P(None, None, "row"),
        P(None, None, "row"),
        P(None, "row", None, "col"),
        P(None, None, ("col", "row")),
        P(None, "col", "row"),
        P(None, "row"),
        P(None, "row", "col"),
        P(None, ("col", "row")),
        P(None, "col", "row"),
        P(None, "row"),
    )
    shape = mesh.shape

    def on_device(*arrays):
        if fits_pairs(shape, arrays):
            return pair_plan(*arrays)
        return general_plan(*arrays)

    return jax.shard_map(
        on_device, mesh=mesh, in_specs=in_specs, out_specs=out_specs, check_vma=False
    )
```

```python
import math

import jax
import jax.numpy as jnp
from jax import lax
from jax.experimental import pallas as pl
from jax.experimental.pallas import tpu as pltpu
from jax.sharding import PartitionSpec as P

D = 1024
HD = 64
LAYERS = 2
LEN = 1024


eps = 1e-05
masked = -1000000000.0


def norm_forward(stream, gain, shift):
    totals = lax.psum((jnp.sum(stream, axis=1), jnp.sum(stream * stream, axis=1)), "row")
    center = totals[0] / D
    second = totals[1] / D - center * center
    inv_std = lax.rsqrt(second + eps)
    normed = (stream - center[:, None]) * inv_std[:, None]
    return (normed, inv_std, normed * gain + shift)


def norm_backward(grad_out, normed, inv_std, gain):
    scaled = grad_out * gain
    totals = lax.psum((jnp.sum(scaled, axis=1), jnp.sum(scaled * normed, axis=1)), "row")
    grad_in = inv_std[:, None] * (
        scaled - totals[0][:, None] / D - normed * (totals[1][:, None] / D)
    )
    return (grad_in, jnp.sum(grad_out * normed, axis=0), jnp.sum(grad_out, axis=0))


def gather_rows(block):
    return lax.all_gather(block, "row", axis=1, tiled=True)


def col_total(partial_sums):
    return lax.psum(partial_sums, "col")


def rows_back(partial_sums):
    return lax.psum_scatter(
        partial_sums.astype(jnp.bfloat16), "row", scatter_dimension=1, tiled=True
    ).astype(jnp.float32)


def in_parts(partial_sums):
    return lax.psum_scatter(partial_sums, "row", scatter_dimension=2, tiled=True)


def grad_gather(block):
    return lax.all_gather(block, "row", axis=2, tiled=True)


def pack_scores(queries, key_rows, seg_pack, scale):
    position = jnp.arange(queries.shape[0])
    allowed = (seg_pack[:, None] == seg_pack[None, :]) & (position[None, :] <= position[:, None])
    scores = (
        jnp.einsum("qhd,khd->hqk", queries, key_rows, preferred_element_type=jnp.float32) * scale
    )
    return jnp.where(allowed[None], scores, masked)


def split_packs(triple, seg_rows):
    length, three, width = triple.shape
    count = length // LEN
    return (triple.reshape(count, LEN, three, width // HD, HD), seg_rows.reshape(count, LEN))


def attend_forward(triple, seg_rows, scale):
    length, three, width = triple.shape
    packs, seg_packs = split_packs(triple, seg_rows)

    def one_pack(pieces):
        pack_rows, seg_pack = pieces
        scores = pack_scores(pack_rows[:, 0], pack_rows[:, 1], seg_pack, scale)
        row_peak = jnp.max(scores, axis=-1, keepdims=True)
        exponent = jnp.exp(scores - row_peak)
        denominator = jnp.sum(exponent, axis=-1, keepdims=True)
        soft_weights = (exponent / denominator).astype(jnp.bfloat16)
        blended = jnp.einsum(
            "hqk,khd->qhd", soft_weights, pack_rows[:, 2], preferred_element_type=jnp.float32
        )
        return (blended.astype(jnp.bfloat16), (row_peak + jnp.log(denominator))[..., 0])

    blended, log_totals = lax.map(one_pack, (packs, seg_packs))
    return (blended.reshape(length, width), log_totals)


def attend_backward(triple, seg_rows, log_totals, grad_mixed, scale):
    length, three, width = triple.shape
    packs, seg_packs = split_packs(triple, seg_rows)
    grad_packs = grad_mixed.reshape(length // LEN, LEN, width // HD, HD)

    def one_pack(pieces):
        pack_rows, seg_pack, pack_totals, grad_pack = pieces
        queries = pack_rows[:, 0]
        key_rows = pack_rows[:, 1]
        value_rows = pack_rows[:, 2]
        scores = pack_scores(queries, key_rows, seg_pack, scale)
        chances = jnp.exp(scores - pack_totals[:, :, None])
        chance_grad = jnp.einsum(
            "qhd,khd->hqk", grad_pack, value_rows, preferred_element_type=jnp.float32
        )
        inner = jnp.sum(chances * chance_grad, axis=-1, keepdims=True)
        score_grad = (chances * (chance_grad - inner)).astype(jnp.bfloat16)
        query_grad = (
            jnp.einsum("hqk,khd->qhd", score_grad, key_rows, preferred_element_type=jnp.float32)
            * scale
        )
        key_grad = (
            jnp.einsum("hqk,qhd->khd", score_grad, queries, preferred_element_type=jnp.float32)
            * scale
        )
        value_grad = jnp.einsum(
            "hqk,qhd->khd",
            chances.astype(jnp.bfloat16),
            grad_pack,
            preferred_element_type=jnp.float32,
        )
        return jnp.stack([query_grad, key_grad, value_grad], axis=1).astype(jnp.bfloat16)

    triple_rows = lax.map(one_pack, (packs, seg_packs, log_totals, grad_packs))
    return triple_rows.reshape(length, three, width)


def layer_forward(stream, weights, small, seg_rows):
    triple_w, output_w, up_w, down_w = weights
    gains, shifts, triple_b, output_b, up_b, down_b = small
    scale = 1.0 / math.sqrt(HD)
    normed_one, inv_one, attn_in = norm_forward(stream, gains[0], shifts[0])
    attn_in = attn_in.astype(jnp.bfloat16)
    triple = in_parts(
        jnp.einsum("td,dke->tke", attn_in, triple_w, preferred_element_type=jnp.float32)
    )
    bias_rows = jnp.stack([triple_b[0], jnp.zeros_like(triple_b[0]), triple_b[1]])
    triple = (triple + bias_rows).astype(jnp.bfloat16)
    mixed, log_totals = attend_forward(triple, seg_rows, scale)
    mixed_full = gather_rows(mixed)
    middle = stream + (
        col_total(jnp.dot(mixed_full, output_w, preferred_element_type=jnp.float32)) + output_b
    )
    normed_two, inv_two, mlp_in = norm_forward(middle, gains[1], shifts[1])
    mlp_in = mlp_in.astype(jnp.bfloat16)
    hidden_pre = (
        in_parts(jnp.dot(mlp_in, up_w, preferred_element_type=jnp.float32)[:, None, :])[:, 0] + up_b
    )
    active = jax.nn.gelu(hidden_pre, approximate=True).astype(jnp.bfloat16)
    active_full = gather_rows(active)
    after = middle + (
        col_total(jnp.dot(active_full, down_w, preferred_element_type=jnp.float32)) + down_b
    )
    saved = (
        normed_one,
        inv_one,
        attn_in,
        triple,
        log_totals,
        mixed_full,
        normed_two,
        inv_two,
        mlp_in,
        hidden_pre,
        active_full,
        None,
    )
    return (after, saved)


def layer_backward(grad, saved, weights, gains, seg_rows):
    (
        normed_one,
        inv_one,
        attn_rows,
        triple,
        log_totals,
        mixed_full,
        normed_two,
        inv_two,
        mlp_rows,
        hidden_pre,
        active_full,
        columns_in,
    ) = saved
    triple_w, output_w, up_w, down_w = weights
    scale = 1.0 / math.sqrt(HD)
    down_in = grad.astype(jnp.bfloat16)
    down_bias_grad = jnp.sum(down_in, axis=0, dtype=jnp.float32)
    down_grad = jnp.einsum("tf,td->fd", active_full, down_in, preferred_element_type=jnp.float32)
    active_grad = rows_back(
        jnp.einsum("td,fd->tf", down_in, down_w, preferred_element_type=jnp.float32)
    )
    gelu_pull = jax.vjp(lambda value: jax.nn.gelu(value, approximate=True), hidden_pre)[1]
    hidden_grad = gelu_pull(active_grad)[0].astype(jnp.bfloat16)
    up_bias_grad = jnp.sum(hidden_grad, axis=0, dtype=jnp.float32)
    hidden_rows = grad_gather(hidden_grad[:, None, :])[:, 0]
    up_grad = jnp.einsum("td,tf->df", mlp_rows, hidden_rows, preferred_element_type=jnp.float32)
    mlp_grad = col_total(
        jnp.einsum("tf,df->td", hidden_rows, up_w, preferred_element_type=jnp.float32)
    )
    norm_two_grad, gain_two, shift_two = norm_backward(mlp_grad, normed_two, inv_two, gains[1])
    middle_grad = grad + norm_two_grad
    branch_grad = middle_grad.astype(jnp.bfloat16)
    output_bias_grad = jnp.sum(branch_grad, axis=0, dtype=jnp.float32)
    output_grad = jnp.einsum(
        "td,te->de", mixed_full, branch_grad, preferred_element_type=jnp.float32
    )
    mixed_grad = rows_back(
        jnp.einsum("te,de->td", branch_grad, output_w, preferred_element_type=jnp.float32)
    ).astype(jnp.bfloat16)
    triple_rows = attend_backward(triple, seg_rows, log_totals, mixed_grad, scale)
    triple_bias_grad = jnp.sum(triple_rows[:, 0::2], axis=0, dtype=jnp.float32)
    full_rows = grad_gather(triple_rows)
    triple_grad = jnp.einsum(
        "td,tke->dke", attn_rows, full_rows, preferred_element_type=jnp.float32
    )
    attn_grad = col_total(
        jnp.einsum("tke,dke->td", full_rows, triple_w, preferred_element_type=jnp.float32)
    )
    norm_one_grad, gain_one, shift_one = norm_backward(attn_grad, normed_one, inv_one, gains[0])
    start_grad = middle_grad + norm_one_grad
    terms = (
        jnp.stack([gain_one, gain_two]),
        jnp.stack([shift_one, shift_two]),
        triple_grad,
        triple_bias_grad,
        output_grad,
        output_bias_grad,
        up_grad,
        up_bias_grad,
        down_grad,
        down_bias_grad,
    )
    return (start_grad, terms)


def general_plan(
    tokens,
    segments,
    norm_gain,
    norm_shift,
    triple_weight,
    triple_bias,
    output_weight,
    output_bias,
    up_weight,
    up_bias,
    down_weight,
    down_bias,
    cotangent,
):

    def weights_of(layer_id):
        return (
            triple_weight[layer_id],
            output_weight[layer_id],
            up_weight[layer_id],
            down_weight[layer_id],
        )

    def small_of(layer_id):
        return (
            norm_gain[layer_id].astype(jnp.float32),
            norm_shift[layer_id].astype(jnp.float32),
            triple_bias[layer_id].astype(jnp.float32),
            output_bias[layer_id].astype(jnp.float32),
            up_bias[layer_id].astype(jnp.float32),
            down_bias[layer_id].astype(jnp.float32),
        )

    stream = tokens.astype(jnp.float32)
    stored = []
    for layer_id in range(LAYERS):
        stream, saved = layer_forward(stream, weights_of(layer_id), small_of(layer_id), segments)
        stored.append(saved)
    result = stream.astype(jnp.bfloat16)
    grad = cotangent.astype(jnp.float32)
    summed = [None] * LAYERS
    for layer_id in reversed(range(LAYERS)):
        grad, terms = layer_backward(
            grad, stored[layer_id], weights_of(layer_id), small_of(layer_id)[0], segments
        )
        summed[layer_id] = (
            lax.psum(terms[0].astype(jnp.bfloat16), "dp").astype(jnp.float32),
            lax.psum(terms[1].astype(jnp.bfloat16), "dp").astype(jnp.float32),
            lax.psum(terms[2].astype(jnp.bfloat16), "dp").astype(jnp.float32),
            lax.psum(terms[3].astype(jnp.bfloat16), "dp").astype(jnp.float32),
            lax.psum(terms[4].astype(jnp.bfloat16), "dp").astype(jnp.float32),
            lax.psum(terms[5].astype(jnp.bfloat16), "dp").astype(jnp.float32),
            lax.psum(terms[6].astype(jnp.bfloat16), "dp").astype(jnp.float32),
            lax.psum(terms[7].astype(jnp.bfloat16), "dp").astype(jnp.float32),
            lax.psum(terms[8].astype(jnp.bfloat16), "dp").astype(jnp.float32),
            lax.psum(terms[9].astype(jnp.bfloat16), "dp").astype(jnp.float32),
        )
    stacks = [
        jnp.stack([summed[layer_id][member] for layer_id in range(LAYERS)]) for member in range(10)
    ]
    return (
        result,
        grad,
        stacks[0],
        stacks[1],
        stacks[2],
        stacks[3],
        stacks[4],
        stacks[5],
        stacks[6],
        stacks[7],
        stacks[8],
        stacks[9],
    )


f32 = jnp.float32
bf16 = jnp.bfloat16
CHUNKS = 2
SPAN = LEN // CHUNKS
OWN = SPAN // 2
WIDTH = D // 4
QB = 256


def fits_pairs(shape, arrays):
    return (
        shape["row"] == 4
        and shape["col"] == 2
        and shape["dp"] == 4
        and arrays[0].shape == (2 * LEN, WIDTH)
        and arrays[8].shape[2] == 8 * WIDTH
    )


def dot(a, b):
    return lax.dot_general(a, b, (((1,), (0,)), ((), ())), preferred_element_type=f32)


def dot_nt(a, b):
    return lax.dot_general(a, b, (((1,), (1,)), ((), ())), preferred_element_type=f32)


def dot_tn(a, b):
    return lax.dot_general(a, b, (((0,), (0,)), ((), ())), preferred_element_type=f32)


def like(shape, kind):
    return jax.ShapeDtypeStruct(shape, kind)


def mean_lanes(v):
    return jnp.sum(v, axis=1, keepdims=True) * (1.0 / D)


def norm_parts(v):
    center = mean_lanes(v)
    second = mean_lanes(v * v) - center * center
    inv_std = lax.rsqrt(second + eps)
    return (v - center) * inv_std, inv_std


GELU = math.sqrt(2.0 / math.pi)


MESH = pl.DeviceIdType.MESH
HEADS_HERE = WIDTH // HD
SMALL = 24
SEG = 64


class Place:
    def __init__(self):
        self.row = lax.axis_index("row")
        self.col = lax.axis_index("col")
        self.dp = lax.axis_index("dp")
        self.core = self.row % 2
        self.chip = self.row // 2
        self.half = self.dp % 2
        sibling = self.row + 1 - 2 * self.core
        self.rows = [self.row, sibling, (self.row + 2) % 4, (sibling + 2) % 4]
        self.cores = [self.core, 1 - self.core, self.core, 1 - self.core]

    def to_row(self, j):
        return {"row": self.rows[j]}

    def to_col(self):
        return {"col": 1 - self.col}

    def to_dp(self):
        return {"dp": self.dp + 1 - 2 * self.half}


class Copies:
    def __init__(self, sems):
        self.sems = sems
        self.used = 0
        self.open = []

    def sem(self):
        self.used += 1
        return self.sems.at[self.used - 1]

    def local(self, src, dst):
        copy = pltpu.make_async_copy(src, dst, self.sem())
        copy.start()
        return copy

    def save(self, src, dst):
        self.open.append(self.local(src, dst).wait)

    def trade(self, src, dst, landing, device):
        sent, got = self.sem(), self.sem()
        out = pltpu.make_async_remote_copy(src, dst, sent, got, device_id=device, device_id_type=MESH)
        back = pltpu.make_async_remote_copy(
            landing, landing, sent, got, device_id=device, device_id_type=MESH
        )
        out.start()
        return out.wait_send, back.wait_recv

    def finish(self):
        for wait in self.open:
            wait()


def greet(place, devices):
    barrier = pltpu.get_barrier_semaphore()
    for device in devices:
        pl.semaphore_signal(barrier, inc=1, device_id=device, device_id_type=MESH)
    pl.semaphore_wait(barrier, len(devices))


def span(start, size):
    return pl.ds(pl.multiple_of(start, size), size)


def weight_cuts(kind, layer, wide, local):
    w = WIDTH
    if kind == 0:

        def source(core, half):
            rows = slice(None) if half is None else span(half * (w // 2), w // 2)
            return local.at[layer, :, rows, span(core * w, w)]

        def target(row, half):
            rows = span(row * w, w) if half is None else span(row * w + half * (w // 2), w // 2)
            return wide.at[layer, :, rows, :]

    elif kind == 2:
        units = wide.shape[2]

        def source(core, half):
            rows = slice(None) if half is None else span(half * (w // 2), w // 2)
            return local.at[layer, rows, span(core * units, units)]

        def target(row, half):
            rows = span(row * w, w) if half is None else span(row * w + half * (w // 2), w // 2)
            return wide.at[layer, rows, :]

    else:
        high = wide.shape[1]

        def source(core, half):
            if half is None:
                return local.at[layer, span(core * high, high), :]
            return local.at[layer, span(core * high + half * (high // 2), high // 2), :]

        def target(row, half):
            rows = slice(None) if half is None else span(half * (high // 2), high // 2)
            return wide.at[layer, rows, span(row * w, w)]

    return source, target


def strips(count, body):
    def step(i, carry):
        body(pl.multiple_of(i * 32, 32))
        return carry

    lax.fori_loop(0, count // 32, step, 0)


def causal(seg_col, seg_row, start, keys):
    query = lax.broadcasted_iota(jnp.int32, (QB, keys), 0) + start
    key = lax.broadcasted_iota(jnp.int32, (QB, keys), 1)
    return (seg_col == seg_row) & (key <= query)


def lanes_of(h):
    lane = lax.broadcasted_iota(jnp.int32, (1, WIDTH), 1)
    return (lane >= h * HD) & (lane < (h + 1) * HD)


def attend_chunk(k, triples, seg_col_ref, seg_row_ref, kv_ref, mixed_ref, log_ref):
    scale = 1.0 / math.sqrt(HD)
    kv_ref[k * SPAN : (k + 1) * SPAN, :] = triples[k][:, WIDTH:]
    for block in range(SPAN // QB):
        rows = slice(block * QB, (block + 1) * QB)
        start = k * SPAN + block * QB
        keys = start + QB
        allowed = causal(seg_col_ref[start : start + QB, :], seg_row_ref[:, :keys], start, keys)
        queries = triples[k][rows, :WIDTH] * scale
        key_rows = kv_ref[:keys, :WIDTH]
        value_rows = kv_ref[:keys, WIDTH:]
        blended = jnp.zeros((QB, WIDTH), f32)
        for h in range(HEADS_HERE):
            lanes = lanes_of(h)
            scores = dot_nt(jnp.where(lanes, queries, 0).astype(bf16), key_rows)
            scores = jnp.where(allowed, scores, masked)
            peak = jnp.max(scores, axis=1, keepdims=True)
            exponent = jnp.exp(scores - peak)
            total = jnp.sum(exponent, axis=1, keepdims=True)
            soft = (exponent * (1.0 / total)).astype(bf16)
            blended = jnp.where(lanes, dot(soft, value_rows), blended)
            log_ref[rows, h : h + 1] = peak + jnp.log(total)
        log_ref[rows, SEG : SEG + 1] = seg_col_ref[start : start + QB, :].astype(f32)
        mixed_ref[rows, :] = blended.astype(bf16)


def forward_body(*refs):
    (
        tokens_ref,
        cotangent_ref,
        small_ref,
        seg_col_ref,
        seg_row_ref,
        triple_in,
        output_in,
        up_in,
        down_in,
        result_ref,
        grad_ref,
        wide_out,
        triple_out,
        output_out,
        up_out,
        down_out,
        attn_out,
        rows_out,
        mixed_out,
        log_out,
        mlp_out,
        slope_out,
        active_out,
        stream_out,
        triple_w,
        output_w,
        up_w,
        down_w,
        attn,
        rows,
        mixed,
        logs,
        mlp,
        slope,
        active,
        stream,
        taken,
        wide,
        kv,
        mine,
        give,
        got_core,
        chip_sum,
        got_col,
        final,
        sems,
    ) = refs
    place = Place()
    copies = Copies(sems)
    core, sibling = place.core, 1 - place.core
    greet(place, [place.to_row(1), place.to_row(2), place.to_row(3), place.to_col(), place.to_dp()])

    own_lanes = span(place.row * WIDTH, WIDTH)

    def held(j, k):
        return span(place.rows[j] // 2 * LEN + k * SPAN + place.cores[j] * OWN, OWN)

    def part(c):
        return span(c * OWN, OWN)

    small_waits = []
    copy = copies.local(small_ref, wide.at[:, own_lanes])
    small_waits.append(copy.wait)
    for j in range(1, 4):
        sent, got = copies.trade(
            small_ref,
            wide.at[:, own_lanes],
            wide.at[:, span(place.rows[j] * WIDTH, WIDTH)],
            place.to_row(j),
        )
        copies.open.append(sent)
        small_waits.append(got)
    token_waits = [[] for _ in range(CHUNKS)]

    def scatter_in(block_ref, target, k, waits):
        waits.append(copies.local(block_ref.at[held(0, k), :], target.at[k, :, own_lanes]).wait)
        for j in range(1, 4):
            sent, got = copies.trade(
                block_ref.at[held(j, k), :],
                target.at[k, :, own_lanes],
                target.at[k, :, span(place.rows[j] * WIDTH, WIDTH)],
                place.to_row(j),
            )
            copies.open.append(sent)
            waits.append(got)

    arrivals, ready_waits = {}, {}

    def send_weight(layer, kind):
        local = (triple_in, output_in, up_in, down_in)[kind]
        whole = (triple_w, output_w, up_w, down_w)[kind]
        source, target = weight_cuts(kind, layer, whole, local)
        here = []
        for j in (2, 3):
            sent, got = copies.trade(
                source(place.cores[j], place.half),
                target(place.row, place.half),
                target(place.rows[j], place.half),
                place.to_row(j),
            )
            copies.open.append(sent)
            here.append((got, target(place.rows[j], place.half), target(place.rows[j], 1 - place.half)))
        arrivals[layer, kind] = here
        sent, got = copies.trade(
            source(sibling, None),
            target(place.row, None),
            target(place.rows[1], None),
            place.to_row(1),
        )
        copies.open.append(sent)
        own = copies.local(source(core, None), target(place.row, None))
        ready_waits[layer, kind] = [got, own.wait]

    def relay_weight(layer, kind):
        for got, arrived, missing in arrivals[layer, kind]:
            got()
            sent, back = copies.trade(arrived, arrived, missing, place.to_dp())
            copies.open.append(sent)
            ready_waits[layer, kind].append(back)

    def ready_weight(layer, kind):
        for wait in ready_waits[layer, kind]:
            wait()
        whole = (triple_w, output_w, up_w, down_w)[kind]
        out = (triple_out, output_out, up_out, down_out)[kind]
        copies.save(whole.at[layer], out.at[layer])

    scatter_in(tokens_ref, taken, 0, token_waits[0])
    send_weight(0, 0)
    scatter_in(tokens_ref, taken, 1, token_waits[1])
    for layer, kind in ((0, 1), (0, 2), (0, 3), (1, 0), (1, 1), (1, 2), (1, 3)):
        send_weight(layer, kind)
    grad_waits = []
    for k in range(CHUNKS):
        scatter_in(cotangent_ref, grad_ref, k, grad_waits)

    for wait in small_waits:
        wait()
    copies.save(wide, wide_out)

    def gain(layer, which):
        return wide[2 * layer + which : 2 * layer + which + 1, :]

    def shift(layer, which):
        return wide[4 + 2 * layer + which : 5 + 2 * layer + which, :]

    def output_bias(layer):
        return wide[8 + layer : 9 + layer, :]

    def down_bias(layer):
        return wide[10 + layer : 11 + layer, :]

    def of_core(line, start, size):
        return wide[line : line + 1, span(start, size)]

    def triple_bias(layer, which):
        at = 2 * core * WIDTH + which * (WIDTH // 2)
        size = WIDTH // 2
        return jnp.concatenate(
            [of_core(12 + layer, at, size), of_core(12 + layer, at + WIDTH, size)], axis=1
        )

    def up_bias(layer):
        line, at = 14 + 2 * layer, 2 * core * WIDTH
        return jnp.concatenate(
            [of_core(line + a, at + b * WIDTH, WIDTH) for b in range(2) for a in range(2)], axis=1
        )

    def norm_to(value, layer, which, target, at):
        center = jnp.mean(value, axis=1, keepdims=True)
        second = jnp.mean(value * value, axis=1, keepdims=True) - center * center
        normed = (value - center) * lax.rsqrt(second + eps)
        target[pl.ds(pl.multiple_of(core * OWN + at, 32), 32), :] = (
            normed * gain(layer, which) + shift(layer, which)
        ).astype(bf16)

    def share(target):
        return copies.trade(target.at[part(core)], target.at[part(core)], target.at[part(sibling)], place.to_row(1))

    def give_rows(k, value):
        give[k] = value.astype(bf16)

    sent_core, sent_col = [None] * CHUNKS, [None] * CHUNKS
    col_waits = [None] * CHUNKS
    saves = {}

    def settle(stage, k, got):
        got()
        if sent_col[k] is not None:
            sent_col[k]()

        def add(at):
            lines = pl.ds(at, 32)
            chip_sum[k, lines, :] = (
                mine[k, lines, :] + got_core[stage, k, lines, :].astype(f32)
            ).astype(bf16)

        strips(OWN, add)
        sent_col[k], col_waits[k] = copies.trade(
            chip_sum.at[k], got_col.at[stage, k], got_col.at[stage, k], place.to_col()
        )

    def start_core(stage, k):
        sent, got = copies.trade(
            give.at[k], got_core.at[stage, k], got_core.at[stage, k], place.to_row(1)
        )
        sent_core[k] = sent
        return got

    def take_col(stage, k, layer, bias, after_ref):
        col_waits[k]()

        def add(at):
            lines = pl.ds(at, 32)
            total = chip_sum[k, lines, :].astype(f32) + got_col[stage, k, lines, :].astype(f32)
            value = stream[stage, k, lines, :] + (total + bias)
            stream[1 - stage, k, lines, :] = value
            after_ref(value, at)

        strips(OWN, add)

    shares = [None] * CHUNKS
    for k in range(CHUNKS):
        for wait in token_waits[k]:
            wait()
        if k == 0:
            pass

        def first(at, k=k):
            value = taken[k, pl.ds(at, 32), :].astype(f32)
            stream[0, k, pl.ds(at, 32), :] = value
            norm_to(value, 0, 0, attn.at[0, k], at)

        strips(OWN, first)
        saves[0, 0, k] = copies.local(stream.at[0, k], stream_out.at[0, 0, k])
        shares[k] = share(attn.at[0, k])
        if k == 0:
            relay_weight(0, 0)
    relay_weight(0, 1)
    pump = [(0, 2), (0, 3), (1, 0), (1, 1), (1, 2), (1, 3)]

    def pump_one():
        if pump:
            relay_weight(*pump.pop(0))

    for layer in range(LAYERS):
        for k in range(CHUNKS):
            if layer:
                saves.pop((layer - 1, 0, k)).wait()
                take_col(
                    1, k, layer, down_bias(layer - 1), lambda v, at, k=k: norm_to(v, layer, 0, attn.at[layer, k], at)
                )
                saves[layer, 0, k] = copies.local(stream.at[0, k], stream_out.at[layer, 0, k])
                shares[k] = share(attn.at[layer, k])
            if k == 0:
                ready_weight(layer, 0)
            bias = [triple_bias(layer, 0), None, triple_bias(layer, 1)]

            def project(c, k=k, bias=bias):
                for third in range(3):
                    value = dot(attn[layer, k, part(c), :], triple_w[layer, third])
                    if bias[third] is not None:
                        value = value + bias[third]
                    rows[layer, k, part(c), third * WIDTH : (third + 1) * WIDTH] = value.astype(bf16)

            project(core)
            sent, got = shares[k]
            got()
            project(sibling)
            attend_chunk(
                k,
                [rows.at[layer, i] for i in range(k + 1)],
                seg_col_ref,
                seg_row_ref,
                kv,
                mixed.at[layer, k],
                logs.at[layer, k],
            )
            if k == 0:
                ready_weight(layer, 1)
            if sent_core[k] is not None:
                sent_core[k]()
            give[k] = dot(mixed[layer, k, part(sibling), :], output_w[layer]).astype(bf16)
            got = start_core(0, k)
            mine[k] = dot(mixed[layer, k, part(core), :], output_w[layer])
            sent()
            copies.save(attn.at[layer, k], attn_out.at[layer, k])
            copies.save(rows.at[layer, k], rows_out.at[layer, k])
            copies.save(mixed.at[layer, k], mixed_out.at[layer, k])
            copies.save(logs.at[layer, k], log_out.at[layer, k])
            settle(0, k, got)
            pump_one()
        for k in range(CHUNKS):
            if layer:
                saves.pop((layer - 1, 1, k)).wait()
            take_col(
                0, k, layer, output_bias(layer), lambda v, at, k=k: norm_to(v, layer, 1, mlp.at[layer, k], at)
            )
            saves[layer, 1, k] = copies.local(stream.at[1, k], stream_out.at[layer, 1, k])
            shares[k] = share(mlp.at[layer, k])
            if k == 0:
                ready_weight(layer, 2)
            bias = up_bias(layer)

            def widen(c, k=k, bias=bias):
                for block in range(4):
                    cols = slice(block * WIDTH, (block + 1) * WIDTH)
                    pre = dot(mlp[layer, k, part(c), :], up_w[layer, :, cols]) + bias[:, cols]
                    square = pre * pre
                    curve = jnp.tanh(GELU * (pre + 0.044715 * (square * pre)))
                    upper = 0.5 * (1.0 + curve)
                    active[layer, k, part(c), cols] = (pre * upper).astype(bf16)
                    slope[layer, k, part(c), cols] = (
                        upper
                        + (0.5 * GELU) * pre * (1.0 - curve * curve) * (1.0 + (3.0 * 0.044715) * square)
                    ).astype(bf16)

            widen(core)
            sent, got = shares[k]
            got()
            widen(sibling)
            if k == 0:
                ready_weight(layer, 3)
            sent_core[k]()
            give[k] = dot(active[layer, k, part(sibling), :], down_w[layer]).astype(bf16)
            got = start_core(1, k)
            mine[k] = dot(active[layer, k, part(core), :], down_w[layer])
            sent()
            copies.save(mlp.at[layer, k], mlp_out.at[layer, k])
            copies.save(slope.at[layer, k], slope_out.at[layer, k])
            copies.save(active.at[layer, k], active_out.at[layer, k])
            settle(1, k, got)
            pump_one()
    result_waits = []
    for k in range(CHUNKS):
        saves.pop((LAYERS - 1, 0, k)).wait()

        def finish(v, at, k=k):
            final[k, pl.ds(at, 32), :] = v.astype(bf16)

        take_col(1, k, LAYERS, down_bias(LAYERS - 1), finish)
        result_waits.append(copies.local(final.at[k, :, own_lanes], result_ref.at[held(0, k), :]).wait)
        for j in range(1, 4):
            sent, got = copies.trade(
                final.at[k, :, span(place.rows[j] * WIDTH, WIDTH)],
                result_ref.at[held(0, k), :],
                result_ref.at[held(j, k), :],
                place.to_row(j),
            )
            result_waits += [sent, got]
    for k in range(CHUNKS):
        saves.pop((LAYERS - 1, 1, k)).wait()
        sent_core[k]()
        sent_col[k]()
    for wait in result_waits + grad_waits:
        wait()
    copies.finish()


def forward_call(tokens, cotangent, small, seg_col, seg_row, triple_w, output_w, up_w, down_w):
    units = up_w.shape[2] // 2
    per_layer = [
        ((LAYERS, CHUNKS, SPAN, D), bf16),
        ((LAYERS, CHUNKS, SPAN, 3 * WIDTH), bf16),
        ((LAYERS, CHUNKS, SPAN, WIDTH), bf16),
        ((LAYERS, CHUNKS, SPAN, 128), f32),
        ((LAYERS, CHUNKS, SPAN, D), bf16),
        ((LAYERS, CHUNKS, SPAN, units), bf16),
        ((LAYERS, CHUNKS, SPAN, units), bf16),
    ]
    wide = [
        ((LAYERS, 3, D, WIDTH), bf16),
        ((LAYERS, WIDTH, D), bf16),
        ((LAYERS, D, units), bf16),
        ((LAYERS, units, D), bf16),
    ]
    outs = [
        (tokens.shape, bf16),
        ((CHUNKS, OWN, D), bf16),
        ((SMALL, D), f32),
        *wide,
        *per_layer,
        ((LAYERS, 2, CHUNKS, OWN, D), f32),
    ]
    scratch = [
        *wide,
        *per_layer,
        ((2, CHUNKS, OWN, D), f32),
        ((CHUNKS, OWN, D), bf16),
        ((SMALL, D), f32),
        ((LEN, 2 * WIDTH), bf16),
        ((CHUNKS, OWN, D), f32),
        ((CHUNKS, OWN, D), bf16),
        ((2, CHUNKS, OWN, D), bf16),
        ((CHUNKS, OWN, D), bf16),
        ((2, CHUNKS, OWN, D), bf16),
        ((CHUNKS, OWN, D), bf16),
    ]
    anywhere = pl.BlockSpec(memory_space=pl.ANY)
    inside = pl.BlockSpec(memory_space=pltpu.VMEM)
    return pl.pallas_call(
        forward_body,
        out_shape=[like(*v) for v in outs],
        in_specs=[anywhere] * 2 + [inside] * 3 + [anywhere] * 4,
        out_specs=[anywhere] * len(outs),
        scratch_shapes=[pltpu.VMEM(*v) for v in scratch] + [pltpu.SemaphoreType.DMA((320,))],
        compiler_params=pltpu.CompilerParams(
            collective_id=0, has_side_effects=True, vmem_limit_bytes=60 * 1024 * 1024
        ),
    )(tokens, cotangent, small, seg_col, seg_row, triple_w, output_w, up_w, down_w)


def pack_small(norm_gain, norm_shift, output_bias, down_bias, triple_bias, up_bias):
    lines = [
        norm_gain.reshape(-1, WIDTH),
        norm_shift.reshape(-1, WIDTH),
        output_bias,
        down_bias,
        triple_bias.reshape(-1, WIDTH),
        up_bias.reshape(-1, WIDTH),
    ]
    lines = jnp.concatenate(lines).astype(f32)
    return jnp.pad(lines, ((0, SMALL - lines.shape[0]), (0, 0)))


PIECES = ((3, WIDTH, WIDTH), (1, WIDTH, WIDTH), (2, WIDTH // 2, D), (2, D // 2, WIDTH))
LINES = 16


def attend_back_chunk(
    k, rows_ref, log_ref, seg_row_ref, grad_ref, total_ref, out_ref
):
    scale = 1.0 / math.sqrt(HD)
    for block in range(SPAN // QB):
        start = k * SPAN + block * QB
        keys = start + QB
        here = slice(start, keys)
        allowed = causal(log_ref[here, SEG : SEG + 1], seg_row_ref[:, :keys], start, keys)
        queries = rows_ref[here, :WIDTH] * scale
        grads = grad_ref[block * QB : (block + 1) * QB, :]
        key_rows = rows_ref[:keys, WIDTH : 2 * WIDTH]
        value_rows = rows_ref[:keys, 2 * WIDTH :]
        query_grad = jnp.zeros((QB, WIDTH), f32)
        for h in range(HEADS_HERE):
            lanes = lanes_of(h)
            query = jnp.where(lanes, queries, 0).astype(bf16)
            grad = jnp.where(lanes, grads, 0).astype(bf16)
            scores = jnp.where(allowed, dot_nt(query, key_rows), masked)
            chances = jnp.exp(scores - log_ref[here, h : h + 1])
            product = chances * dot_nt(grad, value_rows)
            inner = jnp.sum(product, axis=1, keepdims=True)
            score_grad = (product - chances * inner).astype(bf16)
            query_grad = jnp.where(lanes, dot(score_grad, key_rows), query_grad)
            total_ref[:keys, :WIDTH] += dot_tn(score_grad, query)
            total_ref[:keys, WIDTH:] += dot_tn(chances.astype(bf16), grad)
        out_ref[here, :WIDTH] = (query_grad * scale).astype(bf16)
    here = slice(k * SPAN, (k + 1) * SPAN)
    out_ref[here, WIDTH:] = total_ref[here, :].astype(bf16)


def add_pieces(target, left, right):
    high, across = target.shape
    step = 32768 // across

    def body(i, carry):
        lines = pl.ds(pl.multiple_of(i * step, step), step)
        target[lines, :] = (left[lines, :].astype(f32) + right[lines, :].astype(f32)).astype(bf16)
        return carry

    lax.fori_loop(0, high // step, body, 0)


class Reduction:
    def __init__(self, kind, layer, place, copies, grads, land, ends, inner, outs, credits):
        self.kind, self.layer, self.place, self.copies = kind, layer, place, copies
        self.grads, self.land, self.ends, self.inner = grads[kind], land[kind], ends[kind], inner[kind]
        self.out, self.credits = outs[kind], credits
        self.count = PIECES[kind][0]
        self.again = layer < LAYERS - 1
        self.is_end = place.dp * (3 - place.dp) == 0
        self.is_inner = place.dp * (3 - place.dp) > 0

    def home(self, which, s):
        core = self.place.cores[which]
        out, layer = self.out, self.layer
        if self.kind == 0:
            return out.at[layer, s, :, span(core * WIDTH, WIDTH)]
        if self.kind == 1:
            return out.at[layer, span(core * WIDTH, WIDTH), :]
        if self.kind == 2:
            return out.at[layer, s * (WIDTH // 2) : (s + 1) * (WIDTH // 2), span(core * D, D)]
        return out.at[layer, span(core * D + s * (D // 2), D // 2), :]

    def send(self):
        place, copies = self.place, self.copies
        if self.again:
            pl.semaphore_wait(self.credits.at[self.kind], 3)
        self.waits = {}
        self.sent = []
        for s in range(self.count):
            for j in (2, 3, 1):
                sent, got = copies.trade(
                    self.grads.at[place.rows[j], s],
                    self.land.at[j - 1, s],
                    self.land.at[j - 1, s],
                    place.to_row(j),
                )
                self.sent.append(sent)
                self.waits[j, s] = got

    def over_chips(self, s):
        place, copies = self.place, self.copies
        if s == 0:
            self.to_inner = {}
            if self.again:

                @pl.when(self.is_end)
                def _():
                    pl.semaphore_wait(self.credits.at[4 + self.kind], 1)

        for which in range(2):
            if which == 0:
                self.waits[2, s]()
                target = self.land.at[1, s]
                add_pieces(target, self.grads.at[place.row, s], target)
            else:
                self.waits[1, s]()
                self.waits[3, s]()
                target = self.land.at[2, s]
                add_pieces(target, self.land.at[0, s], target)
            copy = pltpu.make_async_remote_copy(
                target,
                self.ends.at[which, s],
                copies.sem(),
                copies.sem(),
                device_id=place.to_dp(),
                device_id_type=MESH,
            )
            self.to_inner[which, s] = copy

            @pl.when(self.is_end)
            def _():
                copy.start()

    def to_middle(self, s):
        place, copies = self.place, self.copies
        if s == 0:
            self.across = {}
            if self.again:

                @pl.when(self.is_inner)
                def _():
                    pl.semaphore_wait(self.credits.at[8 + self.kind], 1)

        for which in range(2):
            half = self.ends.at[which, s]
            copy = pltpu.make_async_remote_copy(
                half,
                self.inner.at[which, s],
                copies.sem(),
                copies.sem(),
                device_id={"dp": 3 - place.dp},
                device_id_type=MESH,
            )
            self.across[which, s] = copy

            @pl.when(self.is_inner)
            def _():
                self.to_inner[which, s].wait_recv()
                add_pieces(half, self.land.at[1 + which, s], half)
                copy.start()

        if s == self.count - 1:

            @pl.when(self.is_end)
            def _():
                for copy in self.to_inner.values():
                    copy.wait_send()

            for sent in self.sent:
                sent()
            if not self.again:
                for j in range(1, 4):
                    pl.semaphore_signal(
                        self.credits.at[self.kind],
                        inc=1,
                        device_id=place.to_row(j),
                        device_id_type=MESH,
                    )

    def back(self, s):
        place, copies = self.place, self.copies
        if s == 0:
            self.out_copies = []
        for which in range(2):
            total = self.inner.at[which, s]
            home = self.home(which, s)
            copy = pltpu.make_async_remote_copy(
                total,
                home,
                copies.sem(),
                copies.sem(),
                device_id=place.to_dp(),
                device_id_type=MESH,
            )
            here = pltpu.make_async_copy(total, home, copies.sem())
            self.out_copies.append((copy, here))

            @pl.when(self.is_inner)
            def _():
                self.across[which, s].wait_recv()
                add_pieces(total, self.ends.at[which, s], total)
                copy.start()
                here.start()

    def finish(self):
        place = self.place

        @pl.when(self.is_inner)
        def _():
            for copy in self.across.values():
                copy.wait_send()
            for copy, here in self.out_copies:
                copy.wait_send()
                here.wait()
            if not self.again:
                pl.semaphore_signal(
                    self.credits.at[4 + self.kind], inc=1, device_id=place.to_dp(), device_id_type=MESH
                )
                pl.semaphore_signal(
                    self.credits.at[8 + self.kind],
                    inc=1,
                    device_id={"dp": 3 - place.dp},
                    device_id_type=MESH,
                )

        @pl.when(self.is_end)
        def _():
            for copy, here in self.out_copies:
                copy.wait_recv()


def backward_body(*refs):
    (
        grad_in,
        wide_ref,
        seg_row_ref,
        triple_in,
        output_in,
        up_in,
        down_in_w,
        attn_in,
        rows_in,
        mixed_in,
        log_in,
        mlp_in,
        slope_in,
        active_in,
        stream_in,
        input_grad_ref,
        small_out,
        triple_out,
        output_out,
        up_out,
        down_out,
        triple_w,
        output_w,
        up_w,
        down_w,
        attn,
        rows,
        mixed,
        logs,
        mlp,
        slope,
        active,
        start,
        middle,
        down_in,
        hidden,
        branch,
        rows_grad,
        mixed_grad,
        pair_total,
        grad,
        mine,
        give,
        got_core,
        chip_sum,
        got_col,
        sums,
        lines,
        line_land,
        dp_land,
        *rest,
    ) = refs
    grads, land, ends, inner = rest[0:4], rest[4:8], rest[8:12], rest[12:16]
    credits, sems = rest[16:]
    place = Place()
    copies = Copies(sems)
    core, sibling = place.core, 1 - place.core
    others = [{"dp": (place.dp + i) % 4} for i in range(1, 4)]
    greet(place, [place.to_row(1), place.to_row(2), place.to_row(3), place.to_col(), *others])
    own_lanes = span(place.row * WIDTH, WIDTH)

    def part(k, c):
        return span(k * SPAN + c * OWN, OWN)

    ready = {}

    def load(name, layer):
        source, target = {
            "triple_w": (triple_in, triple_w),
            "output_w": (output_in, output_w),
            "up_w": (up_in, up_w),
            "down_w": (down_in_w, down_w),
            "attn": (attn_in, attn),
            "rows": (rows_in, rows),
            "mixed": (mixed_in, mixed),
            "logs": (log_in, logs),
            "mlp": (mlp_in, mlp),
            "slope": (slope_in, slope),
            "active": (active_in, active),
            "start": (stream_in, start),
            "middle": (stream_in, middle),
        }[name]
        if name in ("start", "middle"):
            ready[name] = [copies.local(source.at[layer, int(name == "middle")], target).wait]
        elif name.endswith("_w"):
            ready[name] = [copies.local(source.at[layer], target).wait]
        else:
            ready[name] = [
                copies.local(source.at[layer, k], target.at[k * SPAN : (k + 1) * SPAN]).wait
                for k in range(CHUNKS)
            ]

    def need(name):
        for wait in ready.pop(name, ()):
            wait()

    first_waits = [
        copies.local(grad_in.at[k], down_in.at[part(k, core)]).wait for k in range(CHUNKS)
    ]
    top = LAYERS - 1
    for name in ("active", "down_w", "slope", "up_w", "mlp", "middle"):
        load(name, top)
    for name in ("output_w", "rows", "logs", "triple_w", "mixed", "attn", "start"):
        load(name, top)
    sums[...] = jnp.zeros_like(sums)
    lines[...] = jnp.zeros_like(lines)

    def share(target, k):
        return copies.trade(
            target.at[part(k, core)], target.at[part(k, core)], target.at[part(k, sibling)], place.to_row(1)
        )

    def columns(value):
        return jnp.sum(value.reshape(-1, 8, value.shape[1]), axis=0)

    def gain(layer, which):
        return wide_ref[2 * layer + which : 2 * layer + which + 1, :]

    sent_core = []
    sent_col, col_waits = [None] * CHUNKS, [None] * CHUNKS

    def core_free():
        while sent_core:
            sent_core.pop()()

    def start_core(stage, k):
        sent, got = copies.trade(
            give, got_core.at[stage, k], got_core.at[stage, k], place.to_row(1)
        )
        sent_core.append(sent)
        return got

    def settle(stage, k, got):
        got()
        if sent_col[k] is not None:
            sent_col[k]()

        def add(at):
            here = pl.ds(at, 32)
            chip_sum[k, here, :] = (mine[here, :] + got_core[stage, k, here, :].astype(f32)).astype(bf16)

        strips(OWN, add)
        sent_col[k], col_waits[k] = copies.trade(
            chip_sum.at[k], got_col.at[stage, k], got_col.at[stage, k], place.to_col()
        )

    def take_col(stage, k, layer, which, stream, target):
        col_waits[k]()
        scale = gain(layer, which)

        def back(at):
            here = pl.ds(at, 32)
            grad_out = chip_sum[k, here, :].astype(f32) + got_col[stage, k, here, :].astype(f32)
            normed, inv_std = norm_parts(stream[k, here, :])
            scaled = grad_out * scale
            total = grad[k, here, :] + inv_std * (
                scaled - mean_lanes(scaled) - normed * mean_lanes(scaled * normed)
            )
            low = total.astype(bf16)
            grad[k, here, :] = total
            target[pl.ds(pl.multiple_of(k * SPAN + core * OWN + at, 32), 32), :] = low
            sums[layer, which] += columns(grad_out * normed)
            sums[layer, 2 + which] += columns(grad_out)
            if which == 1:
                sums[layer, 4] += columns(low.astype(f32))
            elif layer:
                sums[layer - 1, 5] += columns(low.astype(f32))

        strips(OWN, back)

    shares = [None] * CHUNKS
    for k in reversed(range(CHUNKS)):
        first_waits[k]()
        shares[k] = share(down_in, k)
    for k in reversed(range(CHUNKS)):

        def widen(at, k=k):
            low = down_in[pl.ds(pl.multiple_of(k * SPAN + core * OWN + at, 32), 32), :]
            value = low.astype(f32)
            grad[k, pl.ds(at, 32), :] = value
            sums[top, 5] += columns(value)

        strips(OWN, widen)

    reductions = {
        (layer, kind): Reduction(
            kind,
            layer,
            place,
            copies,
            grads,
            land,
            ends,
            inner,
            (triple_out, output_out, up_out, down_out),
            credits,
        )
        for layer in range(LAYERS)
        for kind in range(4)
    }

    def weight_grad(layer, kind):
        if kind == 0:
            need("attn")
            for pair in range(2):
                for third in range(3):
                    value = dot_tn(
                        attn[:, pair * 512 : (pair + 1) * 512],
                        rows_grad[:, third * WIDTH : (third + 1) * WIDTH],
                    ).astype(bf16)
                    for b in range(2):
                        grads[0][2 * pair + b, third] = value[b * WIDTH : (b + 1) * WIDTH]
        elif kind == 1:
            need("mixed")
            value = dot_tn(mixed[...], branch[...]).astype(bf16)
            for b in range(4):
                grads[1][b, 0] = value[:, b * WIDTH : (b + 1) * WIDTH]
        elif kind == 2:
            need("mlp")
            for b in range(4):
                value = dot_tn(mlp[:, b * WIDTH : (b + 1) * WIDTH], hidden[...]).astype(bf16)
                for s in range(2):
                    grads[2][b, s] = value[s * (WIDTH // 2) : (s + 1) * (WIDTH // 2)]
        else:
            need("active")
            for pair in range(4):
                value = dot_tn(active[:, pair * WIDTH : (pair + 1) * WIDTH], down_in[...]).astype(bf16)
                s, at = pair // 2, pair % 2 * WIDTH
                for b in range(4):
                    grads[3][b, s, at : at + WIDTH] = value[:, b * WIDTH : (b + 1) * WIDTH]
        reductions[layer, kind].send()

    def run(layer, kind, *names):
        item = reductions[layer, kind]
        for name in names:
            if name == "finish":
                item.finish()
            else:
                for s in range(item.count):
                    getattr(item, name)(s)

    for layer in reversed(range(LAYERS)):
        for k in reversed(range(CHUNKS)):
            if k == CHUNKS - 1 and layer == top:
                for i in reversed(range(CHUNKS)):
                    shares[i][1]()
                weight_grad(layer, 3)
            need("down_w")
            need("slope")

            def shrink(c, k=k):
                for block in range(4):
                    cols = slice(block * WIDTH, (block + 1) * WIDTH)
                    value = dot_nt(down_in[part(k, c), :], down_w[cols, :])
                    value = (value * slope[part(k, c), cols].astype(f32)).astype(bf16)
                    hidden[part(k, c), cols] = value
                    lines[layer, 8:16, cols] += columns(value.astype(f32))

            if layer < top:
                shrink(core)
                shares[k][1]()
                shrink(sibling)
            else:
                shrink(core)
                shrink(sibling)
            need("up_w")
            core_free()
            give[...] = dot_nt(hidden[part(k, sibling), :], up_w[...]).astype(bf16)
            got = start_core(0, k)
            mine[...] = dot_nt(hidden[part(k, core), :], up_w[...])
            shares[k][0]()
            settle(0, k, got)
        if layer < top:
            run(layer + 1, 3, "back", "finish")
            run(layer + 1, 2, "to_middle")
            weight_grad(layer, 3)
            weight_grad(layer, 2)
            run(layer + 1, 1, "over_chips")
        else:
            weight_grad(layer, 2)
        if layer:
            for name in ("active", "down_w", "slope", "up_w", "mlp"):
                load(name, layer - 1)
        for k in reversed(range(CHUNKS)):
            need("middle")
            take_col(0, k, layer, 1, middle, branch)
            shares[k] = share(branch, k)
            if layer and k == 0:
                load("middle", layer - 1)
            need("output_w")

            def narrow(c, k=k):
                mixed_grad[part(0, c), :] = dot_nt(branch[part(k, c), :], output_w[...]).astype(bf16)

            narrow(core)
            need("rows")
            need("logs")
            if k == CHUNKS - 1:
                pair_total[...] = jnp.zeros_like(pair_total)
            shares[k][1]()
            narrow(sibling)
            attend_back_chunk(
                k, rows, logs, seg_row_ref, mixed_grad, pair_total, rows_grad
            )
            need("triple_w")
            core_free()

            def project(c, k=k):
                value = dot_nt(rows_grad[part(k, c), :WIDTH], triple_w[0])
                for third in range(1, 3):
                    cols = slice(third * WIDTH, (third + 1) * WIDTH)
                    value += dot_nt(rows_grad[part(k, c), cols], triple_w[third])
                return value

            give[...] = project(sibling).astype(bf16)
            got = start_core(1, k)
            mine[...] = project(core)
            shares[k][0]()
            settle(1, k, got)
            if layer == top and k == CHUNKS - 1:
                run(layer, 3, "over_chips")
        here = rows_grad[:, :WIDTH].astype(f32)
        lines[layer, 0:1, 0:WIDTH] = jnp.sum(here, axis=0, keepdims=True)
        here = rows_grad[:, 2 * WIDTH :].astype(f32)
        lines[layer, 0:1, WIDTH : 2 * WIDTH] = jnp.sum(here, axis=0, keepdims=True)
        if layer < top:
            run(layer + 1, 0, "over_chips")
            run(layer + 1, 2, "back", "finish")
            run(layer + 1, 1, "to_middle", "back", "finish")
            run(layer + 1, 0, "to_middle")
        weight_grad(layer, 1)
        weight_grad(layer, 0)
        if layer:
            run(layer, 3, "to_middle")
            run(layer, 2, "over_chips")
            for name in ("output_w", "rows", "logs", "triple_w", "mixed", "attn"):
                load(name, layer - 1)
        for k in reversed(range(CHUNKS)):
            need("start")
            take_col(1, k, layer, 0, start, down_in)
            if layer:
                shares[k] = share(down_in, k)
            if layer and k == 0:
                load("start", layer - 1)
    landed = []

    def held(j, k):
        return span(place.rows[j] // 2 * LEN + k * SPAN + place.cores[j] * OWN, OWN)

    for k in reversed(range(CHUNKS)):
        mine_rows = part(k, core)
        landed.append(
            copies.local(down_in.at[mine_rows, own_lanes], input_grad_ref.at[held(0, k), :]).wait
        )
        for j in range(1, 4):
            sent, got = copies.trade(
                down_in.at[mine_rows, span(place.rows[j] * WIDTH, WIDTH)],
                input_grad_ref.at[held(0, k), :],
                input_grad_ref.at[held(j, k), :],
                place.to_row(j),
            )
            landed += [sent, got]
    run(top, 0, "back", "finish")
    zero = jnp.zeros((1, WIDTH // 2), f32)
    for layer in range(LAYERS):
        found = [jnp.sum(sums[layer, i], axis=0, keepdims=True) for i in range(6)]
        hidden_sum = jnp.sum(lines[layer, 8:16, :], axis=0, keepdims=True)
        base = layer * LINES
        line_land[0, base : base + LINES, :] = jnp.zeros((LINES, D), f32)
        for i in range(6):
            line_land[0, base + i : base + i + 1, :] = found[i]
        for b in range(2):
            at = span((2 * core + b) * WIDTH, WIDTH)
            half = slice(b * (WIDTH // 2), (b + 1) * (WIDTH // 2))
            line_land[0, base + 6 : base + 7, at] = jnp.concatenate(
                [lines[layer, 0:1, :WIDTH][:, half], lines[layer, 0:1, WIDTH : 2 * WIDTH][:, half]], axis=1
            )
            for a in range(2):
                cols = slice((2 * b + a) * WIDTH, (2 * b + a + 1) * WIDTH)
                line_land[0, base + 7 + a : base + 8 + a, at] = hidden_sum[:, cols]
    line_waits = []
    for j in range(1, 4):
        there = span(place.rows[j] * WIDTH, WIDTH)
        sent, got = copies.trade(
            line_land.at[0, :, there],
            dp_land.at[3 + j],
            dp_land.at[3 + j],
            place.to_row(j),
        )
        copies.open.append(sent)
        line_waits.append(got)
    for wait in line_waits:
        wait()
    total = line_land[0, :, own_lanes]
    dp_land[place.dp] = total + dp_land[4] + dp_land[5] + dp_land[6]
    line_waits = []
    for i, device in enumerate(others):
        back = (place.dp + 3 - i) % 4
        sent, got = copies.sem(), copies.sem()
        out = pltpu.make_async_remote_copy(
            dp_land.at[place.dp], dp_land.at[place.dp], sent, got, device_id=device, device_id_type=MESH
        )
        arriving = pltpu.make_async_remote_copy(
            dp_land.at[back], dp_land.at[back], sent, got, device_id=device, device_id_type=MESH
        )
        out.start()
        copies.open.append(out.wait_send)
        line_waits.append(arriving.wait_recv)
    queue = [(reductions[0, kind], s) for kind in (3, 2, 1, 0) for s in range(PIECES[kind][0])]
    for i in range(len(queue) + 2):
        for lag, name in enumerate(("over_chips", "to_middle", "back")):
            if 0 <= i - lag < len(queue):
                item, s = queue[i - lag]
                getattr(item, name)(s)
    for wait in line_waits:
        wait()
    small_out[...] = dp_land[0] + dp_land[1] + dp_land[2] + dp_land[3]
    for kind in (3, 2, 1, 0):
        reductions[0, kind].finish()
    core_free()
    for k in range(CHUNKS):
        sent_col[k]()
    for wait in landed:
        wait()
    copies.finish()


def backward_call(tokens_shape, grad_in, wide, seg_row, weights, saved, stream):
    units = weights[2].shape[2]
    scratch = [
        ((3, D, WIDTH), bf16),
        ((WIDTH, D), bf16),
        ((D, units), bf16),
        ((units, D), bf16),
        ((LEN, D), bf16),
        ((LEN, 3 * WIDTH), bf16),
        ((LEN, WIDTH), bf16),
        ((LEN, 128), f32),
        ((LEN, D), bf16),
        ((LEN, units), bf16),
        ((LEN, units), bf16),
        ((CHUNKS, OWN, D), f32),
        ((CHUNKS, OWN, D), f32),
        ((LEN, D), bf16),
        ((LEN, units), bf16),
        ((LEN, D), bf16),
        ((LEN, 3 * WIDTH), bf16),
        ((SPAN, WIDTH), bf16),
        ((LEN, 2 * WIDTH), f32),
        ((CHUNKS, OWN, D), f32),
        ((OWN, D), f32),
        ((OWN, D), bf16),
        ((2, CHUNKS, OWN, D), bf16),
        ((CHUNKS, OWN, D), bf16),
        ((2, CHUNKS, OWN, D), bf16),
        ((LAYERS, 6, 8, D), f32),
        ((LAYERS, 16, D), f32),
        ((1, LAYERS * LINES, D), f32),
        ((7, LAYERS * LINES, WIDTH), f32),
    ]
    for parts in (4, 3, 2, 2):
        scratch += [((parts, *piece), bf16) for piece in PIECES]
    outs = [
        (tokens_shape, bf16),
        ((LAYERS * LINES, WIDTH), f32),
        ((LAYERS, 3, WIDTH, 2 * WIDTH), bf16),
        ((LAYERS, 2 * WIDTH, WIDTH), bf16),
        ((LAYERS, WIDTH, 2 * units), bf16),
        ((LAYERS, 2 * units, WIDTH), bf16),
    ]
    anywhere = pl.BlockSpec(memory_space=pl.ANY)
    inside = pl.BlockSpec(memory_space=pltpu.VMEM)
    return pl.pallas_call(
        backward_body,
        out_shape=[like(*v) for v in outs],
        in_specs=[anywhere] + [inside] * 2 + [anywhere] * 12,
        out_specs=[anywhere, inside] + [anywhere] * 4,
        scratch_shapes=[pltpu.VMEM(*v) for v in scratch]
        + [pltpu.SemaphoreType.REGULAR((12,)), pltpu.SemaphoreType.DMA((480,))],
        compiler_params=pltpu.CompilerParams(
            collective_id=1, has_side_effects=True, vmem_limit_bytes=60 * 1024 * 1024
        ),
    )(grad_in, wide, seg_row, *weights, *saved, stream)


def pair_plan(
    tokens,
    segments,
    norm_gain,
    norm_shift,
    triple_weight,
    triple_bias,
    output_weight,
    output_bias,
    up_weight,
    up_bias,
    down_weight,
    down_bias,
    cotangent,
):
    chip = lax.axis_index("row") // 2
    seg_pack = lax.dynamic_slice_in_dim(segments, chip * LEN, LEN, 0)
    seg_col, seg_row = seg_pack[:, None], seg_pack[None, :]
    result, grad_in, wide, *kept, stream = forward_call(
        tokens,
        cotangent,
        pack_small(norm_gain, norm_shift, output_bias, down_bias, triple_bias, up_bias),
        seg_col,
        seg_row,
        jnp.swapaxes(triple_weight, 1, 2),
        output_weight,
        up_weight,
        down_weight,
    )
    input_grad, small, triple_grad, output_grad, up_grad, down_grad = backward_call(
        tokens.shape, grad_in, wide, seg_row.astype(f32), kept[:4], kept[4:], stream
    )
    small = small.reshape(LAYERS, LINES, WIDTH)
    return (
        result,
        input_grad.astype(f32),
        small[:, 0:2],
        small[:, 2:4],
        jnp.swapaxes(triple_grad, 1, 2).astype(f32),
        small[:, 6].reshape(LAYERS, 2, WIDTH // 2),
        output_grad.astype(f32),
        small[:, 4],
        up_grad.astype(f32),
        small[:, 7:9].reshape(LAYERS, 2 * WIDTH),
        down_grad.astype(f32),
        small[:, 5],
    )


def solution(mesh):
    in_specs = (
        P("dp", "row"),
        P("dp"),
        P(None, None, "row"),
        P(None, None, "row"),
        P(None, "row", None, "col"),
        P(None, None, ("col", "row")),
        P(None, "col", "row"),
        P(None, "row"),
        P(None, "row", "col"),
        P(None, ("col", "row")),
        P(None, "col", "row"),
        P(None, "row"),
        P("dp", "row"),
    )
    out_specs = (
        P("dp", "row"),
        P("dp", "row"),
        P(None, None, "row"),
        P(None, None, "row"),
        P(None, "row", None, "col"),
        P(None, None, ("col", "row")),
        P(None, "col", "row"),
        P(None, "row"),
        P(None, "row", "col"),
        P(None, ("col", "row")),
        P(None, "col", "row"),
        P(None, "row"),
    )
    shape = mesh.shape

    def on_device(*arrays):
        if fits_pairs(shape, arrays):
            return pair_plan(*arrays)
        return general_plan(*arrays)

    return jax.shard_map(
        on_device, mesh=mesh, in_specs=in_specs, out_specs=out_specs, check_vma=False
    )
```

```python
import math

import jax
import jax.numpy as jnp
from jax import lax
from jax.experimental import pallas as pl
from jax.experimental.pallas import tpu as pltpu
from jax.sharding import PartitionSpec as P

D = 1024
HD = 64
LAYERS = 2
LEN = 1024


eps = 1e-05
masked = -1000000000.0


def norm_forward(stream, gain, shift):
    totals = lax.psum((jnp.sum(stream, axis=1), jnp.sum(stream * stream, axis=1)), "row")
    center = totals[0] / D
    second = totals[1] / D - center * center
    inv_std = lax.rsqrt(second + eps)
    normed = (stream - center[:, None]) * inv_std[:, None]
    return (normed, inv_std, normed * gain + shift)


def norm_backward(grad_out, normed, inv_std, gain):
    scaled = grad_out * gain
    totals = lax.psum((jnp.sum(scaled, axis=1), jnp.sum(scaled * normed, axis=1)), "row")
    grad_in = inv_std[:, None] * (
        scaled - totals[0][:, None] / D - normed * (totals[1][:, None] / D)
    )
    return (grad_in, jnp.sum(grad_out * normed, axis=0), jnp.sum(grad_out, axis=0))


def gather_rows(block):
    return lax.all_gather(block, "row", axis=1, tiled=True)


def col_total(partial_sums):
    return lax.psum(partial_sums, "col")


def rows_back(partial_sums):
    return lax.psum_scatter(
        partial_sums.astype(jnp.bfloat16), "row", scatter_dimension=1, tiled=True
    ).astype(jnp.float32)


def in_parts(partial_sums):
    return lax.psum_scatter(partial_sums, "row", scatter_dimension=2, tiled=True)


def grad_gather(block):
    return lax.all_gather(block, "row", axis=2, tiled=True)


def pack_scores(queries, key_rows, seg_pack, scale):
    position = jnp.arange(queries.shape[0])
    allowed = (seg_pack[:, None] == seg_pack[None, :]) & (position[None, :] <= position[:, None])
    scores = (
        jnp.einsum("qhd,khd->hqk", queries, key_rows, preferred_element_type=jnp.float32) * scale
    )
    return jnp.where(allowed[None], scores, masked)


def split_packs(triple, seg_rows):
    length, three, width = triple.shape
    count = length // LEN
    return (triple.reshape(count, LEN, three, width // HD, HD), seg_rows.reshape(count, LEN))


def attend_forward(triple, seg_rows, scale):
    length, three, width = triple.shape
    packs, seg_packs = split_packs(triple, seg_rows)

    def one_pack(pieces):
        pack_rows, seg_pack = pieces
        scores = pack_scores(pack_rows[:, 0], pack_rows[:, 1], seg_pack, scale)
        row_peak = jnp.max(scores, axis=-1, keepdims=True)
        exponent = jnp.exp(scores - row_peak)
        denominator = jnp.sum(exponent, axis=-1, keepdims=True)
        soft_weights = (exponent / denominator).astype(jnp.bfloat16)
        blended = jnp.einsum(
            "hqk,khd->qhd", soft_weights, pack_rows[:, 2], preferred_element_type=jnp.float32
        )
        return (blended.astype(jnp.bfloat16), (row_peak + jnp.log(denominator))[..., 0])

    blended, log_totals = lax.map(one_pack, (packs, seg_packs))
    return (blended.reshape(length, width), log_totals)


def attend_backward(triple, seg_rows, log_totals, grad_mixed, scale):
    length, three, width = triple.shape
    packs, seg_packs = split_packs(triple, seg_rows)
    grad_packs = grad_mixed.reshape(length // LEN, LEN, width // HD, HD)

    def one_pack(pieces):
        pack_rows, seg_pack, pack_totals, grad_pack = pieces
        queries = pack_rows[:, 0]
        key_rows = pack_rows[:, 1]
        value_rows = pack_rows[:, 2]
        scores = pack_scores(queries, key_rows, seg_pack, scale)
        chances = jnp.exp(scores - pack_totals[:, :, None])
        chance_grad = jnp.einsum(
            "qhd,khd->hqk", grad_pack, value_rows, preferred_element_type=jnp.float32
        )
        inner = jnp.sum(chances * chance_grad, axis=-1, keepdims=True)
        score_grad = (chances * (chance_grad - inner)).astype(jnp.bfloat16)
        query_grad = (
            jnp.einsum("hqk,khd->qhd", score_grad, key_rows, preferred_element_type=jnp.float32)
            * scale
        )
        key_grad = (
            jnp.einsum("hqk,qhd->khd", score_grad, queries, preferred_element_type=jnp.float32)
            * scale
        )
        value_grad = jnp.einsum(
            "hqk,qhd->khd",
            chances.astype(jnp.bfloat16),
            grad_pack,
            preferred_element_type=jnp.float32,
        )
        return jnp.stack([query_grad, key_grad, value_grad], axis=1).astype(jnp.bfloat16)

    triple_rows = lax.map(one_pack, (packs, seg_packs, log_totals, grad_packs))
    return triple_rows.reshape(length, three, width)


def layer_forward(stream, weights, small, seg_rows):
    triple_w, output_w, up_w, down_w = weights
    gains, shifts, triple_b, output_b, up_b, down_b = small
    scale = 1.0 / math.sqrt(HD)
    normed_one, inv_one, attn_in = norm_forward(stream, gains[0], shifts[0])
    attn_in = attn_in.astype(jnp.bfloat16)
    triple = in_parts(
        jnp.einsum("td,dke->tke", attn_in, triple_w, preferred_element_type=jnp.float32)
    )
    bias_rows = jnp.stack([triple_b[0], jnp.zeros_like(triple_b[0]), triple_b[1]])
    triple = (triple + bias_rows).astype(jnp.bfloat16)
    mixed, log_totals = attend_forward(triple, seg_rows, scale)
    mixed_full = gather_rows(mixed)
    middle = stream + (
        col_total(jnp.dot(mixed_full, output_w, preferred_element_type=jnp.float32)) + output_b
    )
    normed_two, inv_two, mlp_in = norm_forward(middle, gains[1], shifts[1])
    mlp_in = mlp_in.astype(jnp.bfloat16)
    hidden_pre = (
        in_parts(jnp.dot(mlp_in, up_w, preferred_element_type=jnp.float32)[:, None, :])[:, 0] + up_b
    )
    active = jax.nn.gelu(hidden_pre, approximate=True).astype(jnp.bfloat16)
    active_full = gather_rows(active)
    after = middle + (
        col_total(jnp.dot(active_full, down_w, preferred_element_type=jnp.float32)) + down_b
    )
    saved = (
        normed_one,
        inv_one,
        attn_in,
        triple,
        log_totals,
        mixed_full,
        normed_two,
        inv_two,
        mlp_in,
        hidden_pre,
        active_full,
        None,
    )
    return (after, saved)


def layer_backward(grad, saved, weights, gains, seg_rows):
    (
        normed_one,
        inv_one,
        attn_rows,
        triple,
        log_totals,
        mixed_full,
        normed_two,
        inv_two,
        mlp_rows,
        hidden_pre,
        active_full,
        columns_in,
    ) = saved
    triple_w, output_w, up_w, down_w = weights
    scale = 1.0 / math.sqrt(HD)
    down_in = grad.astype(jnp.bfloat16)
    down_bias_grad = jnp.sum(down_in, axis=0, dtype=jnp.float32)
    down_grad = jnp.einsum("tf,td->fd", active_full, down_in, preferred_element_type=jnp.float32)
    active_grad = rows_back(
        jnp.einsum("td,fd->tf", down_in, down_w, preferred_element_type=jnp.float32)
    )
    gelu_pull = jax.vjp(lambda value: jax.nn.gelu(value, approximate=True), hidden_pre)[1]
    hidden_grad = gelu_pull(active_grad)[0].astype(jnp.bfloat16)
    up_bias_grad = jnp.sum(hidden_grad, axis=0, dtype=jnp.float32)
    hidden_rows = grad_gather(hidden_grad[:, None, :])[:, 0]
    up_grad = jnp.einsum("td,tf->df", mlp_rows, hidden_rows, preferred_element_type=jnp.float32)
    mlp_grad = col_total(
        jnp.einsum("tf,df->td", hidden_rows, up_w, preferred_element_type=jnp.float32)
    )
    norm_two_grad, gain_two, shift_two = norm_backward(mlp_grad, normed_two, inv_two, gains[1])
    middle_grad = grad + norm_two_grad
    branch_grad = middle_grad.astype(jnp.bfloat16)
    output_bias_grad = jnp.sum(branch_grad, axis=0, dtype=jnp.float32)
    output_grad = jnp.einsum(
        "td,te->de", mixed_full, branch_grad, preferred_element_type=jnp.float32
    )
    mixed_grad = rows_back(
        jnp.einsum("te,de->td", branch_grad, output_w, preferred_element_type=jnp.float32)
    ).astype(jnp.bfloat16)
    triple_rows = attend_backward(triple, seg_rows, log_totals, mixed_grad, scale)
    triple_bias_grad = jnp.sum(triple_rows[:, 0::2], axis=0, dtype=jnp.float32)
    full_rows = grad_gather(triple_rows)
    triple_grad = jnp.einsum(
        "td,tke->dke", attn_rows, full_rows, preferred_element_type=jnp.float32
    )
    attn_grad = col_total(
        jnp.einsum("tke,dke->td", full_rows, triple_w, preferred_element_type=jnp.float32)
    )
    norm_one_grad, gain_one, shift_one = norm_backward(attn_grad, normed_one, inv_one, gains[0])
    start_grad = middle_grad + norm_one_grad
    terms = (
        jnp.stack([gain_one, gain_two]),
        jnp.stack([shift_one, shift_two]),
        triple_grad,
        triple_bias_grad,
        output_grad,
        output_bias_grad,
        up_grad,
        up_bias_grad,
        down_grad,
        down_bias_grad,
    )
    return (start_grad, terms)


def general_plan(
    tokens,
    segments,
    norm_gain,
    norm_shift,
    triple_weight,
    triple_bias,
    output_weight,
    output_bias,
    up_weight,
    up_bias,
    down_weight,
    down_bias,
    cotangent,
):

    def weights_of(layer_id):
        return (
            triple_weight[layer_id],
            output_weight[layer_id],
            up_weight[layer_id],
            down_weight[layer_id],
        )

    def small_of(layer_id):
        return (
            norm_gain[layer_id].astype(jnp.float32),
            norm_shift[layer_id].astype(jnp.float32),
            triple_bias[layer_id].astype(jnp.float32),
            output_bias[layer_id].astype(jnp.float32),
            up_bias[layer_id].astype(jnp.float32),
            down_bias[layer_id].astype(jnp.float32),
        )

    stream = tokens.astype(jnp.float32)
    stored = []
    for layer_id in range(LAYERS):
        stream, saved = layer_forward(stream, weights_of(layer_id), small_of(layer_id), segments)
        stored.append(saved)
    result = stream.astype(jnp.bfloat16)
    grad = cotangent.astype(jnp.float32)
    summed = [None] * LAYERS
    for layer_id in reversed(range(LAYERS)):
        grad, terms = layer_backward(
            grad, stored[layer_id], weights_of(layer_id), small_of(layer_id)[0], segments
        )
        summed[layer_id] = (
            lax.psum(terms[0].astype(jnp.bfloat16), "dp").astype(jnp.float32),
            lax.psum(terms[1].astype(jnp.bfloat16), "dp").astype(jnp.float32),
            lax.psum(terms[2].astype(jnp.bfloat16), "dp").astype(jnp.float32),
            lax.psum(terms[3].astype(jnp.bfloat16), "dp").astype(jnp.float32),
            lax.psum(terms[4].astype(jnp.bfloat16), "dp").astype(jnp.float32),
            lax.psum(terms[5].astype(jnp.bfloat16), "dp").astype(jnp.float32),
            lax.psum(terms[6].astype(jnp.bfloat16), "dp").astype(jnp.float32),
            lax.psum(terms[7].astype(jnp.bfloat16), "dp").astype(jnp.float32),
            lax.psum(terms[8].astype(jnp.bfloat16), "dp").astype(jnp.float32),
            lax.psum(terms[9].astype(jnp.bfloat16), "dp").astype(jnp.float32),
        )
    stacks = [
        jnp.stack([summed[layer_id][member] for layer_id in range(LAYERS)]) for member in range(10)
    ]
    return (
        result,
        grad,
        stacks[0],
        stacks[1],
        stacks[2],
        stacks[3],
        stacks[4],
        stacks[5],
        stacks[6],
        stacks[7],
        stacks[8],
        stacks[9],
    )


f32 = jnp.float32
bf16 = jnp.bfloat16
CHUNKS = 2
SPAN = LEN // CHUNKS
OWN = SPAN // 2
WIDTH = D // 4
QB = 256


def fits_pairs(shape, arrays):
    return (
        shape["row"] == 4
        and shape["col"] == 2
        and shape["dp"] == 4
        and arrays[0].shape == (2 * LEN, WIDTH)
        and arrays[8].shape[2] == 8 * WIDTH
    )


def dot(a, b):
    return lax.dot_general(a, b, (((1,), (0,)), ((), ())), preferred_element_type=f32)


def dot_nt(a, b):
    return lax.dot_general(a, b, (((1,), (1,)), ((), ())), preferred_element_type=f32)


def dot_tn(a, b):
    return lax.dot_general(a, b, (((0,), (0,)), ((), ())), preferred_element_type=f32)


def like(shape, kind):
    return jax.ShapeDtypeStruct(shape, kind)


def mean_lanes(v):
    return jnp.sum(v, axis=1, keepdims=True) * (1.0 / D)


def norm_parts(v):
    center = mean_lanes(v)
    second = mean_lanes(v * v) - center * center
    inv_std = lax.rsqrt(second + eps)
    return (v - center) * inv_std, inv_std


GELU = math.sqrt(2.0 / math.pi)


MESH = pl.DeviceIdType.MESH
HEADS_HERE = WIDTH // HD
SMALL = 24
SEG = 64


class Place:
    def __init__(self):
        self.row = lax.axis_index("row")
        self.col = lax.axis_index("col")
        self.dp = lax.axis_index("dp")
        self.core = self.row % 2
        self.chip = self.row // 2
        self.half = self.dp % 2
        sibling = self.row + 1 - 2 * self.core
        self.rows = [self.row, sibling, (self.row + 2) % 4, (sibling + 2) % 4]
        self.cores = [self.core, 1 - self.core, self.core, 1 - self.core]

    def to_row(self, j):
        return {"row": self.rows[j]}

    def to_col(self):
        return {"col": 1 - self.col}

    def to_dp(self):
        return {"dp": self.dp + 1 - 2 * self.half}


class Copies:
    def __init__(self, sems):
        self.sems = sems
        self.used = 0
        self.open = []

    def sem(self):
        self.used += 1
        return self.sems.at[self.used - 1]

    def local(self, src, dst):
        copy = pltpu.make_async_copy(src, dst, self.sem())
        copy.start()
        return copy

    def save(self, src, dst):
        self.open.append(self.local(src, dst).wait)

    def trade(self, src, dst, landing, device):
        sent, got = self.sem(), self.sem()
        out = pltpu.make_async_remote_copy(src, dst, sent, got, device_id=device, device_id_type=MESH)
        back = pltpu.make_async_remote_copy(
            landing, landing, sent, got, device_id=device, device_id_type=MESH
        )
        out.start()
        return out.wait_send, back.wait_recv

    def finish(self):
        for wait in self.open:
            wait()


def greet(place, devices):
    barrier = pltpu.get_barrier_semaphore()
    for device in devices:
        pl.semaphore_signal(barrier, inc=1, device_id=device, device_id_type=MESH)
    pl.semaphore_wait(barrier, len(devices))


def span(start, size):
    return pl.ds(pl.multiple_of(start, size), size)


def weight_cuts(kind, layer, wide, local):
    w = WIDTH
    if kind == 0:

        def source(core, half):
            rows = slice(None) if half is None else span(half * (w // 2), w // 2)
            return local.at[layer, :, rows, span(core * w, w)]

        def target(row, half):
            rows = span(row * w, w) if half is None else span(row * w + half * (w // 2), w // 2)
            return wide.at[layer, :, rows, :]

    elif kind == 2:
        units = wide.shape[2]

        def source(core, half):
            rows = slice(None) if half is None else span(half * (w // 2), w // 2)
            return local.at[layer, rows, span(core * units, units)]

        def target(row, half):
            rows = span(row * w, w) if half is None else span(row * w + half * (w // 2), w // 2)
            return wide.at[layer, rows, :]

    else:
        high = wide.shape[1]

        def source(core, half):
            if half is None:
                return local.at[layer, span(core * high, high), :]
            return local.at[layer, span(core * high + half * (high // 2), high // 2), :]

        def target(row, half):
            rows = slice(None) if half is None else span(half * (high // 2), high // 2)
            return wide.at[layer, rows, span(row * w, w)]

    return source, target


STRIP = 64


def strips(count, body):
    def step(i, carry):
        body(pl.multiple_of(i * STRIP, STRIP))
        return carry

    lax.fori_loop(0, count // STRIP, step, 0)


def causal(seg_col, seg_row, start, keys):
    query = lax.broadcasted_iota(jnp.int32, (QB, keys), 0) + start
    key = lax.broadcasted_iota(jnp.int32, (QB, keys), 1)
    return (seg_col == seg_row) & (key <= query)


def lanes_of(h):
    lane = lax.broadcasted_iota(jnp.int32, (1, WIDTH), 1)
    return (lane >= h * HD) & (lane < (h + 1) * HD)


def attend_chunk(k, triples, seg_col_ref, seg_row_ref, kv_ref, mixed_ref, log_ref):
    scale = 1.0 / math.sqrt(HD)
    kv_ref[k * SPAN : (k + 1) * SPAN, :] = triples[k][:, WIDTH:]
    for block in range(SPAN // QB):
        rows = slice(block * QB, (block + 1) * QB)
        start = k * SPAN + block * QB
        keys = start + QB
        allowed = causal(seg_col_ref[start : start + QB, :], seg_row_ref[:, :keys], start, keys)
        queries = triples[k][rows, :WIDTH] * scale
        key_rows = kv_ref[:keys, :WIDTH]
        value_rows = kv_ref[:keys, WIDTH:]
        blended = jnp.zeros((QB, WIDTH), f32)
        for h in range(HEADS_HERE):
            lanes = lanes_of(h)
            scores = dot_nt(jnp.where(lanes, queries, 0).astype(bf16), key_rows)
            scores = jnp.where(allowed, scores, masked)
            peak = jnp.max(scores, axis=1, keepdims=True)
            exponent = jnp.exp(scores - peak)
            total = jnp.sum(exponent, axis=1, keepdims=True)
            soft = (exponent * (1.0 / total)).astype(bf16)
            blended = jnp.where(lanes, dot(soft, value_rows), blended)
            log_ref[rows, h : h + 1] = peak + jnp.log(total)
        log_ref[rows, SEG : SEG + 1] = seg_col_ref[start : start + QB, :].astype(f32)
        mixed_ref[rows, :] = blended.astype(bf16)


def forward_body(*refs):
    (
        tokens_ref,
        cotangent_ref,
        small_ref,
        seg_col_ref,
        seg_row_ref,
        triple_in,
        output_in,
        up_in,
        down_in,
        result_ref,
        grad_ref,
        wide_out,
        triple_out,
        output_out,
        up_out,
        down_out,
        attn_out,
        rows_out,
        mixed_out,
        log_out,
        mlp_out,
        slope_out,
        active_out,
        stream_out,
        triple_w,
        output_w,
        up_w,
        down_w,
        attn,
        rows,
        mixed,
        logs,
        mlp,
        slope,
        active,
        stream,
        taken,
        wide,
        kv,
        mine,
        give,
        got_core,
        chip_sum,
        got_col,
        final,
        sems,
    ) = refs
    place = Place()
    copies = Copies(sems)
    core, sibling = place.core, 1 - place.core
    greet(place, [place.to_row(1), place.to_row(2), place.to_row(3), place.to_col(), place.to_dp()])

    own_lanes = span(place.row * WIDTH, WIDTH)

    def held(j, k):
        return span(place.rows[j] // 2 * LEN + k * SPAN + place.cores[j] * OWN, OWN)

    def part(c):
        return span(c * OWN, OWN)

    small_waits = []
    copy = copies.local(small_ref, wide.at[:, own_lanes])
    small_waits.append(copy.wait)
    for j in range(1, 4):
        sent, got = copies.trade(
            small_ref,
            wide.at[:, own_lanes],
            wide.at[:, span(place.rows[j] * WIDTH, WIDTH)],
            place.to_row(j),
        )
        copies.open.append(sent)
        small_waits.append(got)
    token_waits = [[] for _ in range(CHUNKS)]

    def scatter_in(block_ref, target, k, waits):
        waits.append(copies.local(block_ref.at[held(0, k), :], target.at[k, :, own_lanes]).wait)
        for j in range(1, 4):
            sent, got = copies.trade(
                block_ref.at[held(j, k), :],
                target.at[k, :, own_lanes],
                target.at[k, :, span(place.rows[j] * WIDTH, WIDTH)],
                place.to_row(j),
            )
            copies.open.append(sent)
            waits.append(got)

    arrivals, ready_waits = {}, {}

    def send_weight(layer, kind):
        local = (triple_in, output_in, up_in, down_in)[kind]
        whole = (triple_w, output_w, up_w, down_w)[kind]
        source, target = weight_cuts(kind, layer, whole, local)
        here = []
        for j in (2, 3):
            sent, got = copies.trade(
                source(place.cores[j], place.half),
                target(place.row, place.half),
                target(place.rows[j], place.half),
                place.to_row(j),
            )
            copies.open.append(sent)
            here.append((got, target(place.rows[j], place.half), target(place.rows[j], 1 - place.half)))
        arrivals[layer, kind] = here
        sent, got = copies.trade(
            source(sibling, None),
            target(place.row, None),
            target(place.rows[1], None),
            place.to_row(1),
        )
        copies.open.append(sent)
        own = copies.local(source(core, None), target(place.row, None))
        ready_waits[layer, kind] = [got, own.wait]

    relays = [
        (layer, kind, i) for layer in range(LAYERS) for kind in range(4) for i in range(2)
    ]

    def pump(count):
        for _ in range(count):
            layer, kind, i = relays.pop(0)
            got, arrived, missing = arrivals[layer, kind][i]
            got()
            sent, back = copies.trade(arrived, arrived, missing, place.to_dp())
            copies.open.append(sent)
            ready_waits[layer, kind].append(back)

    def ready_weight(layer, kind):
        for wait in ready_waits[layer, kind]:
            wait()
        whole = (triple_w, output_w, up_w, down_w)[kind]
        out = (triple_out, output_out, up_out, down_out)[kind]
        copies.save(whole.at[layer], out.at[layer])

    scatter_in(tokens_ref, taken, 0, token_waits[0])
    send_weight(0, 0)
    scatter_in(tokens_ref, taken, 1, token_waits[1])
    for layer, kind in ((0, 1), (0, 2), (0, 3), (1, 0), (1, 1), (1, 2), (1, 3)):
        send_weight(layer, kind)
    grad_waits = []
    for k in range(CHUNKS):
        scatter_in(cotangent_ref, grad_ref, k, grad_waits)

    for wait in small_waits:
        wait()
    copies.save(wide, wide_out)

    def gain(layer, which):
        return wide[2 * layer + which : 2 * layer + which + 1, :]

    def shift(layer, which):
        return wide[4 + 2 * layer + which : 5 + 2 * layer + which, :]

    def output_bias(layer):
        return wide[8 + layer : 9 + layer, :]

    def down_bias(layer):
        return wide[10 + layer : 11 + layer, :]

    def of_core(line, start, size):
        return wide[line : line + 1, span(start, size)]

    def triple_bias(layer, which):
        at = 2 * core * WIDTH + which * (WIDTH // 2)
        size = WIDTH // 2
        return jnp.concatenate(
            [of_core(12 + layer, at, size), of_core(12 + layer, at + WIDTH, size)], axis=1
        )

    def up_bias(layer):
        line, at = 14 + 2 * layer, 2 * core * WIDTH
        return jnp.concatenate(
            [of_core(line + a, at + b * WIDTH, WIDTH) for b in range(2) for a in range(2)], axis=1
        )

    def norm_to(value, layer, which, target, at):
        center = jnp.mean(value, axis=1, keepdims=True)
        second = jnp.mean(value * value, axis=1, keepdims=True) - center * center
        normed = (value - center) * lax.rsqrt(second + eps)
        target[pl.ds(pl.multiple_of(core * OWN + at, STRIP), STRIP), :] = (
            normed * gain(layer, which) + shift(layer, which)
        ).astype(bf16)

    def share(target):
        return copies.trade(target.at[part(core)], target.at[part(core)], target.at[part(sibling)], place.to_row(1))

    sent_core, sent_col = [None] * CHUNKS, [None] * CHUNKS
    col_waits = [None] * CHUNKS
    saves = {}

    def settle(stage, k, got):
        got()
        if sent_col[k] is not None:
            sent_col[k]()

        def add(at):
            lines = pl.ds(at, STRIP)
            chip_sum[k, lines, :] = (
                mine[k, lines, :] + got_core[stage, k, lines, :].astype(f32)
            ).astype(bf16)

        strips(OWN, add)
        sent_col[k], col_waits[k] = copies.trade(
            chip_sum.at[k], got_col.at[stage, k], got_col.at[stage, k], place.to_col()
        )

    def start_core(stage, k):
        sent, got = copies.trade(
            give.at[k], got_core.at[stage, k], got_core.at[stage, k], place.to_row(1)
        )
        sent_core[k] = sent
        return got

    def take_col(stage, k, layer, bias, after_ref):
        col_waits[k]()

        def add(at):
            lines = pl.ds(at, STRIP)
            total = chip_sum[k, lines, :].astype(f32) + got_col[stage, k, lines, :].astype(f32)
            value = stream[stage, k, lines, :] + (total + bias)
            stream[1 - stage, k, lines, :] = value
            after_ref(value, at)

        strips(OWN, add)

    shares = [None] * CHUNKS
    for k in range(CHUNKS):
        for wait in token_waits[k]:
            wait()
        def first(at, k=k):
            value = taken[k, pl.ds(at, STRIP), :].astype(f32)
            stream[0, k, pl.ds(at, STRIP), :] = value
            norm_to(value, 0, 0, attn.at[0, k], at)

        strips(OWN, first)
        saves[0, 0, k] = copies.local(stream.at[0, k], stream_out.at[0, 0, k])
        shares[k] = share(attn.at[0, k])
        pump(2)

    for layer in range(LAYERS):
        for k in range(CHUNKS):
            if layer:
                if k == 0:
                    pump(1)
                saves.pop((layer - 1, 0, k)).wait()
                take_col(
                    1, k, layer, down_bias(layer - 1), lambda v, at, k=k: norm_to(v, layer, 0, attn.at[layer, k], at)
                )
                saves[layer, 0, k] = copies.local(stream.at[0, k], stream_out.at[layer, 0, k])
                shares[k] = share(attn.at[layer, k])
            if k == 0:
                ready_weight(layer, 0)
            bias = [triple_bias(layer, 0), None, triple_bias(layer, 1)]

            def project(c, k=k, bias=bias):
                for third in range(3):
                    value = dot(attn[layer, k, part(c), :], triple_w[layer, third])
                    if bias[third] is not None:
                        value = value + bias[third]
                    rows[layer, k, part(c), third * WIDTH : (third + 1) * WIDTH] = value.astype(bf16)

            project(core)
            sent, got = shares[k]
            got()
            project(sibling)
            attend_chunk(
                k,
                [rows.at[layer, i] for i in range(k + 1)],
                seg_col_ref,
                seg_row_ref,
                kv,
                mixed.at[layer, k],
                logs.at[layer, k],
            )
            pump(1)
            if k == 0:
                ready_weight(layer, 1)
            if sent_core[k] is not None:
                sent_core[k]()
            give[k] = dot(mixed[layer, k, part(sibling), :], output_w[layer]).astype(bf16)
            got = start_core(0, k)
            mine[k] = dot(mixed[layer, k, part(core), :], output_w[layer])
            sent()
            copies.save(attn.at[layer, k], attn_out.at[layer, k])
            copies.save(rows.at[layer, k], rows_out.at[layer, k])
            copies.save(mixed.at[layer, k], mixed_out.at[layer, k])
            copies.save(logs.at[layer, k], log_out.at[layer, k])
            settle(0, k, got)
            if k:
                pump(1)
        for k in range(CHUNKS):
            if layer:
                saves.pop((layer - 1, 1, k)).wait()
            elif k:
                pump(1)
            take_col(
                0, k, layer, output_bias(layer), lambda v, at, k=k: norm_to(v, layer, 1, mlp.at[layer, k], at)
            )
            saves[layer, 1, k] = copies.local(stream.at[1, k], stream_out.at[layer, 1, k])
            shares[k] = share(mlp.at[layer, k])
            if k == 0:
                ready_weight(layer, 2)
            bias = up_bias(layer)

            def widen(c, k=k, bias=bias):
                for block in range(4):
                    cols = slice(block * WIDTH, (block + 1) * WIDTH)
                    pre = dot(mlp[layer, k, part(c), :], up_w[layer, :, cols]) + bias[:, cols]
                    square = pre * pre
                    curve = jnp.tanh(GELU * (pre + 0.044715 * (square * pre)))
                    upper = 0.5 * (1.0 + curve)
                    active[layer, k, part(c), cols] = (pre * upper).astype(bf16)
                    slope[layer, k, part(c), cols] = (
                        upper
                        + (0.5 * GELU) * pre * (1.0 - curve * curve) * (1.0 + (3.0 * 0.044715) * square)
                    ).astype(bf16)

            widen(core)
            sent, got = shares[k]
            got()
            widen(sibling)
            if k == 0:
                if layer == 0:
                    pump(1)
                ready_weight(layer, 3)
            sent_core[k]()
            give[k] = dot(active[layer, k, part(sibling), :], down_w[layer]).astype(bf16)
            got = start_core(1, k)
            mine[k] = dot(active[layer, k, part(core), :], down_w[layer])
            sent()
            copies.save(mlp.at[layer, k], mlp_out.at[layer, k])
            copies.save(slope.at[layer, k], slope_out.at[layer, k])
            copies.save(active.at[layer, k], active_out.at[layer, k])
            settle(1, k, got)
            if layer == 0:
                pump(k + 1)
    result_waits = []
    for k in range(CHUNKS):
        saves.pop((LAYERS - 1, 0, k)).wait()

        def finish(v, at, k=k):
            final[k, pl.ds(at, STRIP), :] = v.astype(bf16)

        take_col(1, k, LAYERS, down_bias(LAYERS - 1), finish)
        result_waits.append(copies.local(final.at[k, :, own_lanes], result_ref.at[held(0, k), :]).wait)
        for j in range(1, 4):
            sent, got = copies.trade(
                final.at[k, :, span(place.rows[j] * WIDTH, WIDTH)],
                result_ref.at[held(0, k), :],
                result_ref.at[held(j, k), :],
                place.to_row(j),
            )
            result_waits += [sent, got]
    for k in range(CHUNKS):
        saves.pop((LAYERS - 1, 1, k)).wait()
        sent_core[k]()
        sent_col[k]()
    for wait in result_waits + grad_waits:
        wait()
    copies.finish()


def forward_call(tokens, cotangent, small, seg_col, seg_row, triple_w, output_w, up_w, down_w):
    units = up_w.shape[2] // 2
    per_layer = [
        ((LAYERS, CHUNKS, SPAN, D), bf16),
        ((LAYERS, CHUNKS, SPAN, 3 * WIDTH), bf16),
        ((LAYERS, CHUNKS, SPAN, WIDTH), bf16),
        ((LAYERS, CHUNKS, SPAN, 128), f32),
        ((LAYERS, CHUNKS, SPAN, D), bf16),
        ((LAYERS, CHUNKS, SPAN, units), bf16),
        ((LAYERS, CHUNKS, SPAN, units), bf16),
    ]
    wide = [
        ((LAYERS, 3, D, WIDTH), bf16),
        ((LAYERS, WIDTH, D), bf16),
        ((LAYERS, D, units), bf16),
        ((LAYERS, units, D), bf16),
    ]
    outs = [
        (tokens.shape, bf16),
        ((CHUNKS, OWN, D), bf16),
        ((SMALL, D), f32),
        *wide,
        *per_layer,
        ((LAYERS, 2, CHUNKS, OWN, D), f32),
    ]
    scratch = [
        *wide,
        *per_layer,
        ((2, CHUNKS, OWN, D), f32),
        ((CHUNKS, OWN, D), bf16),
        ((SMALL, D), f32),
        ((LEN, 2 * WIDTH), bf16),
        ((CHUNKS, OWN, D), f32),
        ((CHUNKS, OWN, D), bf16),
        ((2, CHUNKS, OWN, D), bf16),
        ((CHUNKS, OWN, D), bf16),
        ((2, CHUNKS, OWN, D), bf16),
        ((CHUNKS, OWN, D), bf16),
    ]
    anywhere = pl.BlockSpec(memory_space=pl.ANY)
    inside = pl.BlockSpec(memory_space=pltpu.VMEM)
    return pl.pallas_call(
        forward_body,
        out_shape=[like(*v) for v in outs],
        in_specs=[anywhere] * 2 + [inside] * 3 + [anywhere] * 4,
        out_specs=[anywhere] * len(outs),
        scratch_shapes=[pltpu.VMEM(*v) for v in scratch] + [pltpu.SemaphoreType.DMA((320,))],
        compiler_params=pltpu.CompilerParams(
            collective_id=0, has_side_effects=True, vmem_limit_bytes=60 * 1024 * 1024
        ),
    )(tokens, cotangent, small, seg_col, seg_row, triple_w, output_w, up_w, down_w)


def pack_small(norm_gain, norm_shift, output_bias, down_bias, triple_bias, up_bias):
    lines = [
        norm_gain.reshape(-1, WIDTH),
        norm_shift.reshape(-1, WIDTH),
        output_bias,
        down_bias,
        triple_bias.reshape(-1, WIDTH),
        up_bias.reshape(-1, WIDTH),
    ]
    lines = jnp.concatenate(lines).astype(f32)
    return jnp.pad(lines, ((0, SMALL - lines.shape[0]), (0, 0)))


PIECES = ((3, WIDTH, WIDTH), (1, WIDTH, WIDTH), (4, WIDTH // 4, D), (4, D // 4, WIDTH))

PLAN = {
    "a1": ((1, 3, 0, 0),),
    "a0": ((1, 3, 1, 0), (1, 3, 0, 1)),
    "u1": ((1, 3, 2, 0),),
    "c1": ((1, 3, 1, 1), (1, 3, 0, 2), (1, 3, 3, 0)),
    "m1": ((1, 3, 2, 1), (1, 2, 0, 0), (1, 3, 1, 2), (1, 3, 3, 1), (1, 2, 1, 0)),
    "c0": ((1, 2, 2, 0), (1, 3, 2, 2), (1, 2, 0, 1)),
    "m0": ((1, 2, 3, 0), (1, 3, 3, 2), (1, 2, 1, 1)),
    "w1": ((1, 2, 0, 2), (1, 2, 2, 1)),
    "f1": ((1, 3, 0, 3),),
    "g1": ((1, 1, 0, 0), (1, 2, 1, 2), (1, 2, 3, 1)),
    "e0": ((1, 0, 0, 0), (1, 2, 2, 2)),
    "g0": ((1, 1, 0, 1), (1, 0, 1, 0), (1, 2, 3, 2)),
    "v0": ((1, 0, 0, 1), (1, 0, 2, 0)),
    "u0": ((1, 1, 0, 2), (1, 2, 0, 3), (1, 0, 1, 1)),
    "c1L": ((0, 3, 0, 0), (1, 0, 0, 2)),
    "m1L": ((1, 1, 0, 3), (1, 0, 2, 1), (0, 3, 1, 0), (1, 0, 1, 2), (0, 3, 0, 1), (0, 3, 2, 0)),
    "m0L": ((1, 0, 2, 2), (0, 3, 1, 1), (0, 3, 3, 0), (0, 3, 0, 2), (0, 3, 2, 1), (0, 2, 0, 0)),
    "w0": ((0, 2, 1, 0), (1, 0, 0, 3)),
    "h1": ((0, 3, 1, 2), (0, 3, 3, 1)),
    "h0": ((0, 2, 2, 0), (0, 3, 2, 2), (0, 2, 0, 1), (0, 2, 3, 0), (0, 3, 3, 2), (0, 2, 1, 1)),
    "tail": ((0, 1, 0, 0), (0, 2, 2, 1), (0, 2, 0, 2), (0, 0, 0, 0), (0, 2, 3, 1), (0, 2, 1, 2), (0, 0, 1, 0), (0, 1, 0, 1), (0, 2, 2, 2), (0, 0, 2, 0), (0, 0, 0, 1), (0, 2, 3, 2), (0, 0, 1, 1), (0, 1, 0, 2), (0, 0, 2, 1), (0, 0, 0, 2), (0, 0, 1, 2), (0, 0, 2, 2)),
}
LINES = 16


def attend_back_chunk(
    k, rows_ref, log_ref, seg_row_ref, grad_ref, total_ref, out_ref
):
    scale = 1.0 / math.sqrt(HD)
    for block in range(SPAN // QB):
        start = k * SPAN + block * QB
        keys = start + QB
        here = slice(start, keys)
        allowed = causal(log_ref[here, SEG : SEG + 1], seg_row_ref[:, :keys], start, keys)
        queries = rows_ref[here, :WIDTH] * scale
        grads = grad_ref[block * QB : (block + 1) * QB, :]
        key_rows = rows_ref[:keys, WIDTH : 2 * WIDTH]
        value_rows = rows_ref[:keys, 2 * WIDTH :]
        query_grad = jnp.zeros((QB, WIDTH), f32)
        for h in range(HEADS_HERE):
            lanes = lanes_of(h)
            query = jnp.where(lanes, queries, 0).astype(bf16)
            grad = jnp.where(lanes, grads, 0).astype(bf16)
            scores = jnp.where(allowed, dot_nt(query, key_rows), masked)
            chances = jnp.exp(scores - log_ref[here, h : h + 1])
            product = chances * dot_nt(grad, value_rows)
            inner = jnp.sum(product, axis=1, keepdims=True)
            score_grad = (product - chances * inner).astype(bf16)
            query_grad = jnp.where(lanes, dot(score_grad, key_rows), query_grad)
            total_ref[:keys, :WIDTH] += dot_tn(score_grad, query)
            total_ref[:keys, WIDTH:] += dot_tn(chances.astype(bf16), grad)
        out_ref[here, :WIDTH] = (query_grad * scale).astype(bf16)
    here = slice(k * SPAN, (k + 1) * SPAN)
    out_ref[here, WIDTH:] = total_ref[here, :].astype(bf16)


def add_pieces(target, left, right):
    high, across = target.shape
    step = 32768 // across

    def body(i, carry):
        lines = pl.ds(pl.multiple_of(i * step, step), step)
        target[lines, :] = (left[lines, :].astype(f32) + right[lines, :].astype(f32)).astype(bf16)
        return carry

    lax.fori_loop(0, high // step, body, 0)


class Reduction:
    def __init__(self, kind, layer, place, copies, grads, land, ends, inner, outs, credits):
        self.kind, self.layer, self.place, self.copies = kind, layer, place, copies
        self.grads, self.land, self.ends, self.inner = grads[kind], land[kind], ends[kind], inner[kind]
        self.out, self.credits = outs[kind], credits
        self.count = PIECES[kind][0]
        self.again = layer < LAYERS - 1
        self.is_end = place.dp * (3 - place.dp) == 0
        self.is_inner = place.dp * (3 - place.dp) > 0

    def home(self, which, s):
        core = self.place.cores[which]
        out, layer = self.out, self.layer
        if self.kind == 0:
            return out.at[layer, s, :, span(core * WIDTH, WIDTH)]
        if self.kind == 1:
            return out.at[layer, span(core * WIDTH, WIDTH), :]
        if self.kind == 2:
            return out.at[layer, s * (WIDTH // 4) : (s + 1) * (WIDTH // 4), span(core * D, D)]
        return out.at[layer, span(core * D + s * (D // 4), D // 4), :]

    def send(self):
        place, copies = self.place, self.copies
        if self.again:
            pl.semaphore_wait(self.credits.at[self.kind], 3)
        self.waits = {}
        self.sent = []
        for s in range(self.count):
            for j in (2, 3, 1):
                sent, got = copies.trade(
                    self.grads.at[place.rows[j], s],
                    self.land.at[j - 1, s],
                    self.land.at[j - 1, s],
                    place.to_row(j),
                )
                self.sent.append(sent)
                self.waits[j, s] = got

    def over_chips(self, s):
        place, copies = self.place, self.copies
        if s == 0:
            self.to_inner = {}
            if self.again:

                @pl.when(self.is_end)
                def _():
                    pl.semaphore_wait(self.credits.at[4 + self.kind], 1)

        for which in range(2):
            if which == 0:
                self.waits[2, s]()
                target = self.land.at[1, s]
                add_pieces(target, self.grads.at[place.row, s], target)
            else:
                self.waits[1, s]()
                self.waits[3, s]()
                target = self.land.at[2, s]
                add_pieces(target, self.land.at[0, s], target)
            copy = pltpu.make_async_remote_copy(
                target,
                self.ends.at[which, s],
                copies.sem(),
                copies.sem(),
                device_id=place.to_dp(),
                device_id_type=MESH,
            )
            self.to_inner[which, s] = copy

            @pl.when(self.is_end)
            def _():
                copy.start()

    def to_middle(self, s):
        place, copies = self.place, self.copies
        if s == 0:
            self.across = {}
            if self.again:

                @pl.when(self.is_inner)
                def _():
                    pl.semaphore_wait(self.credits.at[8 + self.kind], 1)

        for which in range(2):
            half = self.ends.at[which, s]
            copy = pltpu.make_async_remote_copy(
                half,
                self.inner.at[which, s],
                copies.sem(),
                copies.sem(),
                device_id={"dp": 3 - place.dp},
                device_id_type=MESH,
            )
            self.across[which, s] = copy

            @pl.when(self.is_inner)
            def _():
                self.to_inner[which, s].wait_recv()
                add_pieces(half, self.land.at[1 + which, s], half)
                copy.start()

        if s == self.count - 1:

            @pl.when(self.is_end)
            def _():
                for copy in self.to_inner.values():
                    copy.wait_send()

            for sent in self.sent:
                sent()
            if not self.again:
                for j in range(1, 4):
                    pl.semaphore_signal(
                        self.credits.at[self.kind],
                        inc=1,
                        device_id=place.to_row(j),
                        device_id_type=MESH,
                    )

    def back(self, s):
        place, copies = self.place, self.copies
        if s == 0:
            self.out_copies = []
        for which in range(2):
            total = self.inner.at[which, s]
            home = self.home(which, s)
            copy = pltpu.make_async_remote_copy(
                total,
                home,
                copies.sem(),
                copies.sem(),
                device_id=place.to_dp(),
                device_id_type=MESH,
            )
            here = pltpu.make_async_copy(total, home, copies.sem())
            self.out_copies.append((copy, here))

            @pl.when(self.is_inner)
            def _():
                self.across[which, s].wait_recv()
                add_pieces(total, self.ends.at[which, s], total)
                copy.start()
                here.start()

    def finish(self):
        place = self.place

        @pl.when(self.is_inner)
        def _():
            for copy in self.across.values():
                copy.wait_send()
            for copy, here in self.out_copies:
                copy.wait_send()
                here.wait()
            if not self.again:
                pl.semaphore_signal(
                    self.credits.at[4 + self.kind], inc=1, device_id=place.to_dp(), device_id_type=MESH
                )
                pl.semaphore_signal(
                    self.credits.at[8 + self.kind],
                    inc=1,
                    device_id={"dp": 3 - place.dp},
                    device_id_type=MESH,
                )

        @pl.when(self.is_end)
        def _():
            for copy, here in self.out_copies:
                copy.wait_recv()


def backward_body(*refs):
    (
        grad_in,
        wide_ref,
        seg_row_ref,
        triple_in,
        output_in,
        up_in,
        down_in_w,
        attn_in,
        rows_in,
        mixed_in,
        log_in,
        mlp_in,
        slope_in,
        active_in,
        stream_in,
        input_grad_ref,
        small_out,
        triple_out,
        output_out,
        up_out,
        down_out,
        triple_w,
        output_w,
        up_w,
        down_w,
        attn,
        rows,
        mixed,
        logs,
        mlp,
        slope,
        active,
        start,
        middle,
        down_in,
        hidden,
        branch,
        rows_grad,
        mixed_grad,
        pair_total,
        grad,
        mine,
        give,
        got_core,
        chip_sum,
        got_col,
        sums,
        lines,
        line_land,
        dp_land,
        *rest,
    ) = refs
    grads, land, ends, inner = rest[0:4], rest[4:8], rest[8:12], rest[12:16]
    credits, sems = rest[16:]
    place = Place()
    copies = Copies(sems)
    core, sibling = place.core, 1 - place.core
    others = [{"dp": (place.dp + i) % 4} for i in range(1, 4)]
    greet(place, [place.to_row(1), place.to_row(2), place.to_row(3), place.to_col(), *others])
    own_lanes = span(place.row * WIDTH, WIDTH)

    def part(k, c):
        return span(k * SPAN + c * OWN, OWN)

    ready = {}

    def load(name, layer):
        source, target = {
            "triple_w": (triple_in, triple_w),
            "output_w": (output_in, output_w),
            "up_w": (up_in, up_w),
            "down_w": (down_in_w, down_w),
            "attn": (attn_in, attn),
            "rows": (rows_in, rows),
            "mixed": (mixed_in, mixed),
            "logs": (log_in, logs),
            "mlp": (mlp_in, mlp),
            "slope": (slope_in, slope),
            "active": (active_in, active),
            "start": (stream_in, start),
            "middle": (stream_in, middle),
        }[name]
        if name in ("start", "middle"):
            ready[name] = [copies.local(source.at[layer, int(name == "middle")], target).wait]
        elif name.endswith("_w"):
            ready[name] = [copies.local(source.at[layer], target).wait]
        else:
            ready[name] = [
                copies.local(source.at[layer, k], target.at[k * SPAN : (k + 1) * SPAN]).wait
                for k in range(CHUNKS)
            ]

    def need(name):
        for wait in ready.pop(name, ()):
            wait()

    first_waits = [
        copies.local(grad_in.at[k], down_in.at[part(k, core)]).wait for k in range(CHUNKS)
    ]
    top = LAYERS - 1
    for name in ("active", "down_w", "slope", "up_w", "mlp", "middle"):
        load(name, top)
    for name in ("output_w", "rows", "logs", "triple_w", "mixed", "attn", "start"):
        load(name, top)
    sums[...] = jnp.zeros_like(sums)
    lines[...] = jnp.zeros_like(lines)

    def share(target, k):
        return copies.trade(
            target.at[part(k, core)], target.at[part(k, core)], target.at[part(k, sibling)], place.to_row(1)
        )

    def columns(value):
        return jnp.sum(value.reshape(-1, 8, value.shape[1]), axis=0)

    def gain(layer, which):
        return wide_ref[2 * layer + which : 2 * layer + which + 1, :]

    sent_core = []
    sent_col, col_waits = [None] * CHUNKS, [None] * CHUNKS

    def core_free():
        while sent_core:
            sent_core.pop()()

    def start_core(stage, k):
        sent, got = copies.trade(
            give, got_core.at[stage, k], got_core.at[stage, k], place.to_row(1)
        )
        sent_core.append(sent)
        return got

    def settle(stage, k, got):
        got()
        if sent_col[k] is not None:
            sent_col[k]()

        def add(at):
            here = pl.ds(at, STRIP)
            chip_sum[k, here, :] = (mine[here, :] + got_core[stage, k, here, :].astype(f32)).astype(bf16)

        strips(OWN, add)
        sent_col[k], col_waits[k] = copies.trade(
            chip_sum.at[k], got_col.at[stage, k], got_col.at[stage, k], place.to_col()
        )

    def take_col(stage, k, layer, which, stream, target):
        col_waits[k]()
        scale = gain(layer, which)

        def back(at):
            here = pl.ds(at, STRIP)
            grad_out = chip_sum[k, here, :].astype(f32) + got_col[stage, k, here, :].astype(f32)
            normed, inv_std = norm_parts(stream[k, here, :])
            scaled = grad_out * scale
            total = grad[k, here, :] + inv_std * (
                scaled - mean_lanes(scaled) - normed * mean_lanes(scaled * normed)
            )
            low = total.astype(bf16)
            grad[k, here, :] = total
            target[pl.ds(pl.multiple_of(k * SPAN + core * OWN + at, STRIP), STRIP), :] = low
            sums[layer, which] += columns(grad_out * normed)
            sums[layer, 2 + which] += columns(grad_out)
            if which == 1:
                sums[layer, 4] += columns(low.astype(f32))
            elif layer:
                sums[layer - 1, 5] += columns(low.astype(f32))

        strips(OWN, back)

    shares = [None] * CHUNKS
    for k in reversed(range(CHUNKS)):
        first_waits[k]()
        shares[k] = share(down_in, k)
    for k in reversed(range(CHUNKS)):

        def widen(at, k=k):
            low = down_in[pl.ds(pl.multiple_of(k * SPAN + core * OWN + at, STRIP), STRIP), :]
            value = low.astype(f32)
            grad[k, pl.ds(at, STRIP), :] = value
            sums[top, 5] += columns(value)

        strips(OWN, widen)

    reductions = {
        (layer, kind): Reduction(
            kind,
            layer,
            place,
            copies,
            grads,
            land,
            ends,
            inner,
            (triple_out, output_out, up_out, down_out),
            credits,
        )
        for layer in range(LAYERS)
        for kind in range(4)
    }

    def weight_grad(layer, kind):
        if kind == 0:
            need("attn")
            for pair in range(2):
                for third in range(3):
                    value = dot_tn(
                        attn[:, pair * 512 : (pair + 1) * 512],
                        rows_grad[:, third * WIDTH : (third + 1) * WIDTH],
                    ).astype(bf16)
                    for b in range(2):
                        grads[0][2 * pair + b, third] = value[b * WIDTH : (b + 1) * WIDTH]
        elif kind == 1:
            need("mixed")
            value = dot_tn(mixed[...], branch[...]).astype(bf16)
            for b in range(4):
                grads[1][b, 0] = value[:, b * WIDTH : (b + 1) * WIDTH]
        elif kind == 2:
            need("mlp")
            for b in range(4):
                value = dot_tn(mlp[:, b * WIDTH : (b + 1) * WIDTH], hidden[...]).astype(bf16)
                for s in range(4):
                    grads[2][b, s] = value[s * (WIDTH // 4) : (s + 1) * (WIDTH // 4)]
        else:
            need("active")
            for pair in range(4):
                value = dot_tn(active[:, pair * WIDTH : (pair + 1) * WIDTH], down_in[...]).astype(bf16)
                for b in range(4):
                    grads[3][b, pair] = value[:, b * WIDTH : (b + 1) * WIDTH]
        reductions[layer, kind].send()

    def pump(point):
        for layer, kind, s, step in PLAN.get(point, ()):
            item = reductions[layer, kind]
            if step == 3:
                item.finish()
            else:
                (item.over_chips, item.to_middle, item.back)[step](s)

    landed = []

    def held(j, k):
        return span(place.rows[j] // 2 * LEN + k * SPAN + place.cores[j] * OWN, OWN)

    def send_input_grad(k):
        mine_rows = part(k, core)
        landed.append(
            copies.local(down_in.at[mine_rows, own_lanes], input_grad_ref.at[held(0, k), :]).wait
        )
        for j in (2, 3, 1):
            sent, got = copies.trade(
                down_in.at[mine_rows, span(place.rows[j] * WIDTH, WIDTH)],
                input_grad_ref.at[held(0, k), :],
                input_grad_ref.at[held(j, k), :],
                place.to_row(j),
            )
            landed.extend([sent, got])

    for layer in reversed(range(LAYERS)):
        upper = layer == top
        for k in reversed(range(CHUNKS)):
            if upper:
                if k == CHUNKS - 1:
                    for i in reversed(range(CHUNKS)):
                        shares[i][1]()
                    weight_grad(layer, 3)
            else:
                pump(f"e{k}")
                need("start")
                take_col(1, k, layer + 1, 0, start, down_in)
                shares[k] = share(down_in, k)
                if k == 0:
                    load("start", layer)
                pump(f"f{k}")
            need("down_w")
            need("slope")

            def shrink(c, k=k):
                for block in range(4):
                    cols = slice(block * WIDTH, (block + 1) * WIDTH)
                    value = dot_nt(down_in[part(k, c), :], down_w[cols, :])
                    value = (value * slope[part(k, c), cols].astype(f32)).astype(bf16)
                    hidden[part(k, c), cols] = value
                    lines[layer, 8:16, cols] += columns(value.astype(f32))

            shrink(core)
            if not upper:
                shares[k][1]()
            shrink(sibling)
            need("up_w")
            core_free()
            give[...] = dot_nt(hidden[part(k, sibling), :], up_w[...]).astype(bf16)
            got = start_core(0, k)
            mine[...] = dot_nt(hidden[part(k, core), :], up_w[...])
            shares[k][0]()
            pump(f"a{k}" if upper else f"g{k}")
            settle(0, k, got)
        if not upper:
            weight_grad(layer, 3)
            pump("v0")
        weight_grad(layer, 2)
        pump(f"u{layer}")
        if layer:
            for name in ("active", "down_w", "slope", "up_w", "mlp"):
                load(name, layer - 1)
        for k in reversed(range(CHUNKS)):
            point = f"{k}" if upper else f"{k}L"
            pump(f"b{point}")
            need("middle")
            take_col(0, k, layer, 1, middle, branch)
            shares[k] = share(branch, k)
            if layer and k == 0:
                load("middle", layer - 1)
            need("output_w")

            def narrow(c, k=k):
                mixed_grad[part(0, c), :] = dot_nt(branch[part(k, c), :], output_w[...]).astype(bf16)

            narrow(core)
            need("rows")
            need("logs")
            if k == CHUNKS - 1:
                pair_total[...] = jnp.zeros_like(pair_total)
            pump(f"c{point}")
            shares[k][1]()
            narrow(sibling)
            attend_back_chunk(k, rows, logs, seg_row_ref, mixed_grad, pair_total, rows_grad)
            need("triple_w")
            core_free()
            pump(f"m{point}")

            def project(c, k=k):
                value = dot_nt(rows_grad[part(k, c), :WIDTH], triple_w[0])
                for third in range(1, 3):
                    cols = slice(third * WIDTH, (third + 1) * WIDTH)
                    value += dot_nt(rows_grad[part(k, c), cols], triple_w[third])
                return value

            give[...] = project(sibling).astype(bf16)
            got = start_core(1, k)
            mine[...] = project(core)
            shares[k][0]()
            pump(f"d{point}")
            settle(1, k, got)
        weight_grad(layer, 1)
        weight_grad(layer, 0)
        for line, cols in ((0, slice(0, WIDTH)), (1, slice(2 * WIDTH, 3 * WIDTH))):
            value = rows_grad[:SPAN, cols].astype(f32)
            for k in range(1, CHUNKS):
                value += rows_grad[k * SPAN : (k + 1) * SPAN, cols].astype(f32)
            lines[layer, 0:1, line * WIDTH : (line + 1) * WIDTH] = jnp.sum(value, axis=0, keepdims=True)
        pump(f"w{layer}")
        if layer:
            for name in ("output_w", "rows", "logs", "triple_w", "mixed", "attn"):
                load(name, layer - 1)
    for k in reversed(range(CHUNKS)):
        pump(f"h{k}")
        need("start")
        take_col(1, k, 0, 0, start, down_in)
        send_input_grad(k)
    zero = jnp.zeros((1, WIDTH // 2), f32)
    for layer in range(LAYERS):
        found = [jnp.sum(sums[layer, i], axis=0, keepdims=True) for i in range(6)]
        hidden_sum = jnp.sum(lines[layer, 8:16, :], axis=0, keepdims=True)
        base = layer * LINES
        line_land[0, base : base + LINES, :] = jnp.zeros((LINES, D), f32)
        for i in range(6):
            line_land[0, base + i : base + i + 1, :] = found[i]
        for b in range(2):
            at = span((2 * core + b) * WIDTH, WIDTH)
            half = slice(b * (WIDTH // 2), (b + 1) * (WIDTH // 2))
            line_land[0, base + 6 : base + 7, at] = jnp.concatenate(
                [lines[layer, 0:1, :WIDTH][:, half], lines[layer, 0:1, WIDTH : 2 * WIDTH][:, half]], axis=1
            )
            for a in range(2):
                cols = slice((2 * b + a) * WIDTH, (2 * b + a + 1) * WIDTH)
                line_land[0, base + 7 + a : base + 8 + a, at] = hidden_sum[:, cols]
    line_waits = []
    for j in range(1, 4):
        there = span(place.rows[j] * WIDTH, WIDTH)
        sent, got = copies.trade(
            line_land.at[0, :, there],
            dp_land.at[3 + j],
            dp_land.at[3 + j],
            place.to_row(j),
        )
        copies.open.append(sent)
        line_waits.append(got)
    for wait in line_waits:
        wait()
    total = line_land[0, :, own_lanes]
    dp_land[place.dp] = total + dp_land[4] + dp_land[5] + dp_land[6]
    line_waits = []
    for i, device in enumerate(others):
        back = (place.dp + 3 - i) % 4
        sent, got = copies.sem(), copies.sem()
        out = pltpu.make_async_remote_copy(
            dp_land.at[place.dp], dp_land.at[place.dp], sent, got, device_id=device, device_id_type=MESH
        )
        arriving = pltpu.make_async_remote_copy(
            dp_land.at[back], dp_land.at[back], sent, got, device_id=device, device_id_type=MESH
        )
        out.start()
        copies.open.append(out.wait_send)
        line_waits.append(arriving.wait_recv)
    pump("tail")
    for wait in line_waits:
        wait()
    small_out[...] = dp_land[0] + dp_land[1] + dp_land[2] + dp_land[3]
    for kind in (3, 2, 1, 0):
        reductions[0, kind].finish()
    core_free()
    for k in range(CHUNKS):
        sent_col[k]()
    for wait in landed:
        wait()
    copies.finish()


def backward_call(tokens_shape, grad_in, wide, seg_row, weights, saved, stream):
    units = weights[2].shape[2]
    scratch = [
        ((3, D, WIDTH), bf16),
        ((WIDTH, D), bf16),
        ((D, units), bf16),
        ((units, D), bf16),
        ((LEN, D), bf16),
        ((LEN, 3 * WIDTH), bf16),
        ((LEN, WIDTH), bf16),
        ((LEN, 128), f32),
        ((LEN, D), bf16),
        ((LEN, units), bf16),
        ((LEN, units), bf16),
        ((CHUNKS, OWN, D), f32),
        ((CHUNKS, OWN, D), f32),
        ((LEN, D), bf16),
        ((LEN, units), bf16),
        ((LEN, D), bf16),
        ((LEN, 3 * WIDTH), bf16),
        ((SPAN, WIDTH), bf16),
        ((LEN, 2 * WIDTH), f32),
        ((CHUNKS, OWN, D), f32),
        ((OWN, D), f32),
        ((OWN, D), bf16),
        ((2, CHUNKS, OWN, D), bf16),
        ((CHUNKS, OWN, D), bf16),
        ((2, CHUNKS, OWN, D), bf16),
        ((LAYERS, 6, 8, D), f32),
        ((LAYERS, 16, D), f32),
        ((1, LAYERS * LINES, D), f32),
        ((7, LAYERS * LINES, WIDTH), f32),
    ]
    for parts in (4, 3, 2, 2):
        scratch += [((parts, *piece), bf16) for piece in PIECES]
    outs = [
        (tokens_shape, bf16),
        ((LAYERS * LINES, WIDTH), f32),
        ((LAYERS, 3, WIDTH, 2 * WIDTH), bf16),
        ((LAYERS, 2 * WIDTH, WIDTH), bf16),
        ((LAYERS, WIDTH, 2 * units), bf16),
        ((LAYERS, 2 * units, WIDTH), bf16),
    ]
    anywhere = pl.BlockSpec(memory_space=pl.ANY)
    inside = pl.BlockSpec(memory_space=pltpu.VMEM)
    return pl.pallas_call(
        backward_body,
        out_shape=[like(*v) for v in outs],
        in_specs=[anywhere] + [inside] * 2 + [anywhere] * 12,
        out_specs=[anywhere, inside] + [anywhere] * 4,
        scratch_shapes=[pltpu.VMEM(*v) for v in scratch]
        + [pltpu.SemaphoreType.REGULAR((12,)), pltpu.SemaphoreType.DMA((840,))],
        compiler_params=pltpu.CompilerParams(
            collective_id=1, has_side_effects=True, vmem_limit_bytes=60 * 1024 * 1024
        ),
    )(grad_in, wide, seg_row, *weights, *saved, stream)


def pair_plan(
    tokens,
    segments,
    norm_gain,
    norm_shift,
    triple_weight,
    triple_bias,
    output_weight,
    output_bias,
    up_weight,
    up_bias,
    down_weight,
    down_bias,
    cotangent,
):
    chip = lax.axis_index("row") // 2
    seg_pack = lax.dynamic_slice_in_dim(segments, chip * LEN, LEN, 0)
    seg_col, seg_row = seg_pack[:, None], seg_pack[None, :]
    result, grad_in, wide, *kept, stream = forward_call(
        tokens,
        cotangent,
        pack_small(norm_gain, norm_shift, output_bias, down_bias, triple_bias, up_bias),
        seg_col,
        seg_row,
        jnp.swapaxes(triple_weight, 1, 2),
        output_weight,
        up_weight,
        down_weight,
    )
    input_grad, small, triple_grad, output_grad, up_grad, down_grad = backward_call(
        tokens.shape, grad_in, wide, seg_row.astype(f32), kept[:4], kept[4:], stream
    )
    small = small.reshape(LAYERS, LINES, WIDTH)
    return (
        result,
        input_grad.astype(f32),
        small[:, 0:2],
        small[:, 2:4],
        jnp.swapaxes(triple_grad, 1, 2).astype(f32),
        small[:, 6].reshape(LAYERS, 2, WIDTH // 2),
        output_grad.astype(f32),
        small[:, 4],
        up_grad.astype(f32),
        small[:, 7:9].reshape(LAYERS, 2 * WIDTH),
        down_grad.astype(f32),
        small[:, 5],
    )


def solution(mesh):
    in_specs = (
        P("dp", "row"),
        P("dp"),
        P(None, None, "row"),
        P(None, None, "row"),
        P(None, "row", None, "col"),
        P(None, None, ("col", "row")),
        P(None, "col", "row"),
        P(None, "row"),
        P(None, "row", "col"),
        P(None, ("col", "row")),
        P(None, "col", "row"),
        P(None, "row"),
        P("dp", "row"),
    )
    out_specs = (
        P("dp", "row"),
        P("dp", "row"),
        P(None, None, "row"),
        P(None, None, "row"),
        P(None, "row", None, "col"),
        P(None, None, ("col", "row")),
        P(None, "col", "row"),
        P(None, "row"),
        P(None, "row", "col"),
        P(None, ("col", "row")),
        P(None, "col", "row"),
        P(None, "row"),
    )
    shape = mesh.shape

    def on_device(*arrays):
        if fits_pairs(shape, arrays):
            return pair_plan(*arrays)
        return general_plan(*arrays)

    return jax.shard_map(
        on_device, mesh=mesh, in_specs=in_specs, out_specs=out_specs, check_vma=False
    )
```

```python
import math

import jax
import jax.numpy as jnp
from jax import lax
from jax.experimental import pallas as pl
from jax.experimental.pallas import tpu as pltpu
from jax.sharding import PartitionSpec as P

D = 1024
HD = 64
LAYERS = 2
LEN = 1024


eps = 1e-05
masked = -1000000000.0


def norm_forward(stream, gain, shift):
    totals = lax.psum((jnp.sum(stream, axis=1), jnp.sum(stream * stream, axis=1)), "row")
    center = totals[0] / D
    second = totals[1] / D - center * center
    inv_std = lax.rsqrt(second + eps)
    normed = (stream - center[:, None]) * inv_std[:, None]
    return (normed, inv_std, normed * gain + shift)


def norm_backward(grad_out, normed, inv_std, gain):
    scaled = grad_out * gain
    totals = lax.psum((jnp.sum(scaled, axis=1), jnp.sum(scaled * normed, axis=1)), "row")
    grad_in = inv_std[:, None] * (
        scaled - totals[0][:, None] / D - normed * (totals[1][:, None] / D)
    )
    return (grad_in, jnp.sum(grad_out * normed, axis=0), jnp.sum(grad_out, axis=0))


def gather_rows(block):
    return lax.all_gather(block, "row", axis=1, tiled=True)


def col_total(partial_sums):
    return lax.psum(partial_sums, "col")


def rows_back(partial_sums):
    return lax.psum_scatter(
        partial_sums.astype(jnp.bfloat16), "row", scatter_dimension=1, tiled=True
    ).astype(jnp.float32)


def in_parts(partial_sums):
    return lax.psum_scatter(partial_sums, "row", scatter_dimension=2, tiled=True)


def grad_gather(block):
    return lax.all_gather(block, "row", axis=2, tiled=True)


def pack_scores(queries, key_rows, seg_pack, scale):
    position = jnp.arange(queries.shape[0])
    allowed = (seg_pack[:, None] == seg_pack[None, :]) & (position[None, :] <= position[:, None])
    scores = (
        jnp.einsum("qhd,khd->hqk", queries, key_rows, preferred_element_type=jnp.float32) * scale
    )
    return jnp.where(allowed[None], scores, masked)


def split_packs(triple, seg_rows):
    length, three, width = triple.shape
    count = length // LEN
    return (triple.reshape(count, LEN, three, width // HD, HD), seg_rows.reshape(count, LEN))


def attend_forward(triple, seg_rows, scale):
    length, three, width = triple.shape
    packs, seg_packs = split_packs(triple, seg_rows)

    def one_pack(pieces):
        pack_rows, seg_pack = pieces
        scores = pack_scores(pack_rows[:, 0], pack_rows[:, 1], seg_pack, scale)
        row_peak = jnp.max(scores, axis=-1, keepdims=True)
        exponent = jnp.exp(scores - row_peak)
        denominator = jnp.sum(exponent, axis=-1, keepdims=True)
        soft_weights = (exponent / denominator).astype(jnp.bfloat16)
        blended = jnp.einsum(
            "hqk,khd->qhd", soft_weights, pack_rows[:, 2], preferred_element_type=jnp.float32
        )
        return (blended.astype(jnp.bfloat16), (row_peak + jnp.log(denominator))[..., 0])

    blended, log_totals = lax.map(one_pack, (packs, seg_packs))
    return (blended.reshape(length, width), log_totals)


def attend_backward(triple, seg_rows, log_totals, grad_mixed, scale):
    length, three, width = triple.shape
    packs, seg_packs = split_packs(triple, seg_rows)
    grad_packs = grad_mixed.reshape(length // LEN, LEN, width // HD, HD)

    def one_pack(pieces):
        pack_rows, seg_pack, pack_totals, grad_pack = pieces
        queries = pack_rows[:, 0]
        key_rows = pack_rows[:, 1]
        value_rows = pack_rows[:, 2]
        scores = pack_scores(queries, key_rows, seg_pack, scale)
        chances = jnp.exp(scores - pack_totals[:, :, None])
        chance_grad = jnp.einsum(
            "qhd,khd->hqk", grad_pack, value_rows, preferred_element_type=jnp.float32
        )
        inner = jnp.sum(chances * chance_grad, axis=-1, keepdims=True)
        score_grad = (chances * (chance_grad - inner)).astype(jnp.bfloat16)
        query_grad = (
            jnp.einsum("hqk,khd->qhd", score_grad, key_rows, preferred_element_type=jnp.float32)
            * scale
        )
        key_grad = (
            jnp.einsum("hqk,qhd->khd", score_grad, queries, preferred_element_type=jnp.float32)
            * scale
        )
        value_grad = jnp.einsum(
            "hqk,qhd->khd",
            chances.astype(jnp.bfloat16),
            grad_pack,
            preferred_element_type=jnp.float32,
        )
        return jnp.stack([query_grad, key_grad, value_grad], axis=1).astype(jnp.bfloat16)

    triple_rows = lax.map(one_pack, (packs, seg_packs, log_totals, grad_packs))
    return triple_rows.reshape(length, three, width)


def layer_forward(stream, weights, small, seg_rows):
    triple_w, output_w, up_w, down_w = weights
    gains, shifts, triple_b, output_b, up_b, down_b = small
    scale = 1.0 / math.sqrt(HD)
    normed_one, inv_one, attn_in = norm_forward(stream, gains[0], shifts[0])
    attn_in = attn_in.astype(jnp.bfloat16)
    triple = in_parts(
        jnp.einsum("td,dke->tke", attn_in, triple_w, preferred_element_type=jnp.float32)
    )
    bias_rows = jnp.stack([triple_b[0], jnp.zeros_like(triple_b[0]), triple_b[1]])
    triple = (triple + bias_rows).astype(jnp.bfloat16)
    mixed, log_totals = attend_forward(triple, seg_rows, scale)
    mixed_full = gather_rows(mixed)
    middle = stream + (
        col_total(jnp.dot(mixed_full, output_w, preferred_element_type=jnp.float32)) + output_b
    )
    normed_two, inv_two, mlp_in = norm_forward(middle, gains[1], shifts[1])
    mlp_in = mlp_in.astype(jnp.bfloat16)
    hidden_pre = (
        in_parts(jnp.dot(mlp_in, up_w, preferred_element_type=jnp.float32)[:, None, :])[:, 0] + up_b
    )
    active = jax.nn.gelu(hidden_pre, approximate=True).astype(jnp.bfloat16)
    active_full = gather_rows(active)
    after = middle + (
        col_total(jnp.dot(active_full, down_w, preferred_element_type=jnp.float32)) + down_b
    )
    saved = (
        normed_one,
        inv_one,
        attn_in,
        triple,
        log_totals,
        mixed_full,
        normed_two,
        inv_two,
        mlp_in,
        hidden_pre,
        active_full,
        None,
    )
    return (after, saved)


def layer_backward(grad, saved, weights, gains, seg_rows):
    (
        normed_one,
        inv_one,
        attn_rows,
        triple,
        log_totals,
        mixed_full,
        normed_two,
        inv_two,
        mlp_rows,
        hidden_pre,
        active_full,
        columns_in,
    ) = saved
    triple_w, output_w, up_w, down_w = weights
    scale = 1.0 / math.sqrt(HD)
    down_in = grad.astype(jnp.bfloat16)
    down_bias_grad = jnp.sum(down_in, axis=0, dtype=jnp.float32)
    down_grad = jnp.einsum("tf,td->fd", active_full, down_in, preferred_element_type=jnp.float32)
    active_grad = rows_back(
        jnp.einsum("td,fd->tf", down_in, down_w, preferred_element_type=jnp.float32)
    )
    gelu_pull = jax.vjp(lambda value: jax.nn.gelu(value, approximate=True), hidden_pre)[1]
    hidden_grad = gelu_pull(active_grad)[0].astype(jnp.bfloat16)
    up_bias_grad = jnp.sum(hidden_grad, axis=0, dtype=jnp.float32)
    hidden_rows = grad_gather(hidden_grad[:, None, :])[:, 0]
    up_grad = jnp.einsum("td,tf->df", mlp_rows, hidden_rows, preferred_element_type=jnp.float32)
    mlp_grad = col_total(
        jnp.einsum("tf,df->td", hidden_rows, up_w, preferred_element_type=jnp.float32)
    )
    norm_two_grad, gain_two, shift_two = norm_backward(mlp_grad, normed_two, inv_two, gains[1])
    middle_grad = grad + norm_two_grad
    branch_grad = middle_grad.astype(jnp.bfloat16)
    output_bias_grad = jnp.sum(branch_grad, axis=0, dtype=jnp.float32)
    output_grad = jnp.einsum(
        "td,te->de", mixed_full, branch_grad, preferred_element_type=jnp.float32
    )
    mixed_grad = rows_back(
        jnp.einsum("te,de->td", branch_grad, output_w, preferred_element_type=jnp.float32)
    ).astype(jnp.bfloat16)
    triple_rows = attend_backward(triple, seg_rows, log_totals, mixed_grad, scale)
    triple_bias_grad = jnp.sum(triple_rows[:, 0::2], axis=0, dtype=jnp.float32)
    full_rows = grad_gather(triple_rows)
    triple_grad = jnp.einsum(
        "td,tke->dke", attn_rows, full_rows, preferred_element_type=jnp.float32
    )
    attn_grad = col_total(
        jnp.einsum("tke,dke->td", full_rows, triple_w, preferred_element_type=jnp.float32)
    )
    norm_one_grad, gain_one, shift_one = norm_backward(attn_grad, normed_one, inv_one, gains[0])
    start_grad = middle_grad + norm_one_grad
    terms = (
        jnp.stack([gain_one, gain_two]),
        jnp.stack([shift_one, shift_two]),
        triple_grad,
        triple_bias_grad,
        output_grad,
        output_bias_grad,
        up_grad,
        up_bias_grad,
        down_grad,
        down_bias_grad,
    )
    return (start_grad, terms)


def general_plan(
    tokens,
    segments,
    norm_gain,
    norm_shift,
    triple_weight,
    triple_bias,
    output_weight,
    output_bias,
    up_weight,
    up_bias,
    down_weight,
    down_bias,
    cotangent,
):

    def weights_of(layer_id):
        return (
            triple_weight[layer_id],
            output_weight[layer_id],
            up_weight[layer_id],
            down_weight[layer_id],
        )

    def small_of(layer_id):
        return (
            norm_gain[layer_id].astype(jnp.float32),
            norm_shift[layer_id].astype(jnp.float32),
            triple_bias[layer_id].astype(jnp.float32),
            output_bias[layer_id].astype(jnp.float32),
            up_bias[layer_id].astype(jnp.float32),
            down_bias[layer_id].astype(jnp.float32),
        )

    stream = tokens.astype(jnp.float32)
    stored = []
    for layer_id in range(LAYERS):
        stream, saved = layer_forward(stream, weights_of(layer_id), small_of(layer_id), segments)
        stored.append(saved)
    result = stream.astype(jnp.bfloat16)
    grad = cotangent.astype(jnp.float32)
    summed = [None] * LAYERS
    for layer_id in reversed(range(LAYERS)):
        grad, terms = layer_backward(
            grad, stored[layer_id], weights_of(layer_id), small_of(layer_id)[0], segments
        )
        summed[layer_id] = (
            lax.psum(terms[0].astype(jnp.bfloat16), "dp").astype(jnp.float32),
            lax.psum(terms[1].astype(jnp.bfloat16), "dp").astype(jnp.float32),
            lax.psum(terms[2].astype(jnp.bfloat16), "dp").astype(jnp.float32),
            lax.psum(terms[3].astype(jnp.bfloat16), "dp").astype(jnp.float32),
            lax.psum(terms[4].astype(jnp.bfloat16), "dp").astype(jnp.float32),
            lax.psum(terms[5].astype(jnp.bfloat16), "dp").astype(jnp.float32),
            lax.psum(terms[6].astype(jnp.bfloat16), "dp").astype(jnp.float32),
            lax.psum(terms[7].astype(jnp.bfloat16), "dp").astype(jnp.float32),
            lax.psum(terms[8].astype(jnp.bfloat16), "dp").astype(jnp.float32),
            lax.psum(terms[9].astype(jnp.bfloat16), "dp").astype(jnp.float32),
        )
    stacks = [
        jnp.stack([summed[layer_id][member] for layer_id in range(LAYERS)]) for member in range(10)
    ]
    return (
        result,
        grad,
        stacks[0],
        stacks[1],
        stacks[2],
        stacks[3],
        stacks[4],
        stacks[5],
        stacks[6],
        stacks[7],
        stacks[8],
        stacks[9],
    )


f32 = jnp.float32
bf16 = jnp.bfloat16
CHUNKS = 2
SPAN = LEN // CHUNKS
OWN = SPAN // 2
WIDTH = D // 4
QB = 256


def fits_pairs(shape, arrays):
    return (
        shape["row"] == 4
        and shape["col"] == 2
        and shape["dp"] == 4
        and arrays[0].shape == (2 * LEN, WIDTH)
        and arrays[8].shape[2] == 8 * WIDTH
    )


def dot(a, b):
    return lax.dot_general(a, b, (((1,), (0,)), ((), ())), preferred_element_type=f32)


def dot_nt(a, b):
    return lax.dot_general(a, b, (((1,), (1,)), ((), ())), preferred_element_type=f32)


def dot_tn(a, b):
    return lax.dot_general(a, b, (((0,), (0,)), ((), ())), preferred_element_type=f32)


def like(shape, kind):
    return jax.ShapeDtypeStruct(shape, kind)


def mean_lanes(v):
    return jnp.sum(v, axis=1, keepdims=True) * (1.0 / D)


def norm_parts(v):
    center = mean_lanes(v)
    second = mean_lanes(v * v) - center * center
    inv_std = lax.rsqrt(second + eps)
    return (v - center) * inv_std, inv_std


GELU = math.sqrt(2.0 / math.pi)


MESH = pl.DeviceIdType.MESH
HEADS_HERE = WIDTH // HD
SMALL = 24
SEG = 64


class Place:
    def __init__(self):
        self.row = lax.axis_index("row")
        self.col = lax.axis_index("col")
        self.dp = lax.axis_index("dp")
        self.core = self.row % 2
        self.chip = self.row // 2
        self.half = self.dp % 2
        sibling = self.row + 1 - 2 * self.core
        self.rows = [self.row, sibling, (self.row + 2) % 4, (sibling + 2) % 4]
        self.cores = [self.core, 1 - self.core, self.core, 1 - self.core]

    def to_row(self, j):
        return {"row": self.rows[j]}

    def to_col(self):
        return {"col": 1 - self.col}

    def to_dp(self):
        return {"dp": self.dp + 1 - 2 * self.half}


class Copies:
    def __init__(self, sems):
        self.sems = sems
        self.used = 0
        self.open = []

    def sem(self):
        self.used += 1
        return self.sems.at[self.used - 1]

    def local(self, src, dst):
        copy = pltpu.make_async_copy(src, dst, self.sem())
        copy.start()
        return copy

    def save(self, src, dst):
        self.open.append(self.local(src, dst).wait)

    def trade(self, src, dst, landing, device):
        sent, got = self.sem(), self.sem()
        out = pltpu.make_async_remote_copy(src, dst, sent, got, device_id=device, device_id_type=MESH)
        back = pltpu.make_async_remote_copy(
            landing, landing, sent, got, device_id=device, device_id_type=MESH
        )
        out.start()
        return out.wait_send, back.wait_recv

    def finish(self):
        for wait in self.open:
            wait()


def greet(place, devices):
    barrier = pltpu.get_barrier_semaphore()
    for device in devices:
        pl.semaphore_signal(barrier, inc=1, device_id=device, device_id_type=MESH)
    pl.semaphore_wait(barrier, len(devices))


def span(start, size):
    return pl.ds(pl.multiple_of(start, size), size)


def weight_cuts(kind, layer, wide, local):
    w = WIDTH
    if kind == 0:

        def source(core, half):
            rows = slice(None) if half is None else span(half * (w // 2), w // 2)
            return local.at[layer, :, rows, span(core * w, w)]

        def target(row, half):
            rows = span(row * w, w) if half is None else span(row * w + half * (w // 2), w // 2)
            return wide.at[layer, :, rows, :]

    elif kind == 2:
        units = wide.shape[2]

        def source(core, half):
            rows = slice(None) if half is None else span(half * (w // 2), w // 2)
            return local.at[layer, rows, span(core * units, units)]

        def target(row, half):
            rows = span(row * w, w) if half is None else span(row * w + half * (w // 2), w // 2)
            return wide.at[layer, rows, :]

    else:
        high = wide.shape[1]

        def source(core, half):
            if half is None:
                return local.at[layer, span(core * high, high), :]
            return local.at[layer, span(core * high + half * (high // 2), high // 2), :]

        def target(row, half):
            rows = slice(None) if half is None else span(half * (high // 2), high // 2)
            return wide.at[layer, rows, span(row * w, w)]

    return source, target


STRIP = 64


def strips(count, body):
    def step(i, carry):
        body(pl.multiple_of(i * STRIP, STRIP))
        return carry

    lax.fori_loop(0, count // STRIP, step, 0)


def causal(seg_col, seg_row, start, keys):
    query = lax.broadcasted_iota(jnp.int32, (QB, keys), 0) + start
    key = lax.broadcasted_iota(jnp.int32, (QB, keys), 1)
    return (seg_col == seg_row) & (key <= query)


def lanes_of(h):
    lane = lax.broadcasted_iota(jnp.int32, (1, WIDTH), 1)
    return (lane >= h * HD) & (lane < (h + 1) * HD)


def attend_chunk(k, triples, seg_col_ref, seg_row_ref, kv_ref, mixed_ref, log_ref):
    scale = 1.0 / math.sqrt(HD)
    kv_ref[k * SPAN : (k + 1) * SPAN, :] = triples[k][:, WIDTH:]
    for block in range(SPAN // QB):
        rows = slice(block * QB, (block + 1) * QB)
        start = k * SPAN + block * QB
        keys = start + QB
        allowed = causal(seg_col_ref[start : start + QB, :], seg_row_ref[:, :keys], start, keys)
        queries = triples[k][rows, :WIDTH] * scale
        key_rows = kv_ref[:keys, :WIDTH]
        value_rows = kv_ref[:keys, WIDTH:]
        blended = jnp.zeros((QB, WIDTH), f32)
        for h in range(HEADS_HERE):
            lanes = lanes_of(h)
            scores = dot_nt(jnp.where(lanes, queries, 0).astype(bf16), key_rows)
            scores = jnp.where(allowed, scores, masked)
            peak = jnp.max(scores, axis=1, keepdims=True)
            exponent = jnp.exp(scores - peak)
            total = jnp.sum(exponent, axis=1, keepdims=True)
            soft = (exponent * (1.0 / total)).astype(bf16)
            blended = jnp.where(lanes, dot(soft, value_rows), blended)
            log_ref[rows, h : h + 1] = peak + jnp.log(total)
        log_ref[rows, SEG : SEG + 1] = seg_col_ref[start : start + QB, :].astype(f32)
        mixed_ref[rows, :] = blended.astype(bf16)


def forward_body(*refs):
    (
        tokens_ref,
        cotangent_ref,
        small_ref,
        seg_col_ref,
        seg_row_ref,
        triple_in,
        output_in,
        up_in,
        down_in,
        grad_ref,
        wide_out,
        triple_out,
        output_out,
        up_out,
        down_out,
        attn_out,
        rows_out,
        mixed_out,
        log_out,
        mlp_out,
        slope_out,
        active_out,
        stream_out,
        triple_w,
        output_w,
        up_w,
        down_w,
        attn,
        rows,
        mixed,
        logs,
        mlp,
        slope,
        active,
        stream,
        taken,
        wide,
        kv,
        mine,
        give,
        got_core,
        chip_sum,
        got_col,
        sems,
    ) = refs
    place = Place()
    copies = Copies(sems)
    core, sibling = place.core, 1 - place.core
    greet(place, [place.to_row(1), place.to_row(2), place.to_row(3), place.to_col(), place.to_dp()])

    own_lanes = span(place.row * WIDTH, WIDTH)

    def held(j, k):
        return span(place.rows[j] // 2 * LEN + k * SPAN + place.cores[j] * OWN, OWN)

    def part(c):
        return span(c * OWN, OWN)

    small_waits = []
    copy = copies.local(small_ref, wide.at[:, own_lanes])
    small_waits.append(copy.wait)
    for j in range(1, 4):
        sent, got = copies.trade(
            small_ref,
            wide.at[:, own_lanes],
            wide.at[:, span(place.rows[j] * WIDTH, WIDTH)],
            place.to_row(j),
        )
        copies.open.append(sent)
        small_waits.append(got)
    token_waits = [[] for _ in range(CHUNKS)]

    def scatter_in(block_ref, target, k, waits):
        waits.append(copies.local(block_ref.at[held(0, k), :], target.at[k, :, own_lanes]).wait)
        for j in range(1, 4):
            sent, got = copies.trade(
                block_ref.at[held(j, k), :],
                target.at[k, :, own_lanes],
                target.at[k, :, span(place.rows[j] * WIDTH, WIDTH)],
                place.to_row(j),
            )
            copies.open.append(sent)
            waits.append(got)

    arrivals, ready_waits = {}, {}

    def send_weight(layer, kind):
        local = (triple_in, output_in, up_in, down_in)[kind]
        whole = (triple_w, output_w, up_w, down_w)[kind]
        source, target = weight_cuts(kind, layer, whole, local)
        here = []
        for j in (2, 3):
            sent, got = copies.trade(
                source(place.cores[j], place.half),
                target(place.row, place.half),
                target(place.rows[j], place.half),
                place.to_row(j),
            )
            copies.open.append(sent)
            here.append((got, target(place.rows[j], place.half), target(place.rows[j], 1 - place.half)))
        arrivals[layer, kind] = here
        sent, got = copies.trade(
            source(sibling, None),
            target(place.row, None),
            target(place.rows[1], None),
            place.to_row(1),
        )
        copies.open.append(sent)
        own = copies.local(source(core, None), target(place.row, None))
        ready_waits[layer, kind] = [got, own.wait]

    relays = [
        (layer, kind, i) for layer in range(LAYERS) for kind in range(4) for i in range(2)
    ]

    def pump(count):
        for _ in range(count):
            layer, kind, i = relays.pop(0)
            got, arrived, missing = arrivals[layer, kind][i]
            got()
            sent, back = copies.trade(arrived, arrived, missing, place.to_dp())
            copies.open.append(sent)
            ready_waits[layer, kind].append(back)

    def ready_weight(layer, kind):
        for wait in ready_waits[layer, kind]:
            wait()
        whole = (triple_w, output_w, up_w, down_w)[kind]
        out = (triple_out, output_out, up_out, down_out)[kind]
        copies.save(whole.at[layer], out.at[layer])

    scatter_in(tokens_ref, taken, 0, token_waits[0])
    send_weight(0, 0)
    scatter_in(tokens_ref, taken, 1, token_waits[1])
    for layer, kind in ((0, 1), (0, 2), (0, 3), (1, 0), (1, 1), (1, 2), (1, 3)):
        send_weight(layer, kind)
    grad_waits = []
    for k in range(CHUNKS):
        scatter_in(cotangent_ref, grad_ref, k, grad_waits)

    for wait in small_waits:
        wait()
    copies.save(wide, wide_out)

    def gain(layer, which):
        return wide[2 * layer + which : 2 * layer + which + 1, :]

    def shift(layer, which):
        return wide[4 + 2 * layer + which : 5 + 2 * layer + which, :]

    def output_bias(layer):
        return wide[8 + layer : 9 + layer, :]

    def down_bias(layer):
        return wide[10 + layer : 11 + layer, :]

    def of_core(line, start, size):
        return wide[line : line + 1, span(start, size)]

    def triple_bias(layer, which):
        at = 2 * core * WIDTH + which * (WIDTH // 2)
        size = WIDTH // 2
        return jnp.concatenate(
            [of_core(12 + layer, at, size), of_core(12 + layer, at + WIDTH, size)], axis=1
        )

    def up_bias(layer):
        line, at = 14 + 2 * layer, 2 * core * WIDTH
        return jnp.concatenate(
            [of_core(line + a, at + b * WIDTH, WIDTH) for b in range(2) for a in range(2)], axis=1
        )

    def norm_to(value, layer, which, target, at):
        center = jnp.mean(value, axis=1, keepdims=True)
        second = jnp.mean(value * value, axis=1, keepdims=True) - center * center
        normed = (value - center) * lax.rsqrt(second + eps)
        target[pl.ds(pl.multiple_of(core * OWN + at, STRIP), STRIP), :] = (
            normed * gain(layer, which) + shift(layer, which)
        ).astype(bf16)

    def share(target):
        return copies.trade(target.at[part(core)], target.at[part(core)], target.at[part(sibling)], place.to_row(1))

    sent_core, sent_col = [None] * CHUNKS, [None] * CHUNKS
    col_waits = [None] * CHUNKS
    saves = {}

    def settle(stage, k, got):
        got()
        if sent_col[k] is not None:
            sent_col[k]()

        def add(at):
            lines = pl.ds(at, STRIP)
            chip_sum[k, lines, :] = (
                mine[k, lines, :] + got_core[stage, k, lines, :].astype(f32)
            ).astype(bf16)

        strips(OWN, add)
        sent_col[k], col_waits[k] = copies.trade(
            chip_sum.at[k], got_col.at[stage, k], got_col.at[stage, k], place.to_col()
        )

    def start_core(stage, k):
        sent, got = copies.trade(
            give.at[k], got_core.at[stage, k], got_core.at[stage, k], place.to_row(1)
        )
        sent_core[k] = sent
        return got

    def take_col(stage, k, layer, bias, after_ref):
        col_waits[k]()

        def add(at):
            lines = pl.ds(at, STRIP)
            total = chip_sum[k, lines, :].astype(f32) + got_col[stage, k, lines, :].astype(f32)
            value = stream[stage, k, lines, :] + (total + bias)
            stream[1 - stage, k, lines, :] = value
            after_ref(value, at)

        strips(OWN, add)

    shares = [None] * CHUNKS
    for k in range(CHUNKS):
        for wait in token_waits[k]:
            wait()
        def first(at, k=k):
            value = taken[k, pl.ds(at, STRIP), :].astype(f32)
            stream[0, k, pl.ds(at, STRIP), :] = value
            norm_to(value, 0, 0, attn.at[0, k], at)

        strips(OWN, first)
        saves[0, 0, k] = copies.local(stream.at[0, k], stream_out.at[0, 0, k])
        shares[k] = share(attn.at[0, k])
        pump(2)

    for layer in range(LAYERS):
        for k in range(CHUNKS):
            if layer:
                if k == 0:
                    pump(1)
                saves.pop((layer - 1, 0, k)).wait()
                take_col(
                    1, k, layer, down_bias(layer - 1), lambda v, at, k=k: norm_to(v, layer, 0, attn.at[layer, k], at)
                )
                saves[layer, 0, k] = copies.local(stream.at[0, k], stream_out.at[layer, 0, k])
                shares[k] = share(attn.at[layer, k])
            if k == 0:
                ready_weight(layer, 0)
            bias = [triple_bias(layer, 0), None, triple_bias(layer, 1)]

            def project(c, k=k, bias=bias):
                for third in range(3):
                    value = dot(attn[layer, k, part(c), :], triple_w[layer, third])
                    if bias[third] is not None:
                        value = value + bias[third]
                    rows[layer, k, part(c), third * WIDTH : (third + 1) * WIDTH] = value.astype(bf16)

            project(core)
            sent, got = shares[k]
            got()
            project(sibling)
            attend_chunk(
                k,
                [rows.at[layer, i] for i in range(k + 1)],
                seg_col_ref,
                seg_row_ref,
                kv,
                mixed.at[layer, k],
                logs.at[layer, k],
            )
            pump(1)
            if k == 0:
                ready_weight(layer, 1)
            if sent_core[k] is not None:
                sent_core[k]()
            give[k] = dot(mixed[layer, k, part(sibling), :], output_w[layer]).astype(bf16)
            got = start_core(0, k)
            mine[k] = dot(mixed[layer, k, part(core), :], output_w[layer])
            sent()
            copies.save(attn.at[layer, k], attn_out.at[layer, k])
            copies.save(rows.at[layer, k], rows_out.at[layer, k])
            copies.save(mixed.at[layer, k], mixed_out.at[layer, k])
            copies.save(logs.at[layer, k], log_out.at[layer, k])
            settle(0, k, got)
            if k:
                pump(1)
        for k in range(CHUNKS):
            if layer:
                saves.pop((layer - 1, 1, k)).wait()
            elif k:
                pump(1)
            take_col(
                0, k, layer, output_bias(layer), lambda v, at, k=k: norm_to(v, layer, 1, mlp.at[layer, k], at)
            )
            saves[layer, 1, k] = copies.local(stream.at[1, k], stream_out.at[layer, 1, k])
            shares[k] = share(mlp.at[layer, k])
            if k == 0:
                ready_weight(layer, 2)
            bias = up_bias(layer)

            def widen(c, k=k, bias=bias):
                for block in range(4):
                    cols = slice(block * WIDTH, (block + 1) * WIDTH)
                    pre = dot(mlp[layer, k, part(c), :], up_w[layer, :, cols]) + bias[:, cols]
                    square = pre * pre
                    curve = jnp.tanh(GELU * (pre + 0.044715 * (square * pre)))
                    upper = 0.5 * (1.0 + curve)
                    active[layer, k, part(c), cols] = (pre * upper).astype(bf16)
                    slope[layer, k, part(c), cols] = (
                        upper
                        + (0.5 * GELU) * pre * (1.0 - curve * curve) * (1.0 + (3.0 * 0.044715) * square)
                    ).astype(bf16)

            widen(core)
            sent, got = shares[k]
            got()
            widen(sibling)
            if layer + 1 < LAYERS:
                if k == 0:
                    pump(1)
                    ready_weight(layer, 3)
                sent_core[k]()
                give[k] = dot(active[layer, k, part(sibling), :], down_w[layer]).astype(bf16)
                got = start_core(1, k)
                mine[k] = dot(active[layer, k, part(core), :], down_w[layer])
            sent()
            copies.save(mlp.at[layer, k], mlp_out.at[layer, k])
            copies.save(slope.at[layer, k], slope_out.at[layer, k])
            copies.save(active.at[layer, k], active_out.at[layer, k])
            if layer + 1 < LAYERS:
                settle(1, k, got)
                pump(k + 1)
    ready_weight(LAYERS - 1, 3)
    for k in range(CHUNKS):
        saves.pop((LAYERS - 1, 0, k)).wait()
        saves.pop((LAYERS - 1, 1, k)).wait()
        sent_core[k]()
        sent_col[k]()
    for wait in grad_waits:
        wait()
    copies.finish()


def forward_call(tokens, cotangent, small, seg_col, seg_row, triple_w, output_w, up_w, down_w):
    units = up_w.shape[2] // 2
    per_layer = [
        ((LAYERS, CHUNKS, SPAN, D), bf16),
        ((LAYERS, CHUNKS, SPAN, 3 * WIDTH), bf16),
        ((LAYERS, CHUNKS, SPAN, WIDTH), bf16),
        ((LAYERS, CHUNKS, SPAN, 128), f32),
        ((LAYERS, CHUNKS, SPAN, D), bf16),
        ((LAYERS, CHUNKS, SPAN, units), bf16),
        ((LAYERS, CHUNKS, SPAN, units), bf16),
    ]
    wide = [
        ((LAYERS, 3, D, WIDTH), bf16),
        ((LAYERS, WIDTH, D), bf16),
        ((LAYERS, D, units), bf16),
        ((LAYERS, units, D), bf16),
    ]
    outs = [
        ((CHUNKS, OWN, D), bf16),
        ((SMALL, D), f32),
        *wide,
        *per_layer,
        ((LAYERS, 2, CHUNKS, OWN, D), f32),
    ]
    scratch = [
        *wide,
        *per_layer,
        ((2, CHUNKS, OWN, D), f32),
        ((CHUNKS, OWN, D), bf16),
        ((SMALL, D), f32),
        ((LEN, 2 * WIDTH), bf16),
        ((CHUNKS, OWN, D), f32),
        ((CHUNKS, OWN, D), bf16),
        ((2, CHUNKS, OWN, D), bf16),
        ((CHUNKS, OWN, D), bf16),
        ((2, CHUNKS, OWN, D), bf16),
    ]
    anywhere = pl.BlockSpec(memory_space=pl.ANY)
    inside = pl.BlockSpec(memory_space=pltpu.VMEM)
    return pl.pallas_call(
        forward_body,
        out_shape=[like(*v) for v in outs],
        in_specs=[anywhere] * 2 + [inside] * 3 + [anywhere] * 4,
        out_specs=[anywhere] * len(outs),
        scratch_shapes=[pltpu.VMEM(*v) for v in scratch] + [pltpu.SemaphoreType.DMA((320,))],
        compiler_params=pltpu.CompilerParams(
            collective_id=0, has_side_effects=True, vmem_limit_bytes=60 * 1024 * 1024
        ),
    )(tokens, cotangent, small, seg_col, seg_row, triple_w, output_w, up_w, down_w)


def pack_small(norm_gain, norm_shift, output_bias, down_bias, triple_bias, up_bias):
    lines = [
        norm_gain.reshape(-1, WIDTH),
        norm_shift.reshape(-1, WIDTH),
        output_bias,
        down_bias,
        triple_bias.reshape(-1, WIDTH),
        up_bias.reshape(-1, WIDTH),
    ]
    lines = jnp.concatenate(lines).astype(f32)
    return jnp.pad(lines, ((0, SMALL - lines.shape[0]), (0, 0)))


PIECES = ((3, WIDTH, WIDTH), (1, WIDTH, WIDTH), (4, WIDTH // 4, D), (4, D // 4, WIDTH))

PLAN = {
    "a1": ((1, 3, 0, 0),),
    "a0": ((1, 3, 1, 0), (1, 3, 0, 1)),
    "u1": ((1, 3, 2, 0),),
    "c1": ((1, 3, 1, 1), (1, 3, 0, 2), (1, 3, 3, 0)),
    "m1": ((1, 3, 2, 1), (1, 2, 0, 0), (1, 3, 1, 2), (1, 3, 3, 1), (1, 2, 1, 0)),
    "c0": ((1, 2, 2, 0), (1, 3, 2, 2), (1, 2, 0, 1)),
    "m0": ((1, 2, 3, 0), (1, 3, 3, 2), (1, 2, 1, 1)),
    "w1": ((1, 2, 0, 2), (1, 2, 2, 1)),
    "f1": ((1, 3, 0, 3),),
    "g1": ((1, 1, 0, 0), (1, 2, 1, 2), (1, 2, 3, 1)),
    "e0": ((1, 0, 0, 0), (1, 2, 2, 2)),
    "g0": ((1, 1, 0, 1), (1, 0, 1, 0), (1, 2, 3, 2)),
    "v0": ((1, 0, 0, 1), (1, 0, 2, 0)),
    "u0": ((1, 1, 0, 2), (1, 2, 0, 3), (1, 0, 1, 1)),
    "c1L": ((0, 3, 0, 0), (1, 0, 0, 2)),
    "m1L": ((1, 1, 0, 3), (1, 0, 2, 1), (0, 3, 1, 0), (1, 0, 1, 2), (0, 3, 0, 1), (0, 3, 2, 0)),
    "m0L": ((1, 0, 2, 2), (0, 3, 1, 1), (0, 3, 3, 0), (0, 3, 0, 2), (0, 3, 2, 1), (0, 2, 0, 0)),
    "w0": ((0, 2, 1, 0), (1, 0, 0, 3)),
    "h1": ((0, 3, 1, 2), (0, 3, 3, 1)),
    "h0": ((0, 2, 2, 0), (0, 3, 2, 2), (0, 2, 0, 1), (0, 2, 3, 0), (0, 3, 3, 2), (0, 2, 1, 1)),
    "tail1": ((0, 1, 0, 0), (0, 2, 2, 1), (0, 2, 0, 2), (0, 0, 0, 0), (0, 2, 3, 1), (0, 2, 1, 2), (0, 0, 1, 0)),
    "tail2": ((0, 1, 0, 1), (0, 2, 2, 2), (0, 0, 2, 0), (0, 0, 0, 1), (0, 2, 3, 2), (0, 0, 1, 1)),
    "tail3": ((0, 1, 0, 2), (0, 0, 2, 1), (0, 0, 0, 2), (0, 0, 1, 2), (0, 0, 2, 2)),
}
LINES = 16


def attend_back_chunk(
    k, rows_ref, log_ref, seg_row_ref, grad_ref, total_ref, out_ref
):
    scale = 1.0 / math.sqrt(HD)
    for block in range(SPAN // QB):
        start = k * SPAN + block * QB
        keys = start + QB
        here = slice(start, keys)
        allowed = causal(log_ref[here, SEG : SEG + 1], seg_row_ref[:, :keys], start, keys)
        queries = rows_ref[here, :WIDTH] * scale
        grads = grad_ref[block * QB : (block + 1) * QB, :]
        key_rows = rows_ref[:keys, WIDTH : 2 * WIDTH]
        value_rows = rows_ref[:keys, 2 * WIDTH :]
        query_grad = jnp.zeros((QB, WIDTH), f32)
        for h in range(HEADS_HERE):
            lanes = lanes_of(h)
            query = jnp.where(lanes, queries, 0).astype(bf16)
            grad = jnp.where(lanes, grads, 0).astype(bf16)
            scores = jnp.where(allowed, dot_nt(query, key_rows), masked)
            chances = jnp.exp(scores - log_ref[here, h : h + 1])
            product = chances * dot_nt(grad, value_rows)
            inner = jnp.sum(product, axis=1, keepdims=True)
            score_grad = (product - chances * inner).astype(bf16)
            query_grad = jnp.where(lanes, dot(score_grad, key_rows), query_grad)
            total_ref[:keys, :WIDTH] += dot_tn(score_grad, query)
            total_ref[:keys, WIDTH:] += dot_tn(chances.astype(bf16), grad)
        out_ref[here, :WIDTH] = (query_grad * scale).astype(bf16)
    here = slice(k * SPAN, (k + 1) * SPAN)
    out_ref[here, WIDTH:] = total_ref[here, :].astype(bf16)


def add_pieces(target, left, right):
    high, across = target.shape
    step = 32768 // across

    def body(i, carry):
        lines = pl.ds(pl.multiple_of(i * step, step), step)
        target[lines, :] = (left[lines, :].astype(f32) + right[lines, :].astype(f32)).astype(bf16)
        return carry

    lax.fori_loop(0, high // step, body, 0)


class Reduction:
    def __init__(self, kind, layer, place, copies, grads, land, ends, inner, outs, credits):
        self.kind, self.layer, self.place, self.copies = kind, layer, place, copies
        self.grads, self.land, self.ends, self.inner = grads[kind], land[kind], ends[kind], inner[kind]
        self.out, self.credits = outs[kind], credits
        self.count = PIECES[kind][0]
        self.again = layer < LAYERS - 1
        self.is_end = place.dp * (3 - place.dp) == 0
        self.is_inner = place.dp * (3 - place.dp) > 0

    def home(self, which, s):
        core = self.place.cores[which]
        out, layer = self.out, self.layer
        if self.kind == 0:
            return out.at[layer, s, :, span(core * WIDTH, WIDTH)]
        if self.kind == 1:
            return out.at[layer, span(core * WIDTH, WIDTH), :]
        if self.kind == 2:
            return out.at[layer, s * (WIDTH // 4) : (s + 1) * (WIDTH // 4), span(core * D, D)]
        return out.at[layer, span(core * D + s * (D // 4), D // 4), :]

    def send(self):
        place, copies = self.place, self.copies
        if self.again:
            pl.semaphore_wait(self.credits.at[self.kind], 3)
        self.waits = {}
        self.sent = []
        for s in range(self.count):
            for j in (2, 3, 1):
                sent, got = copies.trade(
                    self.grads.at[place.rows[j], s],
                    self.land.at[j - 1, s],
                    self.land.at[j - 1, s],
                    place.to_row(j),
                )
                self.sent.append(sent)
                self.waits[j, s] = got

    def over_chips(self, s):
        place, copies = self.place, self.copies
        if s == 0:
            self.to_inner = {}
            if self.again:

                @pl.when(self.is_end)
                def _():
                    pl.semaphore_wait(self.credits.at[4 + self.kind], 1)

        for which in range(2):
            if which == 0:
                self.waits[2, s]()
                target = self.land.at[1, s]
                add_pieces(target, self.grads.at[place.row, s], target)
            else:
                self.waits[1, s]()
                self.waits[3, s]()
                target = self.land.at[2, s]
                add_pieces(target, self.land.at[0, s], target)
            copy = pltpu.make_async_remote_copy(
                target,
                self.ends.at[which, s],
                copies.sem(),
                copies.sem(),
                device_id=place.to_dp(),
                device_id_type=MESH,
            )
            self.to_inner[which, s] = copy

            @pl.when(self.is_end)
            def _():
                copy.start()

    def to_middle(self, s):
        place, copies = self.place, self.copies
        if s == 0:
            self.across = {}
            if self.again:

                @pl.when(self.is_inner)
                def _():
                    pl.semaphore_wait(self.credits.at[8 + self.kind], 1)

        for which in range(2):
            half = self.ends.at[which, s]
            copy = pltpu.make_async_remote_copy(
                half,
                self.inner.at[which, s],
                copies.sem(),
                copies.sem(),
                device_id={"dp": 3 - place.dp},
                device_id_type=MESH,
            )
            self.across[which, s] = copy

            @pl.when(self.is_inner)
            def _():
                self.to_inner[which, s].wait_recv()
                add_pieces(half, self.land.at[1 + which, s], half)
                copy.start()

        if s == self.count - 1:

            @pl.when(self.is_end)
            def _():
                for copy in self.to_inner.values():
                    copy.wait_send()

            for sent in self.sent:
                sent()
            if not self.again:
                for j in range(1, 4):
                    pl.semaphore_signal(
                        self.credits.at[self.kind],
                        inc=1,
                        device_id=place.to_row(j),
                        device_id_type=MESH,
                    )

    def back(self, s):
        place, copies = self.place, self.copies
        if s == 0:
            self.out_copies = []
        for which in range(2):
            total = self.inner.at[which, s]
            home = self.home(which, s)
            copy = pltpu.make_async_remote_copy(
                total,
                home,
                copies.sem(),
                copies.sem(),
                device_id=place.to_dp(),
                device_id_type=MESH,
            )
            here = pltpu.make_async_copy(total, home, copies.sem())
            self.out_copies.append((copy, here))

            @pl.when(self.is_inner)
            def _():
                self.across[which, s].wait_recv()
                add_pieces(total, self.ends.at[which, s], total)
                copy.start()
                here.start()

    def finish(self):
        place = self.place

        @pl.when(self.is_inner)
        def _():
            for copy in self.across.values():
                copy.wait_send()
            for copy, here in self.out_copies:
                copy.wait_send()
                here.wait()
            if not self.again:
                pl.semaphore_signal(
                    self.credits.at[4 + self.kind], inc=1, device_id=place.to_dp(), device_id_type=MESH
                )
                pl.semaphore_signal(
                    self.credits.at[8 + self.kind],
                    inc=1,
                    device_id={"dp": 3 - place.dp},
                    device_id_type=MESH,
                )

        @pl.when(self.is_end)
        def _():
            for copy, here in self.out_copies:
                copy.wait_recv()


def backward_body(*refs):
    (
        grad_in,
        wide_ref,
        seg_row_ref,
        triple_in,
        output_in,
        up_in,
        down_in_w,
        attn_in,
        rows_in,
        mixed_in,
        log_in,
        mlp_in,
        slope_in,
        active_in,
        stream_in,
        result_ref,
        input_grad_ref,
        small_out,
        triple_out,
        output_out,
        up_out,
        down_out,
        triple_w,
        output_w,
        up_w,
        down_w,
        attn,
        rows,
        mixed,
        logs,
        mlp,
        slope,
        active,
        start,
        middle,
        down_in,
        hidden,
        branch,
        rows_grad,
        mixed_grad,
        pair_total,
        grad,
        mine,
        give,
        got_core,
        chip_sum,
        got_col,
        sums,
        lines,
        line_land,
        dp_land,
        *rest,
    ) = refs
    grads, land, ends, inner = rest[0:4], rest[4:8], rest[8:12], rest[12:16]
    credits, sems = rest[16:]
    place = Place()
    copies = Copies(sems)
    core, sibling = place.core, 1 - place.core
    others = [{"dp": (place.dp + i) % 4} for i in range(1, 4)]
    greet(place, [place.to_row(1), place.to_row(2), place.to_row(3), place.to_col(), *others])
    own_lanes = span(place.row * WIDTH, WIDTH)

    def part(k, c):
        return span(k * SPAN + c * OWN, OWN)

    ready = {}

    def load(name, layer):
        source, target = {
            "triple_w": (triple_in, triple_w),
            "output_w": (output_in, output_w),
            "up_w": (up_in, up_w),
            "down_w": (down_in_w, down_w),
            "attn": (attn_in, attn),
            "rows": (rows_in, rows),
            "mixed": (mixed_in, mixed),
            "logs": (log_in, logs),
            "mlp": (mlp_in, mlp),
            "slope": (slope_in, slope),
            "active": (active_in, active),
            "start": (stream_in, start),
            "middle": (stream_in, middle),
        }[name]
        if name in ("start", "middle"):
            ready[name] = [copies.local(source.at[layer, int(name == "middle")], target).wait]
        elif name.endswith("_w"):
            ready[name] = [copies.local(source.at[layer], target).wait]
        else:
            ready[name] = [
                copies.local(source.at[layer, k], target.at[k * SPAN : (k + 1) * SPAN]).wait
                for k in range(CHUNKS)
            ]

    def need(name):
        for wait in ready.pop(name, ()):
            wait()

    first_waits = [
        copies.local(grad_in.at[k], down_in.at[part(k, core)]).wait for k in range(CHUNKS)
    ]
    top = LAYERS - 1
    for name in ("active", "down_w", "slope", "up_w", "mlp", "middle"):
        load(name, top)
    for name in ("output_w", "rows", "logs", "triple_w", "mixed", "attn", "start"):
        load(name, top)
    sums[...] = jnp.zeros_like(sums)
    lines[...] = jnp.zeros_like(lines)

    def share(target, k):
        return copies.trade(
            target.at[part(k, core)], target.at[part(k, core)], target.at[part(k, sibling)], place.to_row(1)
        )

    def columns(value):
        return jnp.sum(value.reshape(-1, 8, value.shape[1]), axis=0)

    def gain(layer, which):
        return wide_ref[2 * layer + which : 2 * layer + which + 1, :]

    sent_core = []
    sent_col, col_waits = [None] * CHUNKS, [None] * CHUNKS

    def core_free():
        while sent_core:
            sent_core.pop()()

    def start_core(stage, k):
        sent, got = copies.trade(
            give, got_core.at[stage, k], got_core.at[stage, k], place.to_row(1)
        )
        sent_core.append(sent)
        return got

    def settle(stage, k, got):
        got()
        if sent_col[k] is not None:
            sent_col[k]()

        def add(at):
            here = pl.ds(at, STRIP)
            chip_sum[k, here, :] = (mine[here, :] + got_core[stage, k, here, :].astype(f32)).astype(bf16)

        strips(OWN, add)
        sent_col[k], col_waits[k] = copies.trade(
            chip_sum.at[k], got_col.at[stage, k], got_col.at[stage, k], place.to_col()
        )

    def take_col(stage, k, layer, which, stream, target):
        col_waits[k]()
        scale = gain(layer, which)

        def back(at):
            here = pl.ds(at, STRIP)
            grad_out = chip_sum[k, here, :].astype(f32) + got_col[stage, k, here, :].astype(f32)
            normed, inv_std = norm_parts(stream[k, here, :])
            scaled = grad_out * scale
            total = grad[k, here, :] + inv_std * (
                scaled - mean_lanes(scaled) - normed * mean_lanes(scaled * normed)
            )
            low = total.astype(bf16)
            grad[k, here, :] = total
            target[pl.ds(pl.multiple_of(k * SPAN + core * OWN + at, STRIP), STRIP), :] = low
            sums[layer, which] += columns(grad_out * normed)
            sums[layer, 2 + which] += columns(grad_out)
            if which == 1:
                sums[layer, 4] += columns(low.astype(f32))
            elif layer:
                sums[layer - 1, 5] += columns(low.astype(f32))

        strips(OWN, back)

    shares = [None] * CHUNKS
    for k in reversed(range(CHUNKS)):
        first_waits[k]()
        shares[k] = share(down_in, k)
    for k in reversed(range(CHUNKS)):

        def widen(at, k=k):
            low = down_in[pl.ds(pl.multiple_of(k * SPAN + core * OWN + at, STRIP), STRIP), :]
            value = low.astype(f32)
            grad[k, pl.ds(at, STRIP), :] = value
            sums[top, 5] += columns(value)

        strips(OWN, widen)

    reductions = {
        (layer, kind): Reduction(
            kind,
            layer,
            place,
            copies,
            grads,
            land,
            ends,
            inner,
            (triple_out, output_out, up_out, down_out),
            credits,
        )
        for layer in range(LAYERS)
        for kind in range(4)
    }

    def weight_grad(layer, kind):
        if kind == 0:
            need("attn")
            for pair in range(2):
                for third in range(3):
                    value = dot_tn(
                        attn[:, pair * 512 : (pair + 1) * 512],
                        rows_grad[:, third * WIDTH : (third + 1) * WIDTH],
                    ).astype(bf16)
                    for b in range(2):
                        grads[0][2 * pair + b, third] = value[b * WIDTH : (b + 1) * WIDTH]
        elif kind == 1:
            need("mixed")
            value = dot_tn(mixed[...], branch[...]).astype(bf16)
            for b in range(4):
                grads[1][b, 0] = value[:, b * WIDTH : (b + 1) * WIDTH]
        elif kind == 2:
            need("mlp")
            for b in range(4):
                value = dot_tn(mlp[:, b * WIDTH : (b + 1) * WIDTH], hidden[...]).astype(bf16)
                for s in range(4):
                    grads[2][b, s] = value[s * (WIDTH // 4) : (s + 1) * (WIDTH // 4)]
        else:
            need("active")
            for pair in range(4):
                value = dot_tn(active[:, pair * WIDTH : (pair + 1) * WIDTH], down_in[...]).astype(bf16)
                for b in range(4):
                    grads[3][b, pair] = value[:, b * WIDTH : (b + 1) * WIDTH]
        reductions[layer, kind].send()

    def pump(point):
        for layer, kind, s, step in PLAN.get(point, ()):
            item = reductions[layer, kind]
            if step == 3:
                item.finish()
            else:
                (item.over_chips, item.to_middle, item.back)[step](s)

    landed = []

    def held(j, k):
        return span(place.rows[j] // 2 * LEN + k * SPAN + place.cores[j] * OWN, OWN)

    def to_features(k, source, target):
        mine_rows = part(k, core)
        landed.append(copies.local(source.at[mine_rows, own_lanes], target.at[held(0, k), :]).wait)
        for j in (2, 3, 1):
            sent, got = copies.trade(
                source.at[mine_rows, span(place.rows[j] * WIDTH, WIDTH)],
                target.at[held(0, k), :],
                target.at[held(j, k), :],
                place.to_row(j),
            )
            landed.extend([sent, got])

    for layer in reversed(range(LAYERS)):
        upper = layer == top
        for k in reversed(range(CHUNKS)):
            if upper:
                if k == CHUNKS - 1:
                    for i in reversed(range(CHUNKS)):
                        shares[i][1]()
                    weight_grad(layer, 3)
            else:
                pump(f"e{k}")
                need("start")
                take_col(1, k, layer + 1, 0, start, down_in)
                shares[k] = share(down_in, k)
                if k == 0:
                    load("start", layer)
                pump(f"f{k}")
            need("down_w")
            need("slope")

            def shrink(c, k=k):
                for block in range(4):
                    cols = slice(block * WIDTH, (block + 1) * WIDTH)
                    value = dot_nt(down_in[part(k, c), :], down_w[cols, :])
                    value = (value * slope[part(k, c), cols].astype(f32)).astype(bf16)
                    hidden[part(k, c), cols] = value
                    lines[layer, 8:16, cols] += columns(value.astype(f32))

            shrink(core)
            if not upper:
                shares[k][1]()
            shrink(sibling)
            need("up_w")
            core_free()
            give[...] = dot_nt(hidden[part(k, sibling), :], up_w[...]).astype(bf16)
            got = start_core(0, k)
            mine[...] = dot_nt(hidden[part(k, core), :], up_w[...])
            shares[k][0]()
            pump(f"a{k}" if upper else f"g{k}")
            settle(0, k, got)
        if not upper:
            weight_grad(layer, 3)
            pump("v0")
        weight_grad(layer, 2)
        pump(f"u{layer}")
        if layer:
            for name in ("active", "down_w", "slope", "up_w", "mlp"):
                load(name, layer - 1)
        else:
            load("active", top)
            load("down_w", top)
        for k in reversed(range(CHUNKS)):
            point = f"{k}" if upper else f"{k}L"
            pump(f"b{point}")
            need("middle")
            take_col(0, k, layer, 1, middle, branch)
            shares[k] = share(branch, k)
            if k == 0:
                load("middle", layer - 1 if layer else top)
            need("output_w")

            def narrow(c, k=k):
                mixed_grad[part(0, c), :] = dot_nt(branch[part(k, c), :], output_w[...]).astype(bf16)

            narrow(core)
            need("rows")
            need("logs")
            if k == CHUNKS - 1:
                pair_total[...] = jnp.zeros_like(pair_total)
            pump(f"c{point}")
            shares[k][1]()
            narrow(sibling)
            attend_back_chunk(k, rows, logs, seg_row_ref, mixed_grad, pair_total, rows_grad)
            need("triple_w")
            core_free()
            pump(f"m{point}")

            def project(c, k=k):
                value = dot_nt(rows_grad[part(k, c), :WIDTH], triple_w[0])
                for third in range(1, 3):
                    cols = slice(third * WIDTH, (third + 1) * WIDTH)
                    value += dot_nt(rows_grad[part(k, c), cols], triple_w[third])
                return value

            give[...] = project(sibling).astype(bf16)
            got = start_core(1, k)
            mine[...] = project(core)
            shares[k][0]()
            pump(f"d{point}")
            settle(1, k, got)
        weight_grad(layer, 1)
        weight_grad(layer, 0)
        for line, cols in ((0, slice(0, WIDTH)), (1, slice(2 * WIDTH, 3 * WIDTH))):
            value = rows_grad[:SPAN, cols].astype(f32)
            for k in range(1, CHUNKS):
                value += rows_grad[k * SPAN : (k + 1) * SPAN, cols].astype(f32)
            lines[layer, 0:1, line * WIDTH : (line + 1) * WIDTH] = jnp.sum(value, axis=0, keepdims=True)
        pump(f"w{layer}")
        if layer:
            for name in ("output_w", "rows", "logs", "triple_w", "mixed", "attn"):
                load(name, layer - 1)
    for k in reversed(range(CHUNKS)):
        pump(f"h{k}")
        need("start")
        take_col(1, k, 0, 0, start, down_in)
        to_features(k, down_in, input_grad_ref)
    need("active")
    need("down_w")
    for k in reversed(range(CHUNKS)):
        core_free()
        give[...] = dot(active[part(k, sibling), :], down_w[...]).astype(bf16)
        got = start_core(0, k)
        mine[...] = dot(active[part(k, core), :], down_w[...])
        settle(0, k, got)
    zero = jnp.zeros((1, WIDTH // 2), f32)
    for layer in range(LAYERS):
        found = [jnp.sum(sums[layer, i], axis=0, keepdims=True) for i in range(6)]
        hidden_sum = jnp.sum(lines[layer, 8:16, :], axis=0, keepdims=True)
        base = layer * LINES
        line_land[0, base : base + LINES, :] = jnp.zeros((LINES, D), f32)
        for i in range(6):
            line_land[0, base + i : base + i + 1, :] = found[i]
        for b in range(2):
            at = span((2 * core + b) * WIDTH, WIDTH)
            half = slice(b * (WIDTH // 2), (b + 1) * (WIDTH // 2))
            line_land[0, base + 6 : base + 7, at] = jnp.concatenate(
                [lines[layer, 0:1, :WIDTH][:, half], lines[layer, 0:1, WIDTH : 2 * WIDTH][:, half]], axis=1
            )
            for a in range(2):
                cols = slice((2 * b + a) * WIDTH, (2 * b + a + 1) * WIDTH)
                line_land[0, base + 7 + a : base + 8 + a, at] = hidden_sum[:, cols]
    line_waits = []
    for j in range(1, 4):
        there = span(place.rows[j] * WIDTH, WIDTH)
        sent, got = copies.trade(
            line_land.at[0, :, there],
            dp_land.at[3 + j],
            dp_land.at[3 + j],
            place.to_row(j),
        )
        copies.open.append(sent)
        line_waits.append(got)
    pump("tail1")
    need("middle")
    last_bias = wide_ref[10 + top : 11 + top, :]
    for k in reversed(range(CHUNKS)):
        col_waits[k]()

        def finish(at, k=k):
            here = pl.ds(at, STRIP)
            total = chip_sum[k, here, :].astype(f32) + got_col[0, k, here, :].astype(f32)
            branch[pl.ds(pl.multiple_of(k * SPAN + core * OWN + at, STRIP), STRIP), :] = (
                middle[k, here, :] + (total + last_bias)
            ).astype(bf16)

        strips(OWN, finish)
        to_features(k, branch, result_ref)
    pump("tail2")
    for wait in line_waits:
        wait()
    total = line_land[0, :, own_lanes]
    dp_land[place.dp] = total + dp_land[4] + dp_land[5] + dp_land[6]
    line_waits = []
    for i, device in enumerate(others):
        back = (place.dp + 3 - i) % 4
        sent, got = copies.sem(), copies.sem()
        out = pltpu.make_async_remote_copy(
            dp_land.at[place.dp], dp_land.at[place.dp], sent, got, device_id=device, device_id_type=MESH
        )
        arriving = pltpu.make_async_remote_copy(
            dp_land.at[back], dp_land.at[back], sent, got, device_id=device, device_id_type=MESH
        )
        out.start()
        copies.open.append(out.wait_send)
        line_waits.append(arriving.wait_recv)
    pump("tail3")
    for wait in line_waits:
        wait()
    small_out[...] = dp_land[0] + dp_land[1] + dp_land[2] + dp_land[3]
    for kind in (3, 2, 1, 0):
        reductions[0, kind].finish()
    core_free()
    for k in range(CHUNKS):
        sent_col[k]()
    for wait in landed:
        wait()
    copies.finish()


def backward_call(tokens_shape, grad_in, wide, seg_row, weights, saved, stream):
    units = weights[2].shape[2]
    scratch = [
        ((3, D, WIDTH), bf16),
        ((WIDTH, D), bf16),
        ((D, units), bf16),
        ((units, D), bf16),
        ((LEN, D), bf16),
        ((LEN, 3 * WIDTH), bf16),
        ((LEN, WIDTH), bf16),
        ((LEN, 128), f32),
        ((LEN, D), bf16),
        ((LEN, units), bf16),
        ((LEN, units), bf16),
        ((CHUNKS, OWN, D), f32),
        ((CHUNKS, OWN, D), f32),
        ((LEN, D), bf16),
        ((LEN, units), bf16),
        ((LEN, D), bf16),
        ((LEN, 3 * WIDTH), bf16),
        ((SPAN, WIDTH), bf16),
        ((LEN, 2 * WIDTH), f32),
        ((CHUNKS, OWN, D), f32),
        ((OWN, D), f32),
        ((OWN, D), bf16),
        ((2, CHUNKS, OWN, D), bf16),
        ((CHUNKS, OWN, D), bf16),
        ((2, CHUNKS, OWN, D), bf16),
        ((LAYERS, 6, 8, D), f32),
        ((LAYERS, 16, D), f32),
        ((1, LAYERS * LINES, D), f32),
        ((7, LAYERS * LINES, WIDTH), f32),
    ]
    for parts in (4, 3, 2, 2):
        scratch += [((parts, *piece), bf16) for piece in PIECES]
    outs = [
        (tokens_shape, bf16),
        (tokens_shape, bf16),
        ((LAYERS * LINES, WIDTH), f32),
        ((LAYERS, 3, WIDTH, 2 * WIDTH), bf16),
        ((LAYERS, 2 * WIDTH, WIDTH), bf16),
        ((LAYERS, WIDTH, 2 * units), bf16),
        ((LAYERS, 2 * units, WIDTH), bf16),
    ]
    anywhere = pl.BlockSpec(memory_space=pl.ANY)
    inside = pl.BlockSpec(memory_space=pltpu.VMEM)
    return pl.pallas_call(
        backward_body,
        out_shape=[like(*v) for v in outs],
        in_specs=[anywhere] + [inside] * 2 + [anywhere] * 12,
        out_specs=[anywhere] * 2 + [inside] + [anywhere] * 4,
        scratch_shapes=[pltpu.VMEM(*v) for v in scratch]
        + [pltpu.SemaphoreType.REGULAR((12,)), pltpu.SemaphoreType.DMA((840,))],
        compiler_params=pltpu.CompilerParams(
            collective_id=1, has_side_effects=True, vmem_limit_bytes=60 * 1024 * 1024
        ),
    )(grad_in, wide, seg_row, *weights, *saved, stream)


def pair_plan(
    tokens,
    segments,
    norm_gain,
    norm_shift,
    triple_weight,
    triple_bias,
    output_weight,
    output_bias,
    up_weight,
    up_bias,
    down_weight,
    down_bias,
    cotangent,
):
    chip = lax.axis_index("row") // 2
    seg_pack = lax.dynamic_slice_in_dim(segments, chip * LEN, LEN, 0)
    seg_col, seg_row = seg_pack[:, None], seg_pack[None, :]
    grad_in, wide, *kept, stream = forward_call(
        tokens,
        cotangent,
        pack_small(norm_gain, norm_shift, output_bias, down_bias, triple_bias, up_bias),
        seg_col,
        seg_row,
        jnp.swapaxes(triple_weight, 1, 2),
        output_weight,
        up_weight,
        down_weight,
    )
    result, input_grad, small, triple_grad, output_grad, up_grad, down_grad = backward_call(
        tokens.shape, grad_in, wide, seg_row.astype(f32), kept[:4], kept[4:], stream
    )
    small = small.reshape(LAYERS, LINES, WIDTH)
    return (
        result,
        input_grad.astype(f32),
        small[:, 0:2],
        small[:, 2:4],
        jnp.swapaxes(triple_grad, 1, 2).astype(f32),
        small[:, 6].reshape(LAYERS, 2, WIDTH // 2),
        output_grad.astype(f32),
        small[:, 4],
        up_grad.astype(f32),
        small[:, 7:9].reshape(LAYERS, 2 * WIDTH),
        down_grad.astype(f32),
        small[:, 5],
    )


def solution(mesh):
    in_specs = (
        P("dp", "row"),
        P("dp"),
        P(None, None, "row"),
        P(None, None, "row"),
        P(None, "row", None, "col"),
        P(None, None, ("col", "row")),
        P(None, "col", "row"),
        P(None, "row"),
        P(None, "row", "col"),
        P(None, ("col", "row")),
        P(None, "col", "row"),
        P(None, "row"),
        P("dp", "row"),
    )
    out_specs = (
        P("dp", "row"),
        P("dp", "row"),
        P(None, None, "row"),
        P(None, None, "row"),
        P(None, "row", None, "col"),
        P(None, None, ("col", "row")),
        P(None, "col", "row"),
        P(None, "row"),
        P(None, "row", "col"),
        P(None, ("col", "row")),
        P(None, "col", "row"),
        P(None, "row"),
    )
    shape = mesh.shape

    def on_device(*arrays):
        if fits_pairs(shape, arrays):
            return pair_plan(*arrays)
        return general_plan(*arrays)

    return jax.shard_map(
        on_device, mesh=mesh, in_specs=in_specs, out_specs=out_specs, check_vma=False
    )
```

```python
import math

import jax
import jax.numpy as jnp
from jax import lax
from jax.experimental import pallas as pl
from jax.experimental.pallas import tpu as pltpu
from jax.sharding import PartitionSpec as P

D = 1024
HD = 64
LAYERS = 2
LEN = 1024


eps = 1e-05
masked = -1000000000.0


def norm_forward(stream, gain, shift):
    totals = lax.psum((jnp.sum(stream, axis=1), jnp.sum(stream * stream, axis=1)), "row")
    center = totals[0] / D
    second = totals[1] / D - center * center
    inv_std = lax.rsqrt(second + eps)
    normed = (stream - center[:, None]) * inv_std[:, None]
    return (normed, inv_std, normed * gain + shift)


def norm_backward(grad_out, normed, inv_std, gain):
    scaled = grad_out * gain
    totals = lax.psum((jnp.sum(scaled, axis=1), jnp.sum(scaled * normed, axis=1)), "row")
    grad_in = inv_std[:, None] * (
        scaled - totals[0][:, None] / D - normed * (totals[1][:, None] / D)
    )
    return (grad_in, jnp.sum(grad_out * normed, axis=0), jnp.sum(grad_out, axis=0))


def gather_rows(block):
    return lax.all_gather(block, "row", axis=1, tiled=True)


def col_total(partial_sums):
    return lax.psum(partial_sums, "col")


def rows_back(partial_sums):
    return lax.psum_scatter(
        partial_sums.astype(jnp.bfloat16), "row", scatter_dimension=1, tiled=True
    ).astype(jnp.float32)


def in_parts(partial_sums):
    return lax.psum_scatter(partial_sums, "row", scatter_dimension=2, tiled=True)


def grad_gather(block):
    return lax.all_gather(block, "row", axis=2, tiled=True)


def pack_scores(queries, key_rows, seg_pack, scale):
    position = jnp.arange(queries.shape[0])
    allowed = (seg_pack[:, None] == seg_pack[None, :]) & (position[None, :] <= position[:, None])
    scores = (
        jnp.einsum("qhd,khd->hqk", queries, key_rows, preferred_element_type=jnp.float32) * scale
    )
    return jnp.where(allowed[None], scores, masked)


def split_packs(triple, seg_rows):
    length, three, width = triple.shape
    count = length // LEN
    return (triple.reshape(count, LEN, three, width // HD, HD), seg_rows.reshape(count, LEN))


def attend_forward(triple, seg_rows, scale):
    length, three, width = triple.shape
    packs, seg_packs = split_packs(triple, seg_rows)

    def one_pack(pieces):
        pack_rows, seg_pack = pieces
        scores = pack_scores(pack_rows[:, 0], pack_rows[:, 1], seg_pack, scale)
        row_peak = jnp.max(scores, axis=-1, keepdims=True)
        exponent = jnp.exp(scores - row_peak)
        denominator = jnp.sum(exponent, axis=-1, keepdims=True)
        soft_weights = (exponent / denominator).astype(jnp.bfloat16)
        blended = jnp.einsum(
            "hqk,khd->qhd", soft_weights, pack_rows[:, 2], preferred_element_type=jnp.float32
        )
        return (blended.astype(jnp.bfloat16), (row_peak + jnp.log(denominator))[..., 0])

    blended, log_totals = lax.map(one_pack, (packs, seg_packs))
    return (blended.reshape(length, width), log_totals)


def attend_backward(triple, seg_rows, log_totals, grad_mixed, scale):
    length, three, width = triple.shape
    packs, seg_packs = split_packs(triple, seg_rows)
    grad_packs = grad_mixed.reshape(length // LEN, LEN, width // HD, HD)

    def one_pack(pieces):
        pack_rows, seg_pack, pack_totals, grad_pack = pieces
        queries = pack_rows[:, 0]
        key_rows = pack_rows[:, 1]
        value_rows = pack_rows[:, 2]
        scores = pack_scores(queries, key_rows, seg_pack, scale)
        chances = jnp.exp(scores - pack_totals[:, :, None])
        chance_grad = jnp.einsum(
            "qhd,khd->hqk", grad_pack, value_rows, preferred_element_type=jnp.float32
        )
        inner = jnp.sum(chances * chance_grad, axis=-1, keepdims=True)
        score_grad = (chances * (chance_grad - inner)).astype(jnp.bfloat16)
        query_grad = (
            jnp.einsum("hqk,khd->qhd", score_grad, key_rows, preferred_element_type=jnp.float32)
            * scale
        )
        key_grad = (
            jnp.einsum("hqk,qhd->khd", score_grad, queries, preferred_element_type=jnp.float32)
            * scale
        )
        value_grad = jnp.einsum(
            "hqk,qhd->khd",
            chances.astype(jnp.bfloat16),
            grad_pack,
            preferred_element_type=jnp.float32,
        )
        return jnp.stack([query_grad, key_grad, value_grad], axis=1).astype(jnp.bfloat16)

    triple_rows = lax.map(one_pack, (packs, seg_packs, log_totals, grad_packs))
    return triple_rows.reshape(length, three, width)


def layer_forward(stream, weights, small, seg_rows):
    triple_w, output_w, up_w, down_w = weights
    gains, shifts, triple_b, output_b, up_b, down_b = small
    scale = 1.0 / math.sqrt(HD)
    normed_one, inv_one, attn_in = norm_forward(stream, gains[0], shifts[0])
    attn_in = attn_in.astype(jnp.bfloat16)
    triple = in_parts(
        jnp.einsum("td,dke->tke", attn_in, triple_w, preferred_element_type=jnp.float32)
    )
    bias_rows = jnp.stack([triple_b[0], jnp.zeros_like(triple_b[0]), triple_b[1]])
    triple = (triple + bias_rows).astype(jnp.bfloat16)
    mixed, log_totals = attend_forward(triple, seg_rows, scale)
    mixed_full = gather_rows(mixed)
    middle = stream + (
        col_total(jnp.dot(mixed_full, output_w, preferred_element_type=jnp.float32)) + output_b
    )
    normed_two, inv_two, mlp_in = norm_forward(middle, gains[1], shifts[1])
    mlp_in = mlp_in.astype(jnp.bfloat16)
    hidden_pre = (
        in_parts(jnp.dot(mlp_in, up_w, preferred_element_type=jnp.float32)[:, None, :])[:, 0] + up_b
    )
    active = jax.nn.gelu(hidden_pre, approximate=True).astype(jnp.bfloat16)
    active_full = gather_rows(active)
    after = middle + (
        col_total(jnp.dot(active_full, down_w, preferred_element_type=jnp.float32)) + down_b
    )
    saved = (
        normed_one,
        inv_one,
        attn_in,
        triple,
        log_totals,
        mixed_full,
        normed_two,
        inv_two,
        mlp_in,
        hidden_pre,
        active_full,
        None,
    )
    return (after, saved)


def layer_backward(grad, saved, weights, gains, seg_rows):
    (
        normed_one,
        inv_one,
        attn_rows,
        triple,
        log_totals,
        mixed_full,
        normed_two,
        inv_two,
        mlp_rows,
        hidden_pre,
        active_full,
        columns_in,
    ) = saved
    triple_w, output_w, up_w, down_w = weights
    scale = 1.0 / math.sqrt(HD)
    down_in = grad.astype(jnp.bfloat16)
    down_bias_grad = jnp.sum(down_in, axis=0, dtype=jnp.float32)
    down_grad = jnp.einsum("tf,td->fd", active_full, down_in, preferred_element_type=jnp.float32)
    active_grad = rows_back(
        jnp.einsum("td,fd->tf", down_in, down_w, preferred_element_type=jnp.float32)
    )
    gelu_pull = jax.vjp(lambda value: jax.nn.gelu(value, approximate=True), hidden_pre)[1]
    hidden_grad = gelu_pull(active_grad)[0].astype(jnp.bfloat16)
    up_bias_grad = jnp.sum(hidden_grad, axis=0, dtype=jnp.float32)
    hidden_rows = grad_gather(hidden_grad[:, None, :])[:, 0]
    up_grad = jnp.einsum("td,tf->df", mlp_rows, hidden_rows, preferred_element_type=jnp.float32)
    mlp_grad = col_total(
        jnp.einsum("tf,df->td", hidden_rows, up_w, preferred_element_type=jnp.float32)
    )
    norm_two_grad, gain_two, shift_two = norm_backward(mlp_grad, normed_two, inv_two, gains[1])
    middle_grad = grad + norm_two_grad
    branch_grad = middle_grad.astype(jnp.bfloat16)
    output_bias_grad = jnp.sum(branch_grad, axis=0, dtype=jnp.float32)
    output_grad = jnp.einsum(
        "td,te->de", mixed_full, branch_grad, preferred_element_type=jnp.float32
    )
    mixed_grad = rows_back(
        jnp.einsum("te,de->td", branch_grad, output_w, preferred_element_type=jnp.float32)
    ).astype(jnp.bfloat16)
    triple_rows = attend_backward(triple, seg_rows, log_totals, mixed_grad, scale)
    triple_bias_grad = jnp.sum(triple_rows[:, 0::2], axis=0, dtype=jnp.float32)
    full_rows = grad_gather(triple_rows)
    triple_grad = jnp.einsum(
        "td,tke->dke", attn_rows, full_rows, preferred_element_type=jnp.float32
    )
    attn_grad = col_total(
        jnp.einsum("tke,dke->td", full_rows, triple_w, preferred_element_type=jnp.float32)
    )
    norm_one_grad, gain_one, shift_one = norm_backward(attn_grad, normed_one, inv_one, gains[0])
    start_grad = middle_grad + norm_one_grad
    terms = (
        jnp.stack([gain_one, gain_two]),
        jnp.stack([shift_one, shift_two]),
        triple_grad,
        triple_bias_grad,
        output_grad,
        output_bias_grad,
        up_grad,
        up_bias_grad,
        down_grad,
        down_bias_grad,
    )
    return (start_grad, terms)


def general_plan(
    tokens,
    segments,
    norm_gain,
    norm_shift,
    triple_weight,
    triple_bias,
    output_weight,
    output_bias,
    up_weight,
    up_bias,
    down_weight,
    down_bias,
    cotangent,
):

    def weights_of(layer_id):
        return (
            triple_weight[layer_id],
            output_weight[layer_id],
            up_weight[layer_id],
            down_weight[layer_id],
        )

    def small_of(layer_id):
        return (
            norm_gain[layer_id].astype(jnp.float32),
            norm_shift[layer_id].astype(jnp.float32),
            triple_bias[layer_id].astype(jnp.float32),
            output_bias[layer_id].astype(jnp.float32),
            up_bias[layer_id].astype(jnp.float32),
            down_bias[layer_id].astype(jnp.float32),
        )

    stream = tokens.astype(jnp.float32)
    stored = []
    for layer_id in range(LAYERS):
        stream, saved = layer_forward(stream, weights_of(layer_id), small_of(layer_id), segments)
        stored.append(saved)
    result = stream.astype(jnp.bfloat16)
    grad = cotangent.astype(jnp.float32)
    summed = [None] * LAYERS
    for layer_id in reversed(range(LAYERS)):
        grad, terms = layer_backward(
            grad, stored[layer_id], weights_of(layer_id), small_of(layer_id)[0], segments
        )
        summed[layer_id] = (
            lax.psum(terms[0].astype(jnp.bfloat16), "dp").astype(jnp.float32),
            lax.psum(terms[1].astype(jnp.bfloat16), "dp").astype(jnp.float32),
            lax.psum(terms[2].astype(jnp.bfloat16), "dp").astype(jnp.float32),
            lax.psum(terms[3].astype(jnp.bfloat16), "dp").astype(jnp.float32),
            lax.psum(terms[4].astype(jnp.bfloat16), "dp").astype(jnp.float32),
            lax.psum(terms[5].astype(jnp.bfloat16), "dp").astype(jnp.float32),
            lax.psum(terms[6].astype(jnp.bfloat16), "dp").astype(jnp.float32),
            lax.psum(terms[7].astype(jnp.bfloat16), "dp").astype(jnp.float32),
            lax.psum(terms[8].astype(jnp.bfloat16), "dp").astype(jnp.float32),
            lax.psum(terms[9].astype(jnp.bfloat16), "dp").astype(jnp.float32),
        )
    stacks = [
        jnp.stack([summed[layer_id][member] for layer_id in range(LAYERS)]) for member in range(10)
    ]
    return (
        result,
        grad,
        stacks[0],
        stacks[1],
        stacks[2],
        stacks[3],
        stacks[4],
        stacks[5],
        stacks[6],
        stacks[7],
        stacks[8],
        stacks[9],
    )


f32 = jnp.float32
bf16 = jnp.bfloat16
CHUNKS = 2
SPAN = LEN // CHUNKS
OWN = SPAN // 2
WIDTH = D // 4
QB = 256


def fits_pairs(shape, arrays):
    return (
        shape["row"] == 4
        and shape["col"] == 2
        and shape["dp"] == 4
        and arrays[0].shape == (2 * LEN, WIDTH)
        and arrays[8].shape[2] == 8 * WIDTH
    )


def dot(a, b):
    return lax.dot_general(a, b, (((1,), (0,)), ((), ())), preferred_element_type=f32)


def dot_nt(a, b):
    return lax.dot_general(a, b, (((1,), (1,)), ((), ())), preferred_element_type=f32)


def dot_tn(a, b):
    return lax.dot_general(a, b, (((0,), (0,)), ((), ())), preferred_element_type=f32)


def like(shape, kind):
    return jax.ShapeDtypeStruct(shape, kind)


def mean_lanes(v):
    return jnp.sum(v, axis=1, keepdims=True) * (1.0 / D)


def norm_parts(v):
    center = mean_lanes(v)
    second = mean_lanes(v * v) - center * center
    inv_std = lax.rsqrt(second + eps)
    return (v - center) * inv_std, inv_std


GELU = math.sqrt(2.0 / math.pi)


MESH = pl.DeviceIdType.MESH
HEADS_HERE = WIDTH // HD
SMALL = 24
SEG = 64


class Place:
    def __init__(self):
        self.row = lax.axis_index("row")
        self.col = lax.axis_index("col")
        self.dp = lax.axis_index("dp")
        self.core = self.row % 2
        self.chip = self.row // 2
        self.half = self.dp % 2
        sibling = self.row + 1 - 2 * self.core
        self.rows = [self.row, sibling, (self.row + 2) % 4, (sibling + 2) % 4]
        self.cores = [self.core, 1 - self.core, self.core, 1 - self.core]

    def to_row(self, j):
        return {"row": self.rows[j]}

    def to_col(self):
        return {"col": 1 - self.col}

    def to_dp(self):
        return {"dp": self.dp + 1 - 2 * self.half}


class Copies:
    def __init__(self, sems):
        self.sems = sems
        self.used = 0
        self.open = []

    def sem(self):
        self.used += 1
        return self.sems.at[self.used - 1]

    def local(self, src, dst):
        copy = pltpu.make_async_copy(src, dst, self.sem())
        copy.start()
        return copy

    def save(self, src, dst):
        self.open.append(self.local(src, dst).wait)

    def trade(self, src, dst, landing, device):
        sent, got = self.sem(), self.sem()
        out = pltpu.make_async_remote_copy(src, dst, sent, got, device_id=device, device_id_type=MESH)
        back = pltpu.make_async_remote_copy(
            landing, landing, sent, got, device_id=device, device_id_type=MESH
        )
        out.start()
        return out.wait_send, back.wait_recv

    def finish(self):
        for wait in self.open:
            wait()


def greet(place, devices):
    barrier = pltpu.get_barrier_semaphore()
    for device in devices:
        pl.semaphore_signal(barrier, inc=1, device_id=device, device_id_type=MESH)
    pl.semaphore_wait(barrier, len(devices))


def span(start, size):
    return pl.ds(pl.multiple_of(start, size), size)


def weight_cuts(kind, layer, wide, local):
    w = WIDTH
    if kind == 0:

        def source(core, half):
            rows = slice(None) if half is None else span(half * (w // 2), w // 2)
            return local.at[layer, :, rows, span(core * w, w)]

        def target(row, half):
            rows = span(row * w, w) if half is None else span(row * w + half * (w // 2), w // 2)
            return wide.at[layer, :, rows, :]

    elif kind == 2:
        units = wide.shape[2]

        def source(core, half):
            rows = slice(None) if half is None else span(half * (w // 2), w // 2)
            return local.at[layer, rows, span(core * units, units)]

        def target(row, half):
            rows = span(row * w, w) if half is None else span(row * w + half * (w // 2), w // 2)
            return wide.at[layer, rows, :]

    else:
        high = wide.shape[1]

        def source(core, half):
            if half is None:
                return local.at[layer, span(core * high, high), :]
            return local.at[layer, span(core * high + half * (high // 2), high // 2), :]

        def target(row, half):
            rows = slice(None) if half is None else span(half * (high // 2), high // 2)
            return wide.at[layer, rows, span(row * w, w)]

    return source, target


STRIP = 64


def strips(count, body):
    def step(i, carry):
        body(pl.multiple_of(i * STRIP, STRIP))
        return carry

    lax.fori_loop(0, count // STRIP, step, 0)


def causal(seg_col, seg_row, start, keys):
    query = lax.broadcasted_iota(jnp.int32, (QB, keys), 0) + start
    key = lax.broadcasted_iota(jnp.int32, (QB, keys), 1)
    return (seg_col == seg_row) & (key <= query)


def lanes_of(h):
    lane = lax.broadcasted_iota(jnp.int32, (1, WIDTH), 1)
    return (lane >= h * HD) & (lane < (h + 1) * HD)


def attend_chunk(k, triples, seg_col_ref, seg_row_ref, kv_ref, mixed_ref, log_ref):
    scale = 1.0 / math.sqrt(HD)
    kv_ref[k * SPAN : (k + 1) * SPAN, :] = triples[k][:, WIDTH:]
    for block in range(SPAN // QB):
        rows = slice(block * QB, (block + 1) * QB)
        start = k * SPAN + block * QB
        keys = start + QB
        allowed = causal(seg_col_ref[start : start + QB, :], seg_row_ref[:, :keys], start, keys)
        queries = triples[k][rows, :WIDTH] * scale
        key_rows = kv_ref[:keys, :WIDTH]
        value_rows = kv_ref[:keys, WIDTH:]
        blended = jnp.zeros((QB, WIDTH), f32)
        for h in range(HEADS_HERE):
            lanes = lanes_of(h)
            scores = dot_nt(jnp.where(lanes, queries, 0).astype(bf16), key_rows)
            scores = jnp.where(allowed, scores, masked)
            peak = jnp.max(scores, axis=1, keepdims=True)
            exponent = jnp.exp(scores - peak)
            total = jnp.sum(exponent, axis=1, keepdims=True)
            soft = (exponent * (1.0 / total)).astype(bf16)
            blended = jnp.where(lanes, dot(soft, value_rows), blended)
            log_ref[rows, h : h + 1] = peak + jnp.log(total)
        log_ref[rows, SEG : SEG + 1] = seg_col_ref[start : start + QB, :].astype(f32)
        mixed_ref[rows, :] = blended.astype(bf16)


def forward_body(*refs):
    (
        tokens_ref,
        cotangent_ref,
        gain_in,
        shift_in,
        output_bias_in,
        down_bias_in,
        triple_bias_in,
        up_bias_in,
        seg_col_ref,
        seg_row_ref,
        triple_in,
        output_in,
        up_in,
        down_in,
        grad_ref,
        wide_out,
        triple_out,
        output_out,
        up_out,
        down_out,
        attn_out,
        rows_out,
        mixed_out,
        log_out,
        mlp_out,
        slope_out,
        active_out,
        stream_out,
        triple_w,
        output_w,
        up_w,
        down_w,
        attn,
        rows,
        mixed,
        logs,
        mlp,
        slope,
        active,
        stream,
        taken,
        wide,
        kv,
        mine,
        give,
        got_core,
        chip_sum,
        got_col,
        small_ref,
        sems,
    ) = refs
    place = Place()
    copies = Copies(sems)
    core, sibling = place.core, 1 - place.core
    greet(place, [place.to_row(1), place.to_row(2), place.to_row(3), place.to_col(), place.to_dp()])

    own_lanes = span(place.row * WIDTH, WIDTH)

    def held(j, k):
        return span(place.rows[j] // 2 * LEN + k * SPAN + place.cores[j] * OWN, OWN)

    def part(c):
        return span(c * OWN, OWN)

    small_ref[...] = jnp.zeros_like(small_ref)
    for layer in range(LAYERS):
        small_ref[2 * layer : 2 * layer + 2, :] = gain_in[layer].astype(f32)
        small_ref[4 + 2 * layer : 6 + 2 * layer, :] = shift_in[layer].astype(f32)
        for which in range(2):
            cols = slice(which * (WIDTH // 2), (which + 1) * (WIDTH // 2))
            value = triple_bias_in[layer].astype(f32)
            small_ref[12 + layer : 13 + layer, cols] = value[which : which + 1]
            value = up_bias_in[...].astype(f32)
            at = 14 + 2 * layer + which
            small_ref[at : at + 1, :] = value[layer : layer + 1, which * WIDTH : (which + 1) * WIDTH]
    small_ref[8:10, :] = output_bias_in[...].astype(f32)
    small_ref[10:12, :] = down_bias_in[...].astype(f32)
    small_waits = []
    copy = copies.local(small_ref, wide.at[:, own_lanes])
    small_waits.append(copy.wait)
    for j in range(1, 4):
        sent, got = copies.trade(
            small_ref,
            wide.at[:, own_lanes],
            wide.at[:, span(place.rows[j] * WIDTH, WIDTH)],
            place.to_row(j),
        )
        copies.open.append(sent)
        small_waits.append(got)
    token_waits = [[] for _ in range(CHUNKS)]

    def scatter_in(block_ref, target, k, waits):
        waits.append(copies.local(block_ref.at[held(0, k), :], target.at[k, :, own_lanes]).wait)
        for j in range(1, 4):
            sent, got = copies.trade(
                block_ref.at[held(j, k), :],
                target.at[k, :, own_lanes],
                target.at[k, :, span(place.rows[j] * WIDTH, WIDTH)],
                place.to_row(j),
            )
            copies.open.append(sent)
            waits.append(got)

    arrivals, ready_waits = {}, {}

    def send_weight(layer, kind):
        local = (triple_in, output_in, up_in, down_in)[kind]
        whole = (triple_w, output_w, up_w, down_w)[kind]
        source, target = weight_cuts(kind, layer, whole, local)
        here = []
        for j in (2, 3):
            sent, got = copies.trade(
                source(place.cores[j], place.half),
                target(place.row, place.half),
                target(place.rows[j], place.half),
                place.to_row(j),
            )
            copies.open.append(sent)
            here.append((got, target(place.rows[j], place.half), target(place.rows[j], 1 - place.half)))
        arrivals[layer, kind] = here
        sent, got = copies.trade(
            source(sibling, None),
            target(place.row, None),
            target(place.rows[1], None),
            place.to_row(1),
        )
        copies.open.append(sent)
        own = copies.local(source(core, None), target(place.row, None))
        ready_waits[layer, kind] = [got, own.wait]

    relays = [
        (layer, kind, i) for layer in range(LAYERS) for kind in range(4) for i in range(2)
    ]

    def pump(count):
        for _ in range(count):
            layer, kind, i = relays.pop(0)
            got, arrived, missing = arrivals[layer, kind][i]
            got()
            sent, back = copies.trade(arrived, arrived, missing, place.to_dp())
            copies.open.append(sent)
            ready_waits[layer, kind].append(back)

    def ready_weight(layer, kind):
        for wait in ready_waits[layer, kind]:
            wait()
        whole = (triple_w, output_w, up_w, down_w)[kind]
        out = (triple_out, output_out, up_out, down_out)[kind]
        copies.save(whole.at[layer], out.at[layer])

    scatter_in(tokens_ref, taken, 0, token_waits[0])
    send_weight(0, 0)
    scatter_in(tokens_ref, taken, 1, token_waits[1])
    for layer, kind in ((0, 1), (0, 2), (0, 3), (1, 0), (1, 1), (1, 2), (1, 3)):
        send_weight(layer, kind)
    grad_waits = []
    for k in range(CHUNKS):
        scatter_in(cotangent_ref, grad_ref, k, grad_waits)

    for wait in small_waits:
        wait()
    copies.save(wide, wide_out)

    def gain(layer, which):
        return wide[2 * layer + which : 2 * layer + which + 1, :]

    def shift(layer, which):
        return wide[4 + 2 * layer + which : 5 + 2 * layer + which, :]

    def output_bias(layer):
        return wide[8 + layer : 9 + layer, :]

    def down_bias(layer):
        return wide[10 + layer : 11 + layer, :]

    def of_core(line, start, size):
        return wide[line : line + 1, span(start, size)]

    def triple_bias(layer, which):
        at = 2 * core * WIDTH + which * (WIDTH // 2)
        size = WIDTH // 2
        return jnp.concatenate(
            [of_core(12 + layer, at, size), of_core(12 + layer, at + WIDTH, size)], axis=1
        )

    def up_bias(layer):
        line, at = 14 + 2 * layer, 2 * core * WIDTH
        return jnp.concatenate(
            [of_core(line + a, at + b * WIDTH, WIDTH) for b in range(2) for a in range(2)], axis=1
        )

    def norm_to(value, layer, which, target, at):
        center = jnp.mean(value, axis=1, keepdims=True)
        second = jnp.mean(value * value, axis=1, keepdims=True) - center * center
        normed = (value - center) * lax.rsqrt(second + eps)
        target[pl.ds(pl.multiple_of(core * OWN + at, STRIP), STRIP), :] = (
            normed * gain(layer, which) + shift(layer, which)
        ).astype(bf16)

    def share(target):
        return copies.trade(target.at[part(core)], target.at[part(core)], target.at[part(sibling)], place.to_row(1))

    sent_core, sent_col = [None] * CHUNKS, [None] * CHUNKS
    col_waits = [None] * CHUNKS
    saves = {}

    def settle(stage, k, got):
        got()
        if sent_col[k] is not None:
            sent_col[k]()

        def add(at):
            lines = pl.ds(at, STRIP)
            chip_sum[k, lines, :] = (
                mine[k, lines, :] + got_core[stage, k, lines, :].astype(f32)
            ).astype(bf16)

        strips(OWN, add)
        sent_col[k], col_waits[k] = copies.trade(
            chip_sum.at[k], got_col.at[stage, k], got_col.at[stage, k], place.to_col()
        )

    def start_core(stage, k):
        sent, got = copies.trade(
            give.at[k], got_core.at[stage, k], got_core.at[stage, k], place.to_row(1)
        )
        sent_core[k] = sent
        return got

    def take_col(stage, k, layer, bias, after_ref):
        col_waits[k]()

        def add(at):
            lines = pl.ds(at, STRIP)
            total = chip_sum[k, lines, :].astype(f32) + got_col[stage, k, lines, :].astype(f32)
            value = stream[stage, k, lines, :] + (total + bias)
            stream[1 - stage, k, lines, :] = value
            after_ref(value, at)

        strips(OWN, add)

    shares = [None] * CHUNKS
    for k in range(CHUNKS):
        for wait in token_waits[k]:
            wait()
        def first(at, k=k):
            value = taken[k, pl.ds(at, STRIP), :].astype(f32)
            stream[0, k, pl.ds(at, STRIP), :] = value
            norm_to(value, 0, 0, attn.at[0, k], at)

        strips(OWN, first)
        saves[0, 0, k] = copies.local(stream.at[0, k], stream_out.at[0, 0, k])
        shares[k] = share(attn.at[0, k])
        pump(2)

    for layer in range(LAYERS):
        for k in range(CHUNKS):
            if layer:
                if k == 0:
                    pump(1)
                saves.pop((layer - 1, 0, k)).wait()
                take_col(
                    1, k, layer, down_bias(layer - 1), lambda v, at, k=k: norm_to(v, layer, 0, attn.at[layer, k], at)
                )
                saves[layer, 0, k] = copies.local(stream.at[0, k], stream_out.at[layer, 0, k])
                shares[k] = share(attn.at[layer, k])
            if k == 0:
                ready_weight(layer, 0)
            bias = [triple_bias(layer, 0), None, triple_bias(layer, 1)]

            def project(c, k=k, bias=bias):
                for third in range(3):
                    value = dot(attn[layer, k, part(c), :], triple_w[layer, third])
                    if bias[third] is not None:
                        value = value + bias[third]
                    rows[layer, k, part(c), third * WIDTH : (third + 1) * WIDTH] = value.astype(bf16)

            project(core)
            sent, got = shares[k]
            got()
            project(sibling)
            attend_chunk(
                k,
                [rows.at[layer, i] for i in range(k + 1)],
                seg_col_ref,
                seg_row_ref,
                kv,
                mixed.at[layer, k],
                logs.at[layer, k],
            )
            pump(1)
            if k == 0:
                ready_weight(layer, 1)
            if sent_core[k] is not None:
                sent_core[k]()
            give[k] = dot(mixed[layer, k, part(sibling), :], output_w[layer]).astype(bf16)
            got = start_core(0, k)
            mine[k] = dot(mixed[layer, k, part(core), :], output_w[layer])
            sent()
            copies.save(attn.at[layer, k], attn_out.at[layer, k])
            copies.save(rows.at[layer, k], rows_out.at[layer, k])
            copies.save(mixed.at[layer, k], mixed_out.at[layer, k])
            copies.save(logs.at[layer, k], log_out.at[layer, k])
            settle(0, k, got)
            if k:
                pump(1)
        for k in range(CHUNKS):
            if layer:
                saves.pop((layer - 1, 1, k)).wait()
            elif k:
                pump(1)
            take_col(
                0, k, layer, output_bias(layer), lambda v, at, k=k: norm_to(v, layer, 1, mlp.at[layer, k], at)
            )
            saves[layer, 1, k] = copies.local(stream.at[1, k], stream_out.at[layer, 1, k])
            shares[k] = share(mlp.at[layer, k])
            if k == 0:
                ready_weight(layer, 2)
            bias = up_bias(layer)

            def widen(c, k=k, bias=bias):
                for block in range(4):
                    cols = slice(block * WIDTH, (block + 1) * WIDTH)
                    pre = dot(mlp[layer, k, part(c), :], up_w[layer, :, cols]) + bias[:, cols]
                    square = pre * pre
                    curve = jnp.tanh(GELU * (pre + 0.044715 * (square * pre)))
                    upper = 0.5 * (1.0 + curve)
                    active[layer, k, part(c), cols] = (pre * upper).astype(bf16)
                    slope[layer, k, part(c), cols] = (
                        upper
                        + (0.5 * GELU) * pre * (1.0 - curve * curve) * (1.0 + (3.0 * 0.044715) * square)
                    ).astype(bf16)

            widen(core)
            sent, got = shares[k]
            got()
            widen(sibling)
            if layer + 1 < LAYERS:
                if k == 0:
                    pump(1)
                    ready_weight(layer, 3)
                sent_core[k]()
                give[k] = dot(active[layer, k, part(sibling), :], down_w[layer]).astype(bf16)
                got = start_core(1, k)
                mine[k] = dot(active[layer, k, part(core), :], down_w[layer])
            sent()
            copies.save(mlp.at[layer, k], mlp_out.at[layer, k])
            copies.save(slope.at[layer, k], slope_out.at[layer, k])
            copies.save(active.at[layer, k], active_out.at[layer, k])
            if layer + 1 < LAYERS:
                settle(1, k, got)
                pump(k + 1)
    ready_weight(LAYERS - 1, 3)
    for k in range(CHUNKS):
        saves.pop((LAYERS - 1, 0, k)).wait()
        saves.pop((LAYERS - 1, 1, k)).wait()
        sent_core[k]()
        sent_col[k]()
    for wait in grad_waits:
        wait()
    copies.finish()


def forward_call(tokens, cotangent, small_params, seg_col, seg_row, triple_w, output_w, up_w, down_w):
    units = up_w.shape[2] // 2
    per_layer = [
        ((LAYERS, CHUNKS, SPAN, D), bf16),
        ((LAYERS, CHUNKS, SPAN, 3 * WIDTH), bf16),
        ((LAYERS, CHUNKS, SPAN, WIDTH), bf16),
        ((LAYERS, CHUNKS, SPAN, 128), f32),
        ((LAYERS, CHUNKS, SPAN, D), bf16),
        ((LAYERS, CHUNKS, SPAN, units), bf16),
        ((LAYERS, CHUNKS, SPAN, units), bf16),
    ]
    wide = [
        ((LAYERS, 3, D, WIDTH), bf16),
        ((LAYERS, WIDTH, D), bf16),
        ((LAYERS, D, units), bf16),
        ((LAYERS, units, D), bf16),
    ]
    outs = [
        ((CHUNKS, OWN, D), bf16),
        ((SMALL, D), f32),
        *wide,
        *per_layer,
        ((LAYERS, 2, CHUNKS, OWN, D), f32),
    ]
    scratch = [
        *wide,
        *per_layer,
        ((2, CHUNKS, OWN, D), f32),
        ((CHUNKS, OWN, D), bf16),
        ((SMALL, D), f32),
        ((LEN, 2 * WIDTH), bf16),
        ((CHUNKS, OWN, D), f32),
        ((CHUNKS, OWN, D), bf16),
        ((2, CHUNKS, OWN, D), bf16),
        ((CHUNKS, OWN, D), bf16),
        ((2, CHUNKS, OWN, D), bf16),
        ((SMALL, WIDTH), f32),
    ]
    anywhere = pl.BlockSpec(memory_space=pl.ANY)
    inside = pl.BlockSpec(memory_space=pltpu.VMEM)
    return pl.pallas_call(
        forward_body,
        out_shape=[like(*v) for v in outs],
        in_specs=[anywhere] * 2 + [inside] * 8 + [anywhere] * 4,
        out_specs=[anywhere] * len(outs),
        scratch_shapes=[pltpu.VMEM(*v) for v in scratch] + [pltpu.SemaphoreType.DMA((320,))],
        compiler_params=pltpu.CompilerParams(
            collective_id=0, has_side_effects=True, vmem_limit_bytes=60 * 1024 * 1024
        ),
    )(tokens, cotangent, *small_params, seg_col, seg_row, triple_w, output_w, up_w, down_w)


PIECES = ((3, WIDTH, WIDTH), (1, WIDTH, WIDTH), (4, WIDTH // 4, D), (4, D // 4, WIDTH))

PLAN = {
    "p1": ((1, 3, 0, 0),),
    "p0": ((1, 3, 1, 0), (1, 3, 0, 1)),
    "u1": ((1, 3, 2, 0), (1, 3, 1, 1), (1, 3, 0, 2)),
    "c1": ((1, 3, 3, 0), (1, 3, 2, 1), (1, 3, 1, 2)),
    "n1": ((1, 2, 0, 0),),
    "m1": ((1, 3, 3, 1), (1, 3, 2, 2), (1, 2, 1, 0)),
    "d1": ((1, 2, 0, 1),),
    "c0": ((1, 2, 2, 0), (1, 3, 3, 2)),
    "n0": ((1, 2, 1, 1),),
    "m0": ((1, 3, 0, 3), (1, 2, 3, 0), (1, 2, 0, 2), (1, 2, 2, 1)),
    "w1": ((1, 2, 1, 2),),
    "e1": ((1, 2, 3, 1),),
    "f1": ((1, 1, 0, 0), (1, 2, 2, 2)),
    "g1": ((1, 1, 0, 1), (1, 0, 0, 0)),
    "e0": ((1, 2, 3, 2),),
    "q0": ((1, 0, 0, 1), (1, 0, 1, 0), (1, 1, 0, 2)),
    "v0": ((1, 2, 0, 3), (1, 0, 2, 0), (1, 0, 1, 1), (1, 0, 0, 2)),
    "u0": ((1, 1, 0, 3),),
    "b1L": ((1, 0, 2, 1), (0, 3, 0, 0), (1, 0, 1, 2)),
    "n1L": ((0, 3, 0, 1), (0, 3, 1, 0), (1, 0, 2, 2)),
    "m1L": ((0, 3, 2, 0), (0, 3, 0, 2), (0, 3, 1, 1)),
    "b0L": ((1, 0, 0, 3),),
    "c0L": ((0, 3, 3, 0), (0, 3, 1, 2), (0, 3, 2, 1)),
    "m0L": ((0, 2, 0, 0), (0, 3, 2, 2), (0, 3, 3, 1)),
    "w0": ((0, 2, 1, 0), (0, 2, 0, 1), (0, 3, 3, 2)),
    "h0": ((0, 2, 2, 0), (0, 2, 1, 1), (0, 2, 0, 2), (0, 2, 3, 0)),
    "tail1": ((0, 1, 0, 0), (0, 2, 2, 1), (0, 2, 1, 2), (0, 0, 0, 0), (0, 2, 3, 1), (0, 2, 2, 2), (0, 0, 1, 0), (0, 1, 0, 1)),
    "tail2": ((0, 2, 3, 2), (0, 0, 2, 0), (0, 0, 0, 1), (0, 1, 0, 2), (0, 0, 1, 1), (0, 0, 0, 2), (0, 0, 2, 1), (0, 0, 1, 2), (0, 0, 2, 2)),
    "tail3": (),
}
LINES = 16


def attend_back_chunk(
    k, rows_ref, log_ref, seg_row_ref, grad_ref, total_ref, out_ref, pause
):
    scale = 1.0 / math.sqrt(HD)
    for block in range(SPAN // QB):
        start = k * SPAN + block * QB
        keys = start + QB
        here = slice(start, keys)
        allowed = causal(log_ref[here, SEG : SEG + 1], seg_row_ref[:, :keys], start, keys)
        queries = rows_ref[here, :WIDTH] * scale
        grads = grad_ref[block * QB : (block + 1) * QB, :]
        key_rows = rows_ref[:keys, WIDTH : 2 * WIDTH]
        value_rows = rows_ref[:keys, 2 * WIDTH :]
        query_grad = jnp.zeros((QB, WIDTH), f32)
        for h in range(HEADS_HERE):
            lanes = lanes_of(h)
            query = jnp.where(lanes, queries, 0).astype(bf16)
            grad = jnp.where(lanes, grads, 0).astype(bf16)
            scores = jnp.where(allowed, dot_nt(query, key_rows), masked)
            chances = jnp.exp(scores - log_ref[here, h : h + 1])
            product = chances * dot_nt(grad, value_rows)
            inner = jnp.sum(product, axis=1, keepdims=True)
            score_grad = (product - chances * inner).astype(bf16)
            query_grad = jnp.where(lanes, dot(score_grad, key_rows), query_grad)
            total_ref[:keys, :WIDTH] += dot_tn(score_grad, query)
            total_ref[:keys, WIDTH:] += dot_tn(chances.astype(bf16), grad)
        out_ref[here, :WIDTH] = (query_grad * scale).astype(bf16)
        if keys < (k + 1) * SPAN:
            pause()
    here = slice(k * SPAN, (k + 1) * SPAN)
    out_ref[here, WIDTH:] = total_ref[here, :].astype(bf16)


def add_pieces(target, left, right):
    high, across = target.shape
    step = 32768 // across

    def body(i, carry):
        lines = pl.ds(pl.multiple_of(i * step, step), step)
        target[lines, :] = (left[lines, :].astype(f32) + right[lines, :].astype(f32)).astype(bf16)
        return carry

    lax.fori_loop(0, high // step, body, 0)


class Reduction:
    def __init__(self, kind, layer, place, copies, grads, land, ends, inner, outs, credits):
        self.kind, self.layer, self.place, self.copies = kind, layer, place, copies
        self.grads, self.land, self.ends, self.inner = grads[kind], land[kind], ends[kind], inner[kind]
        self.out, self.credits = outs[kind], credits
        self.count = PIECES[kind][0]
        self.again = layer < LAYERS - 1
        self.is_end = place.dp * (3 - place.dp) == 0
        self.is_inner = place.dp * (3 - place.dp) > 0

    def home(self, which, s):
        core = self.place.cores[which]
        out, layer = self.out, self.layer
        if self.kind == 0:
            return out.at[layer, s, :, span(core * WIDTH, WIDTH)]
        if self.kind == 1:
            return out.at[layer, span(core * WIDTH, WIDTH), :]
        if self.kind == 2:
            return out.at[layer, s * (WIDTH // 4) : (s + 1) * (WIDTH // 4), span(core * D, D)]
        return out.at[layer, span(core * D + s * (D // 4), D // 4), :]

    def send(self):
        place, copies = self.place, self.copies
        if self.again:
            pl.semaphore_wait(self.credits.at[self.kind], 3)
        self.waits = {}
        self.sent = []
        for s in range(self.count):
            for j in (2, 3, 1):
                sent, got = copies.trade(
                    self.grads.at[place.rows[j], s],
                    self.land.at[j - 1, s],
                    self.land.at[j - 1, s],
                    place.to_row(j),
                )
                self.sent.append(sent)
                self.waits[j, s] = got

    def over_chips(self, s):
        place, copies = self.place, self.copies
        if s == 0:
            self.to_inner = {}
            if self.again:

                @pl.when(self.is_end)
                def _():
                    pl.semaphore_wait(self.credits.at[4 + self.kind], 1)

        for which in range(2):
            if which == 0:
                self.waits[2, s]()
                target = self.land.at[1, s]
                add_pieces(target, self.grads.at[place.row, s], target)
            else:
                self.waits[1, s]()
                self.waits[3, s]()
                target = self.land.at[2, s]
                add_pieces(target, self.land.at[0, s], target)
            copy = pltpu.make_async_remote_copy(
                target,
                self.ends.at[which, s],
                copies.sem(),
                copies.sem(),
                device_id=place.to_dp(),
                device_id_type=MESH,
            )
            self.to_inner[which, s] = copy

            @pl.when(self.is_end)
            def _():
                copy.start()

    def to_middle(self, s):
        place, copies = self.place, self.copies
        if s == 0:
            self.across = {}
            if self.again:

                @pl.when(self.is_inner)
                def _():
                    pl.semaphore_wait(self.credits.at[8 + self.kind], 1)

        for which in range(2):
            half = self.ends.at[which, s]
            copy = pltpu.make_async_remote_copy(
                half,
                self.inner.at[which, s],
                copies.sem(),
                copies.sem(),
                device_id={"dp": 3 - place.dp},
                device_id_type=MESH,
            )
            self.across[which, s] = copy

            @pl.when(self.is_inner)
            def _():
                self.to_inner[which, s].wait_recv()
                add_pieces(half, self.land.at[1 + which, s], half)
                copy.start()

        if s == self.count - 1:

            @pl.when(self.is_end)
            def _():
                for copy in self.to_inner.values():
                    copy.wait_send()

            for sent in self.sent:
                sent()
            if not self.again:
                for j in range(1, 4):
                    pl.semaphore_signal(
                        self.credits.at[self.kind],
                        inc=1,
                        device_id=place.to_row(j),
                        device_id_type=MESH,
                    )

    def back(self, s):
        place, copies = self.place, self.copies
        if s == 0:
            self.out_copies = []
        for which in range(2):
            total = self.inner.at[which, s]
            home = self.home(which, s)
            copy = pltpu.make_async_remote_copy(
                total,
                home,
                copies.sem(),
                copies.sem(),
                device_id=place.to_dp(),
                device_id_type=MESH,
            )
            here = pltpu.make_async_copy(total, home, copies.sem())
            self.out_copies.append((copy, here))

            @pl.when(self.is_inner)
            def _():
                self.across[which, s].wait_recv()
                add_pieces(total, self.ends.at[which, s], total)
                copy.start()
                here.start()

    def finish(self):
        place = self.place

        @pl.when(self.is_inner)
        def _():
            for copy in self.across.values():
                copy.wait_send()
            for copy, here in self.out_copies:
                copy.wait_send()
                here.wait()
            if not self.again:
                pl.semaphore_signal(
                    self.credits.at[4 + self.kind], inc=1, device_id=place.to_dp(), device_id_type=MESH
                )
                pl.semaphore_signal(
                    self.credits.at[8 + self.kind],
                    inc=1,
                    device_id={"dp": 3 - place.dp},
                    device_id_type=MESH,
                )

        @pl.when(self.is_end)
        def _():
            for copy, here in self.out_copies:
                copy.wait_recv()


def backward_body(*refs):
    (
        grad_in,
        wide_ref,
        seg_row_ref,
        triple_in,
        output_in,
        up_in,
        down_in_w,
        attn_in,
        rows_in,
        mixed_in,
        log_in,
        mlp_in,
        slope_in,
        active_in,
        stream_in,
        result_ref,
        input_grad_ref,
        small_out,
        triple_out,
        output_out,
        up_out,
        down_out,
        triple_w,
        output_w,
        up_w,
        down_w,
        attn,
        rows,
        mixed,
        logs,
        mlp,
        slope,
        active,
        start,
        middle,
        down_in,
        hidden,
        branch,
        rows_grad,
        mixed_grad,
        pair_total,
        grad,
        mine,
        give,
        got_core,
        chip_sum,
        got_col,
        sums,
        lines,
        line_land,
        dp_land,
        *rest,
    ) = refs
    grads, land, ends, inner = rest[0:4], rest[4:8], rest[8:12], rest[12:16]
    credits, sems = rest[16:]
    place = Place()
    copies = Copies(sems)
    core, sibling = place.core, 1 - place.core
    others = [{"dp": (place.dp + i) % 4} for i in range(1, 4)]
    greet(place, [place.to_row(1), place.to_row(2), place.to_row(3), place.to_col(), *others])
    own_lanes = span(place.row * WIDTH, WIDTH)

    def part(k, c):
        return span(k * SPAN + c * OWN, OWN)

    ready = {}

    def load(name, layer):
        source, target = {
            "triple_w": (triple_in, triple_w),
            "output_w": (output_in, output_w),
            "up_w": (up_in, up_w),
            "down_w": (down_in_w, down_w),
            "attn": (attn_in, attn),
            "rows": (rows_in, rows),
            "mixed": (mixed_in, mixed),
            "logs": (log_in, logs),
            "mlp": (mlp_in, mlp),
            "slope": (slope_in, slope),
            "active": (active_in, active),
            "start": (stream_in, start),
            "middle": (stream_in, middle),
        }[name]
        if name in ("start", "middle"):
            ready[name] = [copies.local(source.at[layer, int(name == "middle")], target).wait]
        elif name.endswith("_w"):
            ready[name] = [copies.local(source.at[layer], target).wait]
        else:
            ready[name] = [
                copies.local(source.at[layer, k], target.at[k * SPAN : (k + 1) * SPAN]).wait
                for k in range(CHUNKS)
            ]

    def need(name):
        for wait in ready.pop(name, ()):
            wait()

    first_waits = [
        copies.local(grad_in.at[k], down_in.at[part(k, core)]).wait for k in range(CHUNKS)
    ]
    top = LAYERS - 1
    for name in ("active", "down_w", "slope", "up_w", "mlp", "middle"):
        load(name, top)
    for name in ("output_w", "rows", "logs", "triple_w", "mixed", "attn", "start"):
        load(name, top)
    sums[...] = jnp.zeros_like(sums)
    lines[...] = jnp.zeros_like(lines)

    def share(target, k):
        return copies.trade(
            target.at[part(k, core)], target.at[part(k, core)], target.at[part(k, sibling)], place.to_row(1)
        )

    def columns(value):
        return jnp.sum(value.reshape(-1, 8, value.shape[1]), axis=0)

    def gain(layer, which):
        return wide_ref[2 * layer + which : 2 * layer + which + 1, :]

    sent_core = []
    sent_col, col_waits = [None] * CHUNKS, [None] * CHUNKS

    def core_free():
        while sent_core:
            sent_core.pop()()

    def start_core(stage, k):
        sent, got = copies.trade(
            give, got_core.at[stage, k], got_core.at[stage, k], place.to_row(1)
        )
        sent_core.append(sent)
        return got

    def settle(stage, k, got):
        got()
        if sent_col[k] is not None:
            sent_col[k]()

        def add(at):
            here = pl.ds(at, STRIP)
            chip_sum[k, here, :] = (mine[here, :] + got_core[stage, k, here, :].astype(f32)).astype(bf16)

        strips(OWN, add)
        sent_col[k], col_waits[k] = copies.trade(
            chip_sum.at[k], got_col.at[stage, k], got_col.at[stage, k], place.to_col()
        )

    def take_col(stage, k, layer, which, stream, target):
        col_waits[k]()
        scale = gain(layer, which)

        def back(at):
            here = pl.ds(at, STRIP)
            grad_out = chip_sum[k, here, :].astype(f32) + got_col[stage, k, here, :].astype(f32)
            normed, inv_std = norm_parts(stream[k, here, :])
            scaled = grad_out * scale
            total = grad[k, here, :] + inv_std * (
                scaled - mean_lanes(scaled) - normed * mean_lanes(scaled * normed)
            )
            low = total.astype(bf16)
            grad[k, here, :] = total
            target[pl.ds(pl.multiple_of(k * SPAN + core * OWN + at, STRIP), STRIP), :] = low
            sums[layer, which] += columns(grad_out * normed)
            sums[layer, 2 + which] += columns(grad_out)
            if which == 1:
                sums[layer, 4] += columns(low.astype(f32))
            elif layer:
                sums[layer - 1, 5] += columns(low.astype(f32))

        strips(OWN, back)

    shares = [None] * CHUNKS
    for k in reversed(range(CHUNKS)):
        first_waits[k]()
        shares[k] = share(down_in, k)
    for k in reversed(range(CHUNKS)):

        def widen(at, k=k):
            low = down_in[pl.ds(pl.multiple_of(k * SPAN + core * OWN + at, STRIP), STRIP), :]
            value = low.astype(f32)
            grad[k, pl.ds(at, STRIP), :] = value
            sums[top, 5] += columns(value)

        strips(OWN, widen)

    reductions = {
        (layer, kind): Reduction(
            kind,
            layer,
            place,
            copies,
            grads,
            land,
            ends,
            inner,
            (triple_out, output_out, up_out, down_out),
            credits,
        )
        for layer in range(LAYERS)
        for kind in range(4)
    }

    def weight_grad(layer, kind):
        if kind == 0:
            need("attn")
            for pair in range(2):
                for third in range(3):
                    value = dot_tn(
                        attn[:, pair * 512 : (pair + 1) * 512],
                        rows_grad[:, third * WIDTH : (third + 1) * WIDTH],
                    ).astype(bf16)
                    for b in range(2):
                        grads[0][2 * pair + b, third] = value[b * WIDTH : (b + 1) * WIDTH]
        elif kind == 1:
            need("mixed")
            value = dot_tn(mixed[...], branch[...]).astype(bf16)
            for b in range(4):
                grads[1][b, 0] = value[:, b * WIDTH : (b + 1) * WIDTH]
        elif kind == 2:
            need("mlp")
            for b in range(4):
                value = dot_tn(mlp[:, b * WIDTH : (b + 1) * WIDTH], hidden[...]).astype(bf16)
                for s in range(4):
                    grads[2][b, s] = value[s * (WIDTH // 4) : (s + 1) * (WIDTH // 4)]
        else:
            need("active")
            for pair in range(4):
                value = dot_tn(active[:, pair * WIDTH : (pair + 1) * WIDTH], down_in[...]).astype(bf16)
                for b in range(4):
                    grads[3][b, pair] = value[:, b * WIDTH : (b + 1) * WIDTH]
        reductions[layer, kind].send()

    def pump(point):
        for layer, kind, s, step in PLAN.get(point, ()):
            item = reductions[layer, kind]
            if step == 3:
                item.finish()
            else:
                (item.over_chips, item.to_middle, item.back)[step](s)

    landed = []

    def held(j, k):
        return span(place.rows[j] // 2 * LEN + k * SPAN + place.cores[j] * OWN, OWN)

    def to_features(k, source, target):
        mine_rows = part(k, core)
        landed.append(copies.local(source.at[mine_rows, own_lanes], target.at[held(0, k), :]).wait)
        for j in (2, 3, 1):
            sent, got = copies.trade(
                source.at[mine_rows, span(place.rows[j] * WIDTH, WIDTH)],
                target.at[held(0, k), :],
                target.at[held(j, k), :],
                place.to_row(j),
            )
            landed.extend([sent, got])

    for layer in reversed(range(LAYERS)):
        upper = layer == top
        for k in reversed(range(CHUNKS)):
            if upper:
                if k == CHUNKS - 1:
                    for i in reversed(range(CHUNKS)):
                        shares[i][1]()
                    weight_grad(layer, 3)
            else:
                pump(f"e{k}")
                need("start")
                take_col(1, k, layer + 1, 0, start, down_in)
                shares[k] = share(down_in, k)
                if k == 0:
                    load("start", layer)
                pump(f"f{k}")
            need("down_w")
            need("slope")

            def shrink(c, k=k):
                for block in range(4):
                    cols = slice(block * WIDTH, (block + 1) * WIDTH)
                    value = dot_nt(down_in[part(k, c), :], down_w[cols, :])
                    value = (value * slope[part(k, c), cols].astype(f32)).astype(bf16)
                    hidden[part(k, c), cols] = value
                    lines[layer, 8:16, cols] += columns(value.astype(f32))

            shrink(core)
            if not upper:
                shares[k][1]()
            shrink(sibling)
            need("up_w")
            core_free()
            pump(f"p{k}" if upper else f"q{k}")
            give[...] = dot_nt(hidden[part(k, sibling), :], up_w[...]).astype(bf16)
            got = start_core(0, k)
            mine[...] = dot_nt(hidden[part(k, core), :], up_w[...])
            shares[k][0]()
            pump(f"a{k}" if upper else f"g{k}")
            settle(0, k, got)
        if not upper:
            weight_grad(layer, 3)
            pump("v0")
        weight_grad(layer, 2)
        pump(f"u{layer}")
        if layer:
            for name in ("active", "down_w", "slope", "up_w", "mlp"):
                load(name, layer - 1)
        else:
            load("active", top)
            load("down_w", top)
        for k in reversed(range(CHUNKS)):
            point = f"{k}" if upper else f"{k}L"
            pump(f"b{point}")
            need("middle")
            take_col(0, k, layer, 1, middle, branch)
            shares[k] = share(branch, k)
            if k == 0:
                load("middle", layer - 1 if layer else top)
            need("output_w")

            def narrow(c, k=k):
                mixed_grad[part(0, c), :] = dot_nt(branch[part(k, c), :], output_w[...]).astype(bf16)

            narrow(core)
            need("rows")
            need("logs")
            if k == CHUNKS - 1:
                pair_total[...] = jnp.zeros_like(pair_total)
            pump(f"c{point}")
            shares[k][1]()
            narrow(sibling)
            attend_back_chunk(
                k,
                rows,
                logs,
                seg_row_ref,
                mixed_grad,
                pair_total,
                rows_grad,
                lambda point=point: pump(f"n{point}"),
            )
            need("triple_w")
            core_free()
            pump(f"m{point}")

            def project(c, k=k):
                value = dot_nt(rows_grad[part(k, c), :WIDTH], triple_w[0])
                for third in range(1, 3):
                    cols = slice(third * WIDTH, (third + 1) * WIDTH)
                    value += dot_nt(rows_grad[part(k, c), cols], triple_w[third])
                return value

            give[...] = project(sibling).astype(bf16)
            got = start_core(1, k)
            mine[...] = project(core)
            shares[k][0]()
            pump(f"d{point}")
            settle(1, k, got)
        weight_grad(layer, 1)
        weight_grad(layer, 0)
        for line, cols in ((0, slice(0, WIDTH)), (1, slice(2 * WIDTH, 3 * WIDTH))):
            value = rows_grad[:SPAN, cols].astype(f32)
            for k in range(1, CHUNKS):
                value += rows_grad[k * SPAN : (k + 1) * SPAN, cols].astype(f32)
            lines[layer, 0:1, line * WIDTH : (line + 1) * WIDTH] = jnp.sum(value, axis=0, keepdims=True)
        pump(f"w{layer}")
        if layer:
            for name in ("output_w", "rows", "logs", "triple_w", "mixed", "attn"):
                load(name, layer - 1)
    for k in reversed(range(CHUNKS)):
        pump(f"h{k}")
        need("start")
        take_col(1, k, 0, 0, start, down_in)
        to_features(k, down_in, input_grad_ref)
    need("active")
    need("down_w")
    for k in reversed(range(CHUNKS)):
        core_free()
        give[...] = dot(active[part(k, sibling), :], down_w[...]).astype(bf16)
        got = start_core(0, k)
        mine[...] = dot(active[part(k, core), :], down_w[...])
        settle(0, k, got)
    zero = jnp.zeros((1, WIDTH // 2), f32)
    for layer in range(LAYERS):
        found = [jnp.sum(sums[layer, i], axis=0, keepdims=True) for i in range(6)]
        hidden_sum = jnp.sum(lines[layer, 8:16, :], axis=0, keepdims=True)
        base = layer * LINES
        line_land[0, base : base + LINES, :] = jnp.zeros((LINES, D), f32)
        for i in range(6):
            line_land[0, base + i : base + i + 1, :] = found[i]
        for b in range(2):
            at = span((2 * core + b) * WIDTH, WIDTH)
            half = slice(b * (WIDTH // 2), (b + 1) * (WIDTH // 2))
            line_land[0, base + 6 : base + 7, at] = jnp.concatenate(
                [lines[layer, 0:1, :WIDTH][:, half], lines[layer, 0:1, WIDTH : 2 * WIDTH][:, half]], axis=1
            )
            for a in range(2):
                cols = slice((2 * b + a) * WIDTH, (2 * b + a + 1) * WIDTH)
                line_land[0, base + 7 + a : base + 8 + a, at] = hidden_sum[:, cols]
    line_waits = []
    for j in range(1, 4):
        there = span(place.rows[j] * WIDTH, WIDTH)
        sent, got = copies.trade(
            line_land.at[0, :, there],
            dp_land.at[3 + j],
            dp_land.at[3 + j],
            place.to_row(j),
        )
        copies.open.append(sent)
        line_waits.append(got)
    pump("tail1")
    need("middle")
    last_bias = wide_ref[10 + top : 11 + top, :]
    for k in reversed(range(CHUNKS)):
        col_waits[k]()

        def finish(at, k=k):
            here = pl.ds(at, STRIP)
            total = chip_sum[k, here, :].astype(f32) + got_col[0, k, here, :].astype(f32)
            branch[pl.ds(pl.multiple_of(k * SPAN + core * OWN + at, STRIP), STRIP), :] = (
                middle[k, here, :] + (total + last_bias)
            ).astype(bf16)

        strips(OWN, finish)
        to_features(k, branch, result_ref)
    pump("tail2")
    for wait in line_waits:
        wait()
    total = line_land[0, :, own_lanes]
    dp_land[place.dp] = total + dp_land[4] + dp_land[5] + dp_land[6]
    line_waits = []
    for i, device in enumerate(others):
        back = (place.dp + 3 - i) % 4
        sent, got = copies.sem(), copies.sem()
        out = pltpu.make_async_remote_copy(
            dp_land.at[place.dp], dp_land.at[place.dp], sent, got, device_id=device, device_id_type=MESH
        )
        arriving = pltpu.make_async_remote_copy(
            dp_land.at[back], dp_land.at[back], sent, got, device_id=device, device_id_type=MESH
        )
        out.start()
        copies.open.append(out.wait_send)
        line_waits.append(arriving.wait_recv)
    pump("tail3")
    for wait in line_waits:
        wait()
    small_out[...] = dp_land[0] + dp_land[1] + dp_land[2] + dp_land[3]
    for kind in (3, 2, 1, 0):
        reductions[0, kind].finish()
    core_free()
    for k in range(CHUNKS):
        sent_col[k]()
    for wait in landed:
        wait()
    copies.finish()


def backward_call(tokens_shape, grad_in, wide, seg_row, weights, saved, stream):
    units = weights[2].shape[2]
    scratch = [
        ((3, D, WIDTH), bf16),
        ((WIDTH, D), bf16),
        ((D, units), bf16),
        ((units, D), bf16),
        ((LEN, D), bf16),
        ((LEN, 3 * WIDTH), bf16),
        ((LEN, WIDTH), bf16),
        ((LEN, 128), f32),
        ((LEN, D), bf16),
        ((LEN, units), bf16),
        ((LEN, units), bf16),
        ((CHUNKS, OWN, D), f32),
        ((CHUNKS, OWN, D), f32),
        ((LEN, D), bf16),
        ((LEN, units), bf16),
        ((LEN, D), bf16),
        ((LEN, 3 * WIDTH), bf16),
        ((SPAN, WIDTH), bf16),
        ((LEN, 2 * WIDTH), f32),
        ((CHUNKS, OWN, D), f32),
        ((OWN, D), f32),
        ((OWN, D), bf16),
        ((2, CHUNKS, OWN, D), bf16),
        ((CHUNKS, OWN, D), bf16),
        ((2, CHUNKS, OWN, D), bf16),
        ((LAYERS, 6, 8, D), f32),
        ((LAYERS, 16, D), f32),
        ((1, LAYERS * LINES, D), f32),
        ((7, LAYERS * LINES, WIDTH), f32),
    ]
    for parts in (4, 3, 2, 2):
        scratch += [((parts, *piece), bf16) for piece in PIECES]
    outs = [
        (tokens_shape, bf16),
        (tokens_shape, bf16),
        ((LAYERS * LINES, WIDTH), f32),
        ((LAYERS, 3, WIDTH, 2 * WIDTH), bf16),
        ((LAYERS, 2 * WIDTH, WIDTH), bf16),
        ((LAYERS, WIDTH, 2 * units), bf16),
        ((LAYERS, 2 * units, WIDTH), bf16),
    ]
    anywhere = pl.BlockSpec(memory_space=pl.ANY)
    inside = pl.BlockSpec(memory_space=pltpu.VMEM)
    return pl.pallas_call(
        backward_body,
        out_shape=[like(*v) for v in outs],
        in_specs=[anywhere] + [inside] * 2 + [anywhere] * 12,
        out_specs=[anywhere] * 2 + [inside] + [anywhere] * 4,
        scratch_shapes=[pltpu.VMEM(*v) for v in scratch]
        + [pltpu.SemaphoreType.REGULAR((12,)), pltpu.SemaphoreType.DMA((840,))],
        compiler_params=pltpu.CompilerParams(
            collective_id=1, has_side_effects=True, vmem_limit_bytes=60 * 1024 * 1024
        ),
    )(grad_in, wide, seg_row, *weights, *saved, stream)


def pair_plan(
    tokens,
    segments,
    norm_gain,
    norm_shift,
    triple_weight,
    triple_bias,
    output_weight,
    output_bias,
    up_weight,
    up_bias,
    down_weight,
    down_bias,
    cotangent,
):
    chip = lax.axis_index("row") // 2
    seg_pack = lax.dynamic_slice_in_dim(segments, chip * LEN, LEN, 0)
    seg_col, seg_row = seg_pack[:, None], seg_pack[None, :]
    grad_in, wide, *kept, stream = forward_call(
        tokens,
        cotangent,
        (norm_gain, norm_shift, output_bias, down_bias, triple_bias, up_bias),
        seg_col,
        seg_row,
        jnp.swapaxes(triple_weight, 1, 2),
        output_weight,
        up_weight,
        down_weight,
    )
    result, input_grad, small, triple_grad, output_grad, up_grad, down_grad = backward_call(
        tokens.shape, grad_in, wide, seg_row.astype(f32), kept[:4], kept[4:], stream
    )
    small = small.reshape(LAYERS, LINES, WIDTH)
    return (
        result,
        input_grad.astype(f32),
        small[:, 0:2],
        small[:, 2:4],
        jnp.swapaxes(triple_grad, 1, 2).astype(f32),
        small[:, 6].reshape(LAYERS, 2, WIDTH // 2),
        output_grad.astype(f32),
        small[:, 4],
        up_grad.astype(f32),
        small[:, 7:9].reshape(LAYERS, 2 * WIDTH),
        down_grad.astype(f32),
        small[:, 5],
    )


def solution(mesh):
    in_specs = (
        P("dp", "row"),
        P("dp"),
        P(None, None, "row"),
        P(None, None, "row"),
        P(None, "row", None, "col"),
        P(None, None, ("col", "row")),
        P(None, "col", "row"),
        P(None, "row"),
        P(None, "row", "col"),
        P(None, ("col", "row")),
        P(None, "col", "row"),
        P(None, "row"),
        P("dp", "row"),
    )
    out_specs = (
        P("dp", "row"),
        P("dp", "row"),
        P(None, None, "row"),
        P(None, None, "row"),
        P(None, "row", None, "col"),
        P(None, None, ("col", "row")),
        P(None, "col", "row"),
        P(None, "row"),
        P(None, "row", "col"),
        P(None, ("col", "row")),
        P(None, "col", "row"),
        P(None, "row"),
    )
    shape = mesh.shape

    def on_device(*arrays):
        if fits_pairs(shape, arrays):
            return pair_plan(*arrays)
        return general_plan(*arrays)

    return jax.shard_map(
        on_device, mesh=mesh, in_specs=in_specs, out_specs=out_specs, check_vma=False
    )
```

```python
import math

import jax
import jax.numpy as jnp
from jax import lax
from jax.experimental import pallas as pl
from jax.experimental.pallas import tpu as pltpu
from jax.sharding import PartitionSpec as P

D = 1024
HD = 64
LAYERS = 2
LEN = 1024


eps = 1e-05
masked = -1000000000.0


def norm_forward(stream, gain, shift):
    totals = lax.psum((jnp.sum(stream, axis=1), jnp.sum(stream * stream, axis=1)), "row")
    center = totals[0] / D
    second = totals[1] / D - center * center
    inv_std = lax.rsqrt(second + eps)
    normed = (stream - center[:, None]) * inv_std[:, None]
    return (normed, inv_std, normed * gain + shift)


def norm_backward(grad_out, normed, inv_std, gain):
    scaled = grad_out * gain
    totals = lax.psum((jnp.sum(scaled, axis=1), jnp.sum(scaled * normed, axis=1)), "row")
    grad_in = inv_std[:, None] * (
        scaled - totals[0][:, None] / D - normed * (totals[1][:, None] / D)
    )
    return (grad_in, jnp.sum(grad_out * normed, axis=0), jnp.sum(grad_out, axis=0))


def gather_rows(block):
    return lax.all_gather(block, "row", axis=1, tiled=True)


def col_total(partial_sums):
    return lax.psum(partial_sums, "col")


def rows_back(partial_sums):
    return lax.psum_scatter(
        partial_sums.astype(jnp.bfloat16), "row", scatter_dimension=1, tiled=True
    ).astype(jnp.float32)


def in_parts(partial_sums):
    return lax.psum_scatter(partial_sums, "row", scatter_dimension=2, tiled=True)


def grad_gather(block):
    return lax.all_gather(block, "row", axis=2, tiled=True)


def pack_scores(queries, key_rows, seg_pack, scale):
    position = jnp.arange(queries.shape[0])
    allowed = (seg_pack[:, None] == seg_pack[None, :]) & (position[None, :] <= position[:, None])
    scores = (
        jnp.einsum("qhd,khd->hqk", queries, key_rows, preferred_element_type=jnp.float32) * scale
    )
    return jnp.where(allowed[None], scores, masked)


def split_packs(triple, seg_rows):
    length, three, width = triple.shape
    count = length // LEN
    return (triple.reshape(count, LEN, three, width // HD, HD), seg_rows.reshape(count, LEN))


def attend_forward(triple, seg_rows, scale):
    length, three, width = triple.shape
    packs, seg_packs = split_packs(triple, seg_rows)

    def one_pack(pieces):
        pack_rows, seg_pack = pieces
        scores = pack_scores(pack_rows[:, 0], pack_rows[:, 1], seg_pack, scale)
        row_peak = jnp.max(scores, axis=-1, keepdims=True)
        exponent = jnp.exp(scores - row_peak)
        denominator = jnp.sum(exponent, axis=-1, keepdims=True)
        soft_weights = (exponent / denominator).astype(jnp.bfloat16)
        blended = jnp.einsum(
            "hqk,khd->qhd", soft_weights, pack_rows[:, 2], preferred_element_type=jnp.float32
        )
        return (blended.astype(jnp.bfloat16), (row_peak + jnp.log(denominator))[..., 0])

    blended, log_totals = lax.map(one_pack, (packs, seg_packs))
    return (blended.reshape(length, width), log_totals)


def attend_backward(triple, seg_rows, log_totals, grad_mixed, scale):
    length, three, width = triple.shape
    packs, seg_packs = split_packs(triple, seg_rows)
    grad_packs = grad_mixed.reshape(length // LEN, LEN, width // HD, HD)

    def one_pack(pieces):
        pack_rows, seg_pack, pack_totals, grad_pack = pieces
        queries = pack_rows[:, 0]
        key_rows = pack_rows[:, 1]
        value_rows = pack_rows[:, 2]
        scores = pack_scores(queries, key_rows, seg_pack, scale)
        chances = jnp.exp(scores - pack_totals[:, :, None])
        chance_grad = jnp.einsum(
            "qhd,khd->hqk", grad_pack, value_rows, preferred_element_type=jnp.float32
        )
        inner = jnp.sum(chances * chance_grad, axis=-1, keepdims=True)
        score_grad = (chances * (chance_grad - inner)).astype(jnp.bfloat16)
        query_grad = (
            jnp.einsum("hqk,khd->qhd", score_grad, key_rows, preferred_element_type=jnp.float32)
            * scale
        )
        key_grad = (
            jnp.einsum("hqk,qhd->khd", score_grad, queries, preferred_element_type=jnp.float32)
            * scale
        )
        value_grad = jnp.einsum(
            "hqk,qhd->khd",
            chances.astype(jnp.bfloat16),
            grad_pack,
            preferred_element_type=jnp.float32,
        )
        return jnp.stack([query_grad, key_grad, value_grad], axis=1).astype(jnp.bfloat16)

    triple_rows = lax.map(one_pack, (packs, seg_packs, log_totals, grad_packs))
    return triple_rows.reshape(length, three, width)


def layer_forward(stream, weights, small, seg_rows):
    triple_w, output_w, up_w, down_w = weights
    gains, shifts, triple_b, output_b, up_b, down_b = small
    scale = 1.0 / math.sqrt(HD)
    normed_one, inv_one, attn_in = norm_forward(stream, gains[0], shifts[0])
    attn_in = attn_in.astype(jnp.bfloat16)
    triple = in_parts(
        jnp.einsum("td,dke->tke", attn_in, triple_w, preferred_element_type=jnp.float32)
    )
    bias_rows = jnp.stack([triple_b[0], jnp.zeros_like(triple_b[0]), triple_b[1]])
    triple = (triple + bias_rows).astype(jnp.bfloat16)
    mixed, log_totals = attend_forward(triple, seg_rows, scale)
    mixed_full = gather_rows(mixed)
    middle = stream + (
        col_total(jnp.dot(mixed_full, output_w, preferred_element_type=jnp.float32)) + output_b
    )
    normed_two, inv_two, mlp_in = norm_forward(middle, gains[1], shifts[1])
    mlp_in = mlp_in.astype(jnp.bfloat16)
    hidden_pre = (
        in_parts(jnp.dot(mlp_in, up_w, preferred_element_type=jnp.float32)[:, None, :])[:, 0] + up_b
    )
    active = jax.nn.gelu(hidden_pre, approximate=True).astype(jnp.bfloat16)
    active_full = gather_rows(active)
    after = middle + (
        col_total(jnp.dot(active_full, down_w, preferred_element_type=jnp.float32)) + down_b
    )
    saved = (
        normed_one,
        inv_one,
        attn_in,
        triple,
        log_totals,
        mixed_full,
        normed_two,
        inv_two,
        mlp_in,
        hidden_pre,
        active_full,
        None,
    )
    return (after, saved)


def layer_backward(grad, saved, weights, gains, seg_rows):
    (
        normed_one,
        inv_one,
        attn_rows,
        triple,
        log_totals,
        mixed_full,
        normed_two,
        inv_two,
        mlp_rows,
        hidden_pre,
        active_full,
        columns_in,
    ) = saved
    triple_w, output_w, up_w, down_w = weights
    scale = 1.0 / math.sqrt(HD)
    down_in = grad.astype(jnp.bfloat16)
    down_bias_grad = jnp.sum(down_in, axis=0, dtype=jnp.float32)
    down_grad = jnp.einsum("tf,td->fd", active_full, down_in, preferred_element_type=jnp.float32)
    active_grad = rows_back(
        jnp.einsum("td,fd->tf", down_in, down_w, preferred_element_type=jnp.float32)
    )
    gelu_pull = jax.vjp(lambda value: jax.nn.gelu(value, approximate=True), hidden_pre)[1]
    hidden_grad = gelu_pull(active_grad)[0].astype(jnp.bfloat16)
    up_bias_grad = jnp.sum(hidden_grad, axis=0, dtype=jnp.float32)
    hidden_rows = grad_gather(hidden_grad[:, None, :])[:, 0]
    up_grad = jnp.einsum("td,tf->df", mlp_rows, hidden_rows, preferred_element_type=jnp.float32)
    mlp_grad = col_total(
        jnp.einsum("tf,df->td", hidden_rows, up_w, preferred_element_type=jnp.float32)
    )
    norm_two_grad, gain_two, shift_two = norm_backward(mlp_grad, normed_two, inv_two, gains[1])
    middle_grad = grad + norm_two_grad
    branch_grad = middle_grad.astype(jnp.bfloat16)
    output_bias_grad = jnp.sum(branch_grad, axis=0, dtype=jnp.float32)
    output_grad = jnp.einsum(
        "td,te->de", mixed_full, branch_grad, preferred_element_type=jnp.float32
    )
    mixed_grad = rows_back(
        jnp.einsum("te,de->td", branch_grad, output_w, preferred_element_type=jnp.float32)
    ).astype(jnp.bfloat16)
    triple_rows = attend_backward(triple, seg_rows, log_totals, mixed_grad, scale)
    triple_bias_grad = jnp.sum(triple_rows[:, 0::2], axis=0, dtype=jnp.float32)
    full_rows = grad_gather(triple_rows)
    triple_grad = jnp.einsum(
        "td,tke->dke", attn_rows, full_rows, preferred_element_type=jnp.float32
    )
    attn_grad = col_total(
        jnp.einsum("tke,dke->td", full_rows, triple_w, preferred_element_type=jnp.float32)
    )
    norm_one_grad, gain_one, shift_one = norm_backward(attn_grad, normed_one, inv_one, gains[0])
    start_grad = middle_grad + norm_one_grad
    terms = (
        jnp.stack([gain_one, gain_two]),
        jnp.stack([shift_one, shift_two]),
        triple_grad,
        triple_bias_grad,
        output_grad,
        output_bias_grad,
        up_grad,
        up_bias_grad,
        down_grad,
        down_bias_grad,
    )
    return (start_grad, terms)


def general_plan(
    tokens,
    segments,
    norm_gain,
    norm_shift,
    triple_weight,
    triple_bias,
    output_weight,
    output_bias,
    up_weight,
    up_bias,
    down_weight,
    down_bias,
    cotangent,
):

    def weights_of(layer_id):
        return (
            triple_weight[layer_id],
            output_weight[layer_id],
            up_weight[layer_id],
            down_weight[layer_id],
        )

    def small_of(layer_id):
        return (
            norm_gain[layer_id].astype(jnp.float32),
            norm_shift[layer_id].astype(jnp.float32),
            triple_bias[layer_id].astype(jnp.float32),
            output_bias[layer_id].astype(jnp.float32),
            up_bias[layer_id].astype(jnp.float32),
            down_bias[layer_id].astype(jnp.float32),
        )

    stream = tokens.astype(jnp.float32)
    stored = []
    for layer_id in range(LAYERS):
        stream, saved = layer_forward(stream, weights_of(layer_id), small_of(layer_id), segments)
        stored.append(saved)
    result = stream.astype(jnp.bfloat16)
    grad = cotangent.astype(jnp.float32)
    summed = [None] * LAYERS
    for layer_id in reversed(range(LAYERS)):
        grad, terms = layer_backward(
            grad, stored[layer_id], weights_of(layer_id), small_of(layer_id)[0], segments
        )
        summed[layer_id] = (
            lax.psum(terms[0].astype(jnp.bfloat16), "dp").astype(jnp.float32),
            lax.psum(terms[1].astype(jnp.bfloat16), "dp").astype(jnp.float32),
            lax.psum(terms[2].astype(jnp.bfloat16), "dp").astype(jnp.float32),
            lax.psum(terms[3].astype(jnp.bfloat16), "dp").astype(jnp.float32),
            lax.psum(terms[4].astype(jnp.bfloat16), "dp").astype(jnp.float32),
            lax.psum(terms[5].astype(jnp.bfloat16), "dp").astype(jnp.float32),
            lax.psum(terms[6].astype(jnp.bfloat16), "dp").astype(jnp.float32),
            lax.psum(terms[7].astype(jnp.bfloat16), "dp").astype(jnp.float32),
            lax.psum(terms[8].astype(jnp.bfloat16), "dp").astype(jnp.float32),
            lax.psum(terms[9].astype(jnp.bfloat16), "dp").astype(jnp.float32),
        )
    stacks = [
        jnp.stack([summed[layer_id][member] for layer_id in range(LAYERS)]) for member in range(10)
    ]
    return (
        result,
        grad,
        stacks[0],
        stacks[1],
        stacks[2],
        stacks[3],
        stacks[4],
        stacks[5],
        stacks[6],
        stacks[7],
        stacks[8],
        stacks[9],
    )


f32 = jnp.float32
bf16 = jnp.bfloat16
CHUNKS = 2
SPAN = LEN // CHUNKS
OWN = SPAN // 2
WIDTH = D // 4
QB = 256


def fits_pairs(shape, arrays):
    return (
        shape["row"] == 4
        and shape["col"] == 2
        and shape["dp"] == 4
        and arrays[0].shape == (2 * LEN, WIDTH)
        and arrays[8].shape[2] == 8 * WIDTH
    )


def dot(a, b):
    return lax.dot_general(a, b, (((1,), (0,)), ((), ())), preferred_element_type=f32)


def dot_nt(a, b):
    return lax.dot_general(a, b, (((1,), (1,)), ((), ())), preferred_element_type=f32)


def dot_tn(a, b):
    return lax.dot_general(a, b, (((0,), (0,)), ((), ())), preferred_element_type=f32)


def like(shape, kind):
    return jax.ShapeDtypeStruct(shape, kind)


def mean_lanes(v):
    return jnp.sum(v, axis=1, keepdims=True) * (1.0 / D)


def norm_parts(v):
    center = mean_lanes(v)
    second = mean_lanes(v * v) - center * center
    inv_std = lax.rsqrt(second + eps)
    return (v - center) * inv_std, inv_std


GELU = math.sqrt(2.0 / math.pi)


MESH = pl.DeviceIdType.MESH
HEADS_HERE = WIDTH // HD
SMALL = 24
SEG = 64


class Place:
    def __init__(self):
        self.row = lax.axis_index("row")
        self.col = lax.axis_index("col")
        self.dp = lax.axis_index("dp")
        self.core = self.row % 2
        self.chip = self.row // 2
        self.half = self.dp % 2
        sibling = self.row + 1 - 2 * self.core
        self.rows = [self.row, sibling, (self.row + 2) % 4, (sibling + 2) % 4]
        self.cores = [self.core, 1 - self.core, self.core, 1 - self.core]

    def to_row(self, j):
        return {"row": self.rows[j]}

    def to_col(self):
        return {"col": 1 - self.col}

    def to_dp(self):
        return {"dp": self.dp + 1 - 2 * self.half}


class Copies:
    def __init__(self, sems):
        self.sems = sems
        self.used = 0
        self.open = []

    def sem(self):
        self.used += 1
        return self.sems.at[self.used - 1]

    def local(self, src, dst):
        copy = pltpu.make_async_copy(src, dst, self.sem())
        copy.start()
        return copy

    def save(self, src, dst):
        self.open.append(self.local(src, dst).wait)

    def trade(self, src, dst, landing, device):
        sent, got = self.sem(), self.sem()
        out = pltpu.make_async_remote_copy(src, dst, sent, got, device_id=device, device_id_type=MESH)
        back = pltpu.make_async_remote_copy(
            landing, landing, sent, got, device_id=device, device_id_type=MESH
        )
        out.start()
        return out.wait_send, back.wait_recv

    def finish(self):
        for wait in self.open:
            wait()


def greet(place, devices):
    barrier = pltpu.get_barrier_semaphore()
    for device in devices:
        pl.semaphore_signal(barrier, inc=1, device_id=device, device_id_type=MESH)
    pl.semaphore_wait(barrier, len(devices))


def span(start, size):
    return pl.ds(pl.multiple_of(start, size), size)


def weight_cuts(kind, layer, wide, local):
    w = WIDTH
    if kind == 0:

        def source(core, half):
            rows = slice(None) if half is None else span(half * (w // 2), w // 2)
            return local.at[layer, :, rows, span(core * w, w)]

        def target(row, half):
            rows = span(row * w, w) if half is None else span(row * w + half * (w // 2), w // 2)
            return wide.at[layer, :, rows, :]

    elif kind == 2:
        units = wide.shape[2]

        def source(core, half):
            rows = slice(None) if half is None else span(half * (w // 2), w // 2)
            return local.at[layer, rows, span(core * units, units)]

        def target(row, half):
            rows = span(row * w, w) if half is None else span(row * w + half * (w // 2), w // 2)
            return wide.at[layer, rows, :]

    else:
        high = wide.shape[1]

        def source(core, half):
            if half is None:
                return local.at[layer, span(core * high, high), :]
            return local.at[layer, span(core * high + half * (high // 2), high // 2), :]

        def target(row, half):
            rows = slice(None) if half is None else span(half * (high // 2), high // 2)
            return wide.at[layer, rows, span(row * w, w)]

    return source, target


STRIP = 64


def strips(count, body):
    def step(i, carry):
        body(pl.multiple_of(i * STRIP, STRIP))
        return carry

    lax.fori_loop(0, count // STRIP, step, 0)


def causal(seg_col, seg_row, start, keys):
    query = lax.broadcasted_iota(jnp.int32, (QB, keys), 0) + start
    key = lax.broadcasted_iota(jnp.int32, (QB, keys), 1)
    return (seg_col == seg_row) & (key <= query)


def lanes_of(h):
    lane = lax.broadcasted_iota(jnp.int32, (1, WIDTH), 1)
    return (lane >= h * HD) & (lane < (h + 1) * HD)


def attend_chunk(k, triples, seg_col_ref, seg_row_ref, kv_ref, mixed_ref, log_ref):
    scale = 1.0 / math.sqrt(HD)
    kv_ref[k * SPAN : (k + 1) * SPAN, :] = triples[k][:, WIDTH:]
    for block in range(SPAN // QB):
        rows = slice(block * QB, (block + 1) * QB)
        start = k * SPAN + block * QB
        keys = start + QB
        allowed = causal(seg_col_ref[start : start + QB, :], seg_row_ref[:, :keys], start, keys)
        queries = triples[k][rows, :WIDTH] * scale
        key_rows = kv_ref[:keys, :WIDTH]
        value_rows = kv_ref[:keys, WIDTH:]
        blended = jnp.zeros((QB, WIDTH), f32)
        for h in range(HEADS_HERE):
            lanes = lanes_of(h)
            scores = dot_nt(jnp.where(lanes, queries, 0).astype(bf16), key_rows)
            scores = jnp.where(allowed, scores, masked)
            peak = jnp.max(scores, axis=1, keepdims=True)
            exponent = jnp.exp(scores - peak)
            total = jnp.sum(exponent, axis=1, keepdims=True)
            soft = (exponent * (1.0 / total)).astype(bf16)
            blended = jnp.where(lanes, dot(soft, value_rows), blended)
            log_ref[rows, h : h + 1] = peak + jnp.log(total)
        log_ref[rows, SEG : SEG + 1] = seg_col_ref[start : start + QB, :].astype(f32)
        mixed_ref[rows, :] = blended.astype(bf16)


def forward_body(*refs):
    (
        tokens_ref,
        cotangent_ref,
        gain_in,
        shift_in,
        output_bias_in,
        down_bias_in,
        triple_bias_in,
        up_bias_in,
        seg_col_ref,
        seg_row_ref,
        triple_in,
        output_in,
        up_in,
        down_in,
        grad_ref,
        wide_out,
        triple_out,
        output_out,
        up_out,
        down_out,
        attn_out,
        rows_out,
        mixed_out,
        log_out,
        mlp_out,
        slope_out,
        active_out,
        stream_out,
        triple_w,
        output_w,
        up_w,
        down_w,
        attn,
        rows,
        mixed,
        logs,
        mlp,
        slope,
        active,
        stream,
        taken,
        wide,
        kv,
        mine,
        give,
        got_core,
        chip_sum,
        got_col,
        small_ref,
        sems,
    ) = refs
    place = Place()
    copies = Copies(sems)
    core, sibling = place.core, 1 - place.core
    greet(place, [place.to_row(1), place.to_row(2), place.to_row(3), place.to_col(), place.to_dp()])

    own_lanes = span(place.row * WIDTH, WIDTH)

    def held(j, k):
        return span(place.rows[j] // 2 * LEN + k * SPAN + place.cores[j] * OWN, OWN)

    def part(c):
        return span(c * OWN, OWN)

    small_ref[...] = jnp.zeros_like(small_ref)
    for layer in range(LAYERS):
        small_ref[2 * layer : 2 * layer + 2, :] = gain_in[layer].astype(f32)
        small_ref[4 + 2 * layer : 6 + 2 * layer, :] = shift_in[layer].astype(f32)
        for which in range(2):
            cols = slice(which * (WIDTH // 2), (which + 1) * (WIDTH // 2))
            value = triple_bias_in[layer].astype(f32)
            small_ref[12 + layer : 13 + layer, cols] = value[which : which + 1]
            value = up_bias_in[...].astype(f32)
            at = 14 + 2 * layer + which
            small_ref[at : at + 1, :] = value[layer : layer + 1, which * WIDTH : (which + 1) * WIDTH]
    small_ref[8:10, :] = output_bias_in[...].astype(f32)
    small_ref[10:12, :] = down_bias_in[...].astype(f32)
    small_waits = []
    copy = copies.local(small_ref, wide.at[:, own_lanes])
    small_waits.append(copy.wait)
    for j in range(1, 4):
        sent, got = copies.trade(
            small_ref,
            wide.at[:, own_lanes],
            wide.at[:, span(place.rows[j] * WIDTH, WIDTH)],
            place.to_row(j),
        )
        copies.open.append(sent)
        small_waits.append(got)
    token_waits = [[] for _ in range(CHUNKS)]

    def scatter_in(block_ref, target, k, waits):
        waits.append(copies.local(block_ref.at[held(0, k), :], target.at[k, :, own_lanes]).wait)
        for j in range(1, 4):
            sent, got = copies.trade(
                block_ref.at[held(j, k), :],
                target.at[k, :, own_lanes],
                target.at[k, :, span(place.rows[j] * WIDTH, WIDTH)],
                place.to_row(j),
            )
            copies.open.append(sent)
            waits.append(got)

    arrivals, ready_waits = {}, {}

    def send_weight(layer, kind):
        local = (triple_in, output_in, up_in, down_in)[kind]
        whole = (triple_w, output_w, up_w, down_w)[kind]
        source, target = weight_cuts(kind, layer, whole, local)
        here = []
        for j in (2, 3):
            sent, got = copies.trade(
                source(place.cores[j], place.half),
                target(place.row, place.half),
                target(place.rows[j], place.half),
                place.to_row(j),
            )
            copies.open.append(sent)
            here.append((got, target(place.rows[j], place.half), target(place.rows[j], 1 - place.half)))
        arrivals[layer, kind] = here
        sent, got = copies.trade(
            source(sibling, None),
            target(place.row, None),
            target(place.rows[1], None),
            place.to_row(1),
        )
        copies.open.append(sent)
        own = copies.local(source(core, None), target(place.row, None))
        ready_waits[layer, kind] = [got, own.wait]

    relays = [
        (layer, kind, i) for layer in range(LAYERS) for kind in range(4) for i in range(2)
    ]

    def pump(count):
        for _ in range(count):
            layer, kind, i = relays.pop(0)
            got, arrived, missing = arrivals[layer, kind][i]
            got()
            sent, back = copies.trade(arrived, arrived, missing, place.to_dp())
            copies.open.append(sent)
            ready_waits[layer, kind].append(back)

    def ready_weight(layer, kind):
        for wait in ready_waits[layer, kind]:
            wait()
        whole = (triple_w, output_w, up_w, down_w)[kind]
        out = (triple_out, output_out, up_out, down_out)[kind]
        copies.save(whole.at[layer], out.at[layer])

    scatter_in(tokens_ref, taken, 0, token_waits[0])
    send_weight(0, 0)
    scatter_in(tokens_ref, taken, 1, token_waits[1])
    for layer, kind in ((0, 1), (0, 2), (0, 3), (1, 0), (1, 1), (1, 2), (1, 3)):
        send_weight(layer, kind)
    grad_waits = []
    for k in range(CHUNKS):
        scatter_in(cotangent_ref, grad_ref, k, grad_waits)

    for wait in small_waits:
        wait()
    copies.save(wide, wide_out)

    def gain(layer, which):
        return wide[2 * layer + which : 2 * layer + which + 1, :]

    def shift(layer, which):
        return wide[4 + 2 * layer + which : 5 + 2 * layer + which, :]

    def output_bias(layer):
        return wide[8 + layer : 9 + layer, :]

    def down_bias(layer):
        return wide[10 + layer : 11 + layer, :]

    def of_core(line, start, size):
        return wide[line : line + 1, span(start, size)]

    def triple_bias(layer, which):
        at = 2 * core * WIDTH + which * (WIDTH // 2)
        size = WIDTH // 2
        return jnp.concatenate(
            [of_core(12 + layer, at, size), of_core(12 + layer, at + WIDTH, size)], axis=1
        )

    def up_bias(layer):
        line, at = 14 + 2 * layer, 2 * core * WIDTH
        return jnp.concatenate(
            [of_core(line + a, at + b * WIDTH, WIDTH) for b in range(2) for a in range(2)], axis=1
        )

    def norm_to(value, layer, which, target, at):
        center = jnp.mean(value, axis=1, keepdims=True)
        second = jnp.mean(value * value, axis=1, keepdims=True) - center * center
        normed = (value - center) * lax.rsqrt(second + eps)
        target[pl.ds(pl.multiple_of(core * OWN + at, STRIP), STRIP), :] = (
            normed * gain(layer, which) + shift(layer, which)
        ).astype(bf16)

    def share(target):
        return copies.trade(target.at[part(core)], target.at[part(core)], target.at[part(sibling)], place.to_row(1))

    sent_core, sent_col = [None] * CHUNKS, [None] * CHUNKS
    col_waits = [None] * CHUNKS
    saves = {}

    def settle(stage, k, got):
        got()
        if sent_col[k] is not None:
            sent_col[k]()

        def add(at):
            lines = pl.ds(at, STRIP)
            chip_sum[k, lines, :] = (
                mine[k, lines, :] + got_core[stage, k, lines, :].astype(f32)
            ).astype(bf16)

        strips(OWN, add)
        sent_col[k], col_waits[k] = copies.trade(
            chip_sum.at[k], got_col.at[stage, k], got_col.at[stage, k], place.to_col()
        )

    def start_core(stage, k):
        sent, got = copies.trade(
            give.at[k], got_core.at[stage, k], got_core.at[stage, k], place.to_row(1)
        )
        sent_core[k] = sent
        return got

    def take_col(stage, k, layer, bias, after_ref):
        col_waits[k]()

        def add(at):
            lines = pl.ds(at, STRIP)
            total = chip_sum[k, lines, :].astype(f32) + got_col[stage, k, lines, :].astype(f32)
            value = stream[stage, k, lines, :] + (total + bias)
            stream[1 - stage, k, lines, :] = value
            after_ref(value, at)

        strips(OWN, add)

    shares = [None] * CHUNKS
    for k in range(CHUNKS):
        for wait in token_waits[k]:
            wait()
        def first(at, k=k):
            value = taken[k, pl.ds(at, STRIP), :].astype(f32)
            stream[0, k, pl.ds(at, STRIP), :] = value
            norm_to(value, 0, 0, attn.at[0, k], at)

        strips(OWN, first)
        saves[0, 0, k] = copies.local(stream.at[0, k], stream_out.at[0, 0, k])
        shares[k] = share(attn.at[0, k])
        if k == 0:
            pump(2)

    for layer in range(LAYERS):
        for k in range(CHUNKS):
            if layer:
                if k == 0:
                    pump(1)
                saves.pop((layer - 1, 0, k)).wait()
                take_col(
                    1, k, layer, down_bias(layer - 1), lambda v, at, k=k: norm_to(v, layer, 0, attn.at[layer, k], at)
                )
                saves[layer, 0, k] = copies.local(stream.at[0, k], stream_out.at[layer, 0, k])
                shares[k] = share(attn.at[layer, k])
            if k == 0:
                ready_weight(layer, 0)
            bias = [triple_bias(layer, 0), None, triple_bias(layer, 1)]

            def project(c, k=k, bias=bias):
                for third in range(3):
                    value = dot(attn[layer, k, part(c), :], triple_w[layer, third])
                    if bias[third] is not None:
                        value = value + bias[third]
                    rows[layer, k, part(c), third * WIDTH : (third + 1) * WIDTH] = value.astype(bf16)

            project(core)
            sent, got = shares[k]
            got()
            project(sibling)
            if layer == 0 and k == 0:
                pump(2)
            attend_chunk(
                k,
                [rows.at[layer, i] for i in range(k + 1)],
                seg_col_ref,
                seg_row_ref,
                kv,
                mixed.at[layer, k],
                logs.at[layer, k],
            )
            if layer or k:
                pump(1)
            if k == 0:
                ready_weight(layer, 1)
            if sent_core[k] is not None:
                sent_core[k]()
            give[k] = dot(mixed[layer, k, part(sibling), :], output_w[layer]).astype(bf16)
            got = start_core(0, k)
            mine[k] = dot(mixed[layer, k, part(core), :], output_w[layer])
            if layer == 0 and k == 0:
                pump(1)
            sent()
            copies.save(attn.at[layer, k], attn_out.at[layer, k])
            copies.save(rows.at[layer, k], rows_out.at[layer, k])
            copies.save(mixed.at[layer, k], mixed_out.at[layer, k])
            copies.save(logs.at[layer, k], log_out.at[layer, k])
            settle(0, k, got)
            if k:
                pump(1)
        for k in range(CHUNKS):
            if layer:
                saves.pop((layer - 1, 1, k)).wait()
            elif k:
                pump(1)
            take_col(
                0, k, layer, output_bias(layer), lambda v, at, k=k: norm_to(v, layer, 1, mlp.at[layer, k], at)
            )
            saves[layer, 1, k] = copies.local(stream.at[1, k], stream_out.at[layer, 1, k])
            shares[k] = share(mlp.at[layer, k])
            if k == 0:
                ready_weight(layer, 2)
            bias = up_bias(layer)

            def widen(c, k=k, bias=bias):
                for block in range(4):
                    cols = slice(block * WIDTH, (block + 1) * WIDTH)
                    pre = dot(mlp[layer, k, part(c), :], up_w[layer, :, cols]) + bias[:, cols]
                    square = pre * pre
                    curve = jnp.tanh(GELU * (pre + 0.044715 * (square * pre)))
                    upper = 0.5 * (1.0 + curve)
                    active[layer, k, part(c), cols] = (pre * upper).astype(bf16)
                    slope[layer, k, part(c), cols] = (
                        upper
                        + (0.5 * GELU) * pre * (1.0 - curve * curve) * (1.0 + (3.0 * 0.044715) * square)
                    ).astype(bf16)

            widen(core)
            sent, got = shares[k]
            got()
            widen(sibling)
            if layer + 1 < LAYERS:
                if k == 0:
                    pump(1)
                    ready_weight(layer, 3)
                sent_core[k]()
                give[k] = dot(active[layer, k, part(sibling), :], down_w[layer]).astype(bf16)
                got = start_core(1, k)
                mine[k] = dot(active[layer, k, part(core), :], down_w[layer])
            sent()
            copies.save(mlp.at[layer, k], mlp_out.at[layer, k])
            copies.save(slope.at[layer, k], slope_out.at[layer, k])
            copies.save(active.at[layer, k], active_out.at[layer, k])
            if layer + 1 < LAYERS:
                settle(1, k, got)
                pump(k + 1)
    ready_weight(LAYERS - 1, 3)
    for k in range(CHUNKS):
        saves.pop((LAYERS - 1, 0, k)).wait()
        saves.pop((LAYERS - 1, 1, k)).wait()
        sent_core[k]()
        sent_col[k]()
    for wait in grad_waits:
        wait()
    copies.finish()


def forward_call(tokens, cotangent, small_params, seg_col, seg_row, triple_w, output_w, up_w, down_w):
    units = up_w.shape[2] // 2
    per_layer = [
        ((LAYERS, CHUNKS, SPAN, D), bf16),
        ((LAYERS, CHUNKS, SPAN, 3 * WIDTH), bf16),
        ((LAYERS, CHUNKS, SPAN, WIDTH), bf16),
        ((LAYERS, CHUNKS, SPAN, 128), f32),
        ((LAYERS, CHUNKS, SPAN, D), bf16),
        ((LAYERS, CHUNKS, SPAN, units), bf16),
        ((LAYERS, CHUNKS, SPAN, units), bf16),
    ]
    wide = [
        ((LAYERS, 3, D, WIDTH), bf16),
        ((LAYERS, WIDTH, D), bf16),
        ((LAYERS, D, units), bf16),
        ((LAYERS, units, D), bf16),
    ]
    outs = [
        ((CHUNKS, OWN, D), bf16),
        ((SMALL, D), f32),
        *wide,
        *per_layer,
        ((LAYERS, 2, CHUNKS, OWN, D), f32),
    ]
    scratch = [
        *wide,
        *per_layer,
        ((2, CHUNKS, OWN, D), f32),
        ((CHUNKS, OWN, D), bf16),
        ((SMALL, D), f32),
        ((LEN, 2 * WIDTH), bf16),
        ((CHUNKS, OWN, D), f32),
        ((CHUNKS, OWN, D), bf16),
        ((2, CHUNKS, OWN, D), bf16),
        ((CHUNKS, OWN, D), bf16),
        ((2, CHUNKS, OWN, D), bf16),
        ((SMALL, WIDTH), f32),
    ]
    anywhere = pl.BlockSpec(memory_space=pl.ANY)
    inside = pl.BlockSpec(memory_space=pltpu.VMEM)
    return pl.pallas_call(
        forward_body,
        out_shape=[like(*v) for v in outs],
        in_specs=[anywhere] * 2 + [inside] * 8 + [anywhere] * 4,
        out_specs=[anywhere] * len(outs),
        scratch_shapes=[pltpu.VMEM(*v) for v in scratch] + [pltpu.SemaphoreType.DMA((320,))],
        compiler_params=pltpu.CompilerParams(
            collective_id=0, has_side_effects=True, vmem_limit_bytes=60 * 1024 * 1024
        ),
    )(tokens, cotangent, *small_params, seg_col, seg_row, triple_w, output_w, up_w, down_w)


PIECES = ((3, WIDTH, WIDTH), (1, WIDTH, WIDTH), (4, WIDTH // 4, D), (4, D // 4, WIDTH))

PLAN = {
    "a1": ((1, 3, 0, 0),),
    "a0": ((1, 3, 1, 0), (1, 3, 0, 1)),
    "u1": ((1, 3, 2, 0),),
    "c1": ((1, 3, 1, 1), (1, 3, 0, 2), (1, 3, 3, 0)),
    "m1": ((1, 3, 2, 1), (1, 2, 0, 0), (1, 3, 1, 2), (1, 3, 3, 1), (1, 2, 1, 0)),
    "c0": ((1, 2, 2, 0), (1, 3, 2, 2), (1, 2, 0, 1)),
    "m0": ((1, 2, 3, 0), (1, 3, 3, 2), (1, 2, 1, 1)),
    "w1": ((1, 2, 0, 2), (1, 2, 2, 1)),
    "f1": ((1, 3, 0, 3),),
    "g1": ((1, 1, 0, 0), (1, 2, 1, 2), (1, 2, 3, 1)),
    "e0": ((1, 0, 0, 0), (1, 2, 2, 2)),
    "g0": ((1, 1, 0, 1), (1, 0, 1, 0), (1, 2, 3, 2)),
    "v0": ((1, 0, 0, 1), (1, 0, 2, 0)),
    "u0": ((1, 1, 0, 2), (1, 2, 0, 3), (1, 0, 1, 1)),
    "c1L": ((0, 3, 0, 0), (1, 0, 0, 2)),
    "m1L": ((1, 1, 0, 3), (1, 0, 2, 1), (0, 3, 1, 0), (1, 0, 1, 2), (0, 3, 0, 1), (0, 3, 2, 0)),
    "m0L": ((1, 0, 2, 2), (0, 3, 1, 1), (0, 3, 3, 0), (0, 3, 0, 2), (0, 3, 2, 1), (0, 2, 0, 0)),
    "w0": ((0, 2, 1, 0), (1, 0, 0, 3)),
    "h1": ((0, 3, 1, 2), (0, 3, 3, 1)),
    "h0": ((0, 2, 2, 0), (0, 3, 2, 2), (0, 2, 0, 1), (0, 2, 3, 0), (0, 3, 3, 2), (0, 2, 1, 1)),
    "tail1": ((0, 1, 0, 0), (0, 2, 2, 1), (0, 2, 0, 2), (0, 0, 0, 0), (0, 2, 3, 1), (0, 2, 1, 2), (0, 0, 1, 0)),
    "tail2": ((0, 1, 0, 1), (0, 2, 2, 2), (0, 0, 2, 0), (0, 0, 0, 1), (0, 2, 3, 2), (0, 0, 1, 1)),
    "tail3": ((0, 1, 0, 2), (0, 0, 2, 1), (0, 0, 0, 2), (0, 0, 1, 2), (0, 0, 2, 2)),
}
LINES = 16


def attend_back_chunk(
    k, rows_ref, log_ref, seg_row_ref, grad_ref, total_ref, out_ref
):
    scale = 1.0 / math.sqrt(HD)
    for block in range(SPAN // QB):
        start = k * SPAN + block * QB
        keys = start + QB
        here = slice(start, keys)
        allowed = causal(log_ref[here, SEG : SEG + 1], seg_row_ref[:, :keys], start, keys)
        queries = rows_ref[here, :WIDTH] * scale
        grads = grad_ref[block * QB : (block + 1) * QB, :]
        key_rows = rows_ref[:keys, WIDTH : 2 * WIDTH]
        value_rows = rows_ref[:keys, 2 * WIDTH :]
        query_grad = jnp.zeros((QB, WIDTH), f32)
        for h in range(HEADS_HERE):
            lanes = lanes_of(h)
            query = jnp.where(lanes, queries, 0).astype(bf16)
            grad = jnp.where(lanes, grads, 0).astype(bf16)
            scores = jnp.where(allowed, dot_nt(query, key_rows), masked)
            chances = jnp.exp(scores - log_ref[here, h : h + 1])
            product = chances * dot_nt(grad, value_rows)
            inner = jnp.sum(product, axis=1, keepdims=True)
            score_grad = (product - chances * inner).astype(bf16)
            query_grad = jnp.where(lanes, dot(score_grad, key_rows), query_grad)
            total_ref[:keys, :WIDTH] += dot_tn(score_grad, query)
            total_ref[:keys, WIDTH:] += dot_tn(chances.astype(bf16), grad)
        out_ref[here, :WIDTH] = (query_grad * scale).astype(bf16)
    here = slice(k * SPAN, (k + 1) * SPAN)
    out_ref[here, WIDTH:] = total_ref[here, :].astype(bf16)


def add_pieces(target, left, right):
    high, across = target.shape
    step = 32768 // across

    def body(i, carry):
        lines = pl.ds(pl.multiple_of(i * step, step), step)
        target[lines, :] = (left[lines, :].astype(f32) + right[lines, :].astype(f32)).astype(bf16)
        return carry

    lax.fori_loop(0, high // step, body, 0)


class Reduction:
    def __init__(self, kind, layer, place, copies, grads, land, ends, inner, outs, credits):
        self.kind, self.layer, self.place, self.copies = kind, layer, place, copies
        self.grads, self.land, self.ends, self.inner = grads[kind], land[kind], ends[kind], inner[kind]
        self.out, self.credits = outs[kind], credits
        self.count = PIECES[kind][0]
        self.again = layer < LAYERS - 1
        self.is_end = place.dp * (3 - place.dp) == 0
        self.is_inner = place.dp * (3 - place.dp) > 0

    def home(self, which, s):
        core = self.place.cores[which]
        out, layer = self.out, self.layer
        if self.kind == 0:
            return out.at[layer, s, :, span(core * WIDTH, WIDTH)]
        if self.kind == 1:
            return out.at[layer, span(core * WIDTH, WIDTH), :]
        if self.kind == 2:
            return out.at[layer, s * (WIDTH // 4) : (s + 1) * (WIDTH // 4), span(core * D, D)]
        return out.at[layer, span(core * D + s * (D // 4), D // 4), :]

    def send(self):
        place, copies = self.place, self.copies
        if self.again:
            pl.semaphore_wait(self.credits.at[self.kind], 3)
        self.waits = {}
        self.sent = []
        for s in range(self.count):
            for j in (2, 3, 1):
                sent, got = copies.trade(
                    self.grads.at[place.rows[j], s],
                    self.land.at[j - 1, s],
                    self.land.at[j - 1, s],
                    place.to_row(j),
                )
                self.sent.append(sent)
                self.waits[j, s] = got

    def over_chips(self, s):
        place, copies = self.place, self.copies
        if s == 0:
            self.to_inner = {}
            if self.again:

                @pl.when(self.is_end)
                def _():
                    pl.semaphore_wait(self.credits.at[4 + self.kind], 1)

        for which in range(2):
            if which == 0:
                self.waits[2, s]()
                target = self.land.at[1, s]
                add_pieces(target, self.grads.at[place.row, s], target)
            else:
                self.waits[1, s]()
                self.waits[3, s]()
                target = self.land.at[2, s]
                add_pieces(target, self.land.at[0, s], target)
            copy = pltpu.make_async_remote_copy(
                target,
                self.ends.at[which, s],
                copies.sem(),
                copies.sem(),
                device_id=place.to_dp(),
                device_id_type=MESH,
            )
            self.to_inner[which, s] = copy

            @pl.when(self.is_end)
            def _():
                copy.start()

    def to_middle(self, s):
        place, copies = self.place, self.copies
        if s == 0:
            self.across = {}
            if self.again:

                @pl.when(self.is_inner)
                def _():
                    pl.semaphore_wait(self.credits.at[8 + self.kind], 1)

        for which in range(2):
            half = self.ends.at[which, s]
            copy = pltpu.make_async_remote_copy(
                half,
                self.inner.at[which, s],
                copies.sem(),
                copies.sem(),
                device_id={"dp": 3 - place.dp},
                device_id_type=MESH,
            )
            self.across[which, s] = copy

            @pl.when(self.is_inner)
            def _():
                self.to_inner[which, s].wait_recv()
                add_pieces(half, self.land.at[1 + which, s], half)
                copy.start()

        if s == self.count - 1:

            @pl.when(self.is_end)
            def _():
                for copy in self.to_inner.values():
                    copy.wait_send()

            for sent in self.sent:
                sent()
            if not self.again:
                for j in range(1, 4):
                    pl.semaphore_signal(
                        self.credits.at[self.kind],
                        inc=1,
                        device_id=place.to_row(j),
                        device_id_type=MESH,
                    )

    def back(self, s):
        place, copies = self.place, self.copies
        if s == 0:
            self.out_copies = []
        for which in range(2):
            total = self.inner.at[which, s]
            home = self.home(which, s)
            copy = pltpu.make_async_remote_copy(
                total,
                home,
                copies.sem(),
                copies.sem(),
                device_id=place.to_dp(),
                device_id_type=MESH,
            )
            here = pltpu.make_async_copy(total, home, copies.sem())
            self.out_copies.append((copy, here))

            @pl.when(self.is_inner)
            def _():
                self.across[which, s].wait_recv()
                add_pieces(total, self.ends.at[which, s], total)
                copy.start()
                here.start()

    def finish(self):
        place = self.place

        @pl.when(self.is_inner)
        def _():
            for copy in self.across.values():
                copy.wait_send()
            for copy, here in self.out_copies:
                copy.wait_send()
                here.wait()
            if not self.again:
                pl.semaphore_signal(
                    self.credits.at[4 + self.kind], inc=1, device_id=place.to_dp(), device_id_type=MESH
                )
                pl.semaphore_signal(
                    self.credits.at[8 + self.kind],
                    inc=1,
                    device_id={"dp": 3 - place.dp},
                    device_id_type=MESH,
                )

        @pl.when(self.is_end)
        def _():
            for copy, here in self.out_copies:
                copy.wait_recv()


def backward_body(*refs):
    (
        grad_in,
        wide_ref,
        seg_row_ref,
        triple_in,
        output_in,
        up_in,
        down_in_w,
        attn_in,
        rows_in,
        mixed_in,
        log_in,
        mlp_in,
        slope_in,
        active_in,
        stream_in,
        result_ref,
        input_grad_ref,
        small_out,
        triple_out,
        output_out,
        up_out,
        down_out,
        triple_w,
        output_w,
        up_w,
        down_w,
        attn,
        rows,
        mixed,
        logs,
        mlp,
        slope,
        active,
        start,
        middle,
        down_in,
        hidden,
        branch,
        rows_grad,
        mixed_grad,
        pair_total,
        grad,
        mine,
        give,
        got_core,
        chip_sum,
        got_col,
        sums,
        lines,
        line_land,
        dp_land,
        *rest,
    ) = refs
    grads, land, ends, inner = rest[0:4], rest[4:8], rest[8:12], rest[12:16]
    credits, sems = rest[16:]
    place = Place()
    copies = Copies(sems)
    core, sibling = place.core, 1 - place.core
    others = [{"dp": (place.dp + i) % 4} for i in range(1, 4)]
    greet(place, [place.to_row(1), place.to_row(2), place.to_row(3), place.to_col(), *others])
    own_lanes = span(place.row * WIDTH, WIDTH)

    def part(k, c):
        return span(k * SPAN + c * OWN, OWN)

    ready = {}

    def load(name, layer):
        source, target = {
            "triple_w": (triple_in, triple_w),
            "output_w": (output_in, output_w),
            "up_w": (up_in, up_w),
            "down_w": (down_in_w, down_w),
            "attn": (attn_in, attn),
            "rows": (rows_in, rows),
            "mixed": (mixed_in, mixed),
            "logs": (log_in, logs),
            "mlp": (mlp_in, mlp),
            "slope": (slope_in, slope),
            "active": (active_in, active),
            "start": (stream_in, start),
            "middle": (stream_in, middle),
        }[name]
        if name in ("start", "middle"):
            ready[name] = [copies.local(source.at[layer, int(name == "middle")], target).wait]
        elif name.endswith("_w"):
            ready[name] = [copies.local(source.at[layer], target).wait]
        else:
            ready[name] = [
                copies.local(source.at[layer, k], target.at[k * SPAN : (k + 1) * SPAN]).wait
                for k in range(CHUNKS)
            ]

    def need(name):
        for wait in ready.pop(name, ()):
            wait()

    first_waits = [
        copies.local(grad_in.at[k], down_in.at[part(k, core)]).wait for k in range(CHUNKS)
    ]
    top = LAYERS - 1
    for name in ("active", "down_w", "slope", "up_w", "mlp", "middle"):
        load(name, top)
    for name in ("output_w", "rows", "logs", "triple_w", "mixed", "attn", "start"):
        load(name, top)
    sums[...] = jnp.zeros_like(sums)
    lines[...] = jnp.zeros_like(lines)

    def share(target, k):
        return copies.trade(
            target.at[part(k, core)], target.at[part(k, core)], target.at[part(k, sibling)], place.to_row(1)
        )

    def columns(value):
        return jnp.sum(value.reshape(-1, 8, value.shape[1]), axis=0)

    def gain(layer, which):
        return wide_ref[2 * layer + which : 2 * layer + which + 1, :]

    sent_core = []
    sent_col, col_waits = [None] * CHUNKS, [None] * CHUNKS

    def core_free():
        while sent_core:
            sent_core.pop()()

    def start_core(stage, k):
        sent, got = copies.trade(
            give, got_core.at[stage, k], got_core.at[stage, k], place.to_row(1)
        )
        sent_core.append(sent)
        return got

    def settle(stage, k, got):
        got()
        if sent_col[k] is not None:
            sent_col[k]()

        def add(at):
            here = pl.ds(at, STRIP)
            chip_sum[k, here, :] = (mine[here, :] + got_core[stage, k, here, :].astype(f32)).astype(bf16)

        strips(OWN, add)
        sent_col[k], col_waits[k] = copies.trade(
            chip_sum.at[k], got_col.at[stage, k], got_col.at[stage, k], place.to_col()
        )

    def take_col(stage, k, layer, which, stream, target):
        col_waits[k]()
        scale = gain(layer, which)

        def back(at):
            here = pl.ds(at, STRIP)
            grad_out = chip_sum[k, here, :].astype(f32) + got_col[stage, k, here, :].astype(f32)
            normed, inv_std = norm_parts(stream[k, here, :])
            scaled = grad_out * scale
            total = grad[k, here, :] + inv_std * (
                scaled - mean_lanes(scaled) - normed * mean_lanes(scaled * normed)
            )
            low = total.astype(bf16)
            grad[k, here, :] = total
            target[pl.ds(pl.multiple_of(k * SPAN + core * OWN + at, STRIP), STRIP), :] = low
            sums[layer, which] += columns(grad_out * normed)
            sums[layer, 2 + which] += columns(grad_out)
            if which == 1:
                sums[layer, 4] += columns(low.astype(f32))
            elif layer:
                sums[layer - 1, 5] += columns(low.astype(f32))

        strips(OWN, back)

    shares = [None] * CHUNKS
    for k in reversed(range(CHUNKS)):
        first_waits[k]()
        shares[k] = share(down_in, k)
    for k in reversed(range(CHUNKS)):

        def widen(at, k=k):
            low = down_in[pl.ds(pl.multiple_of(k * SPAN + core * OWN + at, STRIP), STRIP), :]
            value = low.astype(f32)
            grad[k, pl.ds(at, STRIP), :] = value
            sums[top, 5] += columns(value)

        strips(OWN, widen)

    reductions = {
        (layer, kind): Reduction(
            kind,
            layer,
            place,
            copies,
            grads,
            land,
            ends,
            inner,
            (triple_out, output_out, up_out, down_out),
            credits,
        )
        for layer in range(LAYERS)
        for kind in range(4)
    }

    def weight_grad(layer, kind):
        if kind == 0:
            need("attn")
            for pair in range(2):
                for third in range(3):
                    value = dot_tn(
                        attn[:, pair * 512 : (pair + 1) * 512],
                        rows_grad[:, third * WIDTH : (third + 1) * WIDTH],
                    ).astype(bf16)
                    for b in range(2):
                        grads[0][2 * pair + b, third] = value[b * WIDTH : (b + 1) * WIDTH]
        elif kind == 1:
            need("mixed")
            value = dot_tn(mixed[...], branch[...]).astype(bf16)
            for b in range(4):
                grads[1][b, 0] = value[:, b * WIDTH : (b + 1) * WIDTH]
        elif kind == 2:
            need("mlp")
            for b in range(4):
                value = dot_tn(mlp[:, b * WIDTH : (b + 1) * WIDTH], hidden[...]).astype(bf16)
                for s in range(4):
                    grads[2][b, s] = value[s * (WIDTH // 4) : (s + 1) * (WIDTH // 4)]
        else:
            need("active")
            for pair in range(4):
                value = dot_tn(active[:, pair * WIDTH : (pair + 1) * WIDTH], down_in[...]).astype(bf16)
                for b in range(4):
                    grads[3][b, pair] = value[:, b * WIDTH : (b + 1) * WIDTH]
        reductions[layer, kind].send()

    def pump(point):
        for layer, kind, s, step in PLAN.get(point, ()):
            item = reductions[layer, kind]
            if step == 3:
                item.finish()
            else:
                (item.over_chips, item.to_middle, item.back)[step](s)

    landed = []

    def held(j, k):
        return span(place.rows[j] // 2 * LEN + k * SPAN + place.cores[j] * OWN, OWN)

    def to_features(k, source, target):
        mine_rows = part(k, core)
        landed.append(copies.local(source.at[mine_rows, own_lanes], target.at[held(0, k), :]).wait)
        for j in (2, 3, 1):
            sent, got = copies.trade(
                source.at[mine_rows, span(place.rows[j] * WIDTH, WIDTH)],
                target.at[held(0, k), :],
                target.at[held(j, k), :],
                place.to_row(j),
            )
            landed.extend([sent, got])

    for layer in reversed(range(LAYERS)):
        upper = layer == top
        for k in reversed(range(CHUNKS)):
            if upper:
                if k == CHUNKS - 1:
                    for i in reversed(range(CHUNKS)):
                        shares[i][1]()
                    weight_grad(layer, 3)
            else:
                pump(f"e{k}")
                need("start")
                take_col(1, k, layer + 1, 0, start, down_in)
                shares[k] = share(down_in, k)
                if k == 0:
                    load("start", layer)
                pump(f"f{k}")
            need("down_w")
            need("slope")

            def shrink(c, k=k):
                for block in range(4):
                    cols = slice(block * WIDTH, (block + 1) * WIDTH)
                    value = dot_nt(down_in[part(k, c), :], down_w[cols, :])
                    value = (value * slope[part(k, c), cols].astype(f32)).astype(bf16)
                    hidden[part(k, c), cols] = value
                    lines[layer, 8:16, cols] += columns(value.astype(f32))

            shrink(core)
            if not upper:
                shares[k][1]()
            shrink(sibling)
            need("up_w")
            core_free()
            give[...] = dot_nt(hidden[part(k, sibling), :], up_w[...]).astype(bf16)
            got = start_core(0, k)
            mine[...] = dot_nt(hidden[part(k, core), :], up_w[...])
            shares[k][0]()
            pump(f"a{k}" if upper else f"g{k}")
            settle(0, k, got)
        if not upper:
            weight_grad(layer, 3)
            pump("v0")
        weight_grad(layer, 2)
        pump(f"u{layer}")
        if layer:
            for name in ("active", "down_w", "slope", "up_w", "mlp"):
                load(name, layer - 1)
        else:
            load("active", top)
            load("down_w", top)
        for k in reversed(range(CHUNKS)):
            point = f"{k}" if upper else f"{k}L"
            pump(f"b{point}")
            need("middle")
            take_col(0, k, layer, 1, middle, branch)
            shares[k] = share(branch, k)
            if k == 0:
                load("middle", layer - 1 if layer else top)
            need("output_w")

            def narrow(c, k=k):
                mixed_grad[part(0, c), :] = dot_nt(branch[part(k, c), :], output_w[...]).astype(bf16)

            narrow(core)
            need("rows")
            need("logs")
            if k == CHUNKS - 1:
                pair_total[...] = jnp.zeros_like(pair_total)
            pump(f"c{point}")
            shares[k][1]()
            narrow(sibling)
            attend_back_chunk(k, rows, logs, seg_row_ref, mixed_grad, pair_total, rows_grad)
            need("triple_w")
            core_free()
            pump(f"m{point}")

            def project(c, k=k):
                value = dot_nt(rows_grad[part(k, c), :WIDTH], triple_w[0])
                for third in range(1, 3):
                    cols = slice(third * WIDTH, (third + 1) * WIDTH)
                    value += dot_nt(rows_grad[part(k, c), cols], triple_w[third])
                return value

            give[...] = project(sibling).astype(bf16)
            got = start_core(1, k)
            mine[...] = project(core)
            shares[k][0]()
            pump(f"d{point}")
            settle(1, k, got)
        weight_grad(layer, 1)
        weight_grad(layer, 0)
        for line, cols in ((0, slice(0, WIDTH)), (1, slice(2 * WIDTH, 3 * WIDTH))):
            value = rows_grad[:SPAN, cols].astype(f32)
            for k in range(1, CHUNKS):
                value += rows_grad[k * SPAN : (k + 1) * SPAN, cols].astype(f32)
            lines[layer, 0:1, line * WIDTH : (line + 1) * WIDTH] = jnp.sum(value, axis=0, keepdims=True)
        pump(f"w{layer}")
        if layer:
            for name in ("output_w", "rows", "logs", "triple_w", "mixed", "attn"):
                load(name, layer - 1)
    for k in reversed(range(CHUNKS)):
        pump(f"h{k}")
        need("start")
        take_col(1, k, 0, 0, start, down_in)
        to_features(k, down_in, input_grad_ref)
    need("active")
    need("down_w")
    for k in reversed(range(CHUNKS)):
        core_free()
        give[...] = dot(active[part(k, sibling), :], down_w[...]).astype(bf16)
        got = start_core(0, k)
        mine[...] = dot(active[part(k, core), :], down_w[...])
        settle(0, k, got)
    zero = jnp.zeros((1, WIDTH // 2), f32)
    for layer in range(LAYERS):
        found = [jnp.sum(sums[layer, i], axis=0, keepdims=True) for i in range(6)]
        hidden_sum = jnp.sum(lines[layer, 8:16, :], axis=0, keepdims=True)
        base = layer * LINES
        line_land[0, base : base + LINES, :] = jnp.zeros((LINES, D), f32)
        for i in range(6):
            line_land[0, base + i : base + i + 1, :] = found[i]
        for b in range(2):
            at = span((2 * core + b) * WIDTH, WIDTH)
            half = slice(b * (WIDTH // 2), (b + 1) * (WIDTH // 2))
            line_land[0, base + 6 : base + 7, at] = jnp.concatenate(
                [lines[layer, 0:1, :WIDTH][:, half], lines[layer, 0:1, WIDTH : 2 * WIDTH][:, half]], axis=1
            )
            for a in range(2):
                cols = slice((2 * b + a) * WIDTH, (2 * b + a + 1) * WIDTH)
                line_land[0, base + 7 + a : base + 8 + a, at] = hidden_sum[:, cols]
    line_waits = []
    for j in range(1, 4):
        there = span(place.rows[j] * WIDTH, WIDTH)
        sent, got = copies.trade(
            line_land.at[0, :, there],
            dp_land.at[3 + j],
            dp_land.at[3 + j],
            place.to_row(j),
        )
        copies.open.append(sent)
        line_waits.append(got)
    pump("tail1")
    need("middle")
    last_bias = wide_ref[10 + top : 11 + top, :]
    for k in reversed(range(CHUNKS)):
        col_waits[k]()

        def finish(at, k=k):
            here = pl.ds(at, STRIP)
            total = chip_sum[k, here, :].astype(f32) + got_col[0, k, here, :].astype(f32)
            branch[pl.ds(pl.multiple_of(k * SPAN + core * OWN + at, STRIP), STRIP), :] = (
                middle[k, here, :] + (total + last_bias)
            ).astype(bf16)

        strips(OWN, finish)
        to_features(k, branch, result_ref)
    pump("tail2")
    for wait in line_waits:
        wait()
    total = line_land[0, :, own_lanes]
    dp_land[place.dp] = total + dp_land[4] + dp_land[5] + dp_land[6]
    line_waits = []
    for i, device in enumerate(others):
        back = (place.dp + 3 - i) % 4
        sent, got = copies.sem(), copies.sem()
        out = pltpu.make_async_remote_copy(
            dp_land.at[place.dp], dp_land.at[place.dp], sent, got, device_id=device, device_id_type=MESH
        )
        arriving = pltpu.make_async_remote_copy(
            dp_land.at[back], dp_land.at[back], sent, got, device_id=device, device_id_type=MESH
        )
        out.start()
        copies.open.append(out.wait_send)
        line_waits.append(arriving.wait_recv)
    pump("tail3")
    for wait in line_waits:
        wait()
    small_out[...] = dp_land[0] + dp_land[1] + dp_land[2] + dp_land[3]
    for kind in (3, 2, 1, 0):
        reductions[0, kind].finish()
    core_free()
    for k in range(CHUNKS):
        sent_col[k]()
    for wait in landed:
        wait()
    copies.finish()


def backward_call(tokens_shape, grad_in, wide, seg_row, weights, saved, stream):
    units = weights[2].shape[2]
    scratch = [
        ((3, D, WIDTH), bf16),
        ((WIDTH, D), bf16),
        ((D, units), bf16),
        ((units, D), bf16),
        ((LEN, D), bf16),
        ((LEN, 3 * WIDTH), bf16),
        ((LEN, WIDTH), bf16),
        ((LEN, 128), f32),
        ((LEN, D), bf16),
        ((LEN, units), bf16),
        ((LEN, units), bf16),
        ((CHUNKS, OWN, D), f32),
        ((CHUNKS, OWN, D), f32),
        ((LEN, D), bf16),
        ((LEN, units), bf16),
        ((LEN, D), bf16),
        ((LEN, 3 * WIDTH), bf16),
        ((SPAN, WIDTH), bf16),
        ((LEN, 2 * WIDTH), f32),
        ((CHUNKS, OWN, D), f32),
        ((OWN, D), f32),
        ((OWN, D), bf16),
        ((2, CHUNKS, OWN, D), bf16),
        ((CHUNKS, OWN, D), bf16),
        ((2, CHUNKS, OWN, D), bf16),
        ((LAYERS, 6, 8, D), f32),
        ((LAYERS, 16, D), f32),
        ((1, LAYERS * LINES, D), f32),
        ((7, LAYERS * LINES, WIDTH), f32),
    ]
    for parts in (4, 3, 2, 2):
        scratch += [((parts, *piece), bf16) for piece in PIECES]
    outs = [
        (tokens_shape, bf16),
        (tokens_shape, bf16),
        ((LAYERS * LINES, WIDTH), f32),
        ((LAYERS, 3, WIDTH, 2 * WIDTH), bf16),
        ((LAYERS, 2 * WIDTH, WIDTH), bf16),
        ((LAYERS, WIDTH, 2 * units), bf16),
        ((LAYERS, 2 * units, WIDTH), bf16),
    ]
    anywhere = pl.BlockSpec(memory_space=pl.ANY)
    inside = pl.BlockSpec(memory_space=pltpu.VMEM)
    return pl.pallas_call(
        backward_body,
        out_shape=[like(*v) for v in outs],
        in_specs=[anywhere] + [inside] * 2 + [anywhere] * 12,
        out_specs=[anywhere] * 2 + [inside] + [anywhere] * 4,
        scratch_shapes=[pltpu.VMEM(*v) for v in scratch]
        + [pltpu.SemaphoreType.REGULAR((12,)), pltpu.SemaphoreType.DMA((840,))],
        compiler_params=pltpu.CompilerParams(
            collective_id=1, has_side_effects=True, vmem_limit_bytes=60 * 1024 * 1024
        ),
    )(grad_in, wide, seg_row, *weights, *saved, stream)


def pair_plan(
    tokens,
    segments,
    norm_gain,
    norm_shift,
    triple_weight,
    triple_bias,
    output_weight,
    output_bias,
    up_weight,
    up_bias,
    down_weight,
    down_bias,
    cotangent,
):
    chip = lax.axis_index("row") // 2
    seg_pack = lax.dynamic_slice_in_dim(segments, chip * LEN, LEN, 0)
    seg_col, seg_row = seg_pack[:, None], seg_pack[None, :]
    grad_in, wide, *kept, stream = forward_call(
        tokens,
        cotangent,
        (norm_gain, norm_shift, output_bias, down_bias, triple_bias, up_bias),
        seg_col,
        seg_row,
        jnp.swapaxes(triple_weight, 1, 2),
        output_weight,
        up_weight,
        down_weight,
    )
    result, input_grad, small, triple_grad, output_grad, up_grad, down_grad = backward_call(
        tokens.shape, grad_in, wide, seg_row.astype(f32), kept[:4], kept[4:], stream
    )
    small = small.reshape(LAYERS, LINES, WIDTH)
    return (
        result,
        input_grad.astype(f32),
        small[:, 0:2],
        small[:, 2:4],
        jnp.swapaxes(triple_grad, 1, 2).astype(f32),
        small[:, 6].reshape(LAYERS, 2, WIDTH // 2),
        output_grad.astype(f32),
        small[:, 4],
        up_grad.astype(f32),
        small[:, 7:9].reshape(LAYERS, 2 * WIDTH),
        down_grad.astype(f32),
        small[:, 5],
    )


def solution(mesh):
    in_specs = (
        P("dp", "row"),
        P("dp"),
        P(None, None, "row"),
        P(None, None, "row"),
        P(None, "row", None, "col"),
        P(None, None, ("col", "row")),
        P(None, "col", "row"),
        P(None, "row"),
        P(None, "row", "col"),
        P(None, ("col", "row")),
        P(None, "col", "row"),
        P(None, "row"),
        P("dp", "row"),
    )
    out_specs = (
        P("dp", "row"),
        P("dp", "row"),
        P(None, None, "row"),
        P(None, None, "row"),
        P(None, "row", None, "col"),
        P(None, None, ("col", "row")),
        P(None, "col", "row"),
        P(None, "row"),
        P(None, "row", "col"),
        P(None, ("col", "row")),
        P(None, "col", "row"),
        P(None, "row"),
    )
    shape = mesh.shape

    def on_device(*arrays):
        if fits_pairs(shape, arrays):
            return pair_plan(*arrays)
        return general_plan(*arrays)

    return jax.shard_map(
        on_device, mesh=mesh, in_specs=in_specs, out_specs=out_specs, check_vma=False
    )
```
